32 devices in a mesh: fsdp: 4 (over z), replica: 4 (over y, core), tm: 2 (over x).
Axes of the slice: x: 2, y: 2, z: 4, core: 2. Of those that a mesh axis runs over, the one named last changes fastest.
Arguments:
- clip_input: bfloat16 [4, 8, 16, 16, 512], P('replica', 'tm'), may hold values from -6 to 6
- first_kernel: bfloat16 [27, 512, 512], P(None, None, 'fsdp'), may hold values from -0.0546875 to 0.0546875
- second_kernel: bfloat16 [27, 512, 512], P(None, 'fsdp'), may hold values from -0.0546875 to 0.0546875
- out_grad: bfloat16 [4, 2, 4, 4, 512], P('replica', 'tm'), may hold values from -2 to 2
- tap_mix: float32 [2, 27, 27], replicated, may hold values from -0.14 to 1.4
- left_panels: float32 [2, 512, 512], P(None, 'fsdp'), may hold values from -0.05 to 2
- right_panels: float32 [2, 512, 512], P(None, 'fsdp', ('replica', 'tm')), may hold values from -0.05 to 2
Outputs:
- update: bfloat16 [2, 27, 512, 512], P(None, None, 'fsdp', ('replica', 'tm'))
The draws below stay inside these ranges and needn't reach their ends.
All inputs are finite; a program needn't handle non-finite values.
Results may differ from the reference program's by a relative error of at most 0.0049.
Values may be sent and summed in bfloat16 or wider, within the bound.
No kernel may reach another device: no remote copies, remote signals or barrier semaphores. Data moves between devices by JAX's collectives and lax.ppermute only.
A program may use at most 128 MiB of HBM per device.

```python
import jax
import jax.numpy as jnp
from jax import lax

CHANNELS = 512
TAPS = 27
FR_DEV = 4
SIDE = 16
CLIPS = 4
FRAMES = 8
N_REPLICA = 4
N_TM = 2


def symmetric_panels(seed_key):
    off_key, diag_key = jax.random.split(seed_key)
    raw_entries = jax.random.uniform(off_key, (2, CHANNELS, CHANNELS), jnp.float32, -0.05, 0.05)
    symmetric = 0.5 * (raw_entries + jnp.swapaxes(raw_entries, 1, 2))
    diag_vals = jax.random.uniform(diag_key, (2, CHANNELS), jnp.float32, 0.5, 2.0)
    identity = jnp.eye(CHANNELS, dtype=jnp.float32)
    return symmetric * (1.0 - identity) + diag_vals[:, :, None] * identity


def draw_left_panels(key, part):
    return symmetric_panels(jax.random.fold_in(key, 11))


def draw_right_panels(key, part):
    return symmetric_panels(jax.random.fold_in(key, 23))


def draw_tap_mix(key, part):
    off_key, diag_key = jax.random.split(jax.random.fold_in(key, 37))
    off_entries = jax.random.uniform(off_key, (2, TAPS, TAPS), jnp.float32, -0.14, 0.14)
    diag_vals = jax.random.uniform(diag_key, (2, TAPS), jnp.float32, 0.6, 1.4)
    identity = jnp.eye(TAPS, dtype=jnp.float32)
    return off_entries * (1.0 - identity) + diag_vals[:, :, None] * identity


def level_of(rng, shape, shards, low, largest):
    loudness, own = 1.0, jax.random.fold_in(rng, 6)
    for axis_at, parts in shards:
        draws = jnp.exp(jax.random.uniform(jax.random.fold_in(own, axis_at), (parts,), jnp.float32, low / len(shards), largest / len(shards)))
        loudness = loudness * jnp.repeat(draws, shape[axis_at] // parts).reshape([-1 if axis == axis_at else 1 for axis in range(len(shape))])
    return loudness


def bell_draw(stream_key, extent, deviation, limit, cuts=(), held_as=jnp.bfloat16):
    entries = deviation * jax.random.normal(stream_key, extent, jnp.float32)
    if cuts:
        entries = entries * level_of(stream_key, extent, cuts, -0.22, 0.18)
    return jnp.clip(entries, -limit, limit).astype(held_as)


def setup_inputs(seed: int = 0) -> dict:
    arg_keys = jax.random.split(jax.random.key(seed), 8)
    clip_input = bell_draw(arg_keys[0], (CLIPS, FRAMES, SIDE, SIDE, CHANNELS), 1.0, 6.0, ((0, 4), (1, 2)))
    first_kernel = bell_draw(arg_keys[1], (TAPS, CHANNELS, CHANNELS), (TAPS * CHANNELS) ** -0.5, 0.0546875, ((2, 4),))
    second_kernel = bell_draw(arg_keys[2], (TAPS, CHANNELS, CHANNELS), (TAPS * CHANNELS) ** -0.5, 0.0546875, ((1, 4),))
    out_grad = bell_draw(arg_keys[3], (CLIPS, FRAMES // 4, SIDE // 4, SIDE // 4, CHANNELS), ((N_REPLICA * N_TM * FR_DEV * SIDE * SIDE // 144) ** -0.5), 2.0, ((0, 4), (1, 2)))
    tap_mix = draw_tap_mix(jax.random.fold_in(arg_keys[7], 71), 0)
    left_panels = draw_left_panels(jax.random.fold_in(arg_keys[7], 71), 0)
    right_panels = draw_right_panels(jax.random.fold_in(arg_keys[7], 71), 0)
    return dict(clip_input=clip_input, first_kernel=first_kernel, second_kernel=second_kernel, out_grad=out_grad, tap_mix=tap_mix, left_panels=left_panels, right_panels=right_panels)


def tap_patches(padded, out_frames, out_side):
    pieces_list = []
    for tap_index in range(TAPS):
        along_time = tap_index // 9
        along_rows = (tap_index // 3) % 3
        along_cols = tap_index % 3
        pieces_list.append(padded[:, along_time:along_time + 2 * out_frames:2, along_rows:along_rows + 2 * out_side:2, along_cols:along_cols + 2 * out_side:2, :])
    return jnp.concatenate(pieces_list, axis=-1)


def spread_back(grad_shape, columns, out_frames, out_side, channels):
    total = jnp.zeros(grad_shape, jnp.float32)
    for tap_index in range(TAPS):
        along_time = tap_index // 9
        along_rows = (tap_index // 3) % 3
        along_cols = tap_index % 3
        total = total.at[:, along_time:along_time + 2 * out_frames:2, along_rows:along_rows + 2 * out_side:2, along_cols:along_cols + 2 * out_side:2, :].add(columns[..., tap_index * channels:(tap_index + 1) * channels])
    return total


def reference(clip_input, first_kernel, second_kernel, out_grad, tap_mix, left_panels, right_panels):
    highest = lax.Precision.HIGHEST
    clip_count = clip_input.shape[0]
    frames = clip_input.shape[1]
    side_cells = clip_input.shape[2]
    channels = clip_input.shape[4]
    half_frames = frames // 2
    half_side = side_cells // 2
    quarter_frames = frames // 4
    quarter_side = side_cells // 4
    padding = ((0, 0), (1, 0), (1, 0), (1, 0), (0, 0))
    padded_input = jnp.pad(clip_input, padding)
    first_patches = tap_patches(padded_input, half_frames, half_side).reshape(-1, TAPS * channels).astype(jnp.float32)
    pre_act = jnp.dot(first_patches, first_kernel.reshape(TAPS * channels, channels).astype(jnp.float32), precision=highest)
    hidden = jax.nn.silu(pre_act).astype(jnp.bfloat16)
    padded_hidden = jnp.pad(hidden.reshape(clip_count, half_frames, half_side, half_side, channels), padding)
    second_patches = tap_patches(padded_hidden, quarter_frames, quarter_side).reshape(-1, TAPS * channels).astype(jnp.float32)
    grad_rows = out_grad.reshape(-1, channels).astype(jnp.float32)
    second_grad = jnp.dot(grad_rows.T, second_patches, precision=highest).reshape(channels, TAPS, channels).transpose(1, 0, 2)
    back_columns = jnp.dot(grad_rows, second_kernel.reshape(TAPS * channels, channels).astype(jnp.float32).T, precision=highest)
    back_columns = back_columns.reshape(clip_count, quarter_frames, quarter_side, quarter_side, TAPS * channels)
    spread = spread_back(padded_hidden.shape, back_columns, quarter_frames, quarter_side, channels)
    hidden_grad = spread[:, 1:, 1:, 1:, :].reshape(-1, channels)
    sigmoid_vals = jax.nn.sigmoid(pre_act)
    pre_grad = (hidden_grad * sigmoid_vals * (1.0 + pre_act * (1.0 - sigmoid_vals))).astype(jnp.bfloat16)
    first_grad = jnp.dot(first_patches.T, pre_grad.astype(jnp.float32), precision=highest).reshape(TAPS, channels, channels)
    stacked = jnp.stack([first_grad, second_grad])
    tap_mixed = jnp.einsum('lst,ltij->lsij', tap_mix, stacked, precision=highest)
    left_done = jnp.einsum('lik,lskj->lsij', left_panels, tap_mixed, precision=highest)
    result = jnp.einsum('lsij,ljk->lsik', left_done, right_panels, precision=highest)
    return result.astype(jnp.bfloat16)
```

```python
import functools

import jax
import jax.numpy as jnp
import numpy as np
from jax import lax
from jax.experimental import pallas as pl
from jax.experimental.pallas import tpu as pltpu
from jax.sharding import PartitionSpec as P

TAPS = 27
F32, BF16 = jnp.float32, jnp.bfloat16
NT = (((1,), (1,)), ((), ()))
VMEM = pl.BlockSpec(memory_space=pltpu.VMEM)
ANY = pl.BlockSpec(memory_space=pl.ANY)


def shifted(block, axis, distance):
    devices = range(lax.axis_size(axis))
    route = [(i - distance, i) for i in devices if i - distance in devices]
    return lax.ppermute(block, axis, route)


def dot(left, right):
    return jnp.dot(left, right, preferred_element_type=F32)


def dot_nt(left, right):
    return lax.dot_general(left, right, NT, preferred_element_type=F32)


def halves(value):
    high = value.astype(BF16)
    return high, (value - high.astype(F32)).astype(BF16)


def parity_picks(frame_pairs, side):
    half = side // 2
    picks = np.zeros((frame_pairs, half, side, 2, frame_pairs, half, half), np.float32)
    for t in range(frame_pairs):
        for row in range(half):
            for x in range(side):
                picks[t, row, x, x % 2, t, row, x // 2] = 1
    size = frame_pairs * half * side
    return picks.reshape(size, size)


def patch_picks(side):
    half = side // 2
    even = np.zeros((1, 3, half, half, half, side), np.float32)
    odd = np.zeros((2, 3, half, half, half, side), np.float32)
    for c in range(3):
        for y in range(half):
            for x in range(half):
                column = 2 * x + c - 1
                if column < 0:
                    continue
                even[0, c, y, x, y, column] = 1
                if y > 0:
                    odd[0, c, y, x, y - 1, column] = 1
                odd[1, c, y, x, y, column] = 1
    return even.reshape(-1, half * side), odd.reshape(-1, half * side)


def spread_picks(half):
    quarter = half // 2
    picks = np.zeros((3, 3, half, half, quarter, quarter), np.float32)
    for b in range(3):
        for c in range(3):
            for out_y in range(quarter):
                for out_x in range(quarter):
                    y, x = 2 * out_y + b - 1, 2 * out_x + c - 1
                    if y >= 0 and x >= 0:
                        picks[b, c, y, x, out_y, out_x] = 1
    return picks.reshape(9 * half * half, quarter * quarter)


def clip_picks(frames, half):
    quarter = half // 2
    picks = np.zeros((3, 3, 3, frames // 2, quarter, quarter, frames, half, half), np.float32)
    for tap in range(TAPS):
        a, b, c = tap // 9, tap // 3 % 3, tap % 3
        for t in range(frames // 2):
            for y in range(quarter):
                for x in range(quarter):
                    place = (2 * t + a - 1, 2 * y + b - 1, 2 * x + c - 1)
                    if min(place) >= 0:
                        picks[(a, b, c, t, y, x) + place] = 1
    return picks.reshape(TAPS * frames // 2 * quarter * quarter, frames * half * half)


def project_kernel(x_ref, left_ref, pick_ref, out_ref):
    frames, half, _, side, channels = x_ref.shape
    wide = left_ref.shape[0]
    both = jnp.concatenate(halves(left_ref[...]), axis=0)
    for time in range(2):
        for row in range(2):
            block = jnp.concatenate(
                [
                    x_ref[frame, :, row].reshape(half * side, channels)
                    for frame in range(time, frames, 2)
                ],
                axis=0,
            )
            full = dot_nt(both, block)
            small = (full[:wide] + full[wide:]).astype(BF16)
            ordered = dot(small, pick_ref[...]).astype(BF16)
            size = ordered.shape[1] // 2
            for column in range(2):
                at = (4 * time + 2 * row + column) * wide
                out_ref[at : at + wide, :] = ordered[:, column * size : (column + 1) * size]


def hidden_kernel(
    x_ref, prior_ref, grad_ref, later_ref, even_ref, odd_ref, spread_ref, first_any, second_any,
    out_ref, patches, spread, first, second, arrived,
):
    frames, half, _, side, channels = x_ref.shape
    cells = half * half
    copies = {}
    for a in (1, 2, 0):
        for at, (source, target) in enumerate(((second_any, second), (first_any, first))):
            copies[at, a] = pltpu.make_async_copy(
                source.at[pl.ds(9 * a, 9)], target.at[pl.ds(9 * a, 9)], arrived.at[at, a]
            )
    for at in range(2):
        for a in (1, 2, 0):
            copies[at, a].start()
    for which, rows in enumerate((grad_ref, later_ref)):
        picked = dot(spread_ref[...], rows[...]).astype(BF16)
        for tap in range(9):
            spread[which, tap] = picked[tap * cells : (tap + 1) * cells]
    for frame in range(frames + 1):
        block = prior_ref if frame == 0 else x_ref.at[frame - 1]
        even = dot(even_ref[...], block[:, 0].reshape(half * side, channels)).astype(BF16)
        odd = dot(odd_ref[...], block[:, 1].reshape(half * side, channels)).astype(BF16)
        for c in range(3):
            patches[frame, c] = odd[c * cells : (c + 1) * cells]
            patches[frame, 3 + c] = even[c * cells : (c + 1) * cells]
            patches[frame, 6 + c] = odd[(3 + c) * cells : (4 + c) * cells]
    copies[0, 1].wait()
    copies[0, 2].wait()
    early = jnp.zeros((cells, second.shape[1]), F32)
    late = jnp.zeros((cells, second.shape[1]), F32)
    for tap in range(9):
        early += dot_nt(spread[0, tap], second[9 + tap])
        late += dot_nt(spread[0, tap], second[18 + tap])
    copies[0, 0].wait()
    for tap in range(9):
        late += dot_nt(spread[1, tap], second[tap])
    hidden_grad = jnp.concatenate([early, late], axis=0)
    pre = jnp.zeros((2 * cells, first.shape[2]), F32)
    for a in (1, 2, 0):
        copies[1, a].wait()
        for tap in range(9):
            rows = jnp.concatenate([patches[a, tap], patches[a + 2, tap]], axis=0)
            pre += dot(rows, first[9 * a + tap])
    sig = jax.nn.sigmoid(pre)
    out_ref[0] = (pre * sig).astype(BF16)
    out_ref[1] = (hidden_grad * sig * (1.0 + pre * (1.0 - sig))).astype(BF16)


def update_kernel(
    acts_ref, left_rows_ref, right_ref, left_ref, mix_ref, pick_ref,
    out_ref, grads, shifts, placed, raw, mixed, *, clip_parts, half,
):
    parts, slices, _, cells, _ = acts_ref.shape
    wide, channels = left_ref.shape
    lanes = right_ref.shape[2]
    clips = parts // clip_parts
    clip_cells = clip_parts * cells
    frames = clip_cells // (half * half)
    total = parts * cells
    for part in range(parts):
        rows = pl.ds(part * cells, cells)
        hidden, pre_grad = (
            jnp.concatenate([acts_ref[part, at, which] for at in range(slices)], axis=1)
            for which in range(2)
        )
        grads[0, rows, :] = dot(pre_grad, right_ref[0]) + dot(pre_grad, right_ref[1])
        grads[1, rows, :] = dot(hidden, right_ref[2]) + dot(hidden, right_ref[3])
    places = lax.broadcasted_iota(jnp.int32, (total, lanes), 0)
    frame = places // (half * half) % frames
    row = places // half % half
    column = places % half
    for shift in range(8):
        dt, dr, dc = shift // 4, shift // 2 % 2, shift % 2
        moved = grads[0, pl.ds((dt * half + dr) * half + dc, total), :]
        inside = (frame + dt < frames) & (row + dr < half) & (column + dc < half)
        shifts[shift] = jnp.where(inside, moved, 0.0).astype(BF16)
    outputs = clip_cells // 8
    for clip in range(clips):
        own = grads[1, pl.ds(clip * clip_cells, clip_cells), :].astype(BF16)
        picked = dot(pick_ref[...], own).astype(BF16)
        for tap in range(TAPS):
            placed[tap, pl.ds(clip * outputs, outputs), :] = picked[
                tap * outputs : (tap + 1) * outputs
            ]
    own_outputs = outputs // clip_parts
    blocks = channels // cells
    out_grad = jnp.concatenate(
        [
            jnp.concatenate(
                [
                    left_rows_ref[part, pl.ds(8 * wide + own_outputs * at, own_outputs), :]
                    for at in range(blocks)
                ],
                axis=1,
            )
            for part in range(parts)
        ],
        axis=0,
    )
    both = jnp.concatenate(halves(left_ref[...]), axis=0)
    full = dot_nt(both, out_grad)
    second_rows = (full[:wide] + full[wide:]).astype(BF16)
    for kind in range(8):
        time, line, place = kind // 4, kind // 2 % 2, kind % 2
        rows = jnp.concatenate(
            [left_rows_ref[part, pl.ds(kind * wide, wide), :] for part in range(parts)], axis=1
        )
        for a in (0, 2) if time else (1,):
            for b in (0, 2) if line else (1,):
                for c in (0, 2) if place else (1,):
                    tap = 9 * a + 3 * b + c
                    shift = 4 * (a == 0) + 2 * (b == 0) + (c == 0)
                    raw[tap] = dot(rows, shifts[shift]) + dot(second_rows, placed[tap])

    @pl.loop(0, wide // 8)
    def _(step):
        rows = pl.ds(pl.multiple_of(step * 8, 8), 8)
        taps = [raw[tap, rows, :] for tap in range(TAPS)]
        for out_tap in range(TAPS):
            acc = taps[0] * mix_ref[out_tap, pl.ds(0, 1), :]
            for tap in range(1, TAPS):
                acc += taps[tap] * mix_ref[out_tap, pl.ds(tap, 1), :]
            mixed[out_tap, rows, :] = acc

    for tap in range(TAPS):
        out_ref[0, tap] = mixed[tap, :, : lanes // 2].astype(BF16)
        out_ref[1, tap] = mixed[tap, :, lanes // 2 :].astype(BF16)


def shards(clip_input, first_kernel, second_kernel, out_grad, tap_mix, left_panels, right_panels):
    clips, frames, side, _, channels = clip_input.shape
    wide = first_kernel.shape[2]
    own_columns = right_panels.shape[2]
    half, quarter = side // 2, side // 4
    half_frames = frames // 2
    cells = half_frames * half * half
    parts = lax.axis_size("replica") * lax.axis_size("tm")
    slices = lax.axis_size("fsdp")
    assert clips == 1 and frames == 4
    x = clip_input.reshape(frames, half, 2, side, channels)
    grad_rows = out_grad.reshape(quarter * quarter, channels)
    prior = shifted(x[frames - 1 :], "tm", 1)[0]
    later = shifted(grad_rows, "tm", -1)

    picks = jnp.asarray(parity_picks(half_frames, side), BF16)
    projected = pl.pallas_call(
        project_kernel,
        out_shape=jax.ShapeDtypeStruct((8 * wide, cells), BF16),
        in_specs=[VMEM] * 3,
        out_specs=VMEM,
        compiler_params=pltpu.CompilerParams(vmem_limit_bytes=24 << 20),
        cost_estimate=pl.CostEstimate(
            flops=4 * frames * side * side * channels * wide,
            bytes_accessed=2 * frames * side * side * channels,
            transcendentals=0,
        ),
    )(x, left_panels[0], picks)
    blocks = channels // cells
    grad_blocks = grad_rows.reshape(-1, blocks, cells).transpose(1, 0, 2).reshape(-1, cells)
    left_rows = lax.all_gather(
        jnp.concatenate([projected, grad_blocks], axis=0), ("replica", "tm"), axis=0, tiled=False
    )
    right = lax.all_gather(right_panels, "fsdp", axis=1, tiled=True)
    high, low = halves(right)
    pads = (((0, 0), (0, own_columns)), ((0, 0), (own_columns, 0)))
    right = jnp.stack(
        [jnp.pad(value[layer], pads[layer]) for layer in range(2) for value in (high, low)]
    )
    mix = jnp.concatenate(
        [
            jnp.broadcast_to(tap_mix[layer, :, :, None], (TAPS, TAPS, own_columns))
            for layer in range(2)
        ],
        axis=2,
    )

    even, odd = patch_picks(side)
    acts = pl.pallas_call(
        hidden_kernel,
        out_shape=jax.ShapeDtypeStruct((2, cells, wide), BF16),
        in_specs=[VMEM] * 7 + [ANY] * 2,
        out_specs=VMEM,
        scratch_shapes=[
            pltpu.VMEM((frames + 1, 9, half * half, channels), BF16),
            pltpu.VMEM((2, 9, half * half, channels), BF16),
            pltpu.VMEM(first_kernel.shape, BF16),
            pltpu.VMEM(second_kernel.shape, BF16),
            pltpu.SemaphoreType.DMA((2, 3)),
        ],
        compiler_params=pltpu.CompilerParams(vmem_limit_bytes=32 << 20),
        cost_estimate=pl.CostEstimate(
            flops=3 * cells * TAPS * channels * wide,
            bytes_accessed=4 * TAPS * channels * wide,
            transcendentals=cells * wide,
        ),
    )(
        x, prior, grad_rows, later, jnp.asarray(even, BF16), jnp.asarray(odd, BF16),
        jnp.asarray(spread_picks(half), BF16), first_kernel, second_kernel,
    )
    every = lax.all_gather(acts, ("replica", "tm", "fsdp"), axis=0, tiled=False)
    every = every.reshape(parts, slices, 2, cells, wide)
    if wide % 128:
        every = every.transpose(0, 2, 3, 1, 4).reshape(parts, 1, 2, cells, channels)

    lanes = 2 * own_columns
    total = parts * cells
    clip_parts = lax.axis_size("tm")
    tail = (half + 1) * half + 8
    return pl.pallas_call(
        functools.partial(update_kernel, clip_parts=clip_parts, half=half),
        out_shape=jax.ShapeDtypeStruct((2, TAPS, wide, own_columns), BF16),
        in_specs=[VMEM] * 6,
        out_specs=VMEM,
        scratch_shapes=[
            pltpu.VMEM((2, total + tail, lanes), F32),
            pltpu.VMEM((8, total, lanes), BF16),
            pltpu.VMEM((TAPS, total // 8, lanes), BF16),
            pltpu.VMEM((TAPS, wide, lanes), F32),
            pltpu.VMEM((TAPS, wide, lanes), F32),
        ],
        compiler_params=pltpu.CompilerParams(vmem_limit_bytes=58 << 20),
    )(
        every, left_rows, right, left_panels[1], mix,
        jnp.asarray(clip_picks(clip_parts * half_frames, half), BF16),
    )


def solution(mesh):
    in_specs = (
        P("replica", "tm", None, None, None),
        P(None, None, "fsdp"),
        P(None, "fsdp", None),
        P("replica", "tm", None, None, None),
        P(),
        P(None, "fsdp", None),
        P(None, "fsdp", ("replica", "tm")),
    )
    out_specs = P(None, None, "fsdp", ("replica", "tm"))
    return jax.shard_map(shards, mesh=mesh, in_specs=in_specs, out_specs=out_specs, check_vma=False)
```

```python
import functools

import jax
import jax.numpy as jnp
import numpy as np
from jax import lax
from jax.experimental import pallas as pl
from jax.experimental.pallas import tpu as pltpu
from jax.sharding import PartitionSpec as P

TAPS = 27
F32, BF16 = jnp.float32, jnp.bfloat16
NT = (((1,), (1,)), ((), ()))
VMEM = pl.BlockSpec(memory_space=pltpu.VMEM)
HBM = pl.BlockSpec(memory_space=pltpu.HBM)
SMEM = pl.BlockSpec(memory_space=pltpu.SMEM)


def shifted(block, axis, distance):
    devices = range(lax.axis_size(axis))
    route = [(i - distance, i) for i in devices if i - distance in devices]
    return lax.ppermute(block, axis, route)


def dot(left, right):
    return jnp.dot(left, right, preferred_element_type=F32)


def dot_nt(left, right):
    return lax.dot_general(left, right, NT, preferred_element_type=F32)


def halves(value):
    high = value.astype(BF16)
    return high, (value - high.astype(F32)).astype(BF16)


def patch_picks(side):
    half = side // 2
    even = np.zeros((1, 3, half, half, half, side), np.float32)
    odd = np.zeros((2, 3, half, half, half, side), np.float32)
    for c in range(3):
        for y in range(half):
            for x in range(half):
                column = 2 * x + c - 1
                if column < 0:
                    continue
                even[0, c, y, x, y, column] = 1
                if y > 0:
                    odd[0, c, y, x, y - 1, column] = 1
                odd[1, c, y, x, y, column] = 1
    return even.reshape(-1, half * side), odd.reshape(-1, half * side)


def spread_picks(half):
    quarter = half // 2
    picks = np.zeros((3, 3, half, half, quarter, quarter), np.float32)
    for b in range(3):
        for c in range(3):
            for out_y in range(quarter):
                for out_x in range(quarter):
                    y, x = 2 * out_y + b - 1, 2 * out_x + c - 1
                    if y >= 0 and x >= 0:
                        picks[b, c, y, x, out_y, out_x] = 1
    return picks.reshape(9 * half * half, quarter * quarter)


def clip_order(slices, clip_parts, half_frames, half):
    cells = half_frames * half * half
    order = np.arange(clip_parts * cells).reshape(clip_parts, slices, cells // slices)
    return order.transpose(1, 0, 2).reshape(-1)


def shift_picks(order, frames, half):
    size = frames * half * half
    picks = np.zeros((size, 2, 2, 2, frames, half, half), np.float32)
    at = np.empty(size, np.int64)
    at[order] = np.arange(size)
    at = at.reshape(frames, half, half)
    for dt, dr, dc in np.ndindex(2, 2, 2):
        for t, y, x in np.ndindex(frames - dt, half - dr, half - dc):
            picks[at[t + dt, y + dr, x + dc], dt, dr, dc, t, y, x] = 1
    return picks.reshape(size, 8 * size)


def sort_picks(order, frames, half):
    size = frames * half * half
    index = np.arange(size).reshape(frames // 2, 2, half // 2, 2, half // 2, 2)
    wanted = index.transpose(1, 3, 5, 0, 2, 4).reshape(-1)
    at = np.empty(size, np.int64)
    at[order] = np.arange(size)
    picks = np.zeros((size, size), np.float32)
    picks[at[wanted], np.arange(size)] = 1
    return picks


def project_kernel(x_ref, left_ref, grad_ref, out_ref, rows_ref):
    frames, half, _, side, channels = x_ref.shape
    wide = left_ref.shape[1]
    pairs = frames // 2
    size = pairs * half * side
    both = jnp.concatenate(halves(left_ref[0]), axis=0)
    target = lax.broadcasted_iota(jnp.int32, (size, size), 0)
    source = lax.broadcasted_iota(jnp.int32, (size, size), 1)
    cells = size // 2
    wanted = 2 * (target % cells) + target // cells
    pick = jnp.where(source == wanted, 1.0, 0.0).astype(BF16)
    for time in range(2):
        for row in range(2):
            block = jnp.concatenate(
                [
                    x_ref[frame, :, row].reshape(half * side, channels)
                    for frame in range(time, frames, 2)
                ],
                axis=0,
            )
            full = dot_nt(block, both)
            small = (full[:, :wide] + full[:, wide:]).astype(BF16)
            ordered = dot(pick, small).astype(BF16)
            at = (4 * time + 2 * row) * cells
            out_ref[at : at + size, :] = ordered
    rows = stacked_rows(grad_ref, rows_ref)
    count = rows.shape[0]
    for block in range(channels // wide):
        at = 8 * cells + block * count
        out_ref[at : at + count, :] = rows[:, block * wide : (block + 1) * wide]


def stacked_rows(grad_ref, rows_ref):
    quarter = grad_ref.shape[0]
    for row in range(quarter):
        rows_ref[pl.ds(row * quarter, quarter), :] = grad_ref[row].astype(F32)
    return rows_ref[...].astype(BF16)


def transposed_products(rows, kernel, taps):
    total = dot_nt(rows[0], kernel[taps[0]])
    for at in range(1, len(taps)):
        total += dot_nt(rows[at], kernel[taps[at]])
    return total


def spread_rows(picks_ref, rows, cells):
    spread = dot(picks_ref[...], rows).astype(BF16)
    return [spread[tap * cells : (tap + 1) * cells] for tap in range(9)]


def own_grad_kernel(grad_ref, spread_ref, second_any, out_ref, rows_ref, second, arrived):
    copies = [
        pltpu.make_async_copy(
            second_any.at[pl.ds(9 * a, 9)], second.at[pl.ds(9 * (a - 1), 9)], arrived.at[a - 1]
        )
        for a in (1, 2)
    ]
    for copy in copies:
        copy.start()
    cells = out_ref.shape[0] // 2
    rows = spread_rows(spread_ref, stacked_rows(grad_ref, rows_ref), cells)
    for at, copy in enumerate(copies):
        copy.wait()
        out_ref[pl.ds(at * cells, cells), :] = transposed_products(
            rows, second, range(9 * at, 9 * at + 9)
        )


def hidden_kernel(
    x_ref, prior_ref, own_ref, later_ref, even_ref, odd_ref, spread_ref, first_any, second_any,
    out_ref, rows_ref, patches, first, second, arrived, second_arrived,
):
    frames, half, _, side, channels = x_ref.shape
    cells = half * half
    copies = {
        a: pltpu.make_async_copy(
            first_any.at[pl.ds(9 * a, 9)], first.at[pl.ds(9 * a, 9)], arrived.at[a]
        )
        for a in (0, 1, 2)
    }
    second_copy = pltpu.make_async_copy(second_any.at[pl.ds(0, 9)], second, second_arrived)
    copies[1].start()
    copies[2].start()
    copies[0].start()
    second_copy.start()
    for frame in range(frames + 1):
        block = prior_ref if frame == 0 else x_ref.at[frame - 1]
        even = dot(even_ref[...], block[:, 0].reshape(half * side, channels)).astype(BF16)
        odd = dot(odd_ref[...], block[:, 1].reshape(half * side, channels)).astype(BF16)
        for c in range(3):
            patches[frame, c] = odd[c * cells : (c + 1) * cells]
            patches[frame, 3 + c] = even[c * cells : (c + 1) * cells]
            patches[frame, 6 + c] = odd[(3 + c) * cells : (4 + c) * cells]
    pre = jnp.zeros((2 * cells, first.shape[2]), F32)
    for a in (1, 2, 0):
        copies[a].wait()
        for tap in range(9):
            rows = jnp.concatenate([patches[a, tap], patches[a + 2, tap]], axis=0)
            pre += dot(rows, first[9 * a + tap])
    rows = spread_rows(spread_ref, stacked_rows(later_ref, rows_ref), cells)
    second_copy.wait()
    late = own_ref[pl.ds(cells, cells), :] + transposed_products(rows, second, range(9))
    hidden_grad = jnp.concatenate([own_ref[pl.ds(0, cells), :], late], axis=0)
    sig = jax.nn.sigmoid(pre)
    hidden = (pre * sig).astype(BF16)
    pre_grad = (hidden_grad * sig * (1.0 + pre * (1.0 - sig))).astype(BF16)
    groups, slices, _, share, _ = out_ref.shape
    for at in range(slices):
        place = slice(at * share, (at + 1) * share)
        for group in range(groups):
            out_ref[group, at, 0] = pre_grad[place]
            out_ref[group, at, 1] = hidden[place]


def right_kernel(acts_ref, right_ref, out_ref):
    slices, _, columns, _ = right_ref.shape
    parts = acts_ref.shape[0]
    for layer in range(2):
        right = jnp.concatenate([right_ref[at, layer] for at in range(slices)], axis=1)
        both = jnp.concatenate(halves(right), axis=0)
        rows = jnp.concatenate(
            [
                jnp.concatenate([acts_ref[part, at, layer] for at in range(slices)], axis=1)
                for part in range(parts)
            ],
            axis=0,
        )
        full = dot_nt(both, rows)
        out_ref[pl.ds(layer * columns, columns), :] = (full[:columns] + full[columns:]).astype(BF16)


def update_kernel(
    place_ref, *refs, slices, clip_parts, half,
):
    own_refs = refs[:slices]
    (
        left_rows_ref, left_ref, mix_ref, shift_ref, sort_ref,
        out_ref, columns, shifts, grads, raw,
    ) = refs[slices:]
    for distance in range(slices):
        origin = lax.rem(place_ref[0] + (slices - distance), slices)
        columns[origin] = own_refs[distance][...]
    parts = left_rows_ref.shape[0]
    wide, channels = left_ref.shape[1:]
    width = columns.shape[1] // 2
    clips = parts // clip_parts
    share = columns.shape[2] // clips
    clip_cells = slices * share
    cells = clip_cells // clip_parts
    frames = clip_cells // (half * half)
    outputs = clip_cells // 8

    def by_clip(layer):
        return jnp.concatenate(
            [
                jnp.concatenate(
                    [
                        columns[
                            at, pl.ds(layer * width, width), pl.ds(clip * share, share)
                        ]
                        for at in range(slices)
                    ],
                    axis=1,
                )
                for clip in range(clips)
            ],
            axis=0,
        )

    first = by_clip(0)
    for shift in range(8):
        moved = dot(first, shift_ref[:, pl.ds(shift * clip_cells, clip_cells)]).astype(BF16)
        for clip in range(clips):
            shifts[shift, clip] = moved[clip * width : (clip + 1) * width]
    second = dot(by_clip(1), sort_ref[...]).astype(BF16)

    own_outputs = outputs // clip_parts
    blocks = channels // wide
    out_grad = jnp.concatenate(
        [
            jnp.concatenate(
                [
                    left_rows_ref[part, pl.ds(8 * cells + own_outputs * at, own_outputs), :]
                    for at in range(blocks)
                ],
                axis=1,
            )
            for part in range(parts)
        ],
        axis=0,
    )
    full = dot_nt(out_grad, jnp.concatenate(halves(left_ref[1]), axis=0))
    total = parts * own_outputs
    quarter = half // 2
    grads[pl.ds(0, total), :] = full[:, :wide] + full[:, wide:]
    places = lax.broadcasted_iota(jnp.int32, (total, wide), 0)
    frame = places // (quarter * quarter) % (frames // 2)
    row = places // quarter % quarter
    column = places % quarter
    second_rows = []
    for shift in range(8):
        dt, dr, dc = shift // 4, shift // 2 % 2, shift % 2
        moved = grads[pl.ds((dt * quarter + dr) * quarter + dc, total), :]
        inside = (frame + dt < frames // 2) & (row + dr < quarter) & (column + dc < quarter)
        second_rows.append(jnp.where(inside, moved, 0.0).astype(BF16))

    for kind in range(8):
        time, line, place = kind // 4, kind // 2 % 2, kind % 2
        taps = [
            (9 * a + 3 * b + c, 4 * (a == 0) + 2 * (b == 0) + (c == 0))
            for a in ((0, 2) if time else (1,))
            for b in ((0, 2) if line else (1,))
            for c in ((0, 2) if place else (1,))
        ]
        sums = None
        for clip in range(clips):
            left = jnp.concatenate([shifts[shift, clip] for _, shift in taps], axis=0)
            rows = jnp.concatenate(
                [
                    left_rows_ref[clip * clip_parts + part, pl.ds(kind * cells, cells), :]
                    for part in range(clip_parts)
                ],
                axis=0,
            )
            term = dot(left, rows)
            sums = term if sums is None else sums + term
        chosen = jnp.concatenate(
            [
                second[clip * width : (clip + 1) * width, kind * outputs : (kind + 1) * outputs]
                for clip in range(clips)
            ],
            axis=1,
        )
        for at, (tap, shift) in enumerate(taps):
            raw[0, tap] = sums[at * width : (at + 1) * width]
            raw[1, tap] = dot(chosen, second_rows[shift])

    @pl.loop(0, 2 * TAPS)
    def _(step):
        layer, out_tap = step // TAPS, step % TAPS
        acc = raw[layer, 0] * mix_ref[layer, out_tap, 0]
        for tap in range(1, TAPS):
            acc += raw[layer, tap] * mix_ref[layer, out_tap, tap]
        out_ref[layer, out_tap] = acc.astype(BF16)


def ring(block, axis):
    size = lax.axis_size(axis)
    return [block] + [
        lax.ppermute(block, axis, [(i, (i + distance) % size) for i in range(size)])
        for distance in range(1, size)
    ]


def shards(clip_input, first_kernel, second_kernel, out_grad, tap_mix, left_panels, right_panels):
    clips, frames, side, _, channels = clip_input.shape
    wide = first_kernel.shape[2]
    width = right_panels.shape[2]
    half, quarter = side // 2, side // 4
    half_frames = frames // 2
    cells = half_frames * half * half
    clip_parts = lax.axis_size("tm")
    parts = lax.axis_size("replica") * clip_parts
    slices = lax.axis_size("fsdp")
    share = cells // slices
    assert clips == 1 and frames == 4
    x = clip_input.reshape(frames, half, 2, side, channels)
    grad = out_grad.reshape(quarter, quarter, channels)
    prior = shifted(x[frames - 1 :], "tm", 1)[0]
    later = shifted(grad, "tm", -1)
    place = lax.axis_index("fsdp")

    projected = pl.pallas_call(
        project_kernel,
        out_shape=jax.ShapeDtypeStruct((8 * cells + quarter * quarter * channels // wide, wide), BF16),
        in_specs=[VMEM] * 3,
        out_specs=VMEM,
        scratch_shapes=[pltpu.VMEM((quarter * quarter, channels), F32)],
        compiler_params=pltpu.CompilerParams(vmem_limit_bytes=24 << 20),
        cost_estimate=pl.CostEstimate(
            flops=4 * frames * side * side * channels * wide,
            bytes_accessed=2 * frames * side * side * channels,
            transcendentals=0,
        ),
    )(x, left_panels, grad)
    left_rows = lax.all_gather(projected, ("replica", "tm"), axis=0, tiled=False)

    right = right_panels.transpose(0, 2, 1)
    blocks = ring(right, "fsdp")
    right = jnp.zeros((slices,) + right.shape, F32)
    for distance, block in enumerate(blocks):
        right = lax.dynamic_update_slice_in_dim(
            right, block[None], (place + (slices - distance)) % slices, 0
        )

    even, odd = patch_picks(side)
    spread = jnp.asarray(spread_picks(half), BF16)
    own_grad = pl.pallas_call(
        own_grad_kernel,
        out_shape=jax.ShapeDtypeStruct((cells, wide), F32),
        in_specs=[VMEM] * 2 + [HBM],
        out_specs=VMEM,
        scratch_shapes=[
            pltpu.VMEM((quarter * quarter, channels), F32),
            pltpu.VMEM((18, wide, channels), BF16),
            pltpu.SemaphoreType.DMA((2,)),
        ],
        compiler_params=pltpu.CompilerParams(vmem_limit_bytes=24 << 20),
        cost_estimate=pl.CostEstimate(
            flops=2 * cells * 18 * channels * wide,
            bytes_accessed=2 * 18 * channels * wide,
            transcendentals=0,
        ),
    )(grad, spread, second_kernel)
    acts = pl.pallas_call(
        hidden_kernel,
        out_shape=jax.ShapeDtypeStruct((parts, slices, 2, share, wide), BF16),
        in_specs=[VMEM] * 7 + [HBM] * 2,
        out_specs=VMEM,
        scratch_shapes=[
            pltpu.VMEM((quarter * quarter, channels), F32),
            pltpu.VMEM((frames + 1, 9, half * half, channels), BF16),
            pltpu.VMEM(first_kernel.shape, BF16),
            pltpu.VMEM((9, wide, channels), BF16),
            pltpu.SemaphoreType.DMA((3,)),
            pltpu.SemaphoreType.DMA,
        ],
        compiler_params=pltpu.CompilerParams(vmem_limit_bytes=32 << 20),
        cost_estimate=pl.CostEstimate(
            flops=3 * cells * TAPS * channels * wide,
            bytes_accessed=4 * TAPS * channels * wide,
            transcendentals=cells * wide,
        ),
    )(
        x, prior, own_grad, later, jnp.asarray(even, BF16), jnp.asarray(odd, BF16),
        spread, first_kernel, second_kernel,
    )
    every = lax.all_to_all(
        acts.reshape(parts * slices, 2, share, wide), ("replica", "tm", "fsdp"), 0, 0, tiled=True
    ).reshape(parts, slices, 2, share, wide)
    if wide % 128:
        every = every.transpose(0, 2, 3, 1, 4).reshape(parts, 1, 2, share, channels)
        right = right.transpose(1, 2, 0, 3).reshape(1, 2, width, channels)
    own_columns = pl.pallas_call(
        right_kernel,
        out_shape=jax.ShapeDtypeStruct((2 * width, parts * share), BF16),
        in_specs=[VMEM] * 2,
        out_specs=VMEM,
        compiler_params=pltpu.CompilerParams(vmem_limit_bytes=24 << 20),
    )(every, right)

    order = clip_order(slices, clip_parts, half_frames, half)
    clip_frames = clip_parts * half_frames
    clip_cells = clip_parts * cells
    result = pl.pallas_call(
        functools.partial(update_kernel, slices=slices, clip_parts=clip_parts, half=half),
        out_shape=jax.ShapeDtypeStruct((2, TAPS, width, wide), BF16),
        in_specs=[SMEM] + [VMEM] * (slices + 2) + [SMEM] + [VMEM] * 2,
        out_specs=VMEM,
        scratch_shapes=[
            pltpu.VMEM((slices, 2 * width, parts * share), BF16),
            pltpu.VMEM((8, parts // clip_parts, width, clip_cells), BF16),
            pltpu.VMEM((parts * cells // 8 + (quarter + 1) * quarter + 8, wide), F32),
            pltpu.VMEM((2, TAPS, width, wide), F32),
        ],
        compiler_params=pltpu.CompilerParams(vmem_limit_bytes=40 << 20),
    )(
        place.reshape(1), *ring(own_columns, "fsdp"), left_rows, left_panels, tap_mix,
        jnp.asarray(shift_picks(order, clip_frames, half), BF16),
        jnp.asarray(sort_picks(order, clip_frames, half), BF16),
    )
    return result.transpose(0, 1, 3, 2)


def solution(mesh):
    in_specs = (
        P("replica", "tm", None, None, None),
        P(None, None, "fsdp"),
        P(None, "fsdp", None),
        P("replica", "tm", None, None, None),
        P(),
        P(None, "fsdp", None),
        P(None, "fsdp", ("replica", "tm")),
    )
    out_specs = P(None, None, "fsdp", ("replica", "tm"))
    return jax.shard_map(shards, mesh=mesh, in_specs=in_specs, out_specs=out_specs, check_vma=False)
```

```python
import functools

import jax
import jax.numpy as jnp
import numpy as np
from jax import lax
from jax.experimental import pallas as pl
from jax.experimental.pallas import tpu as pltpu
from jax.sharding import PartitionSpec as P

TAPS = 27
F32, BF16 = jnp.float32, jnp.bfloat16
ROOM = 58 << 20
NT = (((1,), (1,)), ((), ()))
VMEM = pl.BlockSpec(memory_space=pltpu.VMEM)
HBM = pl.BlockSpec(memory_space=pltpu.HBM)
SMEM = pl.BlockSpec(memory_space=pltpu.SMEM)


def shifted(block, axis, distance):
    devices = range(lax.axis_size(axis))
    route = [(i - distance, i) for i in devices if i - distance in devices]
    return lax.ppermute(block, axis, route)


def dot(left, right):
    return jnp.dot(left, right, preferred_element_type=F32)


def dot_nt(left, right):
    return lax.dot_general(left, right, NT, preferred_element_type=F32)


def halves(value):
    high = value.astype(BF16)
    return high, (value - high.astype(F32)).astype(BF16)


def patch_picks(side):
    half = side // 2
    even = np.zeros((1, 3, half, half, half, side), np.float32)
    odd = np.zeros((2, 3, half, half, half, side), np.float32)
    for c in range(3):
        for y in range(half):
            for x in range(half):
                column = 2 * x + c - 1
                if column < 0:
                    continue
                even[0, c, y, x, y, column] = 1
                if y > 0:
                    odd[0, c, y, x, y - 1, column] = 1
                odd[1, c, y, x, y, column] = 1
    return even.reshape(-1, half * side), odd.reshape(-1, half * side)


def spread_picks(half):
    quarter = half // 2
    picks = np.zeros((3, 3, half, half, quarter, quarter), np.float32)
    for b in range(3):
        for c in range(3):
            for out_y in range(quarter):
                for out_x in range(quarter):
                    y, x = 2 * out_y + b - 1, 2 * out_x + c - 1
                    if y >= 0 and x >= 0:
                        picks[b, c, y, x, out_y, out_x] = 1
    return picks.reshape(9 * half * half, quarter * quarter)


def clip_order(slices, clip_parts, half_frames, half):
    cells = half_frames * half * half
    order = np.arange(clip_parts * cells).reshape(clip_parts, slices, cells // slices)
    return order.transpose(1, 0, 2).reshape(-1)


def shift_picks(order, frames, half):
    size = frames * half * half
    picks = np.zeros((size, 2, 2, 2, frames, half, half), np.float32)
    at = np.empty(size, np.int64)
    at[order] = np.arange(size)
    at = at.reshape(frames, half, half)
    for dt, dr, dc in np.ndindex(2, 2, 2):
        for t, y, x in np.ndindex(frames - dt, half - dr, half - dc):
            picks[at[t + dt, y + dr, x + dc], dt, dr, dc, t, y, x] = 1
    return picks.reshape(size, 8 * size)


def sort_picks(order, frames, half):
    size = frames * half * half
    index = np.arange(size).reshape(frames // 2, 2, half // 2, 2, half // 2, 2)
    wanted = index.transpose(1, 3, 5, 0, 2, 4).reshape(-1)
    at = np.empty(size, np.int64)
    at[order] = np.arange(size)
    picks = np.zeros((size, size), np.float32)
    picks[at[wanted], np.arange(size)] = 1
    return picks


def project_kernel(x_ref, left_ref, grad_ref, out_ref, rows_ref):
    frames, half, _, side, channels = x_ref.shape
    wide = left_ref.shape[1]
    pairs = frames // 2
    size = pairs * half * side
    both = jnp.concatenate(halves(left_ref[0]), axis=0)
    target = lax.broadcasted_iota(jnp.int32, (size, size), 0)
    source = lax.broadcasted_iota(jnp.int32, (size, size), 1)
    cells = size // 2
    wanted = 2 * (target % cells) + target // cells
    pick = jnp.where(source == wanted, 1.0, 0.0).astype(BF16)
    for time in range(2):
        for row in range(2):
            block = jnp.concatenate(
                [
                    x_ref[frame, :, row].reshape(half * side, channels)
                    for frame in range(time, frames, 2)
                ],
                axis=0,
            )
            full = dot_nt(block, both)
            small = (full[:, :wide] + full[:, wide:]).astype(BF16)
            ordered = dot(pick, small).astype(BF16)
            at = (4 * time + 2 * row) * cells
            out_ref[at : at + size, :] = ordered
    rows = stacked_rows(grad_ref, rows_ref)
    count = rows.shape[0]
    for block in range(channels // wide):
        at = 8 * cells + block * count
        out_ref[at : at + count, :] = rows[:, block * wide : (block + 1) * wide]


def stacked_rows(grad_ref, rows_ref):
    quarter = grad_ref.shape[0]
    for row in range(quarter):
        rows_ref[pl.ds(row * quarter, quarter), :] = grad_ref[row].astype(F32)
    return rows_ref[...].astype(BF16)


def transposed_products(rows, kernel, taps):
    total = dot_nt(rows[0], kernel[taps[0]])
    for at in range(1, len(taps)):
        total += dot_nt(rows[at], kernel[taps[at]])
    return total


def spread_rows(picks_ref, rows, cells):
    spread = dot(picks_ref[...], rows).astype(BF16)
    return [spread[tap * cells : (tap + 1) * cells] for tap in range(9)]


def own_grad_kernel(grad_ref, spread_ref, second_any, out_ref, rows_ref, second, arrived):
    copies = [
        pltpu.make_async_copy(
            second_any.at[pl.ds(9 * a, 9)], second.at[pl.ds(9 * (a - 1), 9)], arrived.at[a - 1]
        )
        for a in (1, 2)
    ]
    for copy in copies:
        copy.start()
    cells = out_ref.shape[0] // 2
    rows = spread_rows(spread_ref, stacked_rows(grad_ref, rows_ref), cells)
    for at, copy in enumerate(copies):
        copy.wait()
        out_ref[pl.ds(at * cells, cells), :] = transposed_products(
            rows, second, range(9 * at, 9 * at + 9)
        )


def hidden_kernel(
    x_ref, prior_ref, own_ref, later_ref, even_ref, odd_ref, spread_ref, right_ref,
    first_any, second_any, out_ref, right_out_ref, rows_ref, patches, first, second, arrived,
    second_arrived,
):
    frames, half, _, side, channels = x_ref.shape
    cells = half * half
    copies = {
        a: pltpu.make_async_copy(
            first_any.at[pl.ds(9 * a, 9)], first.at[pl.ds(9 * a, 9)], arrived.at[a]
        )
        for a in (0, 1, 2)
    }
    second_copy = pltpu.make_async_copy(second_any.at[pl.ds(0, 9)], second, second_arrived)
    copies[1].start()
    copies[2].start()
    copies[0].start()
    second_copy.start()
    for frame in range(frames + 1):
        block = prior_ref if frame == 0 else x_ref.at[frame - 1]
        even = dot(even_ref[...], block[:, 0].reshape(half * side, channels)).astype(BF16)
        odd = dot(odd_ref[...], block[:, 1].reshape(half * side, channels)).astype(BF16)
        for c in range(3):
            patches[frame, c] = odd[c * cells : (c + 1) * cells]
            patches[frame, 3 + c] = even[c * cells : (c + 1) * cells]
            patches[frame, 6 + c] = odd[(3 + c) * cells : (4 + c) * cells]
    pre = jnp.zeros((2 * cells, first.shape[2]), F32)
    for a in (1, 2, 0):
        copies[a].wait()
        for tap in range(9):
            rows = jnp.concatenate([patches[a, tap], patches[a + 2, tap]], axis=0)
            pre += dot(rows, first[9 * a + tap])
    rows = spread_rows(spread_ref, stacked_rows(later_ref, rows_ref), cells)
    second_copy.wait()
    late = own_ref[pl.ds(cells, cells), :] + transposed_products(rows, second, range(9))
    hidden_grad = jnp.concatenate([own_ref[pl.ds(0, cells), :], late], axis=0)
    sig = jax.nn.sigmoid(pre)
    hidden = (pre * sig).astype(BF16)
    pre_grad = (hidden_grad * sig * (1.0 + pre * (1.0 - sig))).astype(BF16)
    slices, _, share, _ = out_ref.shape
    for at in range(slices):
        place = slice(at * share, (at + 1) * share)
        out_ref[at, 0] = pre_grad[place]
        out_ref[at, 1] = hidden[place]
    columns = right_ref.shape[2]
    for layer in range(2):
        right = jnp.concatenate([right_ref[at, layer] for at in range(right_ref.shape[0])], axis=1)
        for at, part in enumerate(halves(right)):
            right_out_ref[layer, pl.ds(at * columns, columns), :] = part


def right_kernel(acts_ref, right_ref, out_ref):
    columns = right_ref.shape[1] // 2
    parts, slices = acts_ref.shape[:2]
    for layer in range(2):
        rows = jnp.concatenate(
            [
                jnp.concatenate([acts_ref[part, at, layer] for at in range(slices)], axis=1)
                for part in range(parts)
            ],
            axis=0,
        )
        full = dot_nt(right_ref[layer], rows)
        product = (full[:columns] + full[columns:]).astype(BF16)
        for at in range(out_ref.shape[0]):
            out_ref[at, pl.ds(layer * columns, columns), :] = product


def update_kernel(
    columns, left_rows_any, left_ref, mix_ref, shift_ref, sort_ref,
    out_ref, left_rows_ref, shifts, grads, raw, arrived, *, clip_parts, half,
):
    copy = pltpu.make_async_copy(left_rows_any, left_rows_ref, arrived)
    copy.start()
    slices = columns.shape[0]
    parts = left_rows_ref.shape[0]
    wide, channels = left_ref.shape[1:]
    width = columns.shape[1] // 2
    clips = parts // clip_parts
    share = columns.shape[2] // clips
    clip_cells = slices * share
    cells = clip_cells // clip_parts
    frames = clip_cells // (half * half)
    outputs = clip_cells // 8

    def by_clip(layer):
        return jnp.concatenate(
            [
                jnp.concatenate(
                    [
                        columns[
                            at, pl.ds(layer * width, width), pl.ds(clip * share, share)
                        ]
                        for at in range(slices)
                    ],
                    axis=1,
                )
                for clip in range(clips)
            ],
            axis=0,
        )

    first = by_clip(0)
    for shift in range(8):
        moved = dot(first, shift_ref[:, pl.ds(shift * clip_cells, clip_cells)]).astype(BF16)
        for clip in range(clips):
            shifts[shift, clip] = moved[clip * width : (clip + 1) * width]
    second = dot(by_clip(1), sort_ref[...]).astype(BF16)

    copy.wait()
    own_outputs = outputs // clip_parts
    blocks = channels // wide
    out_grad = jnp.concatenate(
        [
            jnp.concatenate(
                [
                    left_rows_ref[part, pl.ds(8 * cells + own_outputs * at, own_outputs), :]
                    for at in range(blocks)
                ],
                axis=1,
            )
            for part in range(parts)
        ],
        axis=0,
    )
    full = dot_nt(out_grad, jnp.concatenate(halves(left_ref[1]), axis=0))
    total = parts * own_outputs
    quarter = half // 2
    grads[pl.ds(0, total), :] = full[:, :wide] + full[:, wide:]
    places = lax.broadcasted_iota(jnp.int32, (total, wide), 0)
    frame = places // (quarter * quarter) % (frames // 2)
    row = places // quarter % quarter
    column = places % quarter
    second_rows = []
    for shift in range(8):
        dt, dr, dc = shift // 4, shift // 2 % 2, shift % 2
        moved = grads[pl.ds((dt * quarter + dr) * quarter + dc, total), :]
        inside = (frame + dt < frames // 2) & (row + dr < quarter) & (column + dc < quarter)
        second_rows.append(jnp.where(inside, moved, 0.0).astype(BF16))

    for kind in range(8):
        time, line, place = kind // 4, kind // 2 % 2, kind % 2
        taps = [
            (9 * a + 3 * b + c, 4 * (a == 0) + 2 * (b == 0) + (c == 0))
            for a in ((0, 2) if time else (1,))
            for b in ((0, 2) if line else (1,))
            for c in ((0, 2) if place else (1,))
        ]
        sums = None
        for clip in range(clips):
            left = jnp.concatenate([shifts[shift, clip] for _, shift in taps], axis=0)
            rows = jnp.concatenate(
                [
                    left_rows_ref[clip * clip_parts + part, pl.ds(kind * cells, cells), :]
                    for part in range(clip_parts)
                ],
                axis=0,
            )
            term = dot(left, rows)
            sums = term if sums is None else sums + term
        chosen = jnp.concatenate(
            [
                second[clip * width : (clip + 1) * width, kind * outputs : (kind + 1) * outputs]
                for clip in range(clips)
            ],
            axis=1,
        )
        for at, (tap, shift) in enumerate(taps):
            raw[0, tap] = sums[at * width : (at + 1) * width]
            raw[1, tap] = dot(chosen, second_rows[shift])

    @pl.loop(0, 2 * TAPS)
    def _(step):
        layer, out_tap = step // TAPS, step % TAPS
        acc = raw[layer, 0] * mix_ref[layer, out_tap, 0]
        for tap in range(1, TAPS):
            acc += raw[layer, tap] * mix_ref[layer, out_tap, tap]
        out_ref[layer, out_tap] = acc.astype(BF16)


def to_all(block, axes):
    count = lax.axis_size(axes)
    return lax.all_to_all(
        jnp.broadcast_to(block, (count,) + block.shape), axes, 0, 0, tiled=True
    )


def shards(clip_input, first_kernel, second_kernel, out_grad, tap_mix, left_panels, right_panels):
    clips, frames, side, _, channels = clip_input.shape
    wide = first_kernel.shape[2]
    width = right_panels.shape[2]
    half, quarter = side // 2, side // 4
    half_frames = frames // 2
    cells = half_frames * half * half
    clip_parts = lax.axis_size("tm")
    parts = lax.axis_size("replica") * clip_parts
    slices = lax.axis_size("fsdp")
    share = cells // slices
    assert clips == 1 and frames == 4
    x = clip_input.reshape(frames, half, 2, side, channels)
    grad = out_grad.reshape(quarter, quarter, channels)
    prior = shifted(x[frames - 1 :], "tm", 1)[0]
    later = shifted(grad, "tm", -1)

    projected = pl.pallas_call(
        project_kernel,
        out_shape=jax.ShapeDtypeStruct((8 * cells + quarter * quarter * channels // wide, wide), BF16),
        in_specs=[VMEM] * 3,
        out_specs=VMEM,
        scratch_shapes=[pltpu.VMEM((quarter * quarter, channels), F32)],
        compiler_params=pltpu.CompilerParams(vmem_limit_bytes=ROOM),
        cost_estimate=pl.CostEstimate(
            flops=4 * frames * side * side * channels * wide,
            bytes_accessed=2 * frames * side * side * channels,
            transcendentals=0,
        ),
    )(x, left_panels, grad)
    left_rows = lax.all_gather(projected, ("replica", "tm"), axis=0, tiled=False)

    right = to_all(right_panels.transpose(0, 2, 1), "fsdp")
    if wide % 128:
        right = right.transpose(1, 2, 0, 3).reshape(1, 2, width, channels)

    even, odd = patch_picks(side)
    spread = jnp.asarray(spread_picks(half), BF16)
    own_grad = pl.pallas_call(
        own_grad_kernel,
        out_shape=jax.ShapeDtypeStruct((cells, wide), F32),
        in_specs=[VMEM] * 2 + [HBM],
        out_specs=VMEM,
        scratch_shapes=[
            pltpu.VMEM((quarter * quarter, channels), F32),
            pltpu.VMEM((18, wide, channels), BF16),
            pltpu.SemaphoreType.DMA((2,)),
        ],
        compiler_params=pltpu.CompilerParams(vmem_limit_bytes=ROOM),
        cost_estimate=pl.CostEstimate(
            flops=2 * cells * 18 * channels * wide,
            bytes_accessed=2 * 18 * channels * wide,
            transcendentals=0,
        ),
    )(grad, spread, second_kernel)
    acts, right = pl.pallas_call(
        hidden_kernel,
        out_shape=(
            jax.ShapeDtypeStruct((slices, 2, share, wide), BF16),
            jax.ShapeDtypeStruct((2, 2 * width, channels), BF16),
        ),
        in_specs=[VMEM] * 8 + [HBM] * 2,
        out_specs=(VMEM, VMEM),
        scratch_shapes=[
            pltpu.VMEM((quarter * quarter, channels), F32),
            pltpu.VMEM((frames + 1, 9, half * half, channels), BF16),
            pltpu.VMEM(first_kernel.shape, BF16),
            pltpu.VMEM((9, wide, channels), BF16),
            pltpu.SemaphoreType.DMA((3,)),
            pltpu.SemaphoreType.DMA,
        ],
        compiler_params=pltpu.CompilerParams(vmem_limit_bytes=ROOM),
        cost_estimate=pl.CostEstimate(
            flops=3 * cells * TAPS * channels * wide,
            bytes_accessed=4 * TAPS * channels * wide,
            transcendentals=cells * wide,
        ),
    )(
        x, prior, own_grad, later, jnp.asarray(even, BF16), jnp.asarray(odd, BF16),
        spread, right, first_kernel, second_kernel,
    )
    acts = lax.all_to_all(acts, "fsdp", 0, 0, tiled=True)
    every = to_all(acts, ("replica", "tm"))
    if wide % 128:
        every = every.transpose(0, 2, 3, 1, 4).reshape(parts, 1, 2, share, channels)
    own_columns = pl.pallas_call(
        right_kernel,
        out_shape=jax.ShapeDtypeStruct((slices, 2 * width, parts * share), BF16),
        in_specs=[VMEM] * 2,
        out_specs=VMEM,
        compiler_params=pltpu.CompilerParams(vmem_limit_bytes=ROOM),
    )(every, right)
    columns = lax.all_to_all(own_columns, "fsdp", 0, 0, tiled=True)

    order = clip_order(slices, clip_parts, half_frames, half)
    clip_frames = clip_parts * half_frames
    clip_cells = clip_parts * cells
    result = pl.pallas_call(
        functools.partial(update_kernel, clip_parts=clip_parts, half=half),
        out_shape=jax.ShapeDtypeStruct((2, TAPS, width, wide), BF16),
        in_specs=[VMEM, HBM, VMEM, SMEM, VMEM, VMEM],
        out_specs=VMEM,
        scratch_shapes=[
            pltpu.VMEM(left_rows.shape, BF16),
            pltpu.VMEM((8, parts // clip_parts, width, clip_cells), BF16),
            pltpu.VMEM((parts * cells // 8 + (quarter + 1) * quarter + 8, wide), F32),
            pltpu.VMEM((2, TAPS, width, wide), F32),
            pltpu.SemaphoreType.DMA,
        ],
        compiler_params=pltpu.CompilerParams(vmem_limit_bytes=ROOM),
    )(
        columns, left_rows, left_panels, tap_mix,
        jnp.asarray(shift_picks(order, clip_frames, half), BF16),
        jnp.asarray(sort_picks(order, clip_frames, half), BF16),
    )
    return result.transpose(0, 1, 3, 2)


def solution(mesh):
    in_specs = (
        P("replica", "tm", None, None, None),
        P(None, None, "fsdp"),
        P(None, "fsdp", None),
        P("replica", "tm", None, None, None),
        P(),
        P(None, "fsdp", None),
        P(None, "fsdp", ("replica", "tm")),
    )
    out_specs = P(None, None, "fsdp", ("replica", "tm"))
    return jax.shard_map(shards, mesh=mesh, in_specs=in_specs, out_specs=out_specs, check_vma=False)
```

```python
import functools

import jax
import jax.numpy as jnp
import numpy as np
from jax import lax
from jax.experimental import pallas as pl
from jax.experimental.pallas import tpu as pltpu
from jax.sharding import PartitionSpec as P

TAPS = 27
F32, BF16 = jnp.float32, jnp.bfloat16
ROOM = 58 << 20
HIDDEN_COST = 200 << 20
NT = (((1,), (1,)), ((), ()))
VMEM = pl.BlockSpec(memory_space=pltpu.VMEM)
HBM = pl.BlockSpec(memory_space=pltpu.HBM)
SMEM = pl.BlockSpec(memory_space=pltpu.SMEM)


def shifted(block, axis, distance):
    devices = range(lax.axis_size(axis))
    route = [(i - distance, i) for i in devices if i - distance in devices]
    return lax.ppermute(block, axis, route)


def dot(left, right):
    return jnp.dot(left, right, preferred_element_type=F32)


def dot_nt(left, right):
    return lax.dot_general(left, right, NT, preferred_element_type=F32)


def halves(value):
    high = value.astype(BF16)
    return high, (value - high.astype(F32)).astype(BF16)


def patch_picks(side):
    half = side // 2
    even = np.zeros((1, 3, half, half, half, side), np.float32)
    odd = np.zeros((2, 3, half, half, half, side), np.float32)
    for c in range(3):
        for y in range(half):
            for x in range(half):
                column = 2 * x + c - 1
                if column < 0:
                    continue
                even[0, c, y, x, y, column] = 1
                if y > 0:
                    odd[0, c, y, x, y - 1, column] = 1
                odd[1, c, y, x, y, column] = 1
    return even.reshape(-1, half * side), odd.reshape(-1, half * side)


def spread_picks(half):
    quarter = half // 2
    picks = np.zeros((3, 3, half, half, quarter, quarter), np.float32)
    for b in range(3):
        for c in range(3):
            for out_y in range(quarter):
                for out_x in range(quarter):
                    y, x = 2 * out_y + b - 1, 2 * out_x + c - 1
                    if y >= 0 and x >= 0:
                        picks[b, c, y, x, out_y, out_x] = 1
    return picks.reshape(9 * half * half, quarter * quarter)


def clip_order(slices, clip_parts, half_frames, half):
    cells = half_frames * half * half
    order = np.arange(clip_parts * cells).reshape(clip_parts, slices, cells // slices)
    return order.transpose(1, 0, 2).reshape(-1)


def shift_picks(order, frames, half):
    size = frames * half * half
    picks = np.zeros((size, 2, 2, 2, frames, half, half), np.float32)
    at = np.empty(size, np.int64)
    at[order] = np.arange(size)
    at = at.reshape(frames, half, half)
    for dt, dr, dc in np.ndindex(2, 2, 2):
        for t, y, x in np.ndindex(frames - dt, half - dr, half - dc):
            picks[at[t + dt, y + dr, x + dc], dt, dr, dc, t, y, x] = 1
    return picks.reshape(size, 8 * size)


def sort_picks(order, frames, half):
    size = frames * half * half
    index = np.arange(size).reshape(frames // 2, 2, half // 2, 2, half // 2, 2)
    wanted = index.transpose(1, 3, 5, 0, 2, 4).reshape(-1)
    at = np.empty(size, np.int64)
    at[order] = np.arange(size)
    picks = np.zeros((size, size), np.float32)
    picks[at[wanted], np.arange(size)] = 1
    return picks


def project_kernel(x_ref, left_ref, grad_ref, out_ref, rows_ref):
    frames, half, _, side, channels = x_ref.shape
    wide = left_ref.shape[1]
    pairs = frames // 2
    size = pairs * half * side
    both = jnp.concatenate(halves(left_ref[0]), axis=0)
    target = lax.broadcasted_iota(jnp.int32, (size, size), 0)
    source = lax.broadcasted_iota(jnp.int32, (size, size), 1)
    cells = size // 2
    wanted = 2 * (target % cells) + target // cells
    pick = jnp.where(source == wanted, 1.0, 0.0).astype(BF16)
    for time in range(2):
        for row in range(2):
            block = jnp.concatenate(
                [
                    x_ref[frame, :, row].reshape(half * side, channels)
                    for frame in range(time, frames, 2)
                ],
                axis=0,
            )
            full = dot_nt(block, both)
            small = (full[:, :wide] + full[:, wide:]).astype(BF16)
            ordered = dot(pick, small).astype(BF16)
            at = (4 * time + 2 * row) * cells
            out_ref[at : at + size, :] = ordered
    rows = stacked_rows(grad_ref, rows_ref)
    count = rows.shape[0]
    for block in range(channels // wide):
        at = 8 * cells + block * count
        out_ref[at : at + count, :] = rows[:, block * wide : (block + 1) * wide]


def stacked_rows(grad_ref, rows_ref):
    quarter = grad_ref.shape[0]
    for row in range(quarter):
        rows_ref[pl.ds(row * quarter, quarter), :] = grad_ref[row].astype(F32)
    return rows_ref[...].astype(BF16)


def transposed_products(rows, kernel, taps):
    total = dot_nt(rows[0], kernel[taps[0]])
    for at in range(1, len(taps)):
        total += dot_nt(rows[at], kernel[taps[at]])
    return total


def spread_rows(picks_ref, rows, cells):
    spread = dot(picks_ref[...], rows).astype(BF16)
    return [spread[tap * cells : (tap + 1) * cells] for tap in range(9)]


def hidden_kernel(
    x_ref, prior_ref, grad_ref, later_ref, even_ref, odd_ref, spread_ref, first_any, second_any,
    out_ref, rows_ref, patches, first, second, arrived,
):
    frames, half, _, side, channels = x_ref.shape
    cells = half * half
    copies = {
        (at, a): pltpu.make_async_copy(
            source.at[pl.ds(9 * a, 9)], target.at[pl.ds(9 * a, 9)], arrived.at[at, a]
        )
        for at, (source, target) in enumerate(((second_any, second), (first_any, first)))
        for a in (1, 2, 0)
    }
    for copy in copies.values():
        copy.start()
    own = spread_rows(spread_ref, stacked_rows(grad_ref, rows_ref), cells)
    copies[0, 1].wait()
    early = transposed_products(own, second, range(9, 18))
    copies[0, 2].wait()
    late = transposed_products(own, second, range(18, 27))
    for frame in range(frames + 1):
        block = prior_ref if frame == 0 else x_ref.at[frame - 1]
        even = dot(even_ref[...], block[:, 0].reshape(half * side, channels)).astype(BF16)
        odd = dot(odd_ref[...], block[:, 1].reshape(half * side, channels)).astype(BF16)
        for c in range(3):
            patches[frame, c] = odd[c * cells : (c + 1) * cells]
            patches[frame, 3 + c] = even[c * cells : (c + 1) * cells]
            patches[frame, 6 + c] = odd[(3 + c) * cells : (4 + c) * cells]
    after = spread_rows(spread_ref, stacked_rows(later_ref, rows_ref), cells)
    copies[0, 0].wait()
    late += transposed_products(after, second, range(9))
    hidden_grad = jnp.concatenate([early, late], axis=0)
    pre = jnp.zeros((2 * cells, first.shape[2]), F32)
    for a in (1, 2, 0):
        copies[1, a].wait()
        for tap in range(9):
            rows = jnp.concatenate([patches[a, tap], patches[a + 2, tap]], axis=0)
            pre += dot(rows, first[9 * a + tap])
    sig = jax.nn.sigmoid(pre)
    hidden = (pre * sig).astype(BF16)
    pre_grad = (hidden_grad * sig * (1.0 + pre * (1.0 - sig))).astype(BF16)
    groups, slices, _, share, _ = out_ref.shape
    for at in range(slices):
        place = slice(at * share, (at + 1) * share)
        for group in range(groups):
            out_ref[group, at, 0] = pre_grad[place]
            out_ref[group, at, 1] = hidden[place]


def right_kernel(acts_ref, right_ref, out_ref):
    columns = right_ref.shape[2]
    parts, slices = acts_ref.shape[:2]
    for layer in range(2):
        right = jnp.concatenate([right_ref[at, layer] for at in range(slices)], axis=1)
        both = jnp.concatenate(halves(right), axis=0)
        rows = jnp.concatenate(
            [
                jnp.concatenate([acts_ref[part, at, layer] for at in range(slices)], axis=1)
                for part in range(parts)
            ],
            axis=0,
        )
        full = dot_nt(both, rows)
        out_ref[pl.ds(layer * columns, columns), :] = (full[:columns] + full[columns:]).astype(BF16)


def update_kernel(place_ref, *refs, slices, clip_parts, half):
    own_refs = refs[:slices]
    (
        left_rows_any, left_ref, mix_ref, shift_ref, sort_ref,
        out_ref, left_rows_ref, columns, shifts, grads, raw, arrived,
    ) = refs[slices:]
    copy = pltpu.make_async_copy(left_rows_any, left_rows_ref, arrived)
    copy.start()
    for distance in range(slices):
        origin = lax.rem(place_ref[0] + (slices - distance), slices)
        columns[origin] = own_refs[distance][...]
    parts = left_rows_ref.shape[0]
    wide, channels = left_ref.shape[1:]
    width = columns.shape[1] // 2
    clips = parts // clip_parts
    share = columns.shape[2] // clips
    clip_cells = slices * share
    cells = clip_cells // clip_parts
    frames = clip_cells // (half * half)
    outputs = clip_cells // 8

    def by_clip(layer):
        return jnp.concatenate(
            [
                jnp.concatenate(
                    [
                        columns[
                            at, pl.ds(layer * width, width), pl.ds(clip * share, share)
                        ]
                        for at in range(slices)
                    ],
                    axis=1,
                )
                for clip in range(clips)
            ],
            axis=0,
        )

    first = by_clip(0)
    for shift in range(8):
        moved = dot(first, shift_ref[:, pl.ds(shift * clip_cells, clip_cells)]).astype(BF16)
        for clip in range(clips):
            shifts[shift, clip] = moved[clip * width : (clip + 1) * width]
    second = dot(by_clip(1), sort_ref[...]).astype(BF16)

    copy.wait()
    own_outputs = outputs // clip_parts
    blocks = channels // wide
    out_grad = jnp.concatenate(
        [
            jnp.concatenate(
                [
                    left_rows_ref[part, pl.ds(8 * cells + own_outputs * at, own_outputs), :]
                    for at in range(blocks)
                ],
                axis=1,
            )
            for part in range(parts)
        ],
        axis=0,
    )
    full = dot_nt(out_grad, jnp.concatenate(halves(left_ref[1]), axis=0))
    total = parts * own_outputs
    quarter = half // 2
    grads[pl.ds(0, total), :] = full[:, :wide] + full[:, wide:]
    places = lax.broadcasted_iota(jnp.int32, (total, wide), 0)
    frame = places // (quarter * quarter) % (frames // 2)
    row = places // quarter % quarter
    column = places % quarter
    second_rows = []
    for shift in range(8):
        dt, dr, dc = shift // 4, shift // 2 % 2, shift % 2
        moved = grads[pl.ds((dt * quarter + dr) * quarter + dc, total), :]
        inside = (frame + dt < frames // 2) & (row + dr < quarter) & (column + dc < quarter)
        second_rows.append(jnp.where(inside, moved, 0.0).astype(BF16))

    for kind in range(8):
        time, line, place = kind // 4, kind // 2 % 2, kind % 2
        taps = [
            (9 * a + 3 * b + c, 4 * (a == 0) + 2 * (b == 0) + (c == 0))
            for a in ((0, 2) if time else (1,))
            for b in ((0, 2) if line else (1,))
            for c in ((0, 2) if place else (1,))
        ]
        sums = None
        for clip in range(clips):
            left = jnp.concatenate([shifts[shift, clip] for _, shift in taps], axis=0)
            rows = jnp.concatenate(
                [
                    left_rows_ref[clip * clip_parts + part, pl.ds(kind * cells, cells), :]
                    for part in range(clip_parts)
                ],
                axis=0,
            )
            term = dot(left, rows)
            sums = term if sums is None else sums + term
        chosen = jnp.concatenate(
            [
                second[clip * width : (clip + 1) * width, kind * outputs : (kind + 1) * outputs]
                for clip in range(clips)
            ],
            axis=1,
        )
        for at, (tap, shift) in enumerate(taps):
            raw[0, tap] = sums[at * width : (at + 1) * width]
            raw[1, tap] = dot(chosen, second_rows[shift])

    @pl.loop(0, 2 * TAPS)
    def _(step):
        layer, out_tap = step // TAPS, step % TAPS
        acc = raw[layer, 0] * mix_ref[layer, out_tap, 0]
        for tap in range(1, TAPS):
            acc += raw[layer, tap] * mix_ref[layer, out_tap, tap]
        out_ref[layer, out_tap] = acc.astype(BF16)


def ring(block, axis):
    size = lax.axis_size(axis)
    return [block] + [
        lax.ppermute(block, axis, [(i, (i + distance) % size) for i in range(size)])
        for distance in range(1, size)
    ]


def shards(clip_input, first_kernel, second_kernel, out_grad, tap_mix, left_panels, right_panels):
    clips, frames, side, _, channels = clip_input.shape
    wide = first_kernel.shape[2]
    width = right_panels.shape[2]
    half, quarter = side // 2, side // 4
    half_frames = frames // 2
    cells = half_frames * half * half
    clip_parts = lax.axis_size("tm")
    parts = lax.axis_size("replica") * clip_parts
    slices = lax.axis_size("fsdp")
    share = cells // slices
    assert clips == 1 and frames == 4
    x = clip_input.reshape(frames, half, 2, side, channels)
    grad = out_grad.reshape(quarter, quarter, channels)
    prior = shifted(x[frames - 1 :], "tm", 1)[0]
    later = shifted(grad, "tm", -1)
    place = lax.axis_index("fsdp")

    projected = pl.pallas_call(
        project_kernel,
        out_shape=jax.ShapeDtypeStruct((8 * cells + quarter * quarter * channels // wide, wide), BF16),
        in_specs=[VMEM] * 3,
        out_specs=VMEM,
        scratch_shapes=[pltpu.VMEM((quarter * quarter, channels), F32)],
        compiler_params=pltpu.CompilerParams(vmem_limit_bytes=ROOM),
        cost_estimate=pl.CostEstimate(
            flops=4 * frames * side * side * channels * wide,
            bytes_accessed=2 * frames * side * side * channels,
            transcendentals=0,
        ),
    )(x, left_panels, grad)
    left_rows = lax.all_gather(projected, ("replica", "tm"), axis=0, tiled=False)

    right = lax.all_gather(right_panels.transpose(0, 2, 1).reshape(2 * width, wide), "fsdp")
    right = right.reshape(slices, 2, width, wide)

    even, odd = patch_picks(side)
    spread = jnp.asarray(spread_picks(half), BF16)
    acts = pl.pallas_call(
        hidden_kernel,
        out_shape=jax.ShapeDtypeStruct((parts, slices, 2, share, wide), BF16),
        in_specs=[VMEM] * 7 + [HBM] * 2,
        out_specs=VMEM,
        scratch_shapes=[
            pltpu.VMEM((quarter * quarter, channels), F32),
            pltpu.VMEM((frames + 1, 9, half * half, channels), BF16),
            pltpu.VMEM(first_kernel.shape, BF16),
            pltpu.VMEM(second_kernel.shape, BF16),
            pltpu.SemaphoreType.DMA((2, 3)),
        ],
        compiler_params=pltpu.CompilerParams(vmem_limit_bytes=ROOM),
        cost_estimate=pl.CostEstimate(
            flops=3 * cells * TAPS * channels * wide,
            bytes_accessed=HIDDEN_COST,
            transcendentals=cells * wide,
        ),
    )(
        x, prior, grad, later, jnp.asarray(even, BF16), jnp.asarray(odd, BF16),
        spread, first_kernel, second_kernel,
    )
    every = lax.all_to_all(
        acts.reshape(parts * slices, 2, share, wide), ("replica", "tm", "fsdp"), 0, 0, tiled=True
    ).reshape(parts, slices, 2, share, wide)
    if wide % 128:
        every = every.transpose(0, 2, 3, 1, 4).reshape(parts, 1, 2, share, channels)
        right = right.transpose(1, 2, 0, 3).reshape(1, 2, width, channels)
    own_columns = pl.pallas_call(
        right_kernel,
        out_shape=jax.ShapeDtypeStruct((2 * width, parts * share), BF16),
        in_specs=[VMEM] * 2,
        out_specs=VMEM,
        compiler_params=pltpu.CompilerParams(vmem_limit_bytes=16 << 20),
    )(every, right)

    order = clip_order(slices, clip_parts, half_frames, half)
    clip_frames = clip_parts * half_frames
    clip_cells = clip_parts * cells
    result = pl.pallas_call(
        functools.partial(update_kernel, slices=slices, clip_parts=clip_parts, half=half),
        out_shape=jax.ShapeDtypeStruct((2, TAPS, width, wide), BF16),
        in_specs=[SMEM] + [VMEM] * slices + [HBM, VMEM, SMEM, VMEM, VMEM],
        out_specs=VMEM,
        scratch_shapes=[
            pltpu.VMEM(left_rows.shape, BF16),
            pltpu.VMEM((slices, 2 * width, parts * share), BF16),
            pltpu.VMEM((8, parts // clip_parts, width, clip_cells), BF16),
            pltpu.VMEM((parts * cells // 8 + (quarter + 1) * quarter + 8, wide), F32),
            pltpu.VMEM((2, TAPS, width, wide), F32),
            pltpu.SemaphoreType.DMA,
        ],
        compiler_params=pltpu.CompilerParams(vmem_limit_bytes=ROOM),
    )(
        place.reshape(1), *ring(own_columns, "fsdp"), left_rows, left_panels, tap_mix,
        jnp.asarray(shift_picks(order, clip_frames, half), BF16),
        jnp.asarray(sort_picks(order, clip_frames, half), BF16),
    )
    return result.transpose(0, 1, 3, 2)


def solution(mesh):
    in_specs = (
        P("replica", "tm", None, None, None),
        P(None, None, "fsdp"),
        P(None, "fsdp", None),
        P("replica", "tm", None, None, None),
        P(),
        P(None, "fsdp", None),
        P(None, "fsdp", ("replica", "tm")),
    )
    out_specs = P(None, None, "fsdp", ("replica", "tm"))
    return jax.shard_map(shards, mesh=mesh, in_specs=in_specs, out_specs=out_specs, check_vma=False)
```

```python
import functools

import jax
import jax.numpy as jnp
import numpy as np
from jax import lax
from jax.experimental import pallas as pl
from jax.experimental.pallas import tpu as pltpu
from jax.sharding import PartitionSpec as P

TAPS = 27
F32, BF16 = jnp.float32, jnp.bfloat16
ROOM = 58 << 20
HIDDEN_COST = 200 << 20
NT = (((1,), (1,)), ((), ()))
VMEM = pl.BlockSpec(memory_space=pltpu.VMEM)
HBM = pl.BlockSpec(memory_space=pltpu.HBM)
SMEM = pl.BlockSpec(memory_space=pltpu.SMEM)


def shifted(block, axis, distance):
    devices = range(lax.axis_size(axis))
    route = [(i - distance, i) for i in devices if i - distance in devices]
    return lax.ppermute(block, axis, route)


def dot(left, right):
    return jnp.dot(left, right, preferred_element_type=F32)


def dot_nt(left, right):
    return lax.dot_general(left, right, NT, preferred_element_type=F32)


def halves(value):
    high = value.astype(BF16)
    return high, (value - high.astype(F32)).astype(BF16)


def patch_picks(side):
    half = side // 2
    even = np.zeros((1, 3, half, half, half, side), np.float32)
    odd = np.zeros((2, 3, half, half, half, side), np.float32)
    for c in range(3):
        for y in range(half):
            for x in range(half):
                column = 2 * x + c - 1
                if column < 0:
                    continue
                even[0, c, y, x, y, column] = 1
                if y > 0:
                    odd[0, c, y, x, y - 1, column] = 1
                odd[1, c, y, x, y, column] = 1
    return even.reshape(-1, half * side), odd.reshape(-1, half * side)


def spread_picks(half):
    quarter = half // 2
    picks = np.zeros((3, 3, half, half, quarter, quarter), np.float32)
    for b in range(3):
        for c in range(3):
            for out_y in range(quarter):
                for out_x in range(quarter):
                    y, x = 2 * out_y + b - 1, 2 * out_x + c - 1
                    if y >= 0 and x >= 0:
                        picks[b, c, y, x, out_y, out_x] = 1
    return picks.reshape(9 * half * half, quarter * quarter)


def clip_order(slices, clip_parts, half_frames, half):
    cells = half_frames * half * half
    order = np.arange(clip_parts * cells).reshape(clip_parts, slices, cells // slices)
    return order.transpose(1, 0, 2).reshape(-1)


def shift_picks(order, frames, half):
    size = frames * half * half
    picks = np.zeros((size, 2, 2, 2, frames, half, half), np.float32)
    at = np.empty(size, np.int64)
    at[order] = np.arange(size)
    at = at.reshape(frames, half, half)
    for dt, dr, dc in np.ndindex(2, 2, 2):
        for t, y, x in np.ndindex(frames - dt, half - dr, half - dc):
            picks[at[t + dt, y + dr, x + dc], dt, dr, dc, t, y, x] = 1
    return picks.reshape(size, 8 * size)


def sort_picks(order, frames, half):
    size = frames * half * half
    index = np.arange(size).reshape(frames // 2, 2, half // 2, 2, half // 2, 2)
    wanted = index.transpose(1, 3, 5, 0, 2, 4).reshape(-1)
    at = np.empty(size, np.int64)
    at[order] = np.arange(size)
    picks = np.zeros((size, size), np.float32)
    picks[at[wanted], np.arange(size)] = 1
    return picks


def project_kernel(x_ref, left_ref, grad_ref, out_ref, rows_ref):
    frames, half, _, side, channels = x_ref.shape
    wide = left_ref.shape[1]
    pairs = frames // 2
    size = pairs * half * side
    both = jnp.concatenate(halves(left_ref[0]), axis=0)
    target = lax.broadcasted_iota(jnp.int32, (size, size), 0)
    source = lax.broadcasted_iota(jnp.int32, (size, size), 1)
    cells = size // 2
    wanted = 2 * (target % cells) + target // cells
    pick = jnp.where(source == wanted, 1.0, 0.0).astype(BF16)
    for time in range(2):
        for row in range(2):
            block = jnp.concatenate(
                [
                    x_ref[frame, :, row].reshape(half * side, channels)
                    for frame in range(time, frames, 2)
                ],
                axis=0,
            )
            full = dot_nt(block, both)
            small = (full[:, :wide] + full[:, wide:]).astype(BF16)
            ordered = dot(pick, small).astype(BF16)
            at = (4 * time + 2 * row) * cells
            out_ref[at : at + size, :] = ordered
    rows = stacked_rows(grad_ref, rows_ref)
    count = rows.shape[0]
    for block in range(channels // wide):
        at = 8 * cells + block * count
        out_ref[at : at + count, :] = rows[:, block * wide : (block + 1) * wide]


def stacked_rows(grad_ref, rows_ref):
    quarter = grad_ref.shape[0]
    for row in range(quarter):
        rows_ref[pl.ds(row * quarter, quarter), :] = grad_ref[row].astype(F32)
    return rows_ref[...].astype(BF16)


def transposed_products(rows, kernel, taps):
    total = dot_nt(rows[0], kernel[taps[0]])
    for at in range(1, len(taps)):
        total += dot_nt(rows[at], kernel[taps[at]])
    return total


def spread_rows(picks_ref, rows, cells):
    spread = dot(picks_ref[...], rows).astype(BF16)
    return [spread[tap * cells : (tap + 1) * cells] for tap in range(9)]


def hidden_kernel(
    x_ref, prior_ref, grad_ref, later_ref, even_ref, odd_ref, spread_ref, first_any, second_any,
    out_ref, rows_ref, patches, first, second, arrived,
):
    frames, half, _, side, channels = x_ref.shape
    cells = half * half
    copies = {
        (at, a): pltpu.make_async_copy(
            source.at[pl.ds(9 * a, 9)], target.at[pl.ds(9 * a, 9)], arrived.at[at, a]
        )
        for at, (source, target) in enumerate(((second_any, second), (first_any, first)))
        for a in (1, 2, 0)
    }
    for copy in copies.values():
        copy.start()
    own = spread_rows(spread_ref, stacked_rows(grad_ref, rows_ref), cells)
    copies[0, 1].wait()
    early = transposed_products(own, second, range(9, 18))
    copies[0, 2].wait()
    late = transposed_products(own, second, range(18, 27))
    for frame in range(frames + 1):
        block = prior_ref if frame == 0 else x_ref.at[frame - 1]
        even = dot(even_ref[...], block[:, 0].reshape(half * side, channels)).astype(BF16)
        odd = dot(odd_ref[...], block[:, 1].reshape(half * side, channels)).astype(BF16)
        for c in range(3):
            patches[frame, c] = odd[c * cells : (c + 1) * cells]
            patches[frame, 3 + c] = even[c * cells : (c + 1) * cells]
            patches[frame, 6 + c] = odd[(3 + c) * cells : (4 + c) * cells]
    after = spread_rows(spread_ref, stacked_rows(later_ref, rows_ref), cells)
    copies[0, 0].wait()
    late += transposed_products(after, second, range(9))
    hidden_grad = jnp.concatenate([early, late], axis=0)
    pre = jnp.zeros((2 * cells, first.shape[2]), F32)
    for a in (1, 2, 0):
        copies[1, a].wait()
        for tap in range(9):
            rows = jnp.concatenate([patches[a, tap], patches[a + 2, tap]], axis=0)
            pre += dot(rows, first[9 * a + tap])
    sig = jax.nn.sigmoid(pre)
    hidden = (pre * sig).astype(BF16)
    pre_grad = (hidden_grad * sig * (1.0 + pre * (1.0 - sig))).astype(BF16)
    groups, slices, _, share, _ = out_ref.shape
    for at in range(slices):
        place = slice(at * share, (at + 1) * share)
        for group in range(groups):
            out_ref[group, at, 0] = pre_grad[place]
            out_ref[group, at, 1] = hidden[place]


def right_kernel(place_ref, acts_ref, *refs):
    right_refs, out_ref = refs[:-1], refs[-1]
    columns = right_refs[0].shape[1]
    parts, slices = acts_ref.shape[:2]
    for layer in range(2):
        total = None
        for distance in range(slices):
            origin = lax.rem(place_ref[0] + (slices - distance), slices)
            both = jnp.concatenate(halves(right_refs[distance][layer]), axis=0)
            rows = jnp.concatenate([acts_ref[part, origin, layer] for part in range(parts)], axis=0)
            term = dot_nt(both, rows)
            total = term if total is None else total + term
        out_ref[pl.ds(layer * columns, columns), :] = (total[:columns] + total[columns:]).astype(BF16)


def update_kernel(place_ref, *refs, slices, clip_parts, half):
    own_refs = refs[:slices]
    (
        left_rows_ref, left_ref, mix_ref, shift_ref, sort_ref,
        out_ref, columns, shifts, grads, raw,
    ) = refs[slices:]
    for distance in range(slices):
        origin = lax.rem(place_ref[0] + (slices - distance), slices)
        columns[origin] = own_refs[distance][...]
    parts = left_rows_ref.shape[0]
    wide, channels = left_ref.shape[1:]
    width = columns.shape[1] // 2
    clips = parts // clip_parts
    share = columns.shape[2] // clips
    clip_cells = slices * share
    cells = clip_cells // clip_parts
    frames = clip_cells // (half * half)
    outputs = clip_cells // 8

    def by_clip(layer):
        return jnp.concatenate(
            [
                jnp.concatenate(
                    [
                        columns[
                            at, pl.ds(layer * width, width), pl.ds(clip * share, share)
                        ]
                        for at in range(slices)
                    ],
                    axis=1,
                )
                for clip in range(clips)
            ],
            axis=0,
        )

    first = by_clip(0)
    for shift in range(8):
        moved = dot(first, shift_ref[:, pl.ds(shift * clip_cells, clip_cells)]).astype(BF16)
        for clip in range(clips):
            shifts[shift, clip] = moved[clip * width : (clip + 1) * width]
    second = dot(by_clip(1), sort_ref[...]).astype(BF16)

    own_outputs = outputs // clip_parts
    blocks = channels // wide
    out_grad = jnp.concatenate(
        [
            jnp.concatenate(
                [
                    left_rows_ref[part, pl.ds(8 * cells + own_outputs * at, own_outputs), :]
                    for at in range(blocks)
                ],
                axis=1,
            )
            for part in range(parts)
        ],
        axis=0,
    )
    full = dot_nt(out_grad, jnp.concatenate(halves(left_ref[1]), axis=0))
    total = parts * own_outputs
    quarter = half // 2
    grads[pl.ds(0, total), :] = full[:, :wide] + full[:, wide:]
    places = lax.broadcasted_iota(jnp.int32, (total, wide), 0)
    frame = places // (quarter * quarter) % (frames // 2)
    row = places // quarter % quarter
    column = places % quarter
    second_rows = []
    for shift in range(8):
        dt, dr, dc = shift // 4, shift // 2 % 2, shift % 2
        moved = grads[pl.ds((dt * quarter + dr) * quarter + dc, total), :]
        inside = (frame + dt < frames // 2) & (row + dr < quarter) & (column + dc < quarter)
        second_rows.append(jnp.where(inside, moved, 0.0).astype(BF16))

    for kind in range(8):
        time, line, place = kind // 4, kind // 2 % 2, kind % 2
        taps = [
            (9 * a + 3 * b + c, 4 * (a == 0) + 2 * (b == 0) + (c == 0))
            for a in ((0, 2) if time else (1,))
            for b in ((0, 2) if line else (1,))
            for c in ((0, 2) if place else (1,))
        ]
        sums = None
        for clip in range(clips):
            left = jnp.concatenate([shifts[shift, clip] for _, shift in taps], axis=0)
            rows = jnp.concatenate(
                [
                    left_rows_ref[clip * clip_parts + part, pl.ds(kind * cells, cells), :]
                    for part in range(clip_parts)
                ],
                axis=0,
            )
            term = dot(left, rows)
            sums = term if sums is None else sums + term
        chosen = jnp.concatenate(
            [
                second[clip * width : (clip + 1) * width, kind * outputs : (kind + 1) * outputs]
                for clip in range(clips)
            ],
            axis=1,
        )
        for at, (tap, shift) in enumerate(taps):
            raw[0, tap] = sums[at * width : (at + 1) * width]
            raw[1, tap] = dot(chosen, second_rows[shift])

    @pl.loop(0, 2 * TAPS)
    def _(step):
        layer, out_tap = step // TAPS, step % TAPS
        acc = raw[layer, 0] * mix_ref[layer, out_tap, 0]
        for tap in range(1, TAPS):
            acc += raw[layer, tap] * mix_ref[layer, out_tap, tap]
        out_ref[layer, out_tap] = acc.astype(BF16)


def ring(block, axis):
    size = lax.axis_size(axis)
    return [block] + [
        lax.ppermute(block, axis, [(i, (i + distance) % size) for i in range(size)])
        for distance in range(1, size)
    ]


def shards(clip_input, first_kernel, second_kernel, out_grad, tap_mix, left_panels, right_panels):
    clips, frames, side, _, channels = clip_input.shape
    wide = first_kernel.shape[2]
    width = right_panels.shape[2]
    half, quarter = side // 2, side // 4
    half_frames = frames // 2
    cells = half_frames * half * half
    clip_parts = lax.axis_size("tm")
    parts = lax.axis_size("replica") * clip_parts
    slices = lax.axis_size("fsdp")
    share = cells // slices
    assert clips == 1 and frames == 4
    x = clip_input.reshape(frames, half, 2, side, channels)
    grad = out_grad.reshape(quarter, quarter, channels)
    prior = shifted(x[frames - 1 :], "tm", 1)[0]
    later = shifted(grad, "tm", -1)
    place = lax.axis_index("fsdp")

    projected = pl.pallas_call(
        project_kernel,
        out_shape=jax.ShapeDtypeStruct((8 * cells + quarter * quarter * channels // wide, wide), BF16),
        in_specs=[VMEM] * 3,
        out_specs=VMEM,
        scratch_shapes=[pltpu.VMEM((quarter * quarter, channels), F32)],
        compiler_params=pltpu.CompilerParams(vmem_limit_bytes=ROOM),
        cost_estimate=pl.CostEstimate(
            flops=4 * frames * side * side * channels * wide,
            bytes_accessed=2 * frames * side * side * channels,
            transcendentals=0,
        ),
    )(x, left_panels, grad)
    left_rows = lax.all_gather(projected, ("replica", "tm"), axis=0, tiled=False)

    rights = ring(right_panels.transpose(0, 2, 1), "fsdp")

    even, odd = patch_picks(side)
    spread = jnp.asarray(spread_picks(half), BF16)
    acts = pl.pallas_call(
        hidden_kernel,
        out_shape=jax.ShapeDtypeStruct((parts, slices, 2, share, wide), BF16),
        in_specs=[VMEM] * 7 + [HBM] * 2,
        out_specs=VMEM,
        scratch_shapes=[
            pltpu.VMEM((quarter * quarter, channels), F32),
            pltpu.VMEM((frames + 1, 9, half * half, channels), BF16),
            pltpu.VMEM(first_kernel.shape, BF16),
            pltpu.VMEM(second_kernel.shape, BF16),
            pltpu.SemaphoreType.DMA((2, 3)),
        ],
        compiler_params=pltpu.CompilerParams(vmem_limit_bytes=ROOM),
        cost_estimate=pl.CostEstimate(
            flops=3 * cells * TAPS * channels * wide,
            bytes_accessed=HIDDEN_COST,
            transcendentals=cells * wide,
        ),
    )(
        x, prior, grad, later, jnp.asarray(even, BF16), jnp.asarray(odd, BF16),
        spread, first_kernel, second_kernel,
    )
    acts, *rights = lax.optimization_barrier((acts, *rights))
    every = lax.all_to_all(
        acts.reshape(parts * slices, 2, share, wide), ("replica", "tm", "fsdp"), 0, 0, tiled=True
    ).reshape(parts, slices, 2, share, wide)
    own_columns = pl.pallas_call(
        right_kernel,
        out_shape=jax.ShapeDtypeStruct((2 * width, parts * share), BF16),
        in_specs=[SMEM] + [VMEM] * (slices + 1),
        out_specs=VMEM,
        compiler_params=pltpu.CompilerParams(vmem_limit_bytes=16 << 20),
    )(place.reshape(1), every, *rights)
    own_columns, left_rows = lax.optimization_barrier((own_columns, left_rows))

    order = clip_order(slices, clip_parts, half_frames, half)
    clip_frames = clip_parts * half_frames
    clip_cells = clip_parts * cells
    result = pl.pallas_call(
        functools.partial(update_kernel, slices=slices, clip_parts=clip_parts, half=half),
        out_shape=jax.ShapeDtypeStruct((2, TAPS, width, wide), BF16),
        in_specs=[SMEM] + [VMEM] * (slices + 2) + [SMEM, VMEM, VMEM],
        out_specs=VMEM,
        scratch_shapes=[
            pltpu.VMEM((slices, 2 * width, parts * share), BF16),
            pltpu.VMEM((8, parts // clip_parts, width, clip_cells), BF16),
            pltpu.VMEM((parts * cells // 8 + (quarter + 1) * quarter + 8, wide), F32),
            pltpu.VMEM((2, TAPS, width, wide), F32),
        ],
        compiler_params=pltpu.CompilerParams(vmem_limit_bytes=40 << 20),
    )(
        place.reshape(1), *ring(own_columns, "fsdp"), left_rows, left_panels, tap_mix,
        jnp.asarray(shift_picks(order, clip_frames, half), BF16),
        jnp.asarray(sort_picks(order, clip_frames, half), BF16),
    )
    return result.transpose(0, 1, 3, 2)


def solution(mesh):
    in_specs = (
        P("replica", "tm", None, None, None),
        P(None, None, "fsdp"),
        P(None, "fsdp", None),
        P("replica", "tm", None, None, None),
        P(),
        P(None, "fsdp", None),
        P(None, "fsdp", ("replica", "tm")),
    )
    out_specs = P(None, None, "fsdp", ("replica", "tm"))
    return jax.shard_map(shards, mesh=mesh, in_specs=in_specs, out_specs=out_specs, check_vma=False)
```

```python
import functools

import jax
import jax.numpy as jnp
import numpy as np
from jax import lax
from jax.experimental import pallas as pl
from jax.experimental.pallas import tpu as pltpu
from jax.sharding import PartitionSpec as P

TAPS = 27
F32, BF16 = jnp.float32, jnp.bfloat16
ROOM = 58 << 20
HIDDEN_COST = 200 << 20
NT = (((1,), (1,)), ((), ()))
VMEM = pl.BlockSpec(memory_space=pltpu.VMEM)
HBM = pl.BlockSpec(memory_space=pltpu.HBM)
SMEM = pl.BlockSpec(memory_space=pltpu.SMEM)
ANY = pl.BlockSpec(memory_space=pl.ANY)


def shifted(block, axis, distance):
    devices = range(lax.axis_size(axis))
    route = [(i - distance, i) for i in devices if i - distance in devices]
    return lax.ppermute(block, axis, route)


def dot(left, right):
    return jnp.dot(left, right, preferred_element_type=F32)


def dot_nt(left, right):
    return lax.dot_general(left, right, NT, preferred_element_type=F32)


def halves(value):
    high = value.astype(BF16)
    return high, (value - high.astype(F32)).astype(BF16)


def patch_picks(side):
    half = side // 2
    even = np.zeros((1, 3, half, half, half, side), np.float32)
    odd = np.zeros((2, 3, half, half, half, side), np.float32)
    for c in range(3):
        for y in range(half):
            for x in range(half):
                column = 2 * x + c - 1
                if column < 0:
                    continue
                even[0, c, y, x, y, column] = 1
                if y > 0:
                    odd[0, c, y, x, y - 1, column] = 1
                odd[1, c, y, x, y, column] = 1
    return even.reshape(-1, half * side), odd.reshape(-1, half * side)


def spread_picks(half):
    quarter = half // 2
    picks = np.zeros((3, 3, half, half, quarter, quarter), np.float32)
    for b in range(3):
        for c in range(3):
            for out_y in range(quarter):
                for out_x in range(quarter):
                    y, x = 2 * out_y + b - 1, 2 * out_x + c - 1
                    if y >= 0 and x >= 0:
                        picks[b, c, y, x, out_y, out_x] = 1
    return picks.reshape(9 * half * half, quarter * quarter)


def clip_order(slices, clip_parts, half_frames, half):
    cells = half_frames * half * half
    order = np.arange(clip_parts * cells).reshape(clip_parts, slices, cells // slices)
    return order.transpose(1, 0, 2).reshape(-1)


def shift_picks(order, frames, half):
    size = frames * half * half
    picks = np.zeros((size, 2, 2, 2, frames, half, half), np.float32)
    at = np.empty(size, np.int64)
    at[order] = np.arange(size)
    at = at.reshape(frames, half, half)
    for dt, dr, dc in np.ndindex(2, 2, 2):
        for t, y, x in np.ndindex(frames - dt, half - dr, half - dc):
            picks[at[t + dt, y + dr, x + dc], dt, dr, dc, t, y, x] = 1
    return picks.reshape(size, 8 * size)


def sort_picks(order, frames, half):
    size = frames * half * half
    index = np.arange(size).reshape(frames // 2, 2, half // 2, 2, half // 2, 2)
    wanted = index.transpose(1, 3, 5, 0, 2, 4).reshape(-1)
    at = np.empty(size, np.int64)
    at[order] = np.arange(size)
    picks = np.zeros((size, size), np.float32)
    picks[at[wanted], np.arange(size)] = 1
    return picks


def project_kernel(x_ref, left_ref, grad_ref, out_ref, rows_ref):
    frames, half, _, side, channels = x_ref.shape
    wide = left_ref.shape[1]
    pairs = frames // 2
    size = pairs * half * side
    both = jnp.concatenate(halves(left_ref[0]), axis=0)
    target = lax.broadcasted_iota(jnp.int32, (size, size), 0)
    source = lax.broadcasted_iota(jnp.int32, (size, size), 1)
    cells = size // 2
    wanted = 2 * (target % cells) + target // cells
    pick = jnp.where(source == wanted, 1.0, 0.0).astype(BF16)
    for time in range(2):
        for row in range(2):
            block = jnp.concatenate(
                [
                    x_ref[frame, :, row].reshape(half * side, channels)
                    for frame in range(time, frames, 2)
                ],
                axis=0,
            )
            full = dot_nt(block, both)
            small = (full[:, :wide] + full[:, wide:]).astype(BF16)
            ordered = dot(pick, small).astype(BF16)
            at = (4 * time + 2 * row) * cells
            out_ref[at : at + size, :] = ordered
    rows = stacked_rows(grad_ref, rows_ref)
    count = rows.shape[0]
    for block in range(channels // wide):
        at = 8 * cells + block * count
        out_ref[at : at + count, :] = rows[:, block * wide : (block + 1) * wide]


def stacked_rows(grad_ref, rows_ref):
    quarter = grad_ref.shape[0]
    for row in range(quarter):
        rows_ref[pl.ds(row * quarter, quarter), :] = grad_ref[row].astype(F32)
    return rows_ref[...].astype(BF16)


def transposed_products(rows, kernel, taps):
    total = dot_nt(rows[0], kernel[taps[0]])
    for at in range(1, len(taps)):
        total += dot_nt(rows[at], kernel[taps[at]])
    return total


def spread_rows(picks_ref, rows, cells):
    spread = dot(picks_ref[...], rows).astype(BF16)
    return [spread[tap * cells : (tap + 1) * cells] for tap in range(9)]


def hidden_kernel(
    x_ref, prior_ref, grad_ref, later_ref, even_ref, odd_ref, spread_ref, first_any, second_any,
    out_ref, rows_ref, patches, first, second, arrived,
):
    frames, half, _, side, channels = x_ref.shape
    cells = half * half
    copies = {
        (at, a): pltpu.make_async_copy(
            source.at[pl.ds(9 * a, 9)], target.at[pl.ds(9 * a, 9)], arrived.at[at, a]
        )
        for at, (source, target) in enumerate(((second_any, second), (first_any, first)))
        for a in (1, 2, 0)
    }
    for copy in copies.values():
        copy.start()
    own = spread_rows(spread_ref, stacked_rows(grad_ref, rows_ref), cells)
    copies[0, 1].wait()
    early = transposed_products(own, second, range(9, 18))
    copies[0, 2].wait()
    late = transposed_products(own, second, range(18, 27))
    for frame in range(frames + 1):
        block = prior_ref if frame == 0 else x_ref.at[frame - 1]
        even = dot(even_ref[...], block[:, 0].reshape(half * side, channels)).astype(BF16)
        odd = dot(odd_ref[...], block[:, 1].reshape(half * side, channels)).astype(BF16)
        for c in range(3):
            patches[frame, c] = odd[c * cells : (c + 1) * cells]
            patches[frame, 3 + c] = even[c * cells : (c + 1) * cells]
            patches[frame, 6 + c] = odd[(3 + c) * cells : (4 + c) * cells]
    after = spread_rows(spread_ref, stacked_rows(later_ref, rows_ref), cells)
    copies[0, 0].wait()
    late += transposed_products(after, second, range(9))
    hidden_grad = jnp.concatenate([early, late], axis=0)
    pre = jnp.zeros((2 * cells, first.shape[2]), F32)
    for a in (1, 2, 0):
        copies[1, a].wait()
        for tap in range(9):
            rows = jnp.concatenate([patches[a, tap], patches[a + 2, tap]], axis=0)
            pre += dot(rows, first[9 * a + tap])
    sig = jax.nn.sigmoid(pre)
    hidden = (pre * sig).astype(BF16)
    pre_grad = (hidden_grad * sig * (1.0 + pre * (1.0 - sig))).astype(BF16)
    groups, slices, _, share, _ = out_ref.shape
    for at in range(slices):
        place = slice(at * share, (at + 1) * share)
        for group in range(groups):
            out_ref[group, at, 0] = pre_grad[place]
            out_ref[group, at, 1] = hidden[place]


def right_kernel(place_ref, acts_ref, *refs):
    right_refs, out_ref = refs[:-1], refs[-1]
    columns = right_refs[0].shape[1]
    parts, slices = acts_ref.shape[:2]
    for layer in range(2):
        total = None
        for distance in range(slices):
            origin = lax.rem(place_ref[0] + (slices - distance), slices)
            both = jnp.concatenate(halves(right_refs[distance][layer]), axis=0)
            rows = jnp.concatenate([acts_ref[part, origin, layer] for part in range(parts)], axis=0)
            term = dot_nt(both, rows)
            total = term if total is None else total + term
        out_ref[pl.ds(layer * columns, columns), :] = (total[:columns] + total[columns:]).astype(BF16)


def update_kernel(place_ref, replica_ref, tm_ref, *refs, slices, pairs, clip_parts, half):
    own_refs, piece_refs = refs[:slices], refs[slices : slices + pairs]
    (
        left_ref, mix_ref, shift_ref, sort_ref,
        out_ref, left_rows_ref, columns, shifts, grads, raw, arrived,
    ) = refs[slices + pairs :]
    parts = left_rows_ref.shape[0]
    origins = plane_origins(replica_ref[0], tm_ref[0], parts // clip_parts, clip_parts)
    copies = []
    for at, origin in enumerate(origins):
        pair, block = divmod(at, parts // pairs)
        copies.append(
            pltpu.make_async_copy(
                piece_refs[pair].at[block], left_rows_ref.at[origin], arrived.at[at]
            )
        )
    for copy in copies:
        copy.start()
    for distance in range(slices):
        origin = lax.rem(place_ref[0] + (slices - distance), slices)
        columns[origin] = own_refs[distance][...]
    wide, channels = left_ref.shape[1:]
    width = columns.shape[1] // 2
    clips = parts // clip_parts
    share = columns.shape[2] // clips
    clip_cells = slices * share
    cells = clip_cells // clip_parts
    frames = clip_cells // (half * half)
    outputs = clip_cells // 8

    def by_clip(layer):
        return jnp.concatenate(
            [
                jnp.concatenate(
                    [
                        columns[
                            at, pl.ds(layer * width, width), pl.ds(clip * share, share)
                        ]
                        for at in range(slices)
                    ],
                    axis=1,
                )
                for clip in range(clips)
            ],
            axis=0,
        )

    first = by_clip(0)
    for shift in range(8):
        moved = dot(first, shift_ref[:, pl.ds(shift * clip_cells, clip_cells)]).astype(BF16)
        for clip in range(clips):
            shifts[shift, clip] = moved[clip * width : (clip + 1) * width]
    second = dot(by_clip(1), sort_ref[...]).astype(BF16)

    for copy in copies:
        copy.wait()
    own_outputs = outputs // clip_parts
    blocks = channels // wide
    out_grad = jnp.concatenate(
        [
            jnp.concatenate(
                [
                    left_rows_ref[part, pl.ds(8 * cells + own_outputs * at, own_outputs), :]
                    for at in range(blocks)
                ],
                axis=1,
            )
            for part in range(parts)
        ],
        axis=0,
    )
    full = dot_nt(out_grad, jnp.concatenate(halves(left_ref[1]), axis=0))
    total = parts * own_outputs
    quarter = half // 2
    grads[pl.ds(0, total), :] = full[:, :wide] + full[:, wide:]
    places = lax.broadcasted_iota(jnp.int32, (total, wide), 0)
    frame = places // (quarter * quarter) % (frames // 2)
    row = places // quarter % quarter
    column = places % quarter
    second_rows = []
    for shift in range(8):
        dt, dr, dc = shift // 4, shift // 2 % 2, shift % 2
        moved = grads[pl.ds((dt * quarter + dr) * quarter + dc, total), :]
        inside = (frame + dt < frames // 2) & (row + dr < quarter) & (column + dc < quarter)
        second_rows.append(jnp.where(inside, moved, 0.0).astype(BF16))

    for kind in range(8):
        time, line, place = kind // 4, kind // 2 % 2, kind % 2
        taps = [
            (9 * a + 3 * b + c, 4 * (a == 0) + 2 * (b == 0) + (c == 0))
            for a in ((0, 2) if time else (1,))
            for b in ((0, 2) if line else (1,))
            for c in ((0, 2) if place else (1,))
        ]
        sums = None
        for clip in range(clips):
            left = jnp.concatenate([shifts[shift, clip] for _, shift in taps], axis=0)
            rows = jnp.concatenate(
                [
                    left_rows_ref[clip * clip_parts + part, pl.ds(kind * cells, cells), :]
                    for part in range(clip_parts)
                ],
                axis=0,
            )
            term = dot(left, rows)
            sums = term if sums is None else sums + term
        chosen = jnp.concatenate(
            [
                second[clip * width : (clip + 1) * width, kind * outputs : (kind + 1) * outputs]
                for clip in range(clips)
            ],
            axis=1,
        )
        for at, (tap, shift) in enumerate(taps):
            raw[0, tap] = sums[at * width : (at + 1) * width]
            raw[1, tap] = dot(chosen, second_rows[shift])

    @pl.loop(0, 2 * TAPS)
    def _(step):
        layer, out_tap = step // TAPS, step % TAPS
        acc = raw[layer, 0] * mix_ref[layer, out_tap, 0]
        for tap in range(1, TAPS):
            acc += raw[layer, tap] * mix_ref[layer, out_tap, tap]
        out_ref[layer, out_tap] = acc.astype(BF16)


def ring(block, axis):
    size = lax.axis_size(axis)
    return [block] + [
        lax.ppermute(block, axis, [(i, (i + distance) % size) for i in range(size)])
        for distance in range(1, size)
    ]


def plane_routes(replicas, tm_size):
    pair = 2 if replicas % 2 == 0 else 1
    return pair, list(np.ndindex(replicas // pair, tm_size))


def plane_blocks(block):
    axes = ("replica", "tm")
    replicas, tm_size = lax.axis_size("replica"), lax.axis_size("tm")
    pair, steps = plane_routes(replicas, tm_size)
    pieces = []
    for step, turn in steps:
        route = [
            (r * tm_size + t, (r + pair * step) % replicas * tm_size + (t + turn) % tm_size)
            for r, t in np.ndindex(replicas, tm_size)
        ]
        pieces.append(lax.ppermute(block, axes, route) if step or turn else block)
    return jnp.stack(pieces)


def partner_blocks(held):
    replicas, tm_size = lax.axis_size("replica"), lax.axis_size("tm")
    if replicas % 2:
        return []
    route = [(r * tm_size + t, (r ^ 1) * tm_size + t) for r, t in np.ndindex(replicas, tm_size)]
    return [lax.ppermute(held, ("replica", "tm"), route)]


def plane_origins(replica, half, replicas, tm_size):
    pair, steps = plane_routes(replicas, tm_size)
    origins = []
    for own in (replica, replica + 1 - 2 * lax.rem(replica, 2))[:pair]:
        for step, turn in steps:
            row = lax.rem(own + (replicas - pair * step), replicas)
            origins.append(row * tm_size + lax.rem(half + (tm_size - turn), tm_size))
    return origins


def shards(clip_input, first_kernel, second_kernel, out_grad, tap_mix, left_panels, right_panels):
    clips, frames, side, _, channels = clip_input.shape
    wide = first_kernel.shape[2]
    width = right_panels.shape[2]
    half, quarter = side // 2, side // 4
    half_frames = frames // 2
    cells = half_frames * half * half
    clip_parts = lax.axis_size("tm")
    parts = lax.axis_size("replica") * clip_parts
    slices = lax.axis_size("fsdp")
    share = cells // slices
    assert clips == 1 and frames == 4
    x = clip_input.reshape(frames, half, 2, side, channels)
    grad = out_grad.reshape(quarter, quarter, channels)
    prior = shifted(x[frames - 1 :], "tm", 1)[0]
    later = shifted(grad, "tm", -1)
    place = lax.axis_index("fsdp")

    projected = pl.pallas_call(
        project_kernel,
        out_shape=jax.ShapeDtypeStruct((8 * cells + quarter * quarter * channels // wide, wide), BF16),
        in_specs=[VMEM] * 3,
        out_specs=VMEM,
        scratch_shapes=[pltpu.VMEM((quarter * quarter, channels), F32)],
        compiler_params=pltpu.CompilerParams(vmem_limit_bytes=ROOM),
        cost_estimate=pl.CostEstimate(
            flops=4 * frames * side * side * channels * wide,
            bytes_accessed=2 * frames * side * side * channels,
            transcendentals=0,
        ),
    )(x, left_panels, grad)
    held = plane_blocks(projected)

    rights = ring(right_panels.transpose(0, 2, 1), "fsdp")

    even, odd = patch_picks(side)
    spread = jnp.asarray(spread_picks(half), BF16)
    acts = pl.pallas_call(
        hidden_kernel,
        out_shape=jax.ShapeDtypeStruct((parts, slices, 2, share, wide), BF16),
        in_specs=[VMEM] * 7 + [HBM] * 2,
        out_specs=VMEM,
        scratch_shapes=[
            pltpu.VMEM((quarter * quarter, channels), F32),
            pltpu.VMEM((frames + 1, 9, half * half, channels), BF16),
            pltpu.VMEM(first_kernel.shape, BF16),
            pltpu.VMEM(second_kernel.shape, BF16),
            pltpu.SemaphoreType.DMA((2, 3)),
        ],
        compiler_params=pltpu.CompilerParams(vmem_limit_bytes=ROOM),
        cost_estimate=pl.CostEstimate(
            flops=3 * cells * TAPS * channels * wide,
            bytes_accessed=HIDDEN_COST,
            transcendentals=cells * wide,
        ),
    )(
        x, prior, grad, later, jnp.asarray(even, BF16), jnp.asarray(odd, BF16),
        spread, first_kernel, second_kernel,
    )
    acts, held, *rights = lax.optimization_barrier((acts, held, *rights))
    left_rows = [held] + partner_blocks(held)
    every = lax.all_to_all(
        acts.reshape(parts * slices, 2, share, wide), ("replica", "tm", "fsdp"), 0, 0, tiled=True
    ).reshape(parts, slices, 2, share, wide)
    own_columns = pl.pallas_call(
        right_kernel,
        out_shape=jax.ShapeDtypeStruct((2 * width, parts * share), BF16),
        in_specs=[SMEM] + [VMEM] * (slices + 1),
        out_specs=VMEM,
        compiler_params=pltpu.CompilerParams(vmem_limit_bytes=16 << 20),
    )(place.reshape(1), every, *rights)

    order = clip_order(slices, clip_parts, half_frames, half)
    clip_frames = clip_parts * half_frames
    clip_cells = clip_parts * cells
    result = pl.pallas_call(
        functools.partial(
            update_kernel, slices=slices, pairs=len(left_rows), clip_parts=clip_parts, half=half
        ),
        out_shape=jax.ShapeDtypeStruct((2, TAPS, width, wide), BF16),
        in_specs=[SMEM] * 3
        + [VMEM] * slices
        + [ANY] * len(left_rows)
        + [VMEM, SMEM, VMEM, VMEM],
        out_specs=VMEM,
        scratch_shapes=[
            pltpu.VMEM((parts,) + projected.shape, BF16),
            pltpu.VMEM((slices, 2 * width, parts * share), BF16),
            pltpu.VMEM((8, parts // clip_parts, width, clip_cells), BF16),
            pltpu.VMEM((parts * cells // 8 + (quarter + 1) * quarter + 8, wide), F32),
            pltpu.VMEM((2, TAPS, width, wide), F32),
            pltpu.SemaphoreType.DMA((parts,)),
        ],
        compiler_params=pltpu.CompilerParams(vmem_limit_bytes=40 << 20),
    )(
        place.reshape(1), lax.axis_index("replica").reshape(1), lax.axis_index("tm").reshape(1),
        *ring(own_columns, "fsdp"), *left_rows, left_panels, tap_mix,
        jnp.asarray(shift_picks(order, clip_frames, half), BF16),
        jnp.asarray(sort_picks(order, clip_frames, half), BF16),
    )
    return result.transpose(0, 1, 3, 2)


def solution(mesh):
    in_specs = (
        P("replica", "tm", None, None, None),
        P(None, None, "fsdp"),
        P(None, "fsdp", None),
        P("replica", "tm", None, None, None),
        P(),
        P(None, "fsdp", None),
        P(None, "fsdp", ("replica", "tm")),
    )
    out_specs = P(None, None, "fsdp", ("replica", "tm"))
    return jax.shard_map(shards, mesh=mesh, in_specs=in_specs, out_specs=out_specs, check_vma=False)
```

```python
import functools

import jax
import jax.numpy as jnp
import numpy as np
from jax import lax
from jax.experimental import pallas as pl
from jax.experimental.pallas import tpu as pltpu
from jax.sharding import Mesh, PartitionSpec as P

TAPS = 27
F32, BF16 = jnp.float32, jnp.bfloat16
ROOM = 50 << 20
HIDDEN_COST = 200 << 20
NT = (((1,), (1,)), ((), ()))
VMEM = pl.BlockSpec(memory_space=pltpu.VMEM)
HBM = pl.BlockSpec(memory_space=pltpu.HBM)
SMEM = pl.BlockSpec(memory_space=pltpu.SMEM)
ANY = pl.BlockSpec(memory_space=pl.ANY)


def shifted(block, axis, distance):
    devices = range(lax.axis_size(axis))
    route = [(i - distance, i) for i in devices if i - distance in devices]
    return lax.ppermute(block, axis, route)


def dot(left, right):
    return jnp.dot(left, right, preferred_element_type=F32)


def dot_nt(left, right):
    return lax.dot_general(left, right, NT, preferred_element_type=F32)


def halves(value):
    high = value.astype(BF16)
    return high, (value - high.astype(F32)).astype(BF16)


def patch_picks(side):
    half = side // 2
    even = np.zeros((1, 3, half, half, half, side), np.float32)
    odd = np.zeros((2, 3, half, half, half, side), np.float32)
    for c in range(3):
        for y in range(half):
            for x in range(half):
                column = 2 * x + c - 1
                if column < 0:
                    continue
                even[0, c, y, x, y, column] = 1
                if y > 0:
                    odd[0, c, y, x, y - 1, column] = 1
                odd[1, c, y, x, y, column] = 1
    return even.reshape(-1, half * side), odd.reshape(-1, half * side)


def spread_picks(half):
    quarter = half // 2
    picks = np.zeros((3, 3, half, half, quarter, quarter), np.float32)
    for b in range(3):
        for c in range(3):
            for out_y in range(quarter):
                for out_x in range(quarter):
                    y, x = 2 * out_y + b - 1, 2 * out_x + c - 1
                    if y >= 0 and x >= 0:
                        picks[b, c, y, x, out_y, out_x] = 1
    return picks.reshape(9 * half * half, quarter * quarter)


def clip_order(slices, clip_parts, half_frames, half):
    cells = half_frames * half * half
    order = np.arange(clip_parts * cells).reshape(clip_parts, slices, cells // slices)
    return order.transpose(1, 0, 2).reshape(-1)


def shift_picks(order, frames, half):
    size = frames * half * half
    picks = np.zeros((size, 2, 2, 2, frames, half, half), np.float32)
    at = np.empty(size, np.int64)
    at[order] = np.arange(size)
    at = at.reshape(frames, half, half)
    for dt, dr, dc in np.ndindex(2, 2, 2):
        for t, y, x in np.ndindex(frames - dt, half - dr, half - dc):
            picks[at[t + dt, y + dr, x + dc], dt, dr, dc, t, y, x] = 1
    return picks.reshape(size, 8 * size)


def sort_picks(order, frames, half):
    size = frames * half * half
    index = np.arange(size).reshape(frames // 2, 2, half // 2, 2, half // 2, 2)
    wanted = index.transpose(1, 3, 5, 0, 2, 4).reshape(-1)
    at = np.empty(size, np.int64)
    at[order] = np.arange(size)
    picks = np.zeros((size, size), np.float32)
    picks[at[wanted], np.arange(size)] = 1
    return picks


def project_kernel(x_ref, left_ref, grad_ref, out_ref, rows_ref):
    frames, half, _, side, channels = x_ref.shape
    wide = left_ref.shape[1]
    pairs = frames // 2
    size = pairs * half * side
    both = jnp.concatenate(halves(left_ref[0]), axis=0)
    target = lax.broadcasted_iota(jnp.int32, (size, size), 0)
    source = lax.broadcasted_iota(jnp.int32, (size, size), 1)
    cells = size // 2
    wanted = 2 * (target % cells) + target // cells
    pick = jnp.where(source == wanted, 1.0, 0.0).astype(BF16)
    for time in range(2):
        for row in range(2):
            block = jnp.concatenate(
                [
                    x_ref[frame, :, row].reshape(half * side, channels)
                    for frame in range(time, frames, 2)
                ],
                axis=0,
            )
            full = dot_nt(block, both)
            small = (full[:, :wide] + full[:, wide:]).astype(BF16)
            ordered = dot(pick, small).astype(BF16)
            at = (4 * time + 2 * row) * cells
            out_ref[at : at + size, :] = ordered
    rows = stacked_rows(grad_ref, rows_ref)
    count = rows.shape[0]
    for block in range(channels // wide):
        at = 8 * cells + block * count
        out_ref[at : at + count, :] = rows[:, block * wide : (block + 1) * wide]


def stacked_rows(grad_ref, rows_ref):
    quarter = grad_ref.shape[0]
    for row in range(quarter):
        rows_ref[pl.ds(row * quarter, quarter), :] = grad_ref[row].astype(F32)
    return rows_ref[...].astype(BF16)


def transposed_products(rows, kernel, taps):
    total = dot_nt(rows[0], kernel[taps[0]])
    for at in range(1, len(taps)):
        total += dot_nt(rows[at], kernel[taps[at]])
    return total


def spread_rows(picks_ref, rows, cells):
    spread = dot(picks_ref[...], rows).astype(BF16)
    return [spread[tap * cells : (tap + 1) * cells] for tap in range(9)]


def hidden_kernel(
    x_ref, prior_ref, grad_ref, later_ref, even_ref, odd_ref, spread_ref, *refs, slices
):
    right_refs = refs[:slices]
    (
        first_any, second_any,
        out_ref, right_out_ref, rows_ref, patches, first, second, arrived,
    ) = refs[slices:]
    frames, half, _, side, channels = x_ref.shape
    cells = half * half
    copies = {
        (at, a): pltpu.make_async_copy(
            source.at[pl.ds(9 * a, 9)], target.at[pl.ds(9 * a, 9)], arrived.at[at, a]
        )
        for at, (source, target) in enumerate(((second_any, second), (first_any, first)))
        for a in (1, 2, 0)
    }
    for copy in copies.values():
        copy.start()
    for distance, right_ref in enumerate(right_refs):
        for layer in range(2):
            right = jnp.concatenate(
                [right_ref[core, layer] for core in range(right_ref.shape[0])], axis=0
            )
            right_out_ref[distance, layer] = jnp.concatenate(halves(right), axis=0)
    own = spread_rows(spread_ref, stacked_rows(grad_ref, rows_ref), cells)
    copies[0, 1].wait()
    early = transposed_products(own, second, range(9, 18))
    copies[0, 2].wait()
    late = transposed_products(own, second, range(18, 27))
    for frame in range(frames + 1):
        block = prior_ref if frame == 0 else x_ref.at[frame - 1]
        even = dot(even_ref[...], block[:, 0].reshape(half * side, channels)).astype(BF16)
        odd = dot(odd_ref[...], block[:, 1].reshape(half * side, channels)).astype(BF16)
        for c in range(3):
            patches[frame, c] = odd[c * cells : (c + 1) * cells]
            patches[frame, 3 + c] = even[c * cells : (c + 1) * cells]
            patches[frame, 6 + c] = odd[(3 + c) * cells : (4 + c) * cells]
    after = spread_rows(spread_ref, stacked_rows(later_ref, rows_ref), cells)
    copies[0, 0].wait()
    late += transposed_products(after, second, range(9))
    hidden_grad = jnp.concatenate([early, late], axis=0)
    pre = jnp.zeros((2 * cells, first.shape[2]), F32)
    for a in (1, 2, 0):
        copies[1, a].wait()
        for tap in range(9):
            rows = jnp.concatenate([patches[a, tap], patches[a + 2, tap]], axis=0)
            pre += dot(rows, first[9 * a + tap])
    sig = jax.nn.sigmoid(pre)
    hidden = (pre * sig).astype(BF16)
    pre_grad = (hidden_grad * sig * (1.0 + pre * (1.0 - sig))).astype(BF16)
    groups, _, _, share, _ = out_ref.shape
    for at in range(slices):
        place = slice(at * share, (at + 1) * share)
        for group in range(groups):
            out_ref[group, at, 0] = pre_grad[place]
            out_ref[group, at, 1] = hidden[place]


def right_kernel(place_ref, acts_ref, right_ref, *out_refs):
    parts, slices = acts_ref.shape[:2]
    both = right_ref.shape[2] // 2
    width = both // len(out_refs)
    for layer in range(2):
        total = None
        for distance in range(slices):
            origin = lax.rem(place_ref[0] + (slices - distance), slices)
            rows = jnp.concatenate([acts_ref[part, origin, layer] for part in range(parts)], axis=0)
            term = dot_nt(right_ref[distance, layer], rows)
            total = term if total is None else total + term
        product = (total[:both] + total[both:]).astype(BF16)
        for at, out_ref in enumerate(out_refs):
            out_ref[pl.ds(layer * width, width), :] = product[at * width : (at + 1) * width]


def update_kernel(
    place_ref, chip_ref, core_ref, tm_ref, *refs, slices, cores, clip_parts, half
):
    columns_refs, piece_refs = refs[: slices * cores], refs[slices * cores : (slices + 1) * cores]
    (
        left_ref, mix_ref, shift_ref, sort_ref,
        out_ref, left_rows_ref, columns, shifts, grads, raw, arrived,
    ) = refs[(slices + 1) * cores :]
    parts = left_rows_ref.shape[0]
    chips = parts // (cores * clip_parts)
    copies = []
    for cross, piece_ref in enumerate(piece_refs):
        core = (core_ref[0] + cross) % cores
        for at, (step, turn) in enumerate(np.ndindex(chips, clip_parts)):
            chip = lax.rem(chip_ref[0] + (chips - step), chips)
            place = lax.rem(tm_ref[0] + (clip_parts - turn), clip_parts)
            target = left_rows_ref.at[(chip * cores + core) * clip_parts + place]
            copies.append(
                pltpu.make_async_copy(piece_ref.at[at], target, arrived.at[len(copies)])
            )
    for copy in copies:
        copy.start()
    for cross, distance in np.ndindex(cores, slices):
        origin = lax.rem(place_ref[0] + (slices - distance), slices)
        core = (core_ref[0] + cross) % cores
        columns[origin, core] = columns_refs[cross * slices + distance][...]
    wide, channels = left_ref.shape[1:]
    width = columns.shape[2] // 2
    clips = parts // clip_parts
    share = columns.shape[3] // chips
    clip_cells = slices * share
    cells = clip_cells // clip_parts
    frames = clip_cells // (half * half)
    outputs = clip_cells // 8

    def by_clip(layer):
        return jnp.concatenate(
            [
                jnp.concatenate(
                    [
                        columns[
                            at, clip % cores, pl.ds(layer * width, width),
                            pl.ds(clip // cores * share, share),
                        ]
                        for at in range(slices)
                    ],
                    axis=1,
                )
                for clip in range(clips)
            ],
            axis=0,
        )

    first = by_clip(0)
    for shift in range(8):
        moved = dot(first, shift_ref[:, pl.ds(shift * clip_cells, clip_cells)]).astype(BF16)
        for clip in range(clips):
            shifts[shift, clip] = moved[clip * width : (clip + 1) * width]
    second = dot(by_clip(1), sort_ref[...]).astype(BF16)

    for copy in copies:
        copy.wait()
    own_outputs = outputs // clip_parts
    blocks = channels // wide
    out_grad = jnp.concatenate(
        [
            jnp.concatenate(
                [
                    left_rows_ref[part, pl.ds(8 * cells + own_outputs * at, own_outputs), :]
                    for at in range(blocks)
                ],
                axis=1,
            )
            for part in range(parts)
        ],
        axis=0,
    )
    full = dot_nt(out_grad, jnp.concatenate(halves(left_ref[1]), axis=0))
    total = parts * own_outputs
    quarter = half // 2
    grads[pl.ds(0, total), :] = full[:, :wide] + full[:, wide:]
    places = lax.broadcasted_iota(jnp.int32, (total, wide), 0)
    frame = places // (quarter * quarter) % (frames // 2)
    row = places // quarter % quarter
    column = places % quarter
    second_rows = []
    for shift in range(8):
        dt, dr, dc = shift // 4, shift // 2 % 2, shift % 2
        moved = grads[pl.ds((dt * quarter + dr) * quarter + dc, total), :]
        inside = (frame + dt < frames // 2) & (row + dr < quarter) & (column + dc < quarter)
        second_rows.append(jnp.where(inside, moved, 0.0).astype(BF16))

    for kind in range(8):
        time, line, place = kind // 4, kind // 2 % 2, kind % 2
        taps = [
            (9 * a + 3 * b + c, 4 * (a == 0) + 2 * (b == 0) + (c == 0))
            for a in ((0, 2) if time else (1,))
            for b in ((0, 2) if line else (1,))
            for c in ((0, 2) if place else (1,))
        ]
        sums = None
        for clip in range(clips):
            left = jnp.concatenate([shifts[shift, clip] for _, shift in taps], axis=0)
            rows = jnp.concatenate(
                [
                    left_rows_ref[clip * clip_parts + part, pl.ds(kind * cells, cells), :]
                    for part in range(clip_parts)
                ],
                axis=0,
            )
            term = dot(left, rows)
            sums = term if sums is None else sums + term
        chosen = jnp.concatenate(
            [
                second[clip * width : (clip + 1) * width, kind * outputs : (kind + 1) * outputs]
                for clip in range(clips)
            ],
            axis=1,
        )
        for at, (tap, shift) in enumerate(taps):
            raw[0, tap] = sums[at * width : (at + 1) * width]
            raw[1, tap] = dot(chosen, second_rows[shift])

    @pl.loop(0, 2 * TAPS)
    def _(step):
        layer, out_tap = step // TAPS, step % TAPS
        acc = raw[layer, 0] * mix_ref[layer, out_tap, 0]
        for tap in range(1, TAPS):
            acc += raw[layer, tap] * mix_ref[layer, out_tap, tap]
        out_ref[layer, out_tap] = acc.astype(BF16)


def turned(block, axes, steps):
    sizes = [lax.axis_size(axis) for axis in axes]
    if not any(step % size for step, size in zip(steps, sizes)):
        return block
    route = []
    for place in np.ndindex(*sizes):
        target = [(at + step) % size for at, step, size in zip(place, steps, sizes)]
        route.append(
            (int(np.ravel_multi_index(place, sizes)), int(np.ravel_multi_index(target, sizes)))
        )
    return lax.ppermute(block, axes, route)


def shards(clip_input, first_kernel, second_kernel, out_grad, tap_mix, left_panels, right_panels):
    clips, frames, side, _, channels = clip_input.shape
    wide = first_kernel.shape[2]
    width = right_panels.shape[2]
    half, quarter = side // 2, side // 4
    half_frames = frames // 2
    cells = half_frames * half * half
    clip_parts = lax.axis_size("tm")
    cores, chips = lax.axis_size("core"), lax.axis_size("chip")
    equals = chips * clip_parts
    parts = equals * cores
    slices = lax.axis_size("fsdp")
    share = cells // slices
    assert clips == 1 and frames == 4
    x = clip_input.reshape(frames, half, 2, side, channels)
    grad = out_grad.reshape(quarter, quarter, channels)
    prior = shifted(x[frames - 1 :], "tm", 1)[0]
    later = shifted(grad, "tm", -1)
    grad, later = lax.optimization_barrier((grad, later))
    place = lax.axis_index("fsdp").reshape(1)

    projected = pl.pallas_call(
        project_kernel,
        out_shape=jax.ShapeDtypeStruct((8 * cells + quarter * quarter * channels // wide, wide), BF16),
        in_specs=[VMEM] * 3,
        out_specs=VMEM,
        scratch_shapes=[pltpu.VMEM((quarter * quarter, channels), F32)],
        compiler_params=pltpu.CompilerParams(vmem_limit_bytes=ROOM),
        cost_estimate=pl.CostEstimate(
            flops=4 * frames * side * side * channels * wide,
            bytes_accessed=2 * frames * side * side * channels,
            transcendentals=0,
        ),
    )(x, left_panels, grad)
    projected, prior = lax.optimization_barrier((projected, prior))
    held = jnp.stack(
        [
            turned(projected, ("chip", "tm"), steps)
            for steps in np.ndindex(chips, clip_parts)
        ]
    )

    right = right_panels.transpose(0, 2, 1)
    right = jnp.stack([turned(right, ("core",), (cross,)) for cross in range(cores)])
    rights = [turned(right, ("fsdp",), (distance,)) for distance in range(slices)]

    even, odd = patch_picks(side)
    spread = jnp.asarray(spread_picks(half), BF16)
    acts, right = pl.pallas_call(
        functools.partial(hidden_kernel, slices=slices),
        out_shape=(
            jax.ShapeDtypeStruct((equals, slices, 2, share, wide), BF16),
            jax.ShapeDtypeStruct((slices, 2, 2 * cores * width, wide), BF16),
        ),
        in_specs=[VMEM] * (7 + slices) + [HBM] * 2,
        out_specs=(VMEM, VMEM),
        scratch_shapes=[
            pltpu.VMEM((quarter * quarter, channels), F32),
            pltpu.VMEM((frames + 1, 9, half * half, channels), BF16),
            pltpu.VMEM(first_kernel.shape, BF16),
            pltpu.VMEM(second_kernel.shape, BF16),
            pltpu.SemaphoreType.DMA((2, 3)),
        ],
        compiler_params=pltpu.CompilerParams(vmem_limit_bytes=ROOM),
        cost_estimate=pl.CostEstimate(
            flops=3 * cells * TAPS * channels * wide,
            bytes_accessed=HIDDEN_COST,
            transcendentals=cells * wide,
        ),
    )(
        x, prior, grad, later, jnp.asarray(even, BF16), jnp.asarray(odd, BF16),
        spread, *rights, first_kernel, second_kernel,
    )
    every = lax.all_to_all(
        acts.reshape(equals * slices, 2, share, wide), ("chip", "tm", "fsdp"), 0, 0, tiled=True
    ).reshape(equals, slices, 2, share, wide)
    columns = pl.pallas_call(
        right_kernel,
        out_shape=(jax.ShapeDtypeStruct((2 * width, equals * share), BF16),) * cores,
        in_specs=[SMEM] + [VMEM] * 2,
        out_specs=(VMEM,) * cores,
        compiler_params=pltpu.CompilerParams(vmem_limit_bytes=16 << 20),
    )(place, every, right)
    *columns, held = lax.optimization_barrier((*columns, held))
    columns = [
        turned(columns[cross], ("fsdp", "core"), (distance, cross))
        for cross, distance in np.ndindex(cores, slices)
    ]
    left_rows = [turned(held, ("core",), (cross,)) for cross in range(cores)]

    order = clip_order(slices, clip_parts, half_frames, half)
    clip_frames = clip_parts * half_frames
    clip_cells = clip_parts * cells
    result = pl.pallas_call(
        functools.partial(
            update_kernel, slices=slices, cores=cores, clip_parts=clip_parts, half=half
        ),
        out_shape=jax.ShapeDtypeStruct((2, TAPS, width, wide), BF16),
        in_specs=[SMEM] * 4
        + [VMEM] * len(columns)
        + [ANY] * cores
        + [VMEM, SMEM, VMEM, VMEM],
        out_specs=VMEM,
        scratch_shapes=[
            pltpu.VMEM((parts,) + projected.shape, BF16),
            pltpu.VMEM((slices, cores, 2 * width, equals * share), BF16),
            pltpu.VMEM((8, parts // clip_parts, width, clip_cells), BF16),
            pltpu.VMEM((parts * cells // 8 + (quarter + 1) * quarter + 8, wide), F32),
            pltpu.VMEM((2, TAPS, width, wide), F32),
            pltpu.SemaphoreType.DMA((parts,)),
        ],
        compiler_params=pltpu.CompilerParams(vmem_limit_bytes=40 << 20),
    )(
        place, *(lax.axis_index(axis).reshape(1) for axis in ("chip", "core", "tm")),
        *columns, *left_rows, left_panels, tap_mix,
        jnp.asarray(shift_picks(order, clip_frames, half), BF16),
        jnp.asarray(sort_picks(order, clip_frames, half), BF16),
    )
    return result.transpose(0, 1, 3, 2)


def solution(mesh):
    fsdp, replica, tm = (mesh.shape[axis] for axis in ("fsdp", "replica", "tm"))
    cores = 2 if replica % 2 == 0 else 1
    assert mesh.axis_names == ("fsdp", "replica", "tm")
    mesh = Mesh(
        mesh.devices.reshape(fsdp, replica // cores, cores, tm), ("fsdp", "chip", "core", "tm")
    )
    replica = ("chip", "core")
    in_specs = (
        P(replica, "tm", None, None, None),
        P(None, None, "fsdp"),
        P(None, "fsdp", None),
        P(replica, "tm", None, None, None),
        P(),
        P(None, "fsdp", None),
        P(None, "fsdp", (*replica, "tm")),
    )
    out_specs = P(None, None, "fsdp", (*replica, "tm"))
    return jax.shard_map(shards, mesh=mesh, in_specs=in_specs, out_specs=out_specs, check_vma=False)
```

```python
import functools

import jax
import jax.numpy as jnp
import numpy as np
from jax import lax
from jax.experimental import pallas as pl
from jax.experimental.pallas import tpu as pltpu
from jax.sharding import Mesh, PartitionSpec as P

TAPS = 27
F32, BF16 = jnp.float32, jnp.bfloat16
ROOM = 50 << 20
HIDDEN_COST = 200 << 20
NT = (((1,), (1,)), ((), ()))
VMEM = pl.BlockSpec(memory_space=pltpu.VMEM)
HBM = pl.BlockSpec(memory_space=pltpu.HBM)
SMEM = pl.BlockSpec(memory_space=pltpu.SMEM)
ANY = pl.BlockSpec(memory_space=pl.ANY)


def shifted(block, axis, distance):
    devices = range(lax.axis_size(axis))
    route = [(i - distance, i) for i in devices if i - distance in devices]
    return lax.ppermute(block, axis, route)


def dot(left, right):
    return jnp.dot(left, right, preferred_element_type=F32)


def dot_nt(left, right):
    return lax.dot_general(left, right, NT, preferred_element_type=F32)


def halves(value):
    high = value.astype(BF16)
    return high, (value - high.astype(F32)).astype(BF16)


def patch_picks(side):
    half = side // 2
    even = np.zeros((1, 3, half, half, half, side), np.float32)
    odd = np.zeros((2, 3, half, half, half, side), np.float32)
    for c in range(3):
        for y in range(half):
            for x in range(half):
                column = 2 * x + c - 1
                if column < 0:
                    continue
                even[0, c, y, x, y, column] = 1
                if y > 0:
                    odd[0, c, y, x, y - 1, column] = 1
                odd[1, c, y, x, y, column] = 1
    return even.reshape(-1, half * side), odd.reshape(-1, half * side)


def spread_picks(half):
    quarter = half // 2
    picks = np.zeros((3, 3, half, half, quarter, quarter), np.float32)
    for b in range(3):
        for c in range(3):
            for out_y in range(quarter):
                for out_x in range(quarter):
                    y, x = 2 * out_y + b - 1, 2 * out_x + c - 1
                    if y >= 0 and x >= 0:
                        picks[b, c, y, x, out_y, out_x] = 1
    return picks.reshape(9 * half * half, quarter * quarter)


def clip_order(slices, clip_parts, half_frames, half):
    cells = half_frames * half * half
    order = np.arange(clip_parts * cells).reshape(clip_parts, slices, cells // slices)
    return order.transpose(1, 0, 2).reshape(-1)


def shift_picks(order, frames, half):
    size = frames * half * half
    picks = np.zeros((size, 2, 2, 2, frames, half, half), np.float32)
    at = np.empty(size, np.int64)
    at[order] = np.arange(size)
    at = at.reshape(frames, half, half)
    for dt, dr, dc in np.ndindex(2, 2, 2):
        for t, y, x in np.ndindex(frames - dt, half - dr, half - dc):
            picks[at[t + dt, y + dr, x + dc], dt, dr, dc, t, y, x] = 1
    return picks.reshape(size, 8 * size)


def sort_picks(order, frames, half):
    size = frames * half * half
    index = np.arange(size).reshape(frames // 2, 2, half // 2, 2, half // 2, 2)
    wanted = index.transpose(1, 3, 5, 0, 2, 4).reshape(-1)
    at = np.empty(size, np.int64)
    at[order] = np.arange(size)
    picks = np.zeros((size, size), np.float32)
    picks[at[wanted], np.arange(size)] = 1
    return picks


def project_kernel(x_ref, left_ref, grad_ref, out_ref, rows_ref):
    frames, half, _, side, channels = x_ref.shape
    wide = left_ref.shape[1]
    pairs = frames // 2
    size = pairs * half * side
    both = jnp.concatenate(halves(left_ref[0]), axis=0)
    target = lax.broadcasted_iota(jnp.int32, (size, size), 0)
    source = lax.broadcasted_iota(jnp.int32, (size, size), 1)
    cells = size // 2
    wanted = 2 * (target % cells) + target // cells
    pick = jnp.where(source == wanted, 1.0, 0.0).astype(BF16)
    for time in range(2):
        for row in range(2):
            block = jnp.concatenate(
                [
                    x_ref[frame, :, row].reshape(half * side, channels)
                    for frame in range(time, frames, 2)
                ],
                axis=0,
            )
            full = dot_nt(block, both)
            small = (full[:, :wide] + full[:, wide:]).astype(BF16)
            ordered = dot(pick, small).astype(BF16)
            at = (4 * time + 2 * row) * cells
            out_ref[at : at + size, :] = ordered
    rows = stacked_rows(grad_ref, rows_ref)
    count = rows.shape[0]
    for block in range(channels // wide):
        at = 8 * cells + block * count
        out_ref[at : at + count, :] = rows[:, block * wide : (block + 1) * wide]


def stacked_rows(grad_ref, rows_ref):
    quarter = grad_ref.shape[0]
    for row in range(quarter):
        rows_ref[pl.ds(row * quarter, quarter), :] = grad_ref[row].astype(F32)
    return rows_ref[...].astype(BF16)


def transposed_products(rows, kernel, taps):
    total = dot_nt(rows[0], kernel[taps[0]])
    for at in range(1, len(taps)):
        total += dot_nt(rows[at], kernel[taps[at]])
    return total


def spread_rows(picks_ref, rows, cells):
    spread = dot(picks_ref[...], rows).astype(BF16)
    return [spread[tap * cells : (tap + 1) * cells] for tap in range(9)]


def hidden_kernel(
    x_ref, prior_ref, grad_ref, later_ref, even_ref, odd_ref, spread_ref, first_any, second_any,
    out_ref, rows_ref, patches, first, second, arrived,
):
    frames, half, _, side, channels = x_ref.shape
    cells = half * half
    copies = {
        (at, a): pltpu.make_async_copy(
            source.at[pl.ds(9 * a, 9)], target.at[pl.ds(9 * a, 9)], arrived.at[at, a]
        )
        for at, (source, target) in enumerate(((second_any, second), (first_any, first)))
        for a in (1, 2, 0)
    }
    for copy in copies.values():
        copy.start()
    own = spread_rows(spread_ref, stacked_rows(grad_ref, rows_ref), cells)
    copies[0, 1].wait()
    early = transposed_products(own, second, range(9, 18))
    copies[0, 2].wait()
    late = transposed_products(own, second, range(18, 27))
    for frame in range(frames + 1):
        block = prior_ref if frame == 0 else x_ref.at[frame - 1]
        even = dot(even_ref[...], block[:, 0].reshape(half * side, channels)).astype(BF16)
        odd = dot(odd_ref[...], block[:, 1].reshape(half * side, channels)).astype(BF16)
        for c in range(3):
            patches[frame, c] = odd[c * cells : (c + 1) * cells]
            patches[frame, 3 + c] = even[c * cells : (c + 1) * cells]
            patches[frame, 6 + c] = odd[(3 + c) * cells : (4 + c) * cells]
    after = spread_rows(spread_ref, stacked_rows(later_ref, rows_ref), cells)
    copies[0, 0].wait()
    late += transposed_products(after, second, range(9))
    hidden_grad = jnp.concatenate([early, late], axis=0)
    pre = jnp.zeros((2 * cells, first.shape[2]), F32)
    for a in (1, 2, 0):
        copies[1, a].wait()
        for tap in range(9):
            rows = jnp.concatenate([patches[a, tap], patches[a + 2, tap]], axis=0)
            pre += dot(rows, first[9 * a + tap])
    sig = jax.nn.sigmoid(pre)
    hidden = (pre * sig).astype(BF16)
    pre_grad = (hidden_grad * sig * (1.0 + pre * (1.0 - sig))).astype(BF16)
    groups, slices, _, share, _ = out_ref.shape
    for at in range(slices):
        place = slice(at * share, (at + 1) * share)
        for group in range(groups):
            out_ref[group, at, 0] = pre_grad[place]
            out_ref[group, at, 1] = hidden[place]


def right_kernel(place_ref, acts_ref, *refs):
    parts, slices = acts_ref.shape[:2]
    right_refs, out_refs = refs[:slices], refs[slices:]
    cores, _, width, _ = right_refs[0].shape
    both = cores * width
    for layer in range(2):
        total = None
        for distance, right_ref in enumerate(right_refs):
            origin = lax.rem(place_ref[0] + (slices - distance), slices)
            right = jnp.concatenate([right_ref[core, layer] for core in range(cores)], axis=0)
            rows = jnp.concatenate([acts_ref[part, origin, layer] for part in range(parts)], axis=0)
            term = dot_nt(jnp.concatenate(halves(right), axis=0), rows)
            total = term if total is None else total + term
        product = (total[:both] + total[both:]).astype(BF16)
        for at, out_ref in enumerate(out_refs):
            out_ref[pl.ds(layer * width, width), :] = product[at * width : (at + 1) * width]


def update_kernel(
    place_ref, chip_ref, core_ref, tm_ref, *refs, slices, cores, clip_parts, half
):
    columns_refs, piece_refs = refs[: slices * cores], refs[slices * cores : (slices + 1) * cores]
    (
        left_ref, mix_ref, shift_ref, sort_ref,
        out_ref, left_rows_ref, columns, shifts, grads, raw, arrived,
    ) = refs[(slices + 1) * cores :]
    parts = left_rows_ref.shape[0]
    chips = parts // (cores * clip_parts)
    copies = []
    for cross, piece_ref in enumerate(piece_refs):
        core = (core_ref[0] + cross) % cores
        for at, (step, turn) in enumerate(np.ndindex(chips, clip_parts)):
            chip = lax.rem(chip_ref[0] + (chips - step), chips)
            place = lax.rem(tm_ref[0] + (clip_parts - turn), clip_parts)
            target = left_rows_ref.at[(chip * cores + core) * clip_parts + place]
            copies.append(
                pltpu.make_async_copy(piece_ref.at[at], target, arrived.at[len(copies)])
            )
    for copy in copies:
        copy.start()
    for cross, distance in np.ndindex(cores, slices):
        origin = lax.rem(place_ref[0] + (slices - distance), slices)
        core = (core_ref[0] + cross) % cores
        columns[origin, core] = columns_refs[cross * slices + distance][...]
    wide, channels = left_ref.shape[1:]
    width = columns.shape[2] // 2
    clips = parts // clip_parts
    share = columns.shape[3] // chips
    clip_cells = slices * share
    cells = clip_cells // clip_parts
    frames = clip_cells // (half * half)
    outputs = clip_cells // 8

    def by_clip(layer):
        return jnp.concatenate(
            [
                jnp.concatenate(
                    [
                        columns[
                            at, clip % cores, pl.ds(layer * width, width),
                            pl.ds(clip // cores * share, share),
                        ]
                        for at in range(slices)
                    ],
                    axis=1,
                )
                for clip in range(clips)
            ],
            axis=0,
        )

    first = by_clip(0)
    for shift in range(8):
        moved = dot(first, shift_ref[:, pl.ds(shift * clip_cells, clip_cells)]).astype(BF16)
        for clip in range(clips):
            shifts[shift, clip] = moved[clip * width : (clip + 1) * width]
    second = dot(by_clip(1), sort_ref[...]).astype(BF16)

    for copy in copies:
        copy.wait()
    own_outputs = outputs // clip_parts
    blocks = channels // wide
    out_grad = jnp.concatenate(
        [
            jnp.concatenate(
                [
                    left_rows_ref[part, pl.ds(8 * cells + own_outputs * at, own_outputs), :]
                    for at in range(blocks)
                ],
                axis=1,
            )
            for part in range(parts)
        ],
        axis=0,
    )
    full = dot_nt(out_grad, jnp.concatenate(halves(left_ref[1]), axis=0))
    total = parts * own_outputs
    quarter = half // 2
    grads[pl.ds(0, total), :] = full[:, :wide] + full[:, wide:]
    places = lax.broadcasted_iota(jnp.int32, (total, wide), 0)
    frame = places // (quarter * quarter) % (frames // 2)
    row = places // quarter % quarter
    column = places % quarter
    second_rows = []
    for shift in range(8):
        dt, dr, dc = shift // 4, shift // 2 % 2, shift % 2
        moved = grads[pl.ds((dt * quarter + dr) * quarter + dc, total), :]
        inside = (frame + dt < frames // 2) & (row + dr < quarter) & (column + dc < quarter)
        second_rows.append(jnp.where(inside, moved, 0.0).astype(BF16))

    for kind in range(8):
        time, line, place = kind // 4, kind // 2 % 2, kind % 2
        taps = [
            (9 * a + 3 * b + c, 4 * (a == 0) + 2 * (b == 0) + (c == 0))
            for a in ((0, 2) if time else (1,))
            for b in ((0, 2) if line else (1,))
            for c in ((0, 2) if place else (1,))
        ]
        sums = None
        for clip in range(clips):
            left = jnp.concatenate([shifts[shift, clip] for _, shift in taps], axis=0)
            rows = jnp.concatenate(
                [
                    left_rows_ref[clip * clip_parts + part, pl.ds(kind * cells, cells), :]
                    for part in range(clip_parts)
                ],
                axis=0,
            )
            term = dot(left, rows)
            sums = term if sums is None else sums + term
        chosen = jnp.concatenate(
            [
                second[clip * width : (clip + 1) * width, kind * outputs : (kind + 1) * outputs]
                for clip in range(clips)
            ],
            axis=1,
        )
        for at, (tap, shift) in enumerate(taps):
            raw[0, tap] = sums[at * width : (at + 1) * width]
            raw[1, tap] = dot(chosen, second_rows[shift])

    @pl.loop(0, 2 * TAPS)
    def _(step):
        layer, out_tap = step // TAPS, step % TAPS
        acc = raw[layer, 0] * mix_ref[layer, out_tap, 0]
        for tap in range(1, TAPS):
            acc += raw[layer, tap] * mix_ref[layer, out_tap, tap]
        out_ref[layer, out_tap] = acc.astype(BF16)


def turned(block, axes, steps):
    sizes = [lax.axis_size(axis) for axis in axes]
    if not any(step % size for step, size in zip(steps, sizes)):
        return block
    route = []
    for place in np.ndindex(*sizes):
        target = [(at + step) % size for at, step, size in zip(place, steps, sizes)]
        route.append(
            (int(np.ravel_multi_index(place, sizes)), int(np.ravel_multi_index(target, sizes)))
        )
    return lax.ppermute(block, axes, route)


def shards(clip_input, first_kernel, second_kernel, out_grad, tap_mix, left_panels, right_panels):
    clips, frames, side, _, channels = clip_input.shape
    wide = first_kernel.shape[2]
    width = right_panels.shape[2]
    half, quarter = side // 2, side // 4
    half_frames = frames // 2
    cells = half_frames * half * half
    clip_parts = lax.axis_size("tm")
    cores, chips = lax.axis_size("core"), lax.axis_size("chip")
    equals = chips * clip_parts
    parts = equals * cores
    slices = lax.axis_size("fsdp")
    share = cells // slices
    assert clips == 1 and frames == 4
    x = clip_input.reshape(frames, half, 2, side, channels)
    grad = out_grad.reshape(quarter, quarter, channels)
    prior = shifted(x[frames - 1 :], "tm", 1)[0]
    later = shifted(grad, "tm", -1)
    place = lax.axis_index("fsdp").reshape(1)

    projected = pl.pallas_call(
        project_kernel,
        out_shape=jax.ShapeDtypeStruct((8 * cells + quarter * quarter * channels // wide, wide), BF16),
        in_specs=[VMEM] * 3,
        out_specs=VMEM,
        scratch_shapes=[pltpu.VMEM((quarter * quarter, channels), F32)],
        compiler_params=pltpu.CompilerParams(vmem_limit_bytes=ROOM),
        cost_estimate=pl.CostEstimate(
            flops=4 * frames * side * side * channels * wide,
            bytes_accessed=2 * frames * side * side * channels,
            transcendentals=0,
        ),
    )(x, left_panels, grad)
    projected, prior, later = lax.optimization_barrier((projected, prior, later))
    held = [
        turned(projected, ("chip", "tm"), steps) for steps in np.ndindex(chips, clip_parts)
    ]

    right = right_panels.transpose(0, 2, 1)
    right = jnp.stack([turned(right, ("core",), (cross,)) for cross in range(cores)])
    rights = [turned(right, ("fsdp",), (distance,)) for distance in range(slices)]

    even, odd = patch_picks(side)
    spread = jnp.asarray(spread_picks(half), BF16)
    acts = pl.pallas_call(
        hidden_kernel,
        out_shape=jax.ShapeDtypeStruct((equals, slices, 2, share, wide), BF16),
        in_specs=[VMEM] * 7 + [HBM] * 2,
        out_specs=VMEM,
        scratch_shapes=[
            pltpu.VMEM((quarter * quarter, channels), F32),
            pltpu.VMEM((frames + 1, 9, half * half, channels), BF16),
            pltpu.VMEM(first_kernel.shape, BF16),
            pltpu.VMEM(second_kernel.shape, BF16),
            pltpu.SemaphoreType.DMA((2, 3)),
        ],
        compiler_params=pltpu.CompilerParams(vmem_limit_bytes=ROOM),
        cost_estimate=pl.CostEstimate(
            flops=3 * cells * TAPS * channels * wide,
            bytes_accessed=HIDDEN_COST,
            transcendentals=cells * wide,
        ),
    )(
        x, prior, grad, later, jnp.asarray(even, BF16), jnp.asarray(odd, BF16),
        spread, first_kernel, second_kernel,
    )
    acts, held, rights = lax.optimization_barrier((acts, held, rights))
    held = jnp.stack(held)
    every = lax.all_to_all(
        acts.reshape(equals * slices, 2, share, wide), ("chip", "tm", "fsdp"), 0, 0, tiled=True
    ).reshape(equals, slices, 2, share, wide)
    columns = pl.pallas_call(
        right_kernel,
        out_shape=(jax.ShapeDtypeStruct((2 * width, equals * share), BF16),) * cores,
        in_specs=[SMEM] + [VMEM] * (1 + slices),
        out_specs=(VMEM,) * cores,
        compiler_params=pltpu.CompilerParams(vmem_limit_bytes=16 << 20),
    )(place, every, *rights)
    columns = [
        turned(columns[cross], ("fsdp", "core"), (distance, cross))
        for cross, distance in np.ndindex(cores, slices)
    ]
    left_rows = [turned(held, ("core",), (cross,)) for cross in range(cores)]

    order = clip_order(slices, clip_parts, half_frames, half)
    clip_frames = clip_parts * half_frames
    clip_cells = clip_parts * cells
    result = pl.pallas_call(
        functools.partial(
            update_kernel, slices=slices, cores=cores, clip_parts=clip_parts, half=half
        ),
        out_shape=jax.ShapeDtypeStruct((2, TAPS, width, wide), BF16),
        in_specs=[SMEM] * 4
        + [VMEM] * len(columns)
        + [ANY] * cores
        + [VMEM, SMEM, VMEM, VMEM],
        out_specs=VMEM,
        scratch_shapes=[
            pltpu.VMEM((parts,) + projected.shape, BF16),
            pltpu.VMEM((slices, cores, 2 * width, equals * share), BF16),
            pltpu.VMEM((8, parts // clip_parts, width, clip_cells), BF16),
            pltpu.VMEM((parts * cells // 8 + (quarter + 1) * quarter + 8, wide), F32),
            pltpu.VMEM((2, TAPS, width, wide), F32),
            pltpu.SemaphoreType.DMA((parts,)),
        ],
        compiler_params=pltpu.CompilerParams(vmem_limit_bytes=40 << 20),
    )(
        place, *(lax.axis_index(axis).reshape(1) for axis in ("chip", "core", "tm")),
        *columns, *left_rows, left_panels, tap_mix,
        jnp.asarray(shift_picks(order, clip_frames, half), BF16),
        jnp.asarray(sort_picks(order, clip_frames, half), BF16),
    )
    return result.transpose(0, 1, 3, 2)


def solution(mesh):
    fsdp, replica, tm = (mesh.shape[axis] for axis in ("fsdp", "replica", "tm"))
    cores = 2 if replica % 2 == 0 else 1
    assert mesh.axis_names == ("fsdp", "replica", "tm")
    mesh = Mesh(
        mesh.devices.reshape(fsdp, replica // cores, cores, tm), ("fsdp", "chip", "core", "tm")
    )
    replica = ("chip", "core")
    in_specs = (
        P(replica, "tm", None, None, None),
        P(None, None, "fsdp"),
        P(None, "fsdp", None),
        P(replica, "tm", None, None, None),
        P(),
        P(None, "fsdp", None),
        P(None, "fsdp", (*replica, "tm")),
    )
    out_specs = P(None, None, "fsdp", (*replica, "tm"))
    return jax.shard_map(shards, mesh=mesh, in_specs=in_specs, out_specs=out_specs, check_vma=False)
```

```python
import functools

import jax
import jax.numpy as jnp
import numpy as np
from jax import lax
from jax.experimental import pallas as pl
from jax.experimental.pallas import tpu as pltpu
from jax.sharding import Mesh, PartitionSpec as P

TAPS = 27
F32, BF16 = jnp.float32, jnp.bfloat16
ROOM = 50 << 20
HIDDEN_COST = 200 << 20
NT = (((1,), (1,)), ((), ()))
VMEM = pl.BlockSpec(memory_space=pltpu.VMEM)
HBM = pl.BlockSpec(memory_space=pltpu.HBM)
SMEM = pl.BlockSpec(memory_space=pltpu.SMEM)
ANY = pl.BlockSpec(memory_space=pl.ANY)


def shifted(block, axis, distance):
    devices = range(lax.axis_size(axis))
    route = [(i - distance, i) for i in devices if i - distance in devices]
    return lax.ppermute(block, axis, route)


def dot(left, right):
    return jnp.dot(left, right, preferred_element_type=F32)


def dot_nt(left, right):
    return lax.dot_general(left, right, NT, preferred_element_type=F32)


def quotient(value, size):
    return value >> (size.bit_length() - 1) if size & (size - 1) == 0 else value // size


def remainder(value, size):
    return value & (size - 1) if size & (size - 1) == 0 else value % size


def halves(value):
    high = value.astype(BF16)
    return high, (value - high.astype(F32)).astype(BF16)


def patch_picks(side):
    half = side // 2
    even = np.zeros((1, 3, half, half, half, side), np.float32)
    odd = np.zeros((2, 3, half, half, half, side), np.float32)
    for c in range(3):
        for y in range(half):
            for x in range(half):
                column = 2 * x + c - 1
                if column < 0:
                    continue
                even[0, c, y, x, y, column] = 1
                if y > 0:
                    odd[0, c, y, x, y - 1, column] = 1
                odd[1, c, y, x, y, column] = 1
    return even.reshape(-1, half * side), odd.reshape(-1, half * side)


def spread_picks(half):
    quarter = half // 2
    picks = np.zeros((3, 3, half, half, quarter, quarter), np.float32)
    for b in range(3):
        for c in range(3):
            for out_y in range(quarter):
                for out_x in range(quarter):
                    y, x = 2 * out_y + b - 1, 2 * out_x + c - 1
                    if y >= 0 and x >= 0:
                        picks[b, c, y, x, out_y, out_x] = 1
    return picks.reshape(9 * half * half, quarter * quarter)


def project_kernel(
    x_any, left_any, grad_any, out_ref, halo_ref, x_ref, left_ref, grad_ref, rows_ref, arrived
):
    frames, half, _, side, channels = x_ref.shape
    copies = [
        pltpu.make_async_copy(left_any.at[0], left_ref, arrived.at[0]),
        pltpu.make_async_copy(grad_any, grad_ref, arrived.at[1]),
    ]
    order = [frame for time in (1, 0) for frame in range(time, frames, 2)]
    for frame in order:
        copies.append(
            pltpu.make_async_copy(x_any.at[frame], x_ref.at[frame], arrived.at[2 + frame])
        )
    for copy in copies:
        copy.start()
    wide = left_ref.shape[0]
    pairs = frames // 2
    size = pairs * half * side
    target = lax.broadcasted_iota(jnp.int32, (size, size), 0)
    source = lax.broadcasted_iota(jnp.int32, (size, size), 1)
    cells = size // 2
    wanted = 2 * remainder(target, cells) + quotient(target, cells)
    pick = jnp.where(source == wanted, 1.0, 0.0).astype(BF16)
    copies[0].wait()
    both = jnp.concatenate(halves(left_ref[...]), axis=0)
    for time in (1, 0):
        for copy in copies[2 + (1 - time) * pairs : 2 + (2 - time) * pairs]:
            copy.wait()
        if time:
            halo_ref[pl.ds(0, half)] = x_ref[frames - 1]
        for row in range(2):
            block = jnp.concatenate(
                [
                    x_ref[frame, :, row].reshape(half * side, channels)
                    for frame in range(time, frames, 2)
                ],
                axis=0,
            )
            full = dot_nt(block, both)
            small = (full[:, :wide] + full[:, wide:]).astype(BF16)
            ordered = dot(pick, small).astype(BF16)
            at = (4 * time + 2 * row) * cells
            out_ref[at : at + size, :] = ordered
    copies[1].wait()
    rows = stacked_rows(grad_ref, rows_ref)
    halo_ref[half, 0] = rows
    halo_ref[half, 1] = rows
    count = rows.shape[0]
    for block in range(channels // wide):
        at = 8 * cells + block * count
        out_ref[at : at + count, :] = rows[:, block * wide : (block + 1) * wide]


def stacked_rows(grad_ref, rows_ref):
    quarter = grad_ref.shape[0]
    for row in range(quarter):
        rows_ref[pl.ds(row * quarter, quarter), :] = grad_ref[row].astype(F32)
    return rows_ref[...].astype(BF16)


def transposed_products(rows, kernel, taps):
    total = dot_nt(rows[0], kernel[taps[0]])
    for at in range(1, len(taps)):
        total += dot_nt(rows[at], kernel[taps[at]])
    return total


def spread_rows(picks_ref, rows, cells):
    spread = dot(picks_ref[...], rows).astype(BF16)
    return [spread[tap * cells : (tap + 1) * cells] for tap in range(9)]


def hidden_kernel(
    tm_ref, x_ref, prior_ref, grad_ref, later_ref, even_ref, odd_ref, spread_ref, *refs,
    slices, clip_parts,
):
    right_refs = refs[:slices]
    (
        first_any, second_any,
        out_ref, right_out_ref, rows_ref, patches, first, second, arrived,
    ) = refs[slices:]
    frames, half, _, side, channels = x_ref.shape
    cells = half * half
    has_prior = jnp.where(tm_ref[0] > 0, 1.0, 0.0)
    has_later = jnp.where(tm_ref[0] < clip_parts - 1, 1.0, 0.0)
    copies = {
        (at, a): pltpu.make_async_copy(
            source.at[pl.ds(9 * a, 9)], target.at[pl.ds(9 * a, 9)], arrived.at[at, a]
        )
        for at, (source, target) in enumerate(((second_any, second), (first_any, first)))
        for a in (1, 2, 0)
    }
    for copy in copies.values():
        copy.start()
    for distance, right_ref in enumerate(right_refs):
        for layer in range(2):
            right = jnp.concatenate(
                [right_ref[core, layer] for core in range(right_ref.shape[0])], axis=0
            )
            right_out_ref[distance, layer] = jnp.concatenate(halves(right), axis=0)
    own = spread_rows(spread_ref, stacked_rows(grad_ref, rows_ref), cells)
    copies[0, 1].wait()
    early = transposed_products(own, second, range(9, 18))
    copies[0, 2].wait()
    late = transposed_products(own, second, range(18, 27))
    for frame in range(frames + 1):
        block = prior_ref if frame == 0 else x_ref.at[frame - 1]
        even = dot(even_ref[...], block[:half, 0].reshape(half * side, channels))
        odd = dot(odd_ref[...], block[:half, 1].reshape(half * side, channels))
        if frame == 0:
            even, odd = even * has_prior, odd * has_prior
        even, odd = even.astype(BF16), odd.astype(BF16)
        for c in range(3):
            patches[frame, c] = odd[c * cells : (c + 1) * cells]
            patches[frame, 3 + c] = even[c * cells : (c + 1) * cells]
            patches[frame, 6 + c] = odd[(3 + c) * cells : (4 + c) * cells]
    after = spread_rows(spread_ref, later_ref[half, 0], cells)
    copies[0, 0].wait()
    late += transposed_products(after, second, range(9)) * has_later
    hidden_grad = jnp.concatenate([early, late], axis=0)
    pre = jnp.zeros((2 * cells, first.shape[2]), F32)
    for a in (1, 2, 0):
        copies[1, a].wait()
        for tap in range(9):
            rows = jnp.concatenate([patches[a, tap], patches[a + 2, tap]], axis=0)
            pre += dot(rows, first[9 * a + tap])
    sig = jax.nn.sigmoid(pre)
    hidden = (pre * sig).astype(BF16)
    pre_grad = (hidden_grad * sig * (1.0 + pre * (1.0 - sig))).astype(BF16)
    groups, _, _, share, _ = out_ref.shape
    for at in range(slices):
        place = slice(at * share, (at + 1) * share)
        for group in range(groups):
            out_ref[group, at, 0] = pre_grad[place]
            out_ref[group, at, 1] = hidden[place]


def right_kernel(place_ref, acts_ref, right_ref, *out_refs):
    parts, slices = acts_ref.shape[:2]
    both = right_ref.shape[2] // 2
    width = both // len(out_refs)
    for layer in range(2):
        total = None
        for distance in range(slices):
            origin = lax.rem(place_ref[0] + (slices - distance), slices)
            rows = jnp.concatenate([acts_ref[part, origin, layer] for part in range(parts)], axis=0)
            term = dot_nt(right_ref[distance, layer], rows)
            total = term if total is None else total + term
        product = (total[:both] + total[both:]).astype(BF16)
        for at, out_ref in enumerate(out_refs):
            out_ref[pl.ds(layer * width, width), :] = product[at * width : (at + 1) * width]


def tables_kernel(after_any, mix_ref, shift_ref, sort_ref, mixers_ref, *, slices, clip_parts, half):
    del after_any
    size = shift_ref.shape[0]
    cells = size // clip_parts
    share = cells // slices
    frames = size // (half * half)
    held = lax.broadcasted_iota(jnp.int32, (size, size), 0)
    cell = lax.broadcasted_iota(jnp.int32, (size, size), 1)
    part = remainder(quotient(held, share), clip_parts)
    slot = quotient(held, share * clip_parts)
    natural = part * cells + slot * share + remainder(held, share)
    frame = quotient(cell, half * half)
    row = remainder(quotient(cell, half), half)
    column = remainder(cell, half)
    for shift in range(8):
        dt, dr, dc = shift // 4, shift // 2 % 2, shift % 2
        found = natural == cell + ((dt * half + dr) * half + dc)
        if dt:
            found &= frame < frames - 1
        if dr:
            found &= row < half - 1
        if dc:
            found &= column < half - 1
        shift_ref[:, pl.ds(shift * size, size)] = jnp.where(found, 1.0, 0.0).astype(BF16)
    quarter = half // 2
    outputs = size // 8
    kind = quotient(cell, outputs)
    frame = 2 * remainder(quotient(cell, quarter * quarter), frames // 2) + quotient(kind, 4)
    row = 2 * remainder(quotient(cell, quarter), quarter) + remainder(quotient(kind, 2), 2)
    column = 2 * remainder(cell, quarter) + remainder(kind, 2)
    found = natural == (frame * half + row) * half + column
    sort_ref[...] = jnp.where(found, 1.0, 0.0).astype(BF16)

    count = mixers_ref.shape[2]
    tap = lax.broadcasted_iota(jnp.int32, (count, TAPS), 1)
    line = lax.broadcasted_iota(jnp.int32, (count, TAPS), 0)
    spread = jnp.where(quotient(line, 8) == tap, 1.0, 0.0).astype(BF16)
    lines = lax.broadcasted_iota(jnp.int32, (count, count), 0)
    others = lax.broadcasted_iota(jnp.int32, (count, count), 1)
    same = remainder(lines, 8) == remainder(others, 8)
    for layer in range(2):
        for at, part in enumerate(halves(mix_ref[layer])):
            wider = dot_nt(dot(spread, part).astype(BF16), spread)
            mixers_ref[layer, at] = jnp.where(same, wider, 0.0).astype(BF16)


def update_kernel(
    place_ref, chip_ref, core_ref, tm_ref, *refs, slices, cores, clip_parts, half
):
    columns_refs, piece_refs = refs[: slices * cores], refs[slices * cores : (slices + 1) * cores]
    (
        left_ref, mixers_ref, shift_ref, sort_ref,
        out_ref, left_rows_ref, columns, shifts, grads, raw, arrived,
    ) = refs[(slices + 1) * cores :]
    parts = left_rows_ref.shape[0]
    chips = parts // (cores * clip_parts)
    copies = []
    for cross, piece_ref in enumerate(piece_refs):
        core = (core_ref[0] + cross) % cores
        for at, (step, turn) in enumerate(np.ndindex(chips, clip_parts)):
            chip = lax.rem(chip_ref[0] + (chips - step), chips)
            place = lax.rem(tm_ref[0] + (clip_parts - turn), clip_parts)
            target = left_rows_ref.at[(chip * cores + core) * clip_parts + place]
            copies.append(
                pltpu.make_async_copy(piece_ref.at[at], target, arrived.at[len(copies)])
            )
    for copy in copies:
        copy.start()
    for cross, distance in np.ndindex(cores, slices):
        origin = lax.rem(place_ref[0] + (slices - distance), slices)
        core = (core_ref[0] + cross) % cores
        columns[origin, core] = columns_refs[cross * slices + distance][...]
    wide, channels = left_ref.shape[1:]
    width = columns.shape[2] // 2
    clips = parts // clip_parts
    share = columns.shape[3] // chips
    clip_cells = slices * share
    cells = clip_cells // clip_parts
    frames = clip_cells // (half * half)
    outputs = clip_cells // 8

    def by_clip(layer):
        return jnp.concatenate(
            [
                jnp.concatenate(
                    [
                        columns[
                            at, clip % cores, pl.ds(layer * width, width),
                            pl.ds(clip // cores * share, share),
                        ]
                        for at in range(slices)
                    ],
                    axis=1,
                )
                for clip in range(clips)
            ],
            axis=0,
        )

    first = by_clip(0)
    for shift in range(8):
        moved = dot(first, shift_ref[:, pl.ds(shift * clip_cells, clip_cells)]).astype(BF16)
        for clip in range(clips):
            shifts[shift, clip] = moved[clip * width : (clip + 1) * width]
    second = dot(by_clip(1), sort_ref[...]).astype(BF16)

    for copy in copies:
        copy.wait()
    own_outputs = outputs // clip_parts
    blocks = channels // wide
    out_grad = jnp.concatenate(
        [
            jnp.concatenate(
                [
                    left_rows_ref[part, pl.ds(8 * cells + own_outputs * at, own_outputs), :]
                    for at in range(blocks)
                ],
                axis=1,
            )
            for part in range(parts)
        ],
        axis=0,
    )
    full = dot_nt(out_grad, jnp.concatenate(halves(left_ref[1]), axis=0))
    total = parts * own_outputs
    quarter = half // 2
    grads[pl.ds(0, total), :] = full[:, :wide] + full[:, wide:]
    places = lax.broadcasted_iota(jnp.int32, (total, wide), 0)
    frame = remainder(quotient(places, quarter * quarter), frames // 2)
    row = remainder(quotient(places, quarter), quarter)
    column = remainder(places, quarter)
    second_rows = []
    for shift in range(8):
        dt, dr, dc = shift // 4, shift // 2 % 2, shift % 2
        moved = grads[pl.ds((dt * quarter + dr) * quarter + dc, total), :]
        inside = (frame + dt < frames // 2) & (row + dr < quarter) & (column + dc < quarter)
        second_rows.append(jnp.where(inside, moved, 0.0).astype(BF16))

    for time, line in np.ndindex(2, 2):
        even = [
            (9 * a + 3 * b + 1, 4 * (a == 0) + 2 * (b == 0))
            for a in ((0, 2) if time else (1,))
            for b in ((0, 2) if line else (1,))
        ]
        odd = [(tap + 1, shift) for tap, shift in even] + [
            (tap - 1, shift + 1) for tap, shift in even
        ]
        kind = 4 * time + 2 * line
        sums = None
        for clip in range(clips):
            left = jnp.concatenate([shifts[shift, clip] for _, shift in odd], axis=0)
            rows = jnp.concatenate(
                [
                    jnp.concatenate(
                        [
                            left_rows_ref[
                                clip * clip_parts + part, pl.ds((kind + at) * cells, cells), :
                            ]
                            for part in range(clip_parts)
                        ],
                        axis=0,
                    )
                    for at in range(2)
                ],
                axis=1,
            )
            term = dot(left, rows)
            sums = term if sums is None else sums + term
        for at, (tap, _) in enumerate(even):
            raw[0, tap] = sums[at * width : (at + 1) * width, :wide]
        for at, (tap, _) in enumerate(odd):
            raw[0, tap] = sums[at * width : (at + 1) * width, wide:]
        for place, taps in enumerate((even, odd)):
            chosen = jnp.concatenate(
                [
                    second[
                        clip * width : (clip + 1) * width,
                        (kind + place) * outputs : (kind + place + 1) * outputs,
                    ]
                    for clip in range(clips)
                ],
                axis=1,
            )
            products = dot(
                chosen, jnp.concatenate([second_rows[shift] for _, shift in taps], axis=1)
            )
            for at, (tap, _) in enumerate(taps):
                raw[1, tap] = products[:, at * wide : (at + 1) * wide]

    for layer in range(2):
        for group in range(width // 16):
            lanes = jnp.concatenate(
                [
                    raw[layer, :, pl.ds(16 * group + 8 * at, 8), :].reshape(8 * TAPS, wide)
                    for at in range(2)
                ],
                axis=1,
            )
            high, low = halves(lanes)
            mixed = (
                dot(mixers_ref[layer, 0], high)
                + dot(mixers_ref[layer, 0], low)
                + dot(mixers_ref[layer, 1], high)
            )
            rows = jnp.concatenate(
                [
                    mixed[:, at * wide : (at + 1) * wide].reshape(TAPS, 8, wide)
                    for at in range(2)
                ],
                axis=1,
            )
            out_ref[layer, :, pl.ds(16 * group, 16), :] = rows.astype(BF16)


def turned(block, axes, steps):
    sizes = [lax.axis_size(axis) for axis in axes]
    if not any(step % size for step, size in zip(steps, sizes)):
        return block
    route = []
    for place in np.ndindex(*sizes):
        target = [(at + step) % size for at, step, size in zip(place, steps, sizes)]
        route.append(
            (int(np.ravel_multi_index(place, sizes)), int(np.ravel_multi_index(target, sizes)))
        )
    return lax.ppermute(block, axes, route)


def shards(clip_input, first_kernel, second_kernel, out_grad, tap_mix, left_panels, right_panels):
    clips, frames, side, _, channels = clip_input.shape
    wide = first_kernel.shape[2]
    width = right_panels.shape[2]
    half, quarter = side // 2, side // 4
    half_frames = frames // 2
    cells = half_frames * half * half
    clip_parts = lax.axis_size("tm")
    cores, chips = lax.axis_size("core"), lax.axis_size("chip")
    equals = chips * clip_parts
    parts = equals * cores
    slices = lax.axis_size("fsdp")
    share = cells // slices
    assert clips == 1 and frames == 4 and quarter * quarter == side
    x = clip_input.reshape(frames, half, 2, side, channels)
    grad = out_grad.reshape(quarter, quarter, channels)
    place, chip_at, core_at, half_at = (
        lax.axis_index(axis).reshape(1) for axis in ("fsdp", "chip", "core", "tm")
    )

    projected, halo = pl.pallas_call(
        project_kernel,
        out_shape=(
            jax.ShapeDtypeStruct(
                (8 * cells + quarter * quarter * channels // wide, wide), BF16
            ),
            jax.ShapeDtypeStruct((half + 1, 2, side, channels), BF16),
        ),
        in_specs=[ANY] * 3,
        out_specs=(VMEM, VMEM),
        scratch_shapes=[
            pltpu.VMEM(x.shape, BF16),
            pltpu.VMEM(left_panels.shape[1:], F32),
            pltpu.VMEM(grad.shape, BF16),
            pltpu.VMEM((quarter * quarter, channels), F32),
            pltpu.SemaphoreType.DMA((2 + frames,)),
        ],
        compiler_params=pltpu.CompilerParams(vmem_limit_bytes=58 << 20),
        cost_estimate=pl.CostEstimate(
            flops=4 * frames * side * side * channels * wide,
            bytes_accessed=2 * frames * side * side * channels,
            transcendentals=0,
        ),
    )(x, left_panels, grad)
    if clip_parts == 2:
        prior = later = lax.ppermute(halo, "tm", [(0, 1), (1, 0)])
    else:
        prior, later = shifted(halo, "tm", 1), shifted(halo, "tm", -1)
    projected, prior, later = lax.optimization_barrier((projected, prior, later))
    held = jnp.stack(
        [
            turned(projected, ("chip", "tm"), steps)
            for steps in np.ndindex(chips, clip_parts)
        ]
    )

    right = right_panels.transpose(0, 2, 1)
    right = jnp.stack([turned(right, ("core",), (cross,)) for cross in range(cores)])
    rights = [turned(right, ("fsdp",), (distance,)) for distance in range(slices)]

    even, odd = patch_picks(side)
    spread = jnp.asarray(spread_picks(half), BF16)
    acts, right = pl.pallas_call(
        functools.partial(hidden_kernel, slices=slices, clip_parts=clip_parts),
        out_shape=(
            jax.ShapeDtypeStruct((equals, slices, 2, share, wide), BF16),
            jax.ShapeDtypeStruct((slices, 2, 2 * cores * width, wide), BF16),
        ),
        in_specs=[SMEM] + [VMEM] * (7 + slices) + [HBM] * 2,
        out_specs=(VMEM, VMEM),
        scratch_shapes=[
            pltpu.VMEM((quarter * quarter, channels), F32),
            pltpu.VMEM((frames + 1, 9, half * half, channels), BF16),
            pltpu.VMEM(first_kernel.shape, BF16),
            pltpu.VMEM(second_kernel.shape, BF16),
            pltpu.SemaphoreType.DMA((2, 3)),
        ],
        compiler_params=pltpu.CompilerParams(vmem_limit_bytes=ROOM),
        cost_estimate=pl.CostEstimate(
            flops=3 * cells * TAPS * channels * wide,
            bytes_accessed=HIDDEN_COST,
            transcendentals=cells * wide,
        ),
    )(
        half_at, x, prior, grad, later, jnp.asarray(even, BF16), jnp.asarray(odd, BF16),
        spread, *rights, first_kernel, second_kernel,
    )
    clip_cells = clip_parts * cells
    shift_picks, sort_picks, mixers = pl.pallas_call(
        functools.partial(tables_kernel, slices=slices, clip_parts=clip_parts, half=half),
        out_shape=(
            jax.ShapeDtypeStruct((clip_cells, 8 * clip_cells), BF16),
            jax.ShapeDtypeStruct((clip_cells, clip_cells), BF16),
            jax.ShapeDtypeStruct((2, 2, 8 * TAPS, 8 * TAPS), BF16),
        ),
        in_specs=[ANY, VMEM],
        out_specs=(VMEM,) * 3,
        compiler_params=pltpu.CompilerParams(vmem_limit_bytes=16 << 20),
        cost_estimate=pl.CostEstimate(flops=0, bytes_accessed=4 << 20, transcendentals=0),
    )(acts, tap_mix)
    every = lax.all_to_all(
        acts.reshape(equals * slices, 2, share, wide), ("chip", "tm", "fsdp"), 0, 0, tiled=True
    ).reshape(equals, slices, 2, share, wide)
    columns = pl.pallas_call(
        right_kernel,
        out_shape=(jax.ShapeDtypeStruct((2 * width, equals * share), BF16),) * cores,
        in_specs=[SMEM] + [VMEM] * 2,
        out_specs=(VMEM,) * cores,
        compiler_params=pltpu.CompilerParams(vmem_limit_bytes=16 << 20),
    )(place, every, right)
    *columns, held = lax.optimization_barrier((*columns, held))
    columns = [
        turned(columns[cross], ("fsdp", "core"), (distance, cross))
        for cross, distance in np.ndindex(cores, slices)
    ]
    left_rows = [turned(held, ("core",), (cross,)) for cross in range(cores)]

    result = pl.pallas_call(
        functools.partial(
            update_kernel, slices=slices, cores=cores, clip_parts=clip_parts, half=half
        ),
        out_shape=jax.ShapeDtypeStruct((2, TAPS, width, wide), BF16),
        in_specs=[SMEM] * 4
        + [VMEM] * len(columns)
        + [ANY] * cores
        + [VMEM] * 4,
        out_specs=VMEM,
        scratch_shapes=[
            pltpu.VMEM((parts,) + projected.shape, BF16),
            pltpu.VMEM((slices, cores, 2 * width, equals * share), BF16),
            pltpu.VMEM((8, parts // clip_parts, width, clip_cells), BF16),
            pltpu.VMEM((parts * cells // 8 + (quarter + 1) * quarter + 8, wide), F32),
            pltpu.VMEM((2, TAPS, width, wide), F32),
            pltpu.SemaphoreType.DMA((parts,)),
        ],
        compiler_params=pltpu.CompilerParams(vmem_limit_bytes=40 << 20),
    )(
        place, chip_at, core_at, half_at,
        *columns, *left_rows, left_panels, mixers, shift_picks, sort_picks,
    )
    return result.transpose(0, 1, 3, 2)


def solution(mesh):
    fsdp, replica, tm = (mesh.shape[axis] for axis in ("fsdp", "replica", "tm"))
    cores = 2 if replica % 2 == 0 else 1
    assert mesh.axis_names == ("fsdp", "replica", "tm")
    mesh = Mesh(
        mesh.devices.reshape(fsdp, replica // cores, cores, tm), ("fsdp", "chip", "core", "tm")
    )
    replica = ("chip", "core")
    in_specs = (
        P(replica, "tm", None, None, None),
        P(None, None, "fsdp"),
        P(None, "fsdp", None),
        P(replica, "tm", None, None, None),
        P(),
        P(None, "fsdp", None),
        P(None, "fsdp", (*replica, "tm")),
    )
    out_specs = P(None, None, "fsdp", (*replica, "tm"))
    return jax.shard_map(shards, mesh=mesh, in_specs=in_specs, out_specs=out_specs, check_vma=False)
```

```python
import functools

import jax
import jax.numpy as jnp
import numpy as np
from jax import lax
from jax.experimental import pallas as pl
from jax.experimental.pallas import tpu as pltpu
from jax.sharding import Mesh, PartitionSpec as P

TAPS = 27
F32, BF16 = jnp.float32, jnp.bfloat16
ROOM = 50 << 20
HIDDEN_COST = 200 << 20
NT = (((1,), (1,)), ((), ()))
VMEM = pl.BlockSpec(memory_space=pltpu.VMEM)
HBM = pl.BlockSpec(memory_space=pltpu.HBM)
SMEM = pl.BlockSpec(memory_space=pltpu.SMEM)
ANY = pl.BlockSpec(memory_space=pl.ANY)


def shifted(block, axis, distance):
    devices = range(lax.axis_size(axis))
    route = [(i - distance, i) for i in devices if i - distance in devices]
    return lax.ppermute(block, axis, route)


def dot(left, right):
    return jnp.dot(left, right, preferred_element_type=F32)


def dot_nt(left, right):
    return lax.dot_general(left, right, NT, preferred_element_type=F32)


def quotient(value, size):
    return value >> (size.bit_length() - 1) if size & (size - 1) == 0 else value // size


def remainder(value, size):
    return value & (size - 1) if size & (size - 1) == 0 else value % size


def halves(value):
    high = value.astype(BF16)
    return high, (value - high.astype(F32)).astype(BF16)


def patch_picks(side):
    half = side // 2
    even = np.zeros((1, 3, half, half, half, side), np.float32)
    odd = np.zeros((2, 3, half, half, half, side), np.float32)
    for c in range(3):
        for y in range(half):
            for x in range(half):
                column = 2 * x + c - 1
                if column < 0:
                    continue
                even[0, c, y, x, y, column] = 1
                if y > 0:
                    odd[0, c, y, x, y - 1, column] = 1
                odd[1, c, y, x, y, column] = 1
    return even.reshape(-1, half * side), odd.reshape(-1, half * side)


def spread_picks(half):
    quarter = half // 2
    picks = np.zeros((3, 3, half, half, quarter, quarter), np.float32)
    for b in range(3):
        for c in range(3):
            for out_y in range(quarter):
                for out_x in range(quarter):
                    y, x = 2 * out_y + b - 1, 2 * out_x + c - 1
                    if y >= 0 and x >= 0:
                        picks[b, c, y, x, out_y, out_x] = 1
    return picks.reshape(9 * half * half, quarter * quarter)


def patch_rows(even, odd, even_ref, odd_ref, half):
    cells = half * half
    even = dot(even_ref[...], even).astype(BF16)
    odd = dot(odd_ref[...], odd).astype(BF16)
    rows = [odd[at * cells : (at + 1) * cells] for at in range(6)]
    rows[3:3] = [even[at * cells : (at + 1) * cells] for at in range(3)]
    return rows


def project_kernel(
    x_any, left_any, grad_any, even_any, odd_any, first_any,
    out_ref, halo_ref, x_ref, left_ref, grad_ref, even_ref, odd_ref, first_ref, rows_ref, arrived,
):
    frames, half, _, side, channels = x_ref.shape
    order = [frame for time in (1, 0) for frame in range(time, frames, 2)]
    pairs_of = [
        (left_any.at[0], left_ref),
        (x_any.at[order[0]], x_ref.at[order[0]]),
        (x_any.at[order[1]], x_ref.at[order[1]]),
        (even_any, even_ref),
        (odd_any, odd_ref),
        (first_any.at[pl.ds(0, 9)], first_ref),
        (x_any.at[order[2]], x_ref.at[order[2]]),
        (x_any.at[order[3]], x_ref.at[order[3]]),
        (grad_any, grad_ref),
    ]
    copies = [
        pltpu.make_async_copy(source, target, arrived.at[at])
        for at, (source, target) in enumerate(pairs_of)
    ]
    for copy in copies:
        copy.start()
    wide = left_ref.shape[0]
    pairs = frames // 2
    size = pairs * half * side
    target = lax.broadcasted_iota(jnp.int32, (size, size), 0)
    source = lax.broadcasted_iota(jnp.int32, (size, size), 1)
    cells = size // 2
    wanted = 2 * remainder(target, cells) + quotient(target, cells)
    pick = jnp.where(source == wanted, 1.0, 0.0).astype(BF16)
    copies[0].wait()
    both = jnp.concatenate(halves(left_ref[...]), axis=0)

    def project(time):
        for row in range(2):
            block = jnp.concatenate(
                [
                    x_ref[frame, :, row].reshape(half * side, channels)
                    for frame in range(time, frames, 2)
                ],
                axis=0,
            )
            full = dot_nt(block, both)
            small = (full[:, :wide] + full[:, wide:]).astype(BF16)
            ordered = dot(pick, small).astype(BF16)
            at = (4 * time + 2 * row) * cells
            out_ref[at : at + size, :] = ordered

    copies[1].wait()
    copies[2].wait()
    project(1)
    copies[3].wait()
    copies[4].wait()
    lines = [x_ref[frames - 1, :, row].reshape(half * side, channels) for row in range(2)]
    rows = patch_rows(*lines, even_ref, odd_ref, half)
    copies[5].wait()
    total = dot(rows[0], first_ref[0])
    for tap in range(1, 9):
        total += dot(rows[tap], first_ref[tap])
    halo_ref[pl.ds(0, half * half), :] = total
    copies[6].wait()
    copies[7].wait()
    project(0)
    copies[8].wait()
    grad_rows = stacked_rows(grad_ref, rows_ref)
    count = grad_rows.shape[0]
    for block in range(channels // wide):
        at = 8 * cells + block * count
        out_ref[at : at + count, :] = grad_rows[:, block * wide : (block + 1) * wide]
        at = half * half + block * count
        halo_ref[at : at + count, :] = rows_ref[:, block * wide : (block + 1) * wide]


def stacked_rows(grad_ref, rows_ref):
    quarter = grad_ref.shape[0]
    for row in range(quarter):
        rows_ref[pl.ds(row * quarter, quarter), :] = grad_ref[row].astype(F32)
    return rows_ref[...].astype(BF16)


def transposed_products(rows, kernel, taps):
    total = dot_nt(rows[0], kernel[taps[0]])
    for at in range(1, len(taps)):
        total += dot_nt(rows[at], kernel[taps[at]])
    return total


def spread_rows(picks_ref, rows, cells):
    spread = dot(picks_ref[...], rows).astype(BF16)
    return [spread[tap * cells : (tap + 1) * cells] for tap in range(9)]


def hidden_kernel(
    tm_ref, x_ref, prior_ref, grad_ref, later_ref, even_ref, odd_ref, spread_ref,
    first_any, second_any, out_ref, rows_ref, patches, first, second, arrived, *, clip_parts,
):
    frames, half, _, side, channels = x_ref.shape
    cells = half * half
    has_prior = jnp.where(tm_ref[0] > 0, 1.0, 0.0)
    has_later = jnp.where(tm_ref[0] < clip_parts - 1, 1.0, 0.0)
    copies = {
        (at, a): pltpu.make_async_copy(
            source.at[pl.ds(9 * a, 9)], target.at[pl.ds(9 * a, 9)], arrived.at[at, a]
        )
        for at, (source, target) in enumerate(((second_any, second), (first_any, first)))
        for a in (1, 2, 0)
    }
    for copy in copies.values():
        copy.start()
    own_rows = stacked_rows(grad_ref, rows_ref)
    own = spread_rows(spread_ref, own_rows, cells)
    copies[0, 1].wait()
    early = transposed_products(own, second, range(9, 18))
    copies[0, 2].wait()
    late = transposed_products(own, second, range(18, 27))
    for frame in range(frames):
        lines = [x_ref[frame, :, row].reshape(half * side, channels) for row in range(2)]
        for tap, rows in enumerate(patch_rows(*lines, even_ref, odd_ref, half)):
            patches[frame, tap] = rows
    count = own_rows.shape[0]
    wide = first.shape[2]
    later_rows = jnp.concatenate(
        [
            later_ref[pl.ds(cells + count * block, count), :]
            for block in range(channels // wide)
        ],
        axis=1,
    )
    after = spread_rows(spread_ref, later_rows.astype(BF16), cells)
    copies[0, 0].wait()
    late += transposed_products(after, second, range(9)) * has_later
    hidden_grad = jnp.concatenate([early, late], axis=0)
    pre = jnp.zeros((2 * cells, wide), F32)
    for a in (1, 2):
        copies[1, a].wait()
        for tap in range(9):
            rows = jnp.concatenate([patches[a - 1, tap], patches[a + 1, tap]], axis=0)
            pre += dot(rows, first[9 * a + tap])
    copies[1, 0].wait()
    inner = dot(patches[1, 0], first[0])
    for tap in range(1, 9):
        inner += dot(patches[1, tap], first[tap])
    pre += jnp.concatenate([prior_ref[pl.ds(0, cells), :] * has_prior, inner], axis=0)
    sig = jax.nn.sigmoid(pre)
    hidden = (pre * sig).astype(BF16)
    pre_grad = (hidden_grad * sig * (1.0 + pre * (1.0 - sig))).astype(BF16)
    groups, slices, _, share, _ = out_ref.shape
    for at in range(slices):
        place = slice(at * share, (at + 1) * share)
        for group in range(groups):
            out_ref[group, at, 0] = pre_grad[place]
            out_ref[group, at, 1] = hidden[place]


def right_kernel(place_ref, acts_ref, right_ref, *out_refs):
    parts, slices = acts_ref.shape[:2]
    both = right_ref.shape[2] // 2
    width = both // len(out_refs)
    for layer in range(2):
        total = None
        for distance in range(slices):
            origin = lax.rem(place_ref[0] + (slices - distance), slices)
            rows = jnp.concatenate([acts_ref[part, origin, layer] for part in range(parts)], axis=0)
            term = dot_nt(right_ref[distance, layer], rows)
            total = term if total is None else total + term
        product = (total[:both] + total[both:]).astype(BF16)
        for at, out_ref in enumerate(out_refs):
            out_ref[pl.ds(layer * width, width), :] = product[at * width : (at + 1) * width]


def tables_kernel(after_any, mix_ref, *refs, slices, clip_parts, half):
    del after_any
    right_refs = refs[:slices]
    shift_ref, sort_ref, mixers_ref, right_out_ref = refs[slices:]
    for distance, right_ref in enumerate(right_refs):
        for layer in range(2):
            right = jnp.concatenate(
                [right_ref[core, layer] for core in range(right_ref.shape[0])], axis=0
            )
            right_out_ref[distance, layer] = jnp.concatenate(halves(right), axis=0)
    size = shift_ref.shape[0]
    cells = size // clip_parts
    share = cells // slices
    frames = size // (half * half)
    held = lax.broadcasted_iota(jnp.int32, (size, size), 0)
    cell = lax.broadcasted_iota(jnp.int32, (size, size), 1)
    part = remainder(quotient(held, share), clip_parts)
    slot = quotient(held, share * clip_parts)
    natural = part * cells + slot * share + remainder(held, share)
    frame = quotient(cell, half * half)
    row = remainder(quotient(cell, half), half)
    column = remainder(cell, half)
    for shift in range(8):
        dt, dr, dc = shift // 4, shift // 2 % 2, shift % 2
        found = natural == cell + ((dt * half + dr) * half + dc)
        if dt:
            found &= frame < frames - 1
        if dr:
            found &= row < half - 1
        if dc:
            found &= column < half - 1
        shift_ref[:, pl.ds(shift * size, size)] = jnp.where(found, 1.0, 0.0).astype(BF16)
    quarter = half // 2
    outputs = size // 8
    kind = quotient(cell, outputs)
    frame = 2 * remainder(quotient(cell, quarter * quarter), frames // 2) + quotient(kind, 4)
    row = 2 * remainder(quotient(cell, quarter), quarter) + remainder(quotient(kind, 2), 2)
    column = 2 * remainder(cell, quarter) + remainder(kind, 2)
    found = natural == (frame * half + row) * half + column
    sort_ref[...] = jnp.where(found, 1.0, 0.0).astype(BF16)

    count = mixers_ref.shape[2]
    tap = lax.broadcasted_iota(jnp.int32, (count, TAPS), 1)
    line = lax.broadcasted_iota(jnp.int32, (count, TAPS), 0)
    spread = jnp.where(quotient(line, 8) == tap, 1.0, 0.0).astype(BF16)
    lines = lax.broadcasted_iota(jnp.int32, (count, count), 0)
    others = lax.broadcasted_iota(jnp.int32, (count, count), 1)
    same = remainder(lines, 8) == remainder(others, 8)
    for layer in range(2):
        for at, part in enumerate(halves(mix_ref[layer])):
            wider = dot_nt(dot(spread, part).astype(BF16), spread)
            mixers_ref[layer, at] = jnp.where(same, wider, 0.0).astype(BF16)


def update_kernel(
    place_ref, chip_ref, core_ref, tm_ref, *refs, slices, cores, clip_parts, half
):
    columns_refs, piece_refs = refs[: slices * cores], refs[slices * cores : (slices + 1) * cores]
    (
        left_ref, mixers_ref, shift_ref, sort_ref,
        out_ref, left_rows_ref, columns, shifts, grads, raw, arrived,
    ) = refs[(slices + 1) * cores :]
    parts = left_rows_ref.shape[0]
    chips = parts // (cores * clip_parts)
    copies = []
    for cross, piece_ref in enumerate(piece_refs):
        core = (core_ref[0] + cross) % cores
        for at, (step, turn) in enumerate(np.ndindex(chips, clip_parts)):
            chip = lax.rem(chip_ref[0] + (chips - step), chips)
            place = lax.rem(tm_ref[0] + (clip_parts - turn), clip_parts)
            target = left_rows_ref.at[(chip * cores + core) * clip_parts + place]
            copies.append(
                pltpu.make_async_copy(piece_ref.at[at], target, arrived.at[len(copies)])
            )
    for copy in copies:
        copy.start()
    for cross, distance in np.ndindex(cores, slices):
        origin = lax.rem(place_ref[0] + (slices - distance), slices)
        core = (core_ref[0] + cross) % cores
        columns[origin, core] = columns_refs[cross * slices + distance][...]
    wide, channels = left_ref.shape[1:]
    width = columns.shape[2] // 2
    clips = parts // clip_parts
    share = columns.shape[3] // chips
    clip_cells = slices * share
    cells = clip_cells // clip_parts
    frames = clip_cells // (half * half)
    outputs = clip_cells // 8

    def by_clip(layer):
        return jnp.concatenate(
            [
                jnp.concatenate(
                    [
                        columns[
                            at, clip % cores, pl.ds(layer * width, width),
                            pl.ds(clip // cores * share, share),
                        ]
                        for at in range(slices)
                    ],
                    axis=1,
                )
                for clip in range(clips)
            ],
            axis=0,
        )

    first = by_clip(0)
    for shift in range(8):
        moved = dot(first, shift_ref[:, pl.ds(shift * clip_cells, clip_cells)]).astype(BF16)
        for clip in range(clips):
            shifts[shift, clip] = moved[clip * width : (clip + 1) * width]
    second = dot(by_clip(1), sort_ref[...]).astype(BF16)

    for copy in copies:
        copy.wait()
    own_outputs = outputs // clip_parts
    blocks = channels // wide
    out_grad = jnp.concatenate(
        [
            jnp.concatenate(
                [
                    left_rows_ref[part, pl.ds(8 * cells + own_outputs * at, own_outputs), :]
                    for at in range(blocks)
                ],
                axis=1,
            )
            for part in range(parts)
        ],
        axis=0,
    )
    full = dot_nt(out_grad, jnp.concatenate(halves(left_ref[1]), axis=0))
    total = parts * own_outputs
    quarter = half // 2
    grads[pl.ds(0, total), :] = full[:, :wide] + full[:, wide:]
    places = lax.broadcasted_iota(jnp.int32, (total, wide), 0)
    frame = remainder(quotient(places, quarter * quarter), frames // 2)
    row = remainder(quotient(places, quarter), quarter)
    column = remainder(places, quarter)
    second_rows = []
    for shift in range(8):
        dt, dr, dc = shift // 4, shift // 2 % 2, shift % 2
        moved = grads[pl.ds((dt * quarter + dr) * quarter + dc, total), :]
        inside = (frame + dt < frames // 2) & (row + dr < quarter) & (column + dc < quarter)
        second_rows.append(jnp.where(inside, moved, 0.0).astype(BF16))

    for time, line in np.ndindex(2, 2):
        even = [
            (9 * a + 3 * b + 1, 4 * (a == 0) + 2 * (b == 0))
            for a in ((0, 2) if time else (1,))
            for b in ((0, 2) if line else (1,))
        ]
        odd = [(tap + 1, shift) for tap, shift in even] + [
            (tap - 1, shift + 1) for tap, shift in even
        ]
        kind = 4 * time + 2 * line
        sums = None
        for clip in range(clips):
            left = jnp.concatenate([shifts[shift, clip] for _, shift in odd], axis=0)
            rows = jnp.concatenate(
                [
                    jnp.concatenate(
                        [
                            left_rows_ref[
                                clip * clip_parts + part, pl.ds((kind + at) * cells, cells), :
                            ]
                            for part in range(clip_parts)
                        ],
                        axis=0,
                    )
                    for at in range(2)
                ],
                axis=1,
            )
            term = dot(left, rows)
            sums = term if sums is None else sums + term
        for at, (tap, _) in enumerate(even):
            raw[0, tap] = sums[at * width : (at + 1) * width, :wide]
        for at, (tap, _) in enumerate(odd):
            raw[0, tap] = sums[at * width : (at + 1) * width, wide:]
        for place, taps in enumerate((even, odd)):
            chosen = jnp.concatenate(
                [
                    second[
                        clip * width : (clip + 1) * width,
                        (kind + place) * outputs : (kind + place + 1) * outputs,
                    ]
                    for clip in range(clips)
                ],
                axis=1,
            )
            products = dot(
                chosen, jnp.concatenate([second_rows[shift] for _, shift in taps], axis=1)
            )
            for at, (tap, _) in enumerate(taps):
                raw[1, tap] = products[:, at * wide : (at + 1) * wide]

    for layer in range(2):
        for group in range(width // 16):
            lanes = jnp.concatenate(
                [
                    raw[layer, :, pl.ds(16 * group + 8 * at, 8), :].reshape(8 * TAPS, wide)
                    for at in range(2)
                ],
                axis=1,
            )
            high, low = halves(lanes)
            mixed = (
                dot(mixers_ref[layer, 0], high)
                + dot(mixers_ref[layer, 0], low)
                + dot(mixers_ref[layer, 1], high)
            )
            rows = jnp.concatenate(
                [
                    mixed[:, at * wide : (at + 1) * wide].reshape(TAPS, 8, wide)
                    for at in range(2)
                ],
                axis=1,
            )
            out_ref[layer, :, pl.ds(16 * group, 16), :] = rows.astype(BF16)


def turned(block, axes, steps):
    sizes = [lax.axis_size(axis) for axis in axes]
    if not any(step % size for step, size in zip(steps, sizes)):
        return block
    route = []
    for place in np.ndindex(*sizes):
        target = [(at + step) % size for at, step, size in zip(place, steps, sizes)]
        route.append(
            (int(np.ravel_multi_index(place, sizes)), int(np.ravel_multi_index(target, sizes)))
        )
    return lax.ppermute(block, axes, route)


def shards(clip_input, first_kernel, second_kernel, out_grad, tap_mix, left_panels, right_panels):
    clips, frames, side, _, channels = clip_input.shape
    wide = first_kernel.shape[2]
    width = right_panels.shape[2]
    half, quarter = side // 2, side // 4
    half_frames = frames // 2
    cells = half_frames * half * half
    clip_parts = lax.axis_size("tm")
    cores, chips = lax.axis_size("core"), lax.axis_size("chip")
    equals = chips * clip_parts
    parts = equals * cores
    slices = lax.axis_size("fsdp")
    share = cells // slices
    assert clips == 1 and frames == 4
    x = clip_input.reshape(frames, half, 2, side, channels)
    grad = out_grad.reshape(quarter, quarter, channels)
    place, chip_at, core_at, half_at = (
        lax.axis_index(axis).reshape(1) for axis in ("fsdp", "chip", "core", "tm")
    )

    even, odd = (jnp.asarray(picks, BF16) for picks in patch_picks(side))
    rows = quarter * quarter * channels // wide
    projected, halo = pl.pallas_call(
        project_kernel,
        out_shape=(
            jax.ShapeDtypeStruct((8 * cells + rows, wide), BF16),
            jax.ShapeDtypeStruct((half * half + rows, wide), F32),
        ),
        in_specs=[ANY] * 6,
        out_specs=(VMEM, VMEM),
        scratch_shapes=[
            pltpu.VMEM(x.shape, BF16),
            pltpu.VMEM(left_panels.shape[1:], F32),
            pltpu.VMEM(grad.shape, BF16),
            pltpu.VMEM(even.shape, BF16),
            pltpu.VMEM(odd.shape, BF16),
            pltpu.VMEM((9,) + first_kernel.shape[1:], BF16),
            pltpu.VMEM((quarter * quarter, channels), F32),
            pltpu.SemaphoreType.DMA((9,)),
        ],
        compiler_params=pltpu.CompilerParams(vmem_limit_bytes=58 << 20),
        cost_estimate=pl.CostEstimate(
            flops=4 * frames * side * side * channels * wide,
            bytes_accessed=2 * frames * side * side * channels,
            transcendentals=0,
        ),
    )(x, left_panels, grad, even, odd, first_kernel)
    if clip_parts == 2:
        prior = later = lax.ppermute(halo, "tm", [(0, 1), (1, 0)])
    else:
        prior, later = shifted(halo, "tm", 1), shifted(halo, "tm", -1)
    projected, prior, later = lax.optimization_barrier((projected, prior, later))
    held = jnp.stack(
        [
            turned(projected, ("chip", "tm"), steps)
            for steps in np.ndindex(chips, clip_parts)
        ]
    )

    right = right_panels.transpose(0, 2, 1)
    right = jnp.stack([turned(right, ("core",), (cross,)) for cross in range(cores)])
    rights = [turned(right, ("fsdp",), (distance,)) for distance in range(slices)]

    spread = jnp.asarray(spread_picks(half), BF16)
    acts = pl.pallas_call(
        functools.partial(hidden_kernel, clip_parts=clip_parts),
        out_shape=jax.ShapeDtypeStruct((equals, slices, 2, share, wide), BF16),
        in_specs=[SMEM] + [VMEM] * 7 + [HBM] * 2,
        out_specs=VMEM,
        scratch_shapes=[
            pltpu.VMEM((quarter * quarter, channels), F32),
            pltpu.VMEM((frames, 9, half * half, channels), BF16),
            pltpu.VMEM(first_kernel.shape, BF16),
            pltpu.VMEM(second_kernel.shape, BF16),
            pltpu.SemaphoreType.DMA((2, 3)),
        ],
        compiler_params=pltpu.CompilerParams(vmem_limit_bytes=ROOM),
        cost_estimate=pl.CostEstimate(
            flops=3 * cells * TAPS * channels * wide,
            bytes_accessed=HIDDEN_COST,
            transcendentals=cells * wide,
        ),
    )(
        half_at, x, prior, grad, later, even, odd, spread, first_kernel, second_kernel,
    )
    clip_cells = clip_parts * cells
    shift_picks, sort_picks, mixers, right = pl.pallas_call(
        functools.partial(tables_kernel, slices=slices, clip_parts=clip_parts, half=half),
        out_shape=(
            jax.ShapeDtypeStruct((clip_cells, 8 * clip_cells), BF16),
            jax.ShapeDtypeStruct((clip_cells, clip_cells), BF16),
            jax.ShapeDtypeStruct((2, 2, 8 * TAPS, 8 * TAPS), BF16),
            jax.ShapeDtypeStruct((slices, 2, 2 * cores * width, wide), BF16),
        ),
        in_specs=[ANY] + [VMEM] * (1 + slices),
        out_specs=(VMEM,) * 4,
        compiler_params=pltpu.CompilerParams(vmem_limit_bytes=16 << 20),
        cost_estimate=pl.CostEstimate(flops=0, bytes_accessed=4 << 20, transcendentals=0),
    )(acts, tap_mix, *rights)
    every = lax.all_to_all(
        acts.reshape(equals * slices, 2, share, wide), ("chip", "tm", "fsdp"), 0, 0, tiled=True
    ).reshape(equals, slices, 2, share, wide)
    columns = pl.pallas_call(
        right_kernel,
        out_shape=(jax.ShapeDtypeStruct((2 * width, equals * share), BF16),) * cores,
        in_specs=[SMEM] + [VMEM] * 2,
        out_specs=(VMEM,) * cores,
        compiler_params=pltpu.CompilerParams(vmem_limit_bytes=16 << 20),
    )(place, every, right)
    *columns, held = lax.optimization_barrier((*columns, held))
    columns = [
        turned(columns[cross], ("fsdp", "core"), (distance, cross))
        for cross, distance in np.ndindex(cores, slices)
    ]
    left_rows = [turned(held, ("core",), (cross,)) for cross in range(cores)]

    result = pl.pallas_call(
        functools.partial(
            update_kernel, slices=slices, cores=cores, clip_parts=clip_parts, half=half
        ),
        out_shape=jax.ShapeDtypeStruct((2, TAPS, width, wide), BF16),
        in_specs=[SMEM] * 4
        + [VMEM] * len(columns)
        + [ANY] * cores
        + [VMEM] * 4,
        out_specs=VMEM,
        scratch_shapes=[
            pltpu.VMEM((parts,) + projected.shape, BF16),
            pltpu.VMEM((slices, cores, 2 * width, equals * share), BF16),
            pltpu.VMEM((8, parts // clip_parts, width, clip_cells), BF16),
            pltpu.VMEM((parts * cells // 8 + (quarter + 1) * quarter + 8, wide), F32),
            pltpu.VMEM((2, TAPS, width, wide), F32),
            pltpu.SemaphoreType.DMA((parts,)),
        ],
        compiler_params=pltpu.CompilerParams(vmem_limit_bytes=40 << 20),
    )(
        place, chip_at, core_at, half_at,
        *columns, *left_rows, left_panels, mixers, shift_picks, sort_picks,
    )
    return result.transpose(0, 1, 3, 2)


def solution(mesh):
    fsdp, replica, tm = (mesh.shape[axis] for axis in ("fsdp", "replica", "tm"))
    cores = 2 if replica % 2 == 0 else 1
    assert mesh.axis_names == ("fsdp", "replica", "tm")
    mesh = Mesh(
        mesh.devices.reshape(fsdp, replica // cores, cores, tm), ("fsdp", "chip", "core", "tm")
    )
    replica = ("chip", "core")
    in_specs = (
        P(replica, "tm", None, None, None),
        P(None, None, "fsdp"),
        P(None, "fsdp", None),
        P(replica, "tm", None, None, None),
        P(),
        P(None, "fsdp", None),
        P(None, "fsdp", (*replica, "tm")),
    )
    out_specs = P(None, None, "fsdp", (*replica, "tm"))
    return jax.shard_map(shards, mesh=mesh, in_specs=in_specs, out_specs=out_specs, check_vma=False)
```

```python
import functools

import jax
import jax.numpy as jnp
import numpy as np
from jax import lax
from jax.experimental import pallas as pl
from jax.experimental.pallas import tpu as pltpu
from jax.sharding import Mesh, PartitionSpec as P

TAPS = 27
F32, BF16 = jnp.float32, jnp.bfloat16
ROOM = 50 << 20
PROJECT_COST = 16 << 20
HIDDEN_COST = 200 << 20
NT = (((1,), (1,)), ((), ()))
VMEM = pl.BlockSpec(memory_space=pltpu.VMEM)
HBM = pl.BlockSpec(memory_space=pltpu.HBM)
SMEM = pl.BlockSpec(memory_space=pltpu.SMEM)
ANY = pl.BlockSpec(memory_space=pl.ANY)


def shifted(block, axis, distance):
    devices = range(lax.axis_size(axis))
    route = [(i - distance, i) for i in devices if i - distance in devices]
    return lax.ppermute(block, axis, route)


def dot(left, right):
    return jnp.dot(left, right, preferred_element_type=F32)


def dot_nt(left, right):
    return lax.dot_general(left, right, NT, preferred_element_type=F32)


def quotient(value, size):
    return value >> (size.bit_length() - 1) if size & (size - 1) == 0 else value // size


def remainder(value, size):
    return value & (size - 1) if size & (size - 1) == 0 else value % size


def halves(value):
    high = value.astype(BF16)
    return high, (value - high.astype(F32)).astype(BF16)


def patch_picks(side):
    half = side // 2
    even = np.zeros((1, 3, half, half, half, side), np.float32)
    odd = np.zeros((2, 3, half, half, half, side), np.float32)
    for c in range(3):
        for y in range(half):
            for x in range(half):
                column = 2 * x + c - 1
                if column < 0:
                    continue
                even[0, c, y, x, y, column] = 1
                if y > 0:
                    odd[0, c, y, x, y - 1, column] = 1
                odd[1, c, y, x, y, column] = 1
    return even.reshape(-1, half * side), odd.reshape(-1, half * side)


def spread_picks(half):
    quarter = half // 2
    picks = np.zeros((3, 3, half, half, quarter, quarter), np.float32)
    for b in range(3):
        for c in range(3):
            for out_y in range(quarter):
                for out_x in range(quarter):
                    y, x = 2 * out_y + b - 1, 2 * out_x + c - 1
                    if y >= 0 and x >= 0:
                        picks[b, c, y, x, out_y, out_x] = 1
    return picks.reshape(9 * half * half, quarter * quarter)


def patch_rows(even, odd, even_ref, odd_ref, half):
    cells = half * half
    even = dot(even_ref[...], even).astype(BF16)
    odd = dot(odd_ref[...], odd).astype(BF16)
    rows = [odd[at * cells : (at + 1) * cells] for at in range(6)]
    rows[3:3] = [even[at * cells : (at + 1) * cells] for at in range(3)]
    return rows


def project_kernel(
    x_any, left_any, grad_any, even_any, odd_any, first_any,
    out_ref, halo_ref, x_ref, left_ref, grad_ref, even_ref, odd_ref, first_ref, rows_ref, arrived,
):
    frames, half, _, side, channels = x_ref.shape
    order = [frame for time in (1, 0) for frame in range(time, frames, 2)]
    pairs_of = [
        (left_any.at[0], left_ref),
        (x_any.at[order[0]], x_ref.at[order[0]]),
        (x_any.at[order[1]], x_ref.at[order[1]]),
        (even_any, even_ref),
        (odd_any, odd_ref),
        (first_any.at[pl.ds(0, 9)], first_ref),
        (x_any.at[order[2]], x_ref.at[order[2]]),
        (x_any.at[order[3]], x_ref.at[order[3]]),
        (grad_any, grad_ref),
    ]
    copies = [
        pltpu.make_async_copy(source, target, arrived.at[at])
        for at, (source, target) in enumerate(pairs_of)
    ]
    for copy in copies:
        copy.start()
    wide = left_ref.shape[0]
    pairs = frames // 2
    size = pairs * half * side
    target = lax.broadcasted_iota(jnp.int32, (size, size), 0)
    source = lax.broadcasted_iota(jnp.int32, (size, size), 1)
    cells = size // 2
    wanted = 2 * remainder(target, cells) + quotient(target, cells)
    pick = jnp.where(source == wanted, 1.0, 0.0).astype(BF16)
    copies[0].wait()
    both = jnp.concatenate(halves(left_ref[...]), axis=0)

    def project(time):
        for row in range(2):
            block = jnp.concatenate(
                [
                    x_ref[frame, :, row].reshape(half * side, channels)
                    for frame in range(time, frames, 2)
                ],
                axis=0,
            )
            full = dot_nt(block, both)
            small = (full[:, :wide] + full[:, wide:]).astype(BF16)
            ordered = dot(pick, small).astype(BF16)
            at = (4 * time + 2 * row) * cells
            out_ref[at : at + size, :] = ordered

    copies[1].wait()
    copies[2].wait()
    project(1)
    copies[3].wait()
    copies[4].wait()
    lines = [x_ref[frames - 1, :, row].reshape(half * side, channels) for row in range(2)]
    rows = patch_rows(*lines, even_ref, odd_ref, half)
    copies[5].wait()
    total = dot(rows[0], first_ref[0])
    for tap in range(1, 9):
        total += dot(rows[tap], first_ref[tap])
    halo_ref[pl.ds(0, half * half), :] = total
    copies[6].wait()
    copies[7].wait()
    project(0)
    copies[8].wait()
    grad_rows = stacked_rows(grad_ref, rows_ref)
    count = grad_rows.shape[0]
    for block in range(channels // wide):
        at = 8 * cells + block * count
        out_ref[at : at + count, :] = grad_rows[:, block * wide : (block + 1) * wide]
        at = half * half + block * count
        halo_ref[at : at + count, :] = rows_ref[:, block * wide : (block + 1) * wide]


def stacked_rows(grad_ref, rows_ref):
    quarter = grad_ref.shape[0]
    for row in range(quarter):
        rows_ref[pl.ds(row * quarter, quarter), :] = grad_ref[row].astype(F32)
    return rows_ref[...].astype(BF16)


def transposed_products(rows, kernel, taps):
    total = dot_nt(rows[0], kernel[taps[0]])
    for at in range(1, len(taps)):
        total += dot_nt(rows[at], kernel[taps[at]])
    return total


def spread_rows(picks_ref, rows, cells):
    spread = dot(picks_ref[...], rows).astype(BF16)
    return [spread[tap * cells : (tap + 1) * cells] for tap in range(9)]


def hidden_kernel(
    tm_ref, x_ref, prior_ref, grad_ref, later_ref, even_ref, odd_ref, spread_ref,
    first_any, second_any, out_ref, rows_ref, patches, first, second, arrived, *, clip_parts,
):
    frames, half, _, side, channels = x_ref.shape
    cells = half * half
    has_prior = jnp.where(tm_ref[0] > 0, 1.0, 0.0)
    has_later = jnp.where(tm_ref[0] < clip_parts - 1, 1.0, 0.0)
    copies = {
        (at, a): pltpu.make_async_copy(
            source.at[pl.ds(9 * a, 9)], target.at[pl.ds(9 * a, 9)], arrived.at[at, a]
        )
        for at, (source, target) in enumerate(((second_any, second), (first_any, first)))
        for a in (1, 2, 0)
    }
    for copy in copies.values():
        copy.start()
    own_rows = stacked_rows(grad_ref, rows_ref)
    own = spread_rows(spread_ref, own_rows, cells)
    copies[0, 1].wait()
    early = transposed_products(own, second, range(9, 18))
    copies[0, 2].wait()
    late = transposed_products(own, second, range(18, 27))
    for frame in range(frames):
        lines = [x_ref[frame, :, row].reshape(half * side, channels) for row in range(2)]
        for tap, rows in enumerate(patch_rows(*lines, even_ref, odd_ref, half)):
            patches[frame, tap] = rows
    count = own_rows.shape[0]
    wide = first.shape[2]
    later_rows = jnp.concatenate(
        [
            later_ref[pl.ds(cells + count * block, count), :]
            for block in range(channels // wide)
        ],
        axis=1,
    )
    after = spread_rows(spread_ref, later_rows.astype(BF16), cells)
    copies[0, 0].wait()
    late += transposed_products(after, second, range(9)) * has_later
    hidden_grad = jnp.concatenate([early, late], axis=0)
    pre = jnp.zeros((2 * cells, wide), F32)
    for a in (1, 2):
        copies[1, a].wait()
        for tap in range(9):
            rows = jnp.concatenate([patches[a - 1, tap], patches[a + 1, tap]], axis=0)
            pre += dot(rows, first[9 * a + tap])
    copies[1, 0].wait()
    inner = dot(patches[1, 0], first[0])
    for tap in range(1, 9):
        inner += dot(patches[1, tap], first[tap])
    pre += jnp.concatenate([prior_ref[pl.ds(0, cells), :] * has_prior, inner], axis=0)
    sig = jax.nn.sigmoid(pre)
    hidden = (pre * sig).astype(BF16)
    pre_grad = (hidden_grad * sig * (1.0 + pre * (1.0 - sig))).astype(BF16)
    groups, slices, _, share, _ = out_ref.shape
    for at in range(slices):
        place = slice(at * share, (at + 1) * share)
        for group in range(groups):
            out_ref[group, at, 0] = pre_grad[place]
            out_ref[group, at, 1] = hidden[place]


def split_kernel(*refs):
    *right_refs, out_ref = refs
    slices, _, width, _ = right_refs[0].shape
    for distance in range(slices):
        for layer in range(2):
            right = jnp.concatenate([ref[distance, layer] for ref in right_refs], axis=0)
            out_ref[distance, layer] = jnp.concatenate(halves(right), axis=0)


def right_kernel(place_ref, acts_ref, right_ref, *out_refs):
    parts, slices = acts_ref.shape[:2]
    both = right_ref.shape[2] // 2
    width = both // len(out_refs)
    for layer in range(2):
        total = None
        for distance in range(slices):
            origin = lax.rem(place_ref[0] + (slices - distance), slices)
            rows = jnp.concatenate([acts_ref[part, origin, layer] for part in range(parts)], axis=0)
            term = dot_nt(right_ref[distance, layer], rows)
            total = term if total is None else total + term
        product = (total[:both] + total[both:]).astype(BF16)
        for at, out_ref in enumerate(out_refs):
            out_ref[pl.ds(layer * width, width), :] = product[at * width : (at + 1) * width]


def tables_kernel(after_any, mix_ref, shift_ref, sort_ref, mixers_ref, *, slices, clip_parts, half):
    del after_any
    size = shift_ref.shape[0]
    cells = size // clip_parts
    share = cells // slices
    frames = size // (half * half)
    held = lax.broadcasted_iota(jnp.int32, (size, size), 0)
    cell = lax.broadcasted_iota(jnp.int32, (size, size), 1)
    part = remainder(quotient(held, share), clip_parts)
    slot = quotient(held, share * clip_parts)
    natural = part * cells + slot * share + remainder(held, share)
    frame = quotient(cell, half * half)
    row = remainder(quotient(cell, half), half)
    column = remainder(cell, half)
    for shift in range(8):
        dt, dr, dc = shift // 4, shift // 2 % 2, shift % 2
        found = natural == cell + ((dt * half + dr) * half + dc)
        if dt:
            found &= frame < frames - 1
        if dr:
            found &= row < half - 1
        if dc:
            found &= column < half - 1
        shift_ref[:, pl.ds(shift * size, size)] = jnp.where(found, 1.0, 0.0).astype(BF16)
    quarter = half // 2
    outputs = size // 8
    kind = quotient(cell, outputs)
    frame = 2 * remainder(quotient(cell, quarter * quarter), frames // 2) + quotient(kind, 4)
    row = 2 * remainder(quotient(cell, quarter), quarter) + remainder(quotient(kind, 2), 2)
    column = 2 * remainder(cell, quarter) + remainder(kind, 2)
    found = natural == (frame * half + row) * half + column
    sort_ref[...] = jnp.where(found, 1.0, 0.0).astype(BF16)

    count = mixers_ref.shape[2]
    tap = lax.broadcasted_iota(jnp.int32, (count, TAPS), 1)
    line = lax.broadcasted_iota(jnp.int32, (count, TAPS), 0)
    spread = jnp.where(quotient(line, 8) == tap, 1.0, 0.0).astype(BF16)
    lines = lax.broadcasted_iota(jnp.int32, (count, count), 0)
    others = lax.broadcasted_iota(jnp.int32, (count, count), 1)
    same = remainder(lines, 8) == remainder(others, 8)
    for layer in range(2):
        for at, part in enumerate(halves(mix_ref[layer])):
            wider = dot_nt(dot(spread, part).astype(BF16), spread)
            mixers_ref[layer, at] = jnp.where(same, wider, 0.0).astype(BF16)


def update_kernel(
    place_ref, chip_ref, core_ref, tm_ref, *refs, slices, cores, clip_parts, half
):
    columns_refs, piece_refs = refs[: slices * cores], refs[slices * cores : (slices + 1) * cores]
    (
        left_ref, mixers_ref, shift_ref, sort_ref,
        out_ref, left_rows_ref, columns, shifts, grads, raw, arrived,
    ) = refs[(slices + 1) * cores :]
    parts = left_rows_ref.shape[0]
    chips = parts // (cores * clip_parts)
    copies = []
    for cross, piece_ref in enumerate(piece_refs):
        core = (core_ref[0] + cross) % cores
        for at, (step, turn) in enumerate(np.ndindex(chips, clip_parts)):
            chip = lax.rem(chip_ref[0] + (chips - step), chips)
            place = lax.rem(tm_ref[0] + (clip_parts - turn), clip_parts)
            target = left_rows_ref.at[(chip * cores + core) * clip_parts + place]
            copies.append(
                pltpu.make_async_copy(piece_ref.at[at], target, arrived.at[len(copies)])
            )
    for copy in copies:
        copy.start()
    for cross, distance in np.ndindex(cores, slices):
        origin = lax.rem(place_ref[0] + (slices - distance), slices)
        core = (core_ref[0] + cross) % cores
        columns[origin, core] = columns_refs[cross * slices + distance][...]
    wide, channels = left_ref.shape[1:]
    width = columns.shape[2] // 2
    clips = parts // clip_parts
    share = columns.shape[3] // chips
    clip_cells = slices * share
    cells = clip_cells // clip_parts
    frames = clip_cells // (half * half)
    outputs = clip_cells // 8

    def by_clip(layer):
        return jnp.concatenate(
            [
                jnp.concatenate(
                    [
                        columns[
                            at, clip % cores, pl.ds(layer * width, width),
                            pl.ds(clip // cores * share, share),
                        ]
                        for at in range(slices)
                    ],
                    axis=1,
                )
                for clip in range(clips)
            ],
            axis=0,
        )

    first = by_clip(0)
    for shift in range(8):
        moved = dot(first, shift_ref[:, pl.ds(shift * clip_cells, clip_cells)]).astype(BF16)
        for clip in range(clips):
            shifts[shift, clip] = moved[clip * width : (clip + 1) * width]
    second = dot(by_clip(1), sort_ref[...]).astype(BF16)

    for copy in copies:
        copy.wait()
    own_outputs = outputs // clip_parts
    blocks = channels // wide
    out_grad = jnp.concatenate(
        [
            jnp.concatenate(
                [
                    left_rows_ref[part, pl.ds(8 * cells + own_outputs * at, own_outputs), :]
                    for at in range(blocks)
                ],
                axis=1,
            )
            for part in range(parts)
        ],
        axis=0,
    )
    full = dot_nt(out_grad, jnp.concatenate(halves(left_ref[1]), axis=0))
    total = parts * own_outputs
    quarter = half // 2
    grads[pl.ds(0, total), :] = full[:, :wide] + full[:, wide:]
    places = lax.broadcasted_iota(jnp.int32, (total, wide), 0)
    frame = remainder(quotient(places, quarter * quarter), frames // 2)
    row = remainder(quotient(places, quarter), quarter)
    column = remainder(places, quarter)
    second_rows = []
    for shift in range(8):
        dt, dr, dc = shift // 4, shift // 2 % 2, shift % 2
        moved = grads[pl.ds((dt * quarter + dr) * quarter + dc, total), :]
        inside = (frame + dt < frames // 2) & (row + dr < quarter) & (column + dc < quarter)
        second_rows.append(jnp.where(inside, moved, 0.0).astype(BF16))

    for time, line in np.ndindex(2, 2):
        even = [
            (9 * a + 3 * b + 1, 4 * (a == 0) + 2 * (b == 0))
            for a in ((0, 2) if time else (1,))
            for b in ((0, 2) if line else (1,))
        ]
        odd = [(tap + 1, shift) for tap, shift in even] + [
            (tap - 1, shift + 1) for tap, shift in even
        ]
        kind = 4 * time + 2 * line
        sums = None
        for clip in range(clips):
            left = jnp.concatenate([shifts[shift, clip] for _, shift in odd], axis=0)
            rows = jnp.concatenate(
                [
                    jnp.concatenate(
                        [
                            left_rows_ref[
                                clip * clip_parts + part, pl.ds((kind + at) * cells, cells), :
                            ]
                            for part in range(clip_parts)
                        ],
                        axis=0,
                    )
                    for at in range(2)
                ],
                axis=1,
            )
            term = dot(left, rows)
            sums = term if sums is None else sums + term
        for at, (tap, _) in enumerate(even):
            raw[0, tap] = sums[at * width : (at + 1) * width, :wide]
        for at, (tap, _) in enumerate(odd):
            raw[0, tap] = sums[at * width : (at + 1) * width, wide:]
        for place, taps in enumerate((even, odd)):
            chosen = jnp.concatenate(
                [
                    second[
                        clip * width : (clip + 1) * width,
                        (kind + place) * outputs : (kind + place + 1) * outputs,
                    ]
                    for clip in range(clips)
                ],
                axis=1,
            )
            products = dot(
                chosen, jnp.concatenate([second_rows[shift] for _, shift in taps], axis=1)
            )
            for at, (tap, _) in enumerate(taps):
                raw[1, tap] = products[:, at * wide : (at + 1) * wide]

    for layer in range(2):
        for group in range(width // 16):
            lanes = jnp.concatenate(
                [
                    raw[layer, :, pl.ds(16 * group + 8 * at, 8), :].reshape(8 * TAPS, wide)
                    for at in range(2)
                ],
                axis=1,
            )
            high, low = halves(lanes)
            mixed = (
                dot(mixers_ref[layer, 0], high)
                + dot(mixers_ref[layer, 0], low)
                + dot(mixers_ref[layer, 1], high)
            )
            rows = jnp.concatenate(
                [
                    mixed[:, at * wide : (at + 1) * wide].reshape(TAPS, 8, wide)
                    for at in range(2)
                ],
                axis=1,
            )
            out_ref[layer, :, pl.ds(16 * group, 16), :] = rows.astype(BF16)


def turned(block, axes, steps):
    sizes = [lax.axis_size(axis) for axis in axes]
    if not any(step % size for step, size in zip(steps, sizes)):
        return block
    route = []
    for place in np.ndindex(*sizes):
        target = [(at + step) % size for at, step, size in zip(place, steps, sizes)]
        route.append(
            (int(np.ravel_multi_index(place, sizes)), int(np.ravel_multi_index(target, sizes)))
        )
    return lax.ppermute(block, axes, route)


def shards(clip_input, first_kernel, second_kernel, out_grad, tap_mix, left_panels, right_panels):
    clips, frames, side, _, channels = clip_input.shape
    wide = first_kernel.shape[2]
    width = right_panels.shape[2]
    half, quarter = side // 2, side // 4
    half_frames = frames // 2
    cells = half_frames * half * half
    clip_parts = lax.axis_size("tm")
    cores, chips = lax.axis_size("core"), lax.axis_size("chip")
    equals = chips * clip_parts
    parts = equals * cores
    slices = lax.axis_size("fsdp")
    share = cells // slices
    assert clips == 1 and frames == 4
    x = clip_input.reshape(frames, half, 2, side, channels)
    grad = out_grad.reshape(quarter, quarter, channels)
    place, chip_at, core_at, half_at = (
        lax.axis_index(axis).reshape(1) for axis in ("fsdp", "chip", "core", "tm")
    )

    even, odd = (jnp.asarray(picks, BF16) for picks in patch_picks(side))
    rows = quarter * quarter * channels // wide
    projected, halo = pl.pallas_call(
        project_kernel,
        out_shape=(
            jax.ShapeDtypeStruct((8 * cells + rows, wide), BF16),
            jax.ShapeDtypeStruct((half * half + rows, wide), F32),
        ),
        in_specs=[ANY] * 6,
        out_specs=(VMEM, VMEM),
        scratch_shapes=[
            pltpu.VMEM(x.shape, BF16),
            pltpu.VMEM(left_panels.shape[1:], F32),
            pltpu.VMEM(grad.shape, BF16),
            pltpu.VMEM(even.shape, BF16),
            pltpu.VMEM(odd.shape, BF16),
            pltpu.VMEM((9,) + first_kernel.shape[1:], BF16),
            pltpu.VMEM((quarter * quarter, channels), F32),
            pltpu.SemaphoreType.DMA((9,)),
        ],
        compiler_params=pltpu.CompilerParams(vmem_limit_bytes=58 << 20),
        cost_estimate=pl.CostEstimate(
            flops=4 * frames * side * side * channels * wide,
            bytes_accessed=PROJECT_COST,
            transcendentals=0,
        ),
    )(x, left_panels, grad, even, odd, first_kernel)
    if clip_parts == 2:
        prior = later = lax.ppermute(halo, "tm", [(0, 1), (1, 0)])
    else:
        prior, later = shifted(halo, "tm", 1), shifted(halo, "tm", -1)
    right = right_panels.transpose(0, 2, 1)
    right = [turned(right, ("fsdp",), (distance,)) for distance in range(slices)]
    projected, prior, later, right = lax.optimization_barrier((projected, prior, later, right))
    right = jnp.stack(right)
    rights = [turned(right, ("core",), (cross,)) for cross in range(cores)]
    held = jnp.stack(
        [
            turned(projected, ("chip", "tm"), steps)
            for steps in np.ndindex(chips, clip_parts)
        ]
    )

    spread = jnp.asarray(spread_picks(half), BF16)
    acts = pl.pallas_call(
        functools.partial(hidden_kernel, clip_parts=clip_parts),
        out_shape=jax.ShapeDtypeStruct((equals, slices, 2, share, wide), BF16),
        in_specs=[SMEM] + [VMEM] * 7 + [HBM] * 2,
        out_specs=VMEM,
        scratch_shapes=[
            pltpu.VMEM((quarter * quarter, channels), F32),
            pltpu.VMEM((frames, 9, half * half, channels), BF16),
            pltpu.VMEM(first_kernel.shape, BF16),
            pltpu.VMEM(second_kernel.shape, BF16),
            pltpu.SemaphoreType.DMA((2, 3)),
        ],
        compiler_params=pltpu.CompilerParams(vmem_limit_bytes=ROOM),
        cost_estimate=pl.CostEstimate(
            flops=3 * cells * TAPS * channels * wide,
            bytes_accessed=HIDDEN_COST,
            transcendentals=cells * wide,
        ),
    )(
        half_at, x, prior, grad, later, even, odd, spread, first_kernel, second_kernel,
    )
    acts, *rights = lax.optimization_barrier((acts, *rights))
    right = pl.pallas_call(
        split_kernel,
        out_shape=jax.ShapeDtypeStruct((slices, 2, 2 * cores * width, wide), BF16),
        in_specs=[VMEM] * cores,
        out_specs=VMEM,
        compiler_params=pltpu.CompilerParams(vmem_limit_bytes=16 << 20),
        cost_estimate=pl.CostEstimate(flops=0, bytes_accessed=1 << 20, transcendentals=0),
    )(*rights)
    clip_cells = clip_parts * cells
    shift_picks, sort_picks, mixers = pl.pallas_call(
        functools.partial(tables_kernel, slices=slices, clip_parts=clip_parts, half=half),
        out_shape=(
            jax.ShapeDtypeStruct((clip_cells, 8 * clip_cells), BF16),
            jax.ShapeDtypeStruct((clip_cells, clip_cells), BF16),
            jax.ShapeDtypeStruct((2, 2, 8 * TAPS, 8 * TAPS), BF16),
        ),
        in_specs=[ANY, VMEM],
        out_specs=(VMEM,) * 3,
        compiler_params=pltpu.CompilerParams(vmem_limit_bytes=16 << 20),
        cost_estimate=pl.CostEstimate(flops=0, bytes_accessed=4 << 20, transcendentals=0),
    )(acts, tap_mix)
    every = lax.all_to_all(
        acts.reshape(equals * slices, 2, share, wide), ("chip", "tm", "fsdp"), 0, 0, tiled=True
    ).reshape(equals, slices, 2, share, wide)
    columns = pl.pallas_call(
        right_kernel,
        out_shape=(jax.ShapeDtypeStruct((2 * width, equals * share), BF16),) * cores,
        in_specs=[SMEM] + [VMEM] * 2,
        out_specs=(VMEM,) * cores,
        compiler_params=pltpu.CompilerParams(vmem_limit_bytes=16 << 20),
    )(place, every, right)
    *columns, held = lax.optimization_barrier((*columns, held))
    columns = [
        turned(columns[cross], ("fsdp", "core"), (distance, cross))
        for cross, distance in np.ndindex(cores, slices)
    ]
    left_rows = [turned(held, ("core",), (cross,)) for cross in range(cores)]

    result = pl.pallas_call(
        functools.partial(
            update_kernel, slices=slices, cores=cores, clip_parts=clip_parts, half=half
        ),
        out_shape=jax.ShapeDtypeStruct((2, TAPS, width, wide), BF16),
        in_specs=[SMEM] * 4
        + [VMEM] * len(columns)
        + [ANY] * cores
        + [VMEM] * 4,
        out_specs=VMEM,
        scratch_shapes=[
            pltpu.VMEM((parts,) + projected.shape, BF16),
            pltpu.VMEM((slices, cores, 2 * width, equals * share), BF16),
            pltpu.VMEM((8, parts // clip_parts, width, clip_cells), BF16),
            pltpu.VMEM((parts * cells // 8 + (quarter + 1) * quarter + 8, wide), F32),
            pltpu.VMEM((2, TAPS, width, wide), F32),
            pltpu.SemaphoreType.DMA((parts,)),
        ],
        compiler_params=pltpu.CompilerParams(vmem_limit_bytes=40 << 20),
    )(
        place, chip_at, core_at, half_at,
        *columns, *left_rows, left_panels, mixers, shift_picks, sort_picks,
    )
    return result.transpose(0, 1, 3, 2)


def solution(mesh):
    fsdp, replica, tm = (mesh.shape[axis] for axis in ("fsdp", "replica", "tm"))
    cores = 2 if replica % 2 == 0 else 1
    assert mesh.axis_names == ("fsdp", "replica", "tm")
    mesh = Mesh(
        mesh.devices.reshape(fsdp, replica // cores, cores, tm), ("fsdp", "chip", "core", "tm")
    )
    replica = ("chip", "core")
    in_specs = (
        P(replica, "tm", None, None, None),
        P(None, None, "fsdp"),
        P(None, "fsdp", None),
        P(replica, "tm", None, None, None),
        P(),
        P(None, "fsdp", None),
        P(None, "fsdp", (*replica, "tm")),
    )
    out_specs = P(None, None, "fsdp", (*replica, "tm"))
    return jax.shard_map(shards, mesh=mesh, in_specs=in_specs, out_specs=out_specs, check_vma=False)
```

```python
import functools

import jax
import jax.numpy as jnp
import numpy as np
from jax import lax
from jax.experimental import pallas as pl
from jax.experimental.pallas import tpu as pltpu
from jax.sharding import Mesh, PartitionSpec as P

TAPS = 27
F32, BF16 = jnp.float32, jnp.bfloat16
ROOM = 50 << 20
PROJECT_COST = 16 << 20
HIDDEN_COST = 200 << 20
NT = (((1,), (1,)), ((), ()))
VMEM = pl.BlockSpec(memory_space=pltpu.VMEM)
HBM = pl.BlockSpec(memory_space=pltpu.HBM)
SMEM = pl.BlockSpec(memory_space=pltpu.SMEM)
ANY = pl.BlockSpec(memory_space=pl.ANY)


def shifted(block, axis, distance):
    devices = range(lax.axis_size(axis))
    route = [(i - distance, i) for i in devices if i - distance in devices]
    return lax.ppermute(block, axis, route)


def dot(left, right):
    return jnp.dot(left, right, preferred_element_type=F32)


def dot_nt(left, right):
    return lax.dot_general(left, right, NT, preferred_element_type=F32)


def quotient(value, size):
    return value >> (size.bit_length() - 1) if size & (size - 1) == 0 else value // size


def remainder(value, size):
    return value & (size - 1) if size & (size - 1) == 0 else value % size


def halves(value):
    high = value.astype(BF16)
    return high, (value - high.astype(F32)).astype(BF16)


def patch_picks(side):
    half = side // 2
    even = np.zeros((1, 3, half, half, half, side), np.float32)
    odd = np.zeros((2, 3, half, half, half, side), np.float32)
    for c in range(3):
        for y in range(half):
            for x in range(half):
                column = 2 * x + c - 1
                if column < 0:
                    continue
                even[0, c, y, x, y, column] = 1
                if y > 0:
                    odd[0, c, y, x, y - 1, column] = 1
                odd[1, c, y, x, y, column] = 1
    return even.reshape(-1, half * side), odd.reshape(-1, half * side)


def spread_picks(half):
    quarter = half // 2
    picks = np.zeros((3, 3, half, half, quarter, quarter), np.float32)
    for b in range(3):
        for c in range(3):
            for out_y in range(quarter):
                for out_x in range(quarter):
                    y, x = 2 * out_y + b - 1, 2 * out_x + c - 1
                    if y >= 0 and x >= 0:
                        picks[b, c, y, x, out_y, out_x] = 1
    return picks.reshape(9 * half * half, quarter * quarter)


def patch_rows(even, odd, even_ref, odd_ref, half):
    cells = half * half
    even = dot(even_ref[...], even).astype(BF16)
    odd = dot(odd_ref[...], odd).astype(BF16)
    rows = [odd[at * cells : (at + 1) * cells] for at in range(6)]
    rows[3:3] = [even[at * cells : (at + 1) * cells] for at in range(3)]
    return rows


def project_kernel(
    x_any, left_any, grad_any, even_any, odd_any, first_any,
    out_ref, halo_ref, x_ref, left_ref, grad_ref, even_ref, odd_ref, first_ref, rows_ref, arrived,
):
    frames, half, _, side, channels = x_ref.shape
    order = [frame for time in (1, 0) for frame in range(time, frames, 2)]
    pairs_of = [
        (left_any.at[0], left_ref),
        (x_any.at[order[0]], x_ref.at[order[0]]),
        (x_any.at[order[1]], x_ref.at[order[1]]),
        (even_any, even_ref),
        (odd_any, odd_ref),
        (first_any.at[pl.ds(0, 9)], first_ref),
        (x_any.at[order[2]], x_ref.at[order[2]]),
        (x_any.at[order[3]], x_ref.at[order[3]]),
        (grad_any, grad_ref),
    ]
    copies = [
        pltpu.make_async_copy(source, target, arrived.at[at])
        for at, (source, target) in enumerate(pairs_of)
    ]
    for copy in copies:
        copy.start()
    wide = left_ref.shape[0]
    pairs = frames // 2
    size = pairs * half * side
    target = lax.broadcasted_iota(jnp.int32, (size, size), 0)
    source = lax.broadcasted_iota(jnp.int32, (size, size), 1)
    cells = size // 2
    wanted = 2 * remainder(target, cells) + quotient(target, cells)
    pick = jnp.where(source == wanted, 1.0, 0.0).astype(BF16)
    copies[0].wait()
    both = jnp.concatenate(halves(left_ref[...]), axis=0)

    def project(time):
        for row in range(2):
            block = jnp.concatenate(
                [
                    x_ref[frame, :, row].reshape(half * side, channels)
                    for frame in range(time, frames, 2)
                ],
                axis=0,
            )
            full = dot_nt(block, both)
            small = (full[:, :wide] + full[:, wide:]).astype(BF16)
            ordered = dot(pick, small).astype(BF16)
            at = (4 * time + 2 * row) * cells
            out_ref[at : at + size, :] = ordered

    copies[1].wait()
    copies[2].wait()
    project(1)
    copies[3].wait()
    copies[4].wait()
    lines = [x_ref[frames - 1, :, row].reshape(half * side, channels) for row in range(2)]
    rows = patch_rows(*lines, even_ref, odd_ref, half)
    copies[5].wait()
    total = dot(rows[0], first_ref[0])
    for tap in range(1, 9):
        total += dot(rows[tap], first_ref[tap])
    halo_ref[pl.ds(0, half * half), :] = total
    copies[6].wait()
    copies[7].wait()
    project(0)
    copies[8].wait()
    grad_rows = stacked_rows(grad_ref, rows_ref)
    count = grad_rows.shape[0]
    for block in range(channels // wide):
        at = 8 * cells + block * count
        out_ref[at : at + count, :] = grad_rows[:, block * wide : (block + 1) * wide]
        at = half * half + block * count
        halo_ref[at : at + count, :] = rows_ref[:, block * wide : (block + 1) * wide]


def stacked_rows(grad_ref, rows_ref):
    quarter = grad_ref.shape[0]
    for row in range(quarter):
        rows_ref[pl.ds(row * quarter, quarter), :] = grad_ref[row].astype(F32)
    return rows_ref[...].astype(BF16)


def transposed_products(rows, kernel, taps):
    total = dot_nt(rows[0], kernel[taps[0]])
    for at in range(1, len(taps)):
        total += dot_nt(rows[at], kernel[taps[at]])
    return total


def spread_rows(picks_ref, rows, cells):
    spread = dot(picks_ref[...], rows).astype(BF16)
    return [spread[tap * cells : (tap + 1) * cells] for tap in range(9)]


def hidden_kernel(
    tm_ref, x_ref, prior_ref, grad_ref, later_ref, even_ref, odd_ref, spread_ref,
    first_any, second_any, out_ref, rows_ref, patches, first, second, arrived, *, clip_parts,
):
    frames, half, _, side, channels = x_ref.shape
    cells = half * half
    has_prior = jnp.where(tm_ref[0] > 0, 1.0, 0.0)
    has_later = jnp.where(tm_ref[0] < clip_parts - 1, 1.0, 0.0)
    copies = {
        (at, a): pltpu.make_async_copy(
            source.at[pl.ds(9 * a, 9)], target.at[pl.ds(9 * a, 9)], arrived.at[at, a]
        )
        for at, (source, target) in enumerate(((second_any, second), (first_any, first)))
        for a in (1, 2, 0)
    }
    for copy in copies.values():
        copy.start()
    own_rows = stacked_rows(grad_ref, rows_ref)
    own = spread_rows(spread_ref, own_rows, cells)
    copies[0, 1].wait()
    early = transposed_products(own, second, range(9, 18))
    copies[0, 2].wait()
    late = transposed_products(own, second, range(18, 27))
    for frame in range(frames):
        lines = [x_ref[frame, :, row].reshape(half * side, channels) for row in range(2)]
        for tap, rows in enumerate(patch_rows(*lines, even_ref, odd_ref, half)):
            patches[frame, tap] = rows
    count = own_rows.shape[0]
    wide = first.shape[2]
    later_rows = jnp.concatenate(
        [
            later_ref[pl.ds(cells + count * block, count), :]
            for block in range(channels // wide)
        ],
        axis=1,
    )
    after = spread_rows(spread_ref, later_rows.astype(BF16), cells)
    copies[0, 0].wait()
    late += transposed_products(after, second, range(9)) * has_later
    hidden_grad = jnp.concatenate([early, late], axis=0)
    pre = jnp.zeros((2 * cells, wide), F32)
    for a in (1, 2):
        copies[1, a].wait()
        for tap in range(9):
            rows = jnp.concatenate([patches[a - 1, tap], patches[a + 1, tap]], axis=0)
            pre += dot(rows, first[9 * a + tap])
    copies[1, 0].wait()
    inner = dot(patches[1, 0], first[0])
    for tap in range(1, 9):
        inner += dot(patches[1, tap], first[tap])
    pre += jnp.concatenate([prior_ref[pl.ds(0, cells), :] * has_prior, inner], axis=0)
    sig = jax.nn.sigmoid(pre)
    hidden = (pre * sig).astype(BF16)
    pre_grad = (hidden_grad * sig * (1.0 + pre * (1.0 - sig))).astype(BF16)
    groups, slices, _, share, _ = out_ref.shape
    for at in range(slices):
        place = slice(at * share, (at + 1) * share)
        for group in range(groups):
            out_ref[group, at, 0] = pre_grad[place]
            out_ref[group, at, 1] = hidden[place]


def split_kernel(*refs):
    *right_refs, out_ref = refs
    slices, _, width, _ = right_refs[0].shape
    for distance in range(slices):
        for layer in range(2):
            right = jnp.concatenate([ref[distance, layer] for ref in right_refs], axis=0)
            out_ref[distance, layer] = jnp.concatenate(halves(right), axis=0)


def right_kernel(place_ref, core_ref, acts_ref, right_ref, out_ref):
    parts, slices = acts_ref.shape[:2]
    cores = out_ref.shape[1]
    both = right_ref.shape[2] // 2
    width = both // cores
    for layer in range(2):
        total = None
        for distance in range(slices):
            origin = lax.rem(place_ref[0] + (slices - distance), slices)
            rows = jnp.concatenate([acts_ref[part, origin, layer] for part in range(parts)], axis=0)
            term = dot_nt(right_ref[distance, layer], rows)
            total = term if total is None else total + term
        product = (total[:both] + total[both:]).astype(BF16)
        for cross in range(cores):
            core = lax.rem(core_ref[0] + cross, cores)
            for at in range(slices):
                out_ref[at, core, pl.ds(layer * width, width), :] = product[
                    cross * width : (cross + 1) * width
                ]


def tables_kernel(after_any, mix_ref, shift_ref, sort_ref, mixers_ref, *, slices, clip_parts, half):
    del after_any
    size = shift_ref.shape[0]
    cells = size // clip_parts
    share = cells // slices
    frames = size // (half * half)
    held = lax.broadcasted_iota(jnp.int32, (size, size), 0)
    cell = lax.broadcasted_iota(jnp.int32, (size, size), 1)
    part = remainder(quotient(held, share), clip_parts)
    slot = quotient(held, share * clip_parts)
    natural = part * cells + slot * share + remainder(held, share)
    frame = quotient(cell, half * half)
    row = remainder(quotient(cell, half), half)
    column = remainder(cell, half)
    for shift in range(8):
        dt, dr, dc = shift // 4, shift // 2 % 2, shift % 2
        found = natural == cell + ((dt * half + dr) * half + dc)
        if dt:
            found &= frame < frames - 1
        if dr:
            found &= row < half - 1
        if dc:
            found &= column < half - 1
        shift_ref[:, pl.ds(shift * size, size)] = jnp.where(found, 1.0, 0.0).astype(BF16)
    quarter = half // 2
    outputs = size // 8
    kind = quotient(cell, outputs)
    frame = 2 * remainder(quotient(cell, quarter * quarter), frames // 2) + quotient(kind, 4)
    row = 2 * remainder(quotient(cell, quarter), quarter) + remainder(quotient(kind, 2), 2)
    column = 2 * remainder(cell, quarter) + remainder(kind, 2)
    found = natural == (frame * half + row) * half + column
    sort_ref[...] = jnp.where(found, 1.0, 0.0).astype(BF16)

    count = mixers_ref.shape[2]
    tap = lax.broadcasted_iota(jnp.int32, (count, TAPS), 1)
    line = lax.broadcasted_iota(jnp.int32, (count, TAPS), 0)
    spread = jnp.where(quotient(line, 8) == tap, 1.0, 0.0).astype(BF16)
    lines = lax.broadcasted_iota(jnp.int32, (count, count), 0)
    others = lax.broadcasted_iota(jnp.int32, (count, count), 1)
    same = remainder(lines, 8) == remainder(others, 8)
    for layer in range(2):
        for at, part in enumerate(halves(mix_ref[layer])):
            wider = dot_nt(dot(spread, part).astype(BF16), spread)
            mixers_ref[layer, at] = jnp.where(same, wider, 0.0).astype(BF16)


def update_kernel(
    chip_ref, core_ref, tm_ref, columns, *refs, clip_parts, half
):
    slices, cores = columns.shape[:2]
    piece_refs = refs[:cores]
    (
        left_ref, mixers_ref, shift_ref, sort_ref,
        out_ref, left_rows_ref, shifts, grads, raw, arrived,
    ) = refs[cores:]
    parts = left_rows_ref.shape[0]
    chips = parts // (cores * clip_parts)
    copies = []
    for cross, piece_ref in enumerate(piece_refs):
        core = (core_ref[0] + cross) % cores
        for at, (step, turn) in enumerate(np.ndindex(chips, clip_parts)):
            chip = lax.rem(chip_ref[0] + (chips - step), chips)
            place = lax.rem(tm_ref[0] + (clip_parts - turn), clip_parts)
            target = left_rows_ref.at[(chip * cores + core) * clip_parts + place]
            copies.append(
                pltpu.make_async_copy(piece_ref.at[at], target, arrived.at[len(copies)])
            )
    for copy in copies:
        copy.start()
    wide, channels = left_ref.shape[1:]
    width = columns.shape[2] // 2
    clips = parts // clip_parts
    share = columns.shape[3] // chips
    clip_cells = slices * share
    cells = clip_cells // clip_parts
    frames = clip_cells // (half * half)
    outputs = clip_cells // 8

    def by_clip(layer):
        return jnp.concatenate(
            [
                jnp.concatenate(
                    [
                        columns[
                            at, clip % cores, pl.ds(layer * width, width),
                            pl.ds(clip // cores * share, share),
                        ]
                        for at in range(slices)
                    ],
                    axis=1,
                )
                for clip in range(clips)
            ],
            axis=0,
        )

    first = by_clip(0)
    for shift in range(8):
        moved = dot(first, shift_ref[:, pl.ds(shift * clip_cells, clip_cells)]).astype(BF16)
        for clip in range(clips):
            shifts[shift, clip] = moved[clip * width : (clip + 1) * width]
    second = dot(by_clip(1), sort_ref[...]).astype(BF16)

    for copy in copies:
        copy.wait()
    own_outputs = outputs // clip_parts
    blocks = channels // wide
    out_grad = jnp.concatenate(
        [
            jnp.concatenate(
                [
                    left_rows_ref[part, pl.ds(8 * cells + own_outputs * at, own_outputs), :]
                    for at in range(blocks)
                ],
                axis=1,
            )
            for part in range(parts)
        ],
        axis=0,
    )
    full = dot_nt(out_grad, jnp.concatenate(halves(left_ref[1]), axis=0))
    total = parts * own_outputs
    quarter = half // 2
    grads[pl.ds(0, total), :] = full[:, :wide] + full[:, wide:]
    places = lax.broadcasted_iota(jnp.int32, (total, wide), 0)
    frame = remainder(quotient(places, quarter * quarter), frames // 2)
    row = remainder(quotient(places, quarter), quarter)
    column = remainder(places, quarter)
    second_rows = []
    for shift in range(8):
        dt, dr, dc = shift // 4, shift // 2 % 2, shift % 2
        moved = grads[pl.ds((dt * quarter + dr) * quarter + dc, total), :]
        inside = (frame + dt < frames // 2) & (row + dr < quarter) & (column + dc < quarter)
        second_rows.append(jnp.where(inside, moved, 0.0).astype(BF16))

    for time, line in np.ndindex(2, 2):
        even = [
            (9 * a + 3 * b + 1, 4 * (a == 0) + 2 * (b == 0))
            for a in ((0, 2) if time else (1,))
            for b in ((0, 2) if line else (1,))
        ]
        odd = [(tap + 1, shift) for tap, shift in even] + [
            (tap - 1, shift + 1) for tap, shift in even
        ]
        kind = 4 * time + 2 * line
        sums = None
        for clip in range(clips):
            left = jnp.concatenate([shifts[shift, clip] for _, shift in odd], axis=0)
            rows = jnp.concatenate(
                [
                    jnp.concatenate(
                        [
                            left_rows_ref[
                                clip * clip_parts + part, pl.ds((kind + at) * cells, cells), :
                            ]
                            for part in range(clip_parts)
                        ],
                        axis=0,
                    )
                    for at in range(2)
                ],
                axis=1,
            )
            term = dot(left, rows)
            sums = term if sums is None else sums + term
        for at, (tap, _) in enumerate(even):
            raw[0, tap] = sums[at * width : (at + 1) * width, :wide]
        for at, (tap, _) in enumerate(odd):
            raw[0, tap] = sums[at * width : (at + 1) * width, wide:]
        for place, taps in enumerate((even, odd)):
            chosen = jnp.concatenate(
                [
                    second[
                        clip * width : (clip + 1) * width,
                        (kind + place) * outputs : (kind + place + 1) * outputs,
                    ]
                    for clip in range(clips)
                ],
                axis=1,
            )
            products = dot(
                chosen, jnp.concatenate([second_rows[shift] for _, shift in taps], axis=1)
            )
            for at, (tap, _) in enumerate(taps):
                raw[1, tap] = products[:, at * wide : (at + 1) * wide]

    for layer in range(2):
        for group in range(width // 16):
            lanes = jnp.concatenate(
                [
                    raw[layer, :, pl.ds(16 * group + 8 * at, 8), :].reshape(8 * TAPS, wide)
                    for at in range(2)
                ],
                axis=1,
            )
            high, low = halves(lanes)
            mixed = (
                dot(mixers_ref[layer, 0], high)
                + dot(mixers_ref[layer, 0], low)
                + dot(mixers_ref[layer, 1], high)
            )
            rows = jnp.concatenate(
                [
                    mixed[:, at * wide : (at + 1) * wide].reshape(TAPS, 8, wide)
                    for at in range(2)
                ],
                axis=1,
            )
            out_ref[layer, :, pl.ds(16 * group, 16), :] = rows.astype(BF16)


def turned(block, axes, steps):
    sizes = [lax.axis_size(axis) for axis in axes]
    if not any(step % size for step, size in zip(steps, sizes)):
        return block
    route = []
    for place in np.ndindex(*sizes):
        target = [(at + step) % size for at, step, size in zip(place, steps, sizes)]
        route.append(
            (int(np.ravel_multi_index(place, sizes)), int(np.ravel_multi_index(target, sizes)))
        )
    return lax.ppermute(block, axes, route)


def shards(clip_input, first_kernel, second_kernel, out_grad, tap_mix, left_panels, right_panels):
    clips, frames, side, _, channels = clip_input.shape
    wide = first_kernel.shape[2]
    width = right_panels.shape[2]
    half, quarter = side // 2, side // 4
    half_frames = frames // 2
    cells = half_frames * half * half
    clip_parts = lax.axis_size("tm")
    cores, chips = lax.axis_size("core"), lax.axis_size("chip")
    equals = chips * clip_parts
    parts = equals * cores
    slices = lax.axis_size("fsdp")
    share = cells // slices
    assert clips == 1 and frames == 4
    x = clip_input.reshape(frames, half, 2, side, channels)
    grad = out_grad.reshape(quarter, quarter, channels)
    place, chip_at, core_at, half_at = (
        lax.axis_index(axis).reshape(1) for axis in ("fsdp", "chip", "core", "tm")
    )

    even, odd = (jnp.asarray(picks, BF16) for picks in patch_picks(side))
    rows = quarter * quarter * channels // wide
    projected, halo = pl.pallas_call(
        project_kernel,
        out_shape=(
            jax.ShapeDtypeStruct((8 * cells + rows, wide), BF16),
            jax.ShapeDtypeStruct((half * half + rows, wide), F32),
        ),
        in_specs=[ANY] * 6,
        out_specs=(VMEM, VMEM),
        scratch_shapes=[
            pltpu.VMEM(x.shape, BF16),
            pltpu.VMEM(left_panels.shape[1:], F32),
            pltpu.VMEM(grad.shape, BF16),
            pltpu.VMEM(even.shape, BF16),
            pltpu.VMEM(odd.shape, BF16),
            pltpu.VMEM((9,) + first_kernel.shape[1:], BF16),
            pltpu.VMEM((quarter * quarter, channels), F32),
            pltpu.SemaphoreType.DMA((9,)),
        ],
        compiler_params=pltpu.CompilerParams(vmem_limit_bytes=58 << 20),
        cost_estimate=pl.CostEstimate(
            flops=4 * frames * side * side * channels * wide,
            bytes_accessed=PROJECT_COST,
            transcendentals=0,
        ),
    )(x, left_panels, grad, even, odd, first_kernel)
    if clip_parts == 2:
        prior = later = lax.ppermute(halo, "tm", [(0, 1), (1, 0)])
    else:
        prior, later = shifted(halo, "tm", 1), shifted(halo, "tm", -1)
    right = right_panels.transpose(0, 2, 1)
    right = [turned(right, ("fsdp",), (distance,)) for distance in range(slices)]
    projected, prior, later, right = lax.optimization_barrier((projected, prior, later, right))
    right = jnp.stack(right)
    rights = [turned(right, ("core",), (cross,)) for cross in range(cores)]
    held = [
        turned(projected, ("chip", "tm"), steps) for steps in np.ndindex(chips, clip_parts)
    ]

    spread = jnp.asarray(spread_picks(half), BF16)
    acts = pl.pallas_call(
        functools.partial(hidden_kernel, clip_parts=clip_parts),
        out_shape=jax.ShapeDtypeStruct((equals, slices, 2, share, wide), BF16),
        in_specs=[SMEM] + [VMEM] * 7 + [HBM] * 2,
        out_specs=VMEM,
        scratch_shapes=[
            pltpu.VMEM((quarter * quarter, channels), F32),
            pltpu.VMEM((frames, 9, half * half, channels), BF16),
            pltpu.VMEM(first_kernel.shape, BF16),
            pltpu.VMEM(second_kernel.shape, BF16),
            pltpu.SemaphoreType.DMA((2, 3)),
        ],
        compiler_params=pltpu.CompilerParams(vmem_limit_bytes=ROOM),
        cost_estimate=pl.CostEstimate(
            flops=3 * cells * TAPS * channels * wide,
            bytes_accessed=HIDDEN_COST,
            transcendentals=cells * wide,
        ),
    )(
        half_at, x, prior, grad, later, even, odd, spread, first_kernel, second_kernel,
    )
    acts, *rights = lax.optimization_barrier((acts, *rights))
    _, held = lax.optimization_barrier((acts, held))
    held = jnp.stack(held)
    right = pl.pallas_call(
        split_kernel,
        out_shape=jax.ShapeDtypeStruct((slices, 2, 2 * cores * width, wide), BF16),
        in_specs=[VMEM] * cores,
        out_specs=VMEM,
        compiler_params=pltpu.CompilerParams(vmem_limit_bytes=16 << 20),
        cost_estimate=pl.CostEstimate(flops=0, bytes_accessed=1 << 20, transcendentals=0),
    )(*rights)
    every = lax.all_to_all(
        acts.reshape(equals * slices, 2, share, wide), ("chip", "tm", "fsdp"), 0, 0, tiled=True
    ).reshape(equals, slices, 2, share, wide)
    columns = pl.pallas_call(
        right_kernel,
        out_shape=jax.ShapeDtypeStruct((slices, cores, 2 * width, equals * share), BF16),
        in_specs=[SMEM] * 2 + [VMEM] * 2,
        out_specs=VMEM,
        compiler_params=pltpu.CompilerParams(vmem_limit_bytes=16 << 20),
    )(place, core_at, every, right)
    clip_cells = clip_parts * cells
    shift_picks, sort_picks, mixers = pl.pallas_call(
        functools.partial(tables_kernel, slices=slices, clip_parts=clip_parts, half=half),
        out_shape=(
            jax.ShapeDtypeStruct((clip_cells, 8 * clip_cells), BF16),
            jax.ShapeDtypeStruct((clip_cells, clip_cells), BF16),
            jax.ShapeDtypeStruct((2, 2, 8 * TAPS, 8 * TAPS), BF16),
        ),
        in_specs=[ANY, VMEM],
        out_specs=(VMEM,) * 3,
        compiler_params=pltpu.CompilerParams(vmem_limit_bytes=16 << 20),
        cost_estimate=pl.CostEstimate(flops=0, bytes_accessed=4 << 20, transcendentals=0),
    )(columns, tap_mix)
    columns = lax.all_to_all(
        columns.reshape(slices * cores, 2 * width, equals * share), ("fsdp", "core"), 0, 0, tiled=True
    ).reshape(columns.shape)
    left_rows = [turned(held, ("core",), (cross,)) for cross in range(cores)]

    result = pl.pallas_call(
        functools.partial(
            update_kernel, clip_parts=clip_parts, half=half
        ),
        out_shape=jax.ShapeDtypeStruct((2, TAPS, width, wide), BF16),
        in_specs=[SMEM] * 3
        + [VMEM]
        + [ANY] * cores
        + [VMEM] * 4,
        out_specs=VMEM,
        scratch_shapes=[
            pltpu.VMEM((parts,) + projected.shape, BF16),
            pltpu.VMEM((8, parts // clip_parts, width, clip_cells), BF16),
            pltpu.VMEM((parts * cells // 8 + (quarter + 1) * quarter + 8, wide), F32),
            pltpu.VMEM((2, TAPS, width, wide), F32),
            pltpu.SemaphoreType.DMA((parts,)),
        ],
        compiler_params=pltpu.CompilerParams(vmem_limit_bytes=40 << 20),
    )(
        chip_at, core_at, half_at, columns,
        *left_rows, left_panels, mixers, shift_picks, sort_picks,
    )
    return result.transpose(0, 1, 3, 2)


def solution(mesh):
    fsdp, replica, tm = (mesh.shape[axis] for axis in ("fsdp", "replica", "tm"))
    cores = 2 if replica % 2 == 0 else 1
    assert mesh.axis_names == ("fsdp", "replica", "tm")
    mesh = Mesh(
        mesh.devices.reshape(fsdp, replica // cores, cores, tm), ("fsdp", "chip", "core", "tm")
    )
    replica = ("chip", "core")
    in_specs = (
        P(replica, "tm", None, None, None),
        P(None, None, "fsdp"),
        P(None, "fsdp", None),
        P(replica, "tm", None, None, None),
        P(),
        P(None, "fsdp", None),
        P(None, "fsdp", (*replica, "tm")),
    )
    out_specs = P(None, None, "fsdp", (*replica, "tm"))
    return jax.shard_map(shards, mesh=mesh, in_specs=in_specs, out_specs=out_specs, check_vma=False)
```

```python
import functools

import jax
import jax.numpy as jnp
import numpy as np
from jax import lax
from jax.experimental import pallas as pl
from jax.experimental.pallas import tpu as pltpu
from jax.sharding import Mesh, PartitionSpec as P

TAPS = 27
F32, BF16 = jnp.float32, jnp.bfloat16
ROOM = 50 << 20
PROJECT_COST = 16 << 20
HIDDEN_COST = 200 << 20
NT = (((1,), (1,)), ((), ()))
VMEM = pl.BlockSpec(memory_space=pltpu.VMEM)
HBM = pl.BlockSpec(memory_space=pltpu.HBM)
SMEM = pl.BlockSpec(memory_space=pltpu.SMEM)
ANY = pl.BlockSpec(memory_space=pl.ANY)


def shifted(block, axis, distance):
    devices = range(lax.axis_size(axis))
    route = [(i - distance, i) for i in devices if i - distance in devices]
    return lax.ppermute(block, axis, route)


def dot(left, right):
    return jnp.dot(left, right, preferred_element_type=F32)


def dot_nt(left, right):
    return lax.dot_general(left, right, NT, preferred_element_type=F32)


def quotient(value, size):
    return value >> (size.bit_length() - 1) if size & (size - 1) == 0 else value // size


def remainder(value, size):
    return value & (size - 1) if size & (size - 1) == 0 else value % size


def halves(value):
    high = value.astype(BF16)
    return high, (value - high.astype(F32)).astype(BF16)


def column_picks(side):
    half = side // 2
    picks = np.zeros((2, half, half, half, side), np.float32)
    for row in range(half):
        for x in range(side):
            picks[x % 2, row, x // 2, row, x] = 1
    return picks.reshape(half * side, half * side)


def spread_picks(half):
    quarter = half // 2
    picks = np.zeros((3, 3, half, half, quarter, quarter), np.float32)
    for b in range(3):
        for c in range(3):
            for out_y in range(quarter):
                for out_x in range(quarter):
                    y, x = 2 * out_y + b - 1, 2 * out_x + c - 1
                    if y >= 0 and x >= 0:
                        picks[b, c, y, x, out_y, out_x] = 1
    return picks.reshape(9 * half * half, quarter * quarter)


def parity_rows(lines, pick):
    rows = dot(pick, lines).astype(BF16)
    cells = rows.shape[0] // 2
    return rows[:cells], rows[cells:]


def folded_taps(rows, weights, shift_ref, half):
    sums = {}
    for line, column in np.ndindex(2, 2):
        taps = [(b, c) for b in ((2, 0) if line else (1,)) for c in ((2, 0) if column else (1,))]
        product = dot(rows(line, column), jnp.concatenate([weights(*tap) for tap in taps], axis=1))
        wide = product.shape[1] // len(taps)
        for at, (b, c) in enumerate(taps):
            part = product[:, at * wide : (at + 1) * wide]
            key = (int(b == 0), int(c == 0))
            sums[key] = sums[key] + part if key in sums else part
    total = sums.pop((0, 0))
    count, wide = total.shape
    pad = shift_ref.shape[1] - count
    places = lax.broadcasted_iota(jnp.int32, (count, wide), 0)
    row = remainder(quotient(places, half), half)
    column = remainder(places, half)
    for at, ((dr, dc), part) in enumerate(sums.items()):
        shift_ref[at, pl.ds(pad, count), :] = part
        moved = shift_ref[at, pl.ds(pad - (dr * half + dc), count), :]
        total += jnp.where((row >= dr) & (column >= dc), moved, 0.0)
    return total


def project_kernel(
    x_any, left_any, grad_any, pick_any, first_any,
    out_ref, halo_ref, x_ref, left_ref, grad_ref, pick_ref, first_ref, rows_ref, shift_ref, arrived,
):
    frames, half, _, side, channels = x_ref.shape
    order = [frame for time in (1, 0) for frame in range(time, frames, 2)]
    pairs_of = [
        (left_any.at[0], left_ref),
        (x_any.at[order[0]], x_ref.at[order[0]]),
        (x_any.at[order[1]], x_ref.at[order[1]]),
        (pick_any, pick_ref),
        (first_any.at[pl.ds(0, 9)], first_ref),
        (x_any.at[order[2]], x_ref.at[order[2]]),
        (x_any.at[order[3]], x_ref.at[order[3]]),
        (grad_any, grad_ref),
    ]
    copies = [
        pltpu.make_async_copy(source, target, arrived.at[at])
        for at, (source, target) in enumerate(pairs_of)
    ]
    for copy in copies:
        copy.start()
    wide = left_ref.shape[0]
    pairs = frames // 2
    size = pairs * half * side
    target = lax.broadcasted_iota(jnp.int32, (size, size), 0)
    source = lax.broadcasted_iota(jnp.int32, (size, size), 1)
    cells = size // 2
    wanted = 2 * remainder(target, cells) + quotient(target, cells)
    pick = jnp.where(source == wanted, 1.0, 0.0).astype(BF16)
    copies[0].wait()
    both = jnp.concatenate(halves(left_ref[...]), axis=0)

    def project(time):
        for row in range(2):
            block = jnp.concatenate(
                [
                    x_ref[frame, :, row].reshape(half * side, channels)
                    for frame in range(time, frames, 2)
                ],
                axis=0,
            )
            full = dot_nt(block, both)
            small = (full[:, :wide] + full[:, wide:]).astype(BF16)
            ordered = dot(pick, small).astype(BF16)
            at = (4 * time + 2 * row) * cells
            out_ref[at : at + size, :] = ordered

    copies[1].wait()
    copies[2].wait()
    project(1)
    copies[3].wait()
    classes = [
        parity_rows(x_ref[frames - 1, :, line].reshape(half * side, channels), pick_ref[...])
        for line in range(2)
    ]
    copies[4].wait()
    halo_ref[pl.ds(0, half * half), :] = folded_taps(
        lambda line, column: classes[line][column],
        lambda b, c: first_ref[3 * b + c],
        shift_ref,
        half,
    )
    copies[5].wait()
    copies[6].wait()
    project(0)
    copies[7].wait()
    grad_rows = stacked_rows(grad_ref, rows_ref)
    count = grad_rows.shape[0]
    for block in range(channels // wide):
        at = 8 * cells + block * count
        out_ref[at : at + count, :] = grad_rows[:, block * wide : (block + 1) * wide]
        at = half * half + block * count
        halo_ref[at : at + count, :] = rows_ref[:, block * wide : (block + 1) * wide]


def stacked_rows(grad_ref, rows_ref):
    quarter = grad_ref.shape[0]
    for row in range(quarter):
        rows_ref[pl.ds(row * quarter, quarter), :] = grad_ref[row].astype(F32)
    return rows_ref[...].astype(BF16)


def transposed_products(rows, kernel, taps):
    total = dot_nt(rows[0], kernel[taps[0]])
    for at in range(1, len(taps)):
        total += dot_nt(rows[at], kernel[taps[at]])
    return total


def spread_rows(picks_ref, rows, cells):
    spread = dot(picks_ref[...], rows).astype(BF16)
    return [spread[tap * cells : (tap + 1) * cells] for tap in range(9)]


def hidden_kernel(
    tm_ref, x_ref, prior_ref, grad_ref, later_ref, pick_ref, spread_ref,
    first_any, second_any, out_ref, rows_ref, classes, first, second, shift_ref, arrived, *,
    clip_parts,
):
    frames, half, _, side, channels = x_ref.shape
    cells = half * half
    has_prior = jnp.where(tm_ref[0] > 0, 1.0, 0.0)
    has_later = jnp.where(tm_ref[0] < clip_parts - 1, 1.0, 0.0)
    copies = {
        (at, a): pltpu.make_async_copy(
            source.at[pl.ds(9 * a, 9)], target.at[pl.ds(9 * a, 9)], arrived.at[at, a]
        )
        for at, (source, target) in enumerate(((second_any, second), (first_any, first)))
        for a in (1, 2, 0)
    }
    for copy in copies.values():
        copy.start()
    own_rows = stacked_rows(grad_ref, rows_ref)
    own = spread_rows(spread_ref, own_rows, cells)
    copies[0, 1].wait()
    copies[0, 2].wait()
    both = None
    for tap in range(9):
        pair = jnp.concatenate([second[9 + tap], second[18 + tap]], axis=0)
        term = dot_nt(own[tap], pair)
        both = term if both is None else both + term
    early, late = both[:, : second.shape[1]], both[:, second.shape[1] :]
    for frame in range(frames):
        for line in range(2):
            lines = x_ref[frame, :, line].reshape(half * side, channels)
            classes[frame, line, 0], classes[frame, line, 1] = parity_rows(lines, pick_ref[...])
    count = own_rows.shape[0]
    wide = first.shape[2]
    later_rows = jnp.concatenate(
        [
            later_ref[pl.ds(cells + count * block, count), :]
            for block in range(channels // wide)
        ],
        axis=1,
    )
    after = spread_rows(spread_ref, later_rows.astype(BF16), cells)
    copies[0, 0].wait()
    late += transposed_products(after, second, range(9)) * has_later
    hidden_grad = jnp.concatenate([early, late], axis=0)
    nothing = jnp.zeros((cells, channels), BF16)

    def rows_of(line, column):
        held = [classes[frame, line, column] for frame in range(frames)]
        return jnp.concatenate(
            [
                jnp.concatenate([nothing, held[0], held[1]], axis=1),
                jnp.concatenate([held[1], held[2], held[3]], axis=1),
            ],
            axis=0,
        )

    for a in (1, 2, 0):
        copies[1, a].wait()
    pre = folded_taps(
        rows_of,
        lambda b, c: jnp.concatenate([first[9 * a + 3 * b + c] for a in range(3)], axis=0),
        shift_ref,
        half,
    )
    pre += jnp.concatenate(
        [prior_ref[pl.ds(0, cells), :] * has_prior, jnp.zeros((cells, wide), F32)], axis=0
    )
    sig = jax.nn.sigmoid(pre)
    hidden = (pre * sig).astype(BF16)
    pre_grad = (hidden_grad * sig * (1.0 + pre * (1.0 - sig))).astype(BF16)
    groups, slices, _, share, _ = out_ref.shape
    for at in range(slices):
        place = slice(at * share, (at + 1) * share)
        for group in range(groups):
            out_ref[group, at, 0] = pre_grad[place]
            out_ref[group, at, 1] = hidden[place]


def right_kernel(place_ref, core_ref, *refs, cores):
    acts_refs, right_refs, out_ref = refs[:cores], refs[cores:-1], refs[-1]
    parts, slices = acts_refs[0].shape[:2]
    width = right_refs[0].shape[1]
    for layer in range(2):
        rights = [jnp.concatenate(halves(ref[layer]), axis=0) for ref in right_refs]
        for cross, acts_ref in enumerate(acts_refs):
            total = None
            for distance in range(slices):
                origin = lax.rem(place_ref[0] + (slices - distance), slices)
                rows = jnp.concatenate(
                    [acts_ref[part, origin, layer] for part in range(parts)], axis=0
                )
                term = dot_nt(rights[distance], rows)
                total = term if total is None else total + term
            core = lax.rem(core_ref[0] + cross, cores)
            out_ref[core, pl.ds(layer * width, width), :] = (total[:width] + total[width:]).astype(
                BF16
            )


def tables_kernel(after_any, mix_ref, shift_ref, sort_ref, mixers_ref, *, slices, clip_parts, half):
    del after_any
    size = shift_ref.shape[0]
    cells = size // clip_parts
    share = cells // slices
    frames = size // (half * half)
    held = lax.broadcasted_iota(jnp.int32, (size, size), 0)
    cell = lax.broadcasted_iota(jnp.int32, (size, size), 1)
    part = remainder(quotient(held, share), clip_parts)
    slot = quotient(held, share * clip_parts)
    natural = part * cells + slot * share + remainder(held, share)
    frame = quotient(cell, half * half)
    row = remainder(quotient(cell, half), half)
    column = remainder(cell, half)
    for shift in range(8):
        dt, dr, dc = shift // 4, shift // 2 % 2, shift % 2
        found = natural == cell + ((dt * half + dr) * half + dc)
        if dt:
            found &= frame < frames - 1
        if dr:
            found &= row < half - 1
        if dc:
            found &= column < half - 1
        shift_ref[:, pl.ds(shift * size, size)] = jnp.where(found, 1.0, 0.0).astype(BF16)
    quarter = half // 2
    outputs = size // 8
    kind = quotient(cell, outputs)
    frame = 2 * remainder(quotient(cell, quarter * quarter), frames // 2) + quotient(kind, 4)
    row = 2 * remainder(quotient(cell, quarter), quarter) + remainder(quotient(kind, 2), 2)
    column = 2 * remainder(cell, quarter) + remainder(kind, 2)
    found = natural == (frame * half + row) * half + column
    sort_ref[...] = jnp.where(found, 1.0, 0.0).astype(BF16)

    count = mixers_ref.shape[2]
    tap = lax.broadcasted_iota(jnp.int32, (count, TAPS), 1)
    line = lax.broadcasted_iota(jnp.int32, (count, TAPS), 0)
    spread = jnp.where(quotient(line, 8) == tap, 1.0, 0.0).astype(BF16)
    lines = lax.broadcasted_iota(jnp.int32, (count, count), 0)
    others = lax.broadcasted_iota(jnp.int32, (count, count), 1)
    same = remainder(lines, 8) == remainder(others, 8)
    for layer in range(2):
        for at, part in enumerate(halves(mix_ref[layer])):
            wider = dot_nt(dot(spread, part).astype(BF16), spread)
            mixers_ref[layer, at] = jnp.where(same, wider, 0.0).astype(BF16)


def update_kernel(
    place_ref, chip_ref, core_ref, tm_ref, *refs, slices, cores, clip_parts, half
):
    columns_refs, piece_refs = refs[:slices], refs[slices : slices + cores]
    (
        left_ref, mixers_ref, shift_ref, sort_ref,
        out_ref, left_rows_ref, columns, shifts, grads, raw, arrived,
    ) = refs[slices + cores :]
    parts = left_rows_ref.shape[0]
    chips = parts // (cores * clip_parts)
    copies = []
    for cross, piece_ref in enumerate(piece_refs):
        core = lax.rem(core_ref[0] + cross, cores)
        for at, (step, turn) in enumerate(np.ndindex(chips, clip_parts)):
            chip = lax.rem(chip_ref[0] + (chips - step), chips)
            place = lax.rem(tm_ref[0] + (clip_parts - turn), clip_parts)
            target = left_rows_ref.at[(chip * cores + core) * clip_parts + place]
            copies.append(
                pltpu.make_async_copy(piece_ref.at[at], target, arrived.at[len(copies)])
            )
    for copy in copies:
        copy.start()
    for distance in range(slices):
        origin = lax.rem(place_ref[0] + (slices - distance), slices)
        columns[origin] = columns_refs[distance][...]
    wide, channels = left_ref.shape[1:]
    width = columns.shape[2] // 2
    clips = parts // clip_parts
    share = columns.shape[3] // chips
    clip_cells = slices * share
    cells = clip_cells // clip_parts
    frames = clip_cells // (half * half)
    outputs = clip_cells // 8

    def by_clip(layer):
        return jnp.concatenate(
            [
                jnp.concatenate(
                    [
                        columns[
                            at, clip % cores, pl.ds(layer * width, width),
                            pl.ds(clip // cores * share, share),
                        ]
                        for at in range(slices)
                    ],
                    axis=1,
                )
                for clip in range(clips)
            ],
            axis=0,
        )

    first = by_clip(0)
    for shift in range(8):
        moved = dot(first, shift_ref[:, pl.ds(shift * clip_cells, clip_cells)]).astype(BF16)
        for clip in range(clips):
            shifts[shift, clip] = moved[clip * width : (clip + 1) * width]
    second = dot(by_clip(1), sort_ref[...]).astype(BF16)

    for copy in copies:
        copy.wait()
    own_outputs = outputs // clip_parts
    blocks = channels // wide
    out_grad = jnp.concatenate(
        [
            jnp.concatenate(
                [
                    left_rows_ref[part, pl.ds(8 * cells + own_outputs * at, own_outputs), :]
                    for at in range(blocks)
                ],
                axis=1,
            )
            for part in range(parts)
        ],
        axis=0,
    )
    full = dot_nt(out_grad, jnp.concatenate(halves(left_ref[1]), axis=0))
    total = parts * own_outputs
    quarter = half // 2
    grads[pl.ds(0, total), :] = full[:, :wide] + full[:, wide:]
    places = lax.broadcasted_iota(jnp.int32, (total, wide), 0)
    frame = remainder(quotient(places, quarter * quarter), frames // 2)
    row = remainder(quotient(places, quarter), quarter)
    column = remainder(places, quarter)
    second_rows = []
    for shift in range(8):
        dt, dr, dc = shift // 4, shift // 2 % 2, shift % 2
        moved = grads[pl.ds((dt * quarter + dr) * quarter + dc, total), :]
        inside = (frame + dt < frames // 2) & (row + dr < quarter) & (column + dc < quarter)
        second_rows.append(jnp.where(inside, moved, 0.0).astype(BF16))

    for time, line in np.ndindex(2, 2):
        even = [
            (9 * a + 3 * b + 1, 4 * (a == 0) + 2 * (b == 0))
            for a in ((0, 2) if time else (1,))
            for b in ((0, 2) if line else (1,))
        ]
        odd = [(tap + 1, shift) for tap, shift in even] + [
            (tap - 1, shift + 1) for tap, shift in even
        ]
        kind = 4 * time + 2 * line
        sums = None
        for clip in range(clips):
            left = jnp.concatenate([shifts[shift, clip] for _, shift in odd], axis=0)
            rows = jnp.concatenate(
                [
                    jnp.concatenate(
                        [
                            left_rows_ref[
                                clip * clip_parts + part, pl.ds((kind + at) * cells, cells), :
                            ]
                            for part in range(clip_parts)
                        ],
                        axis=0,
                    )
                    for at in range(2)
                ],
                axis=1,
            )
            term = dot(left, rows)
            sums = term if sums is None else sums + term
        for at, (tap, _) in enumerate(even):
            raw[0, tap] = sums[at * width : (at + 1) * width, :wide]
        for at, (tap, _) in enumerate(odd):
            raw[0, tap] = sums[at * width : (at + 1) * width, wide:]
        for place, taps in enumerate((even, odd)):
            chosen = jnp.concatenate(
                [
                    second[
                        clip * width : (clip + 1) * width,
                        (kind + place) * outputs : (kind + place + 1) * outputs,
                    ]
                    for clip in range(clips)
                ],
                axis=1,
            )
            products = dot(
                chosen, jnp.concatenate([second_rows[shift] for _, shift in taps], axis=1)
            )
            for at, (tap, _) in enumerate(taps):
                raw[1, tap] = products[:, at * wide : (at + 1) * wide]

    for layer in range(2):
        for group in range(width // 16):
            lanes = jnp.concatenate(
                [
                    raw[layer, :, pl.ds(16 * group + 8 * at, 8), :].reshape(8 * TAPS, wide)
                    for at in range(2)
                ],
                axis=1,
            )
            high, low = halves(lanes)
            mixed = (
                dot(mixers_ref[layer, 0], high)
                + dot(mixers_ref[layer, 0], low)
                + dot(mixers_ref[layer, 1], high)
            )
            rows = jnp.concatenate(
                [
                    mixed[:, at * wide : (at + 1) * wide].reshape(TAPS, 8, wide)
                    for at in range(2)
                ],
                axis=1,
            )
            out_ref[layer, :, pl.ds(16 * group, 16), :] = rows.astype(BF16)


def turned(block, axes, steps):
    sizes = [lax.axis_size(axis) for axis in axes]
    if not any(step % size for step, size in zip(steps, sizes)):
        return block
    route = []
    for place in np.ndindex(*sizes):
        target = [(at + step) % size for at, step, size in zip(place, steps, sizes)]
        route.append(
            (int(np.ravel_multi_index(place, sizes)), int(np.ravel_multi_index(target, sizes)))
        )
    return lax.ppermute(block, axes, route)


def shards(clip_input, first_kernel, second_kernel, out_grad, tap_mix, left_panels, right_panels):
    clips, frames, side, _, channels = clip_input.shape
    wide = first_kernel.shape[2]
    width = right_panels.shape[2]
    half, quarter = side // 2, side // 4
    half_frames = frames // 2
    cells = half_frames * half * half
    clip_parts = lax.axis_size("tm")
    cores, chips = lax.axis_size("core"), lax.axis_size("chip")
    equals = chips * clip_parts
    parts = equals * cores
    slices = lax.axis_size("fsdp")
    share = cells // slices
    assert clips == 1 and frames == 4
    x = clip_input.reshape(frames, half, 2, side, channels)
    grad = out_grad.reshape(quarter, quarter, channels)
    place, chip_at, core_at, half_at = (
        lax.axis_index(axis).reshape(1) for axis in ("fsdp", "chip", "core", "tm")
    )

    pick = jnp.asarray(column_picks(side), BF16)
    pad = (half // 8 + 1) * 8
    rows = quarter * quarter * channels // wide
    projected, halo = pl.pallas_call(
        project_kernel,
        out_shape=(
            jax.ShapeDtypeStruct((8 * cells + rows, wide), BF16),
            jax.ShapeDtypeStruct((half * half + rows, wide), F32),
        ),
        in_specs=[ANY] * 5,
        out_specs=(VMEM, VMEM),
        scratch_shapes=[
            pltpu.VMEM(x.shape, BF16),
            pltpu.VMEM(left_panels.shape[1:], F32),
            pltpu.VMEM(grad.shape, BF16),
            pltpu.VMEM(pick.shape, BF16),
            pltpu.VMEM((9,) + first_kernel.shape[1:], BF16),
            pltpu.VMEM((quarter * quarter, channels), F32),
            pltpu.VMEM((3, pad + half * half, wide), F32),
            pltpu.SemaphoreType.DMA((8,)),
        ],
        compiler_params=pltpu.CompilerParams(vmem_limit_bytes=58 << 20),
        cost_estimate=pl.CostEstimate(
            flops=4 * frames * side * side * channels * wide,
            bytes_accessed=PROJECT_COST,
            transcendentals=0,
        ),
    )(x, left_panels, grad, pick, first_kernel)
    if clip_parts == 2:
        prior = later = lax.ppermute(halo, "tm", [(0, 1), (1, 0)])
    else:
        prior, later = shifted(halo, "tm", 1), shifted(halo, "tm", -1)
    right = right_panels.transpose(0, 2, 1)
    right = [turned(right, ("fsdp",), (distance,)) for distance in range(slices)]
    projected, prior, later, right = lax.optimization_barrier((projected, prior, later, right))
    held = jnp.stack(
        [
            turned(projected, ("chip", "tm"), steps)
            for steps in np.ndindex(chips, clip_parts)
        ]
    )

    spread = jnp.asarray(spread_picks(half), BF16)
    acts = pl.pallas_call(
        functools.partial(hidden_kernel, clip_parts=clip_parts),
        out_shape=jax.ShapeDtypeStruct((equals, slices, 2, share, wide), BF16),
        in_specs=[SMEM] + [VMEM] * 6 + [HBM] * 2,
        out_specs=VMEM,
        scratch_shapes=[
            pltpu.VMEM((quarter * quarter, channels), F32),
            pltpu.VMEM((frames, 2, 2, half * half, channels), BF16),
            pltpu.VMEM(first_kernel.shape, BF16),
            pltpu.VMEM(second_kernel.shape, BF16),
            pltpu.VMEM((3, pad + cells, wide), F32),
            pltpu.SemaphoreType.DMA((2, 3)),
        ],
        compiler_params=pltpu.CompilerParams(vmem_limit_bytes=ROOM),
        cost_estimate=pl.CostEstimate(
            flops=3 * cells * TAPS * channels * wide,
            bytes_accessed=HIDDEN_COST,
            transcendentals=cells * wide,
        ),
    )(
        half_at, x, prior, grad, later, pick, spread, first_kernel, second_kernel,
    )
    acts, *right = lax.optimization_barrier((acts, *right))
    clip_cells = clip_parts * cells
    shift_picks, sort_picks, mixers = pl.pallas_call(
        functools.partial(tables_kernel, slices=slices, clip_parts=clip_parts, half=half),
        out_shape=(
            jax.ShapeDtypeStruct((clip_cells, 8 * clip_cells), BF16),
            jax.ShapeDtypeStruct((clip_cells, clip_cells), BF16),
            jax.ShapeDtypeStruct((2, 2, 8 * TAPS, 8 * TAPS), BF16),
        ),
        in_specs=[ANY, VMEM],
        out_specs=(VMEM,) * 3,
        compiler_params=pltpu.CompilerParams(vmem_limit_bytes=16 << 20),
        cost_estimate=pl.CostEstimate(flops=0, bytes_accessed=4 << 20, transcendentals=0),
    )(acts, tap_mix)
    every = lax.all_to_all(
        acts.reshape(equals * slices, 2, share, wide), ("chip", "tm", "fsdp"), 0, 0, tiled=True
    ).reshape(equals, slices, 2, share, wide)
    every = [turned(every, ("core",), (cross,)) for cross in range(cores)]
    columns = pl.pallas_call(
        functools.partial(right_kernel, cores=cores),
        out_shape=jax.ShapeDtypeStruct((cores, 2 * width, equals * share), BF16),
        in_specs=[SMEM] * 2 + [VMEM] * (cores + slices),
        out_specs=VMEM,
        compiler_params=pltpu.CompilerParams(vmem_limit_bytes=16 << 20),
    )(place, core_at, *every, *right)
    columns, held = lax.optimization_barrier((columns, held))
    columns = [turned(columns, ("fsdp",), (distance,)) for distance in range(slices)]
    left_rows = [turned(held, ("core",), (cross,)) for cross in range(cores)]

    result = pl.pallas_call(
        functools.partial(
            update_kernel, slices=slices, cores=cores, clip_parts=clip_parts, half=half
        ),
        out_shape=jax.ShapeDtypeStruct((2, TAPS, width, wide), BF16),
        in_specs=[SMEM] * 4
        + [VMEM] * len(columns)
        + [ANY] * cores
        + [VMEM] * 4,
        out_specs=VMEM,
        scratch_shapes=[
            pltpu.VMEM((parts,) + projected.shape, BF16),
            pltpu.VMEM((slices, cores, 2 * width, equals * share), BF16),
            pltpu.VMEM((8, parts // clip_parts, width, clip_cells), BF16),
            pltpu.VMEM((parts * cells // 8 + (quarter + 1) * quarter + 8, wide), F32),
            pltpu.VMEM((2, TAPS, width, wide), F32),
            pltpu.SemaphoreType.DMA((parts,)),
        ],
        compiler_params=pltpu.CompilerParams(vmem_limit_bytes=40 << 20),
    )(
        place, chip_at, core_at, half_at,
        *columns, *left_rows, left_panels, mixers, shift_picks, sort_picks,
    )
    return result.transpose(0, 1, 3, 2)


def solution(mesh):
    fsdp, replica, tm = (mesh.shape[axis] for axis in ("fsdp", "replica", "tm"))
    cores = 2 if replica % 2 == 0 else 1
    assert mesh.axis_names == ("fsdp", "replica", "tm")
    mesh = Mesh(
        mesh.devices.reshape(fsdp, replica // cores, cores, tm), ("fsdp", "chip", "core", "tm")
    )
    replica = ("chip", "core")
    in_specs = (
        P(replica, "tm", None, None, None),
        P(None, None, "fsdp"),
        P(None, "fsdp", None),
        P(replica, "tm", None, None, None),
        P(),
        P(None, "fsdp", None),
        P(None, "fsdp", (*replica, "tm")),
    )
    out_specs = P(None, None, "fsdp", (*replica, "tm"))
    return jax.shard_map(shards, mesh=mesh, in_specs=in_specs, out_specs=out_specs, check_vma=False)
```

```python
import functools

import jax
import jax.numpy as jnp
import numpy as np
from jax import lax
from jax.experimental import pallas as pl
from jax.experimental.pallas import tpu as pltpu
from jax.sharding import Mesh, PartitionSpec as P

TAPS = 27
F32, BF16 = jnp.float32, jnp.bfloat16
ROOM = 50 << 20
PROJECT_COST = 16 << 20
HIDDEN_COST = 200 << 20
NT = (((1,), (1,)), ((), ()))
VMEM = pl.BlockSpec(memory_space=pltpu.VMEM)
HBM = pl.BlockSpec(memory_space=pltpu.HBM)
SMEM = pl.BlockSpec(memory_space=pltpu.SMEM)
ANY = pl.BlockSpec(memory_space=pl.ANY)


def shifted(block, axis, distance):
    devices = range(lax.axis_size(axis))
    route = [(i - distance, i) for i in devices if i - distance in devices]
    return lax.ppermute(block, axis, route)


def dot(left, right):
    return jnp.dot(left, right, preferred_element_type=F32)


def dot_nt(left, right):
    return lax.dot_general(left, right, NT, preferred_element_type=F32)


def quotient(value, size):
    return value >> (size.bit_length() - 1) if size & (size - 1) == 0 else value // size


def remainder(value, size):
    return value & (size - 1) if size & (size - 1) == 0 else value % size


def halves(value):
    high = value.astype(BF16)
    return high, (value - high.astype(F32)).astype(BF16)


def column_picks(side):
    half = side // 2
    picks = np.zeros((2, half, half, half, side), np.float32)
    for row in range(half):
        for x in range(side):
            picks[x % 2, row, x // 2, row, x] = 1
    return picks.reshape(half * side, half * side)


def spread_picks(half):
    quarter = half // 2
    picks = np.zeros((3, 3, half, half, quarter, quarter), np.float32)
    for b in range(3):
        for c in range(3):
            for out_y in range(quarter):
                for out_x in range(quarter):
                    y, x = 2 * out_y + b - 1, 2 * out_x + c - 1
                    if y >= 0 and x >= 0:
                        picks[b, c, y, x, out_y, out_x] = 1
    return picks.reshape(9 * half * half, quarter * quarter)


def parity_rows(lines, pick):
    rows = dot(pick, lines).astype(BF16)
    cells = rows.shape[0] // 2
    return rows[:cells], rows[cells:]


def folded_taps(rows, weights, shift_ref, half):
    sums = {}
    for line, column in np.ndindex(2, 2):
        taps = [(b, c) for b in ((2, 0) if line else (1,)) for c in ((2, 0) if column else (1,))]
        product = dot(rows(line, column), jnp.concatenate([weights(*tap) for tap in taps], axis=1))
        wide = product.shape[1] // len(taps)
        for at, (b, c) in enumerate(taps):
            part = product[:, at * wide : (at + 1) * wide]
            key = (int(b == 0), int(c == 0))
            sums[key] = sums[key] + part if key in sums else part
    total = sums.pop((0, 0))
    count, wide = total.shape
    pad = shift_ref.shape[1] - count
    places = lax.broadcasted_iota(jnp.int32, (count, wide), 0)
    row = remainder(quotient(places, half), half)
    column = remainder(places, half)
    for at, ((dr, dc), part) in enumerate(sums.items()):
        shift_ref[at, pl.ds(pad, count), :] = part
        moved = shift_ref[at, pl.ds(pad - (dr * half + dc), count), :]
        total += jnp.where((row >= dr) & (column >= dc), moved, 0.0)
    return total


def project_kernel(
    x_any, left_any, grad_any, pick_any, first_any,
    out_ref, halo_ref, x_ref, left_ref, grad_ref, pick_ref, first_ref, rows_ref, shift_ref, arrived,
):
    frames, half, _, side, channels = x_ref.shape
    order = [frame for time in (1, 0) for frame in range(time, frames, 2)]
    pairs_of = [
        (left_any.at[0], left_ref),
        (x_any.at[order[0]], x_ref.at[order[0]]),
        (x_any.at[order[1]], x_ref.at[order[1]]),
        (pick_any, pick_ref),
        (first_any.at[pl.ds(0, 9)], first_ref),
        (x_any.at[order[2]], x_ref.at[order[2]]),
        (x_any.at[order[3]], x_ref.at[order[3]]),
        (grad_any, grad_ref),
    ]
    copies = [
        pltpu.make_async_copy(source, target, arrived.at[at])
        for at, (source, target) in enumerate(pairs_of)
    ]
    for copy in copies:
        copy.start()
    wide = left_ref.shape[0]
    pairs = frames // 2
    size = pairs * half * side
    target = lax.broadcasted_iota(jnp.int32, (size, size), 0)
    source = lax.broadcasted_iota(jnp.int32, (size, size), 1)
    cells = size // 2
    wanted = 2 * remainder(target, cells) + quotient(target, cells)
    pick = jnp.where(source == wanted, 1.0, 0.0).astype(BF16)
    copies[0].wait()
    both = jnp.concatenate(halves(left_ref[...]), axis=0)

    def project(time):
        for row in range(2):
            block = jnp.concatenate(
                [
                    x_ref[frame, :, row].reshape(half * side, channels)
                    for frame in range(time, frames, 2)
                ],
                axis=0,
            )
            full = dot_nt(block, both)
            small = (full[:, :wide] + full[:, wide:]).astype(BF16)
            ordered = dot(pick, small).astype(BF16)
            at = (4 * time + 2 * row) * cells
            out_ref[at : at + size, :] = ordered

    copies[1].wait()
    copies[2].wait()
    project(1)
    copies[3].wait()
    classes = [
        parity_rows(x_ref[frames - 1, :, line].reshape(half * side, channels), pick_ref[...])
        for line in range(2)
    ]
    copies[4].wait()
    halo_ref[pl.ds(0, half * half), :] = folded_taps(
        lambda line, column: classes[line][column],
        lambda b, c: first_ref[3 * b + c],
        shift_ref,
        half,
    )
    copies[5].wait()
    copies[6].wait()
    project(0)
    copies[7].wait()
    grad_rows = stacked_rows(grad_ref, rows_ref)
    count = grad_rows.shape[0]
    for block in range(channels // wide):
        at = 8 * cells + block * count
        out_ref[at : at + count, :] = grad_rows[:, block * wide : (block + 1) * wide]
        at = half * half + block * count
        halo_ref[at : at + count, :] = rows_ref[:, block * wide : (block + 1) * wide]


def stacked_rows(grad_ref, rows_ref):
    quarter = grad_ref.shape[0]
    for row in range(quarter):
        rows_ref[pl.ds(row * quarter, quarter), :] = grad_ref[row].astype(F32)
    return rows_ref[...].astype(BF16)


def transposed_products(rows, kernel, taps):
    total = dot_nt(rows[0], kernel[taps[0]])
    for at in range(1, len(taps)):
        total += dot_nt(rows[at], kernel[taps[at]])
    return total


def spread_rows(picks_ref, rows, cells):
    spread = dot(picks_ref[...], rows).astype(BF16)
    return [spread[tap * cells : (tap + 1) * cells] for tap in range(9)]


def hidden_kernel(
    tm_ref, x_ref, prior_ref, grad_ref, later_ref, pick_ref, spread_ref,
    first_any, second_any, out_ref, rows_ref, classes, first, second, shift_ref, arrived, *,
    clip_parts,
):
    frames, half, _, side, channels = x_ref.shape
    cells = half * half
    has_prior = jnp.where(tm_ref[0] > 0, 1.0, 0.0)
    has_later = jnp.where(tm_ref[0] < clip_parts - 1, 1.0, 0.0)
    copies = {
        (at, a): pltpu.make_async_copy(
            source.at[pl.ds(9 * a, 9)], target.at[pl.ds(9 * a, 9)], arrived.at[at, a]
        )
        for at, (source, target) in enumerate(((second_any, second), (first_any, first)))
        for a in (1, 2, 0)
    }
    for copy in copies.values():
        copy.start()
    own_rows = stacked_rows(grad_ref, rows_ref)
    own = spread_rows(spread_ref, own_rows, cells)
    copies[0, 1].wait()
    copies[0, 2].wait()
    both = None
    for tap in range(9):
        pair = jnp.concatenate([second[9 + tap], second[18 + tap]], axis=0)
        term = dot_nt(own[tap], pair)
        both = term if both is None else both + term
    early, late = both[:, : second.shape[1]], both[:, second.shape[1] :]
    for frame in range(frames):
        for line in range(2):
            lines = x_ref[frame, :, line].reshape(half * side, channels)
            classes[frame, line, 0], classes[frame, line, 1] = parity_rows(lines, pick_ref[...])
    count = own_rows.shape[0]
    wide = first.shape[2]
    later_rows = jnp.concatenate(
        [
            later_ref[pl.ds(cells + count * block, count), :]
            for block in range(channels // wide)
        ],
        axis=1,
    )
    after = spread_rows(spread_ref, later_rows.astype(BF16), cells)
    copies[0, 0].wait()
    late += transposed_products(after, second, range(9)) * has_later
    hidden_grad = jnp.concatenate([early, late], axis=0)
    nothing = jnp.zeros((cells, channels), BF16)

    def rows_of(line, column):
        held = [classes[frame, line, column] for frame in range(frames)]
        return jnp.concatenate(
            [
                jnp.concatenate([nothing, held[0], held[1]], axis=1),
                jnp.concatenate([held[1], held[2], held[3]], axis=1),
            ],
            axis=0,
        )

    for a in (1, 2, 0):
        copies[1, a].wait()
    pre = folded_taps(
        rows_of,
        lambda b, c: jnp.concatenate([first[9 * a + 3 * b + c] for a in range(3)], axis=0),
        shift_ref,
        half,
    )
    pre += jnp.concatenate(
        [prior_ref[pl.ds(0, cells), :] * has_prior, jnp.zeros((cells, wide), F32)], axis=0
    )
    sig = jax.nn.sigmoid(pre)
    hidden = (pre * sig).astype(BF16)
    pre_grad = (hidden_grad * sig * (1.0 + pre * (1.0 - sig))).astype(BF16)
    groups, slices, _, share, _ = out_ref.shape
    for at in range(slices):
        place = slice(at * share, (at + 1) * share)
        for group in range(groups):
            out_ref[group, at, 0] = pre_grad[place]
            out_ref[group, at, 1] = hidden[place]


def right_kernel(place_ref, core_ref, *refs, cores):
    acts_refs, right_refs, out_ref = refs[:cores], refs[cores:-1], refs[-1]
    parts, slices = acts_refs[0].shape[:2]
    width = right_refs[0].shape[1]
    for layer in range(2):
        rights = [jnp.concatenate(halves(ref[layer]), axis=0) for ref in right_refs]
        for cross, acts_ref in enumerate(acts_refs):
            total = None
            for distance in range(slices):
                origin = lax.rem(place_ref[0] + (slices - distance), slices)
                rows = jnp.concatenate(
                    [acts_ref[part, origin, layer] for part in range(parts)], axis=0
                )
                term = dot_nt(rights[distance], rows)
                total = term if total is None else total + term
            core = lax.rem(core_ref[0] + cross, cores)
            out_ref[core, pl.ds(layer * width, width), :] = (total[:width] + total[width:]).astype(
                BF16
            )


def tables_kernel(after_any, mix_ref, shift_ref, sort_ref, mixers_ref, *, slices, clip_parts, half):
    del after_any
    size = shift_ref.shape[0]
    cells = size // clip_parts
    share = cells // slices
    frames = size // (half * half)
    held = lax.broadcasted_iota(jnp.int32, (size, size), 0)
    cell = lax.broadcasted_iota(jnp.int32, (size, size), 1)
    part = remainder(quotient(held, share), clip_parts)
    slot = quotient(held, share * clip_parts)
    natural = part * cells + slot * share + remainder(held, share)
    frame = quotient(cell, half * half)
    row = remainder(quotient(cell, half), half)
    column = remainder(cell, half)
    for shift in range(8):
        dt, dr, dc = shift // 4, shift // 2 % 2, shift % 2
        found = natural == cell + ((dt * half + dr) * half + dc)
        if dt:
            found &= frame < frames - 1
        if dr:
            found &= row < half - 1
        if dc:
            found &= column < half - 1
        shift_ref[:, pl.ds(shift * size, size)] = jnp.where(found, 1.0, 0.0).astype(BF16)
    quarter = half // 2
    outputs = size // 8
    kind = quotient(cell, outputs)
    frame = 2 * remainder(quotient(cell, quarter * quarter), frames // 2) + quotient(kind, 4)
    row = 2 * remainder(quotient(cell, quarter), quarter) + remainder(quotient(kind, 2), 2)
    column = 2 * remainder(cell, quarter) + remainder(kind, 2)
    found = natural == (frame * half + row) * half + column
    sort_ref[...] = jnp.where(found, 1.0, 0.0).astype(BF16)

    count = mixers_ref.shape[2]
    tap = lax.broadcasted_iota(jnp.int32, (count, TAPS), 1)
    line = lax.broadcasted_iota(jnp.int32, (count, TAPS), 0)
    spread = jnp.where(quotient(line, 8) == tap, 1.0, 0.0).astype(BF16)
    lines = lax.broadcasted_iota(jnp.int32, (count, count), 0)
    others = lax.broadcasted_iota(jnp.int32, (count, count), 1)
    same = remainder(lines, 8) == remainder(others, 8)
    for layer in range(2):
        for at, part in enumerate(halves(mix_ref[layer])):
            wider = dot_nt(dot(spread, part).astype(BF16), spread)
            mixers_ref[layer, at] = jnp.where(same, wider, 0.0).astype(BF16)


def update_kernel(
    place_ref, chip_ref, core_ref, tm_ref, *refs, slices, cores, clip_parts, half
):
    columns_refs, piece_refs = refs[:slices], refs[slices : slices + cores]
    (
        left_ref, mixers_ref, shift_ref, sort_ref,
        out_ref, left_rows_ref, columns, shifts, grads, raw, arrived,
    ) = refs[slices + cores :]
    parts = left_rows_ref.shape[0]
    chips = parts // (cores * clip_parts)
    copies = []
    for cross, piece_ref in enumerate(piece_refs):
        core = lax.rem(core_ref[0] + cross, cores)
        for at, (step, turn) in enumerate(np.ndindex(chips, clip_parts)):
            chip = lax.rem(chip_ref[0] + (chips - step), chips)
            place = lax.rem(tm_ref[0] + (clip_parts - turn), clip_parts)
            target = left_rows_ref.at[(chip * cores + core) * clip_parts + place]
            copies.append(
                pltpu.make_async_copy(piece_ref.at[at], target, arrived.at[len(copies)])
            )
    for copy in copies:
        copy.start()
    for distance in range(slices):
        origin = lax.rem(place_ref[0] + (slices - distance), slices)
        columns[origin] = columns_refs[distance][...]
    wide, channels = left_ref.shape[1:]
    width = columns.shape[2] // 2
    clips = parts // clip_parts
    share = columns.shape[3] // chips
    clip_cells = slices * share
    cells = clip_cells // clip_parts
    frames = clip_cells // (half * half)
    outputs = clip_cells // 8

    def by_clip(layer):
        return jnp.concatenate(
            [
                jnp.concatenate(
                    [
                        columns[
                            at, clip % cores, pl.ds(layer * width, width),
                            pl.ds(clip // cores * share, share),
                        ]
                        for at in range(slices)
                    ],
                    axis=1,
                )
                for clip in range(clips)
            ],
            axis=0,
        )

    first = by_clip(0)
    for shift in range(8):
        moved = dot(first, shift_ref[:, pl.ds(shift * clip_cells, clip_cells)]).astype(BF16)
        for clip in range(clips):
            shifts[shift, clip] = moved[clip * width : (clip + 1) * width]
    second = dot(by_clip(1), sort_ref[...]).astype(BF16)

    for copy in copies:
        copy.wait()
    own_outputs = outputs // clip_parts
    blocks = channels // wide
    out_grad = jnp.concatenate(
        [
            jnp.concatenate(
                [
                    left_rows_ref[part, pl.ds(8 * cells + own_outputs * at, own_outputs), :]
                    for at in range(blocks)
                ],
                axis=1,
            )
            for part in range(parts)
        ],
        axis=0,
    )
    full = dot_nt(out_grad, jnp.concatenate(halves(left_ref[1]), axis=0))
    total = parts * own_outputs
    quarter = half // 2
    grads[pl.ds(0, total), :] = full[:, :wide] + full[:, wide:]
    places = lax.broadcasted_iota(jnp.int32, (total, wide), 0)
    frame = remainder(quotient(places, quarter * quarter), frames // 2)
    row = remainder(quotient(places, quarter), quarter)
    column = remainder(places, quarter)
    second_rows = []
    for shift in range(8):
        dt, dr, dc = shift // 4, shift // 2 % 2, shift % 2
        moved = grads[pl.ds((dt * quarter + dr) * quarter + dc, total), :]
        inside = (frame + dt < frames // 2) & (row + dr < quarter) & (column + dc < quarter)
        second_rows.append(jnp.where(inside, moved, 0.0).astype(BF16))

    for time, line in np.ndindex(2, 2):
        even = [
            (9 * a + 3 * b + 1, 4 * (a == 0) + 2 * (b == 0))
            for a in ((0, 2) if time else (1,))
            for b in ((0, 2) if line else (1,))
        ]
        odd = [(tap + 1, shift) for tap, shift in even] + [
            (tap - 1, shift + 1) for tap, shift in even
        ]
        kind = 4 * time + 2 * line
        sums = None
        for clip in range(clips):
            left = jnp.concatenate([shifts[shift, clip] for _, shift in odd], axis=0)
            rows = jnp.concatenate(
                [
                    jnp.concatenate(
                        [
                            left_rows_ref[
                                clip * clip_parts + part, pl.ds((kind + at) * cells, cells), :
                            ]
                            for part in range(clip_parts)
                        ],
                        axis=0,
                    )
                    for at in range(2)
                ],
                axis=1,
            )
            term = dot(left, rows)
            sums = term if sums is None else sums + term
        for at, (tap, _) in enumerate(even):
            raw[0, tap] = sums[at * width : (at + 1) * width, :wide]
        for at, (tap, _) in enumerate(odd):
            raw[0, tap] = sums[at * width : (at + 1) * width, wide:]
        for place, taps in enumerate((even, odd)):
            chosen = jnp.concatenate(
                [
                    second[
                        clip * width : (clip + 1) * width,
                        (kind + place) * outputs : (kind + place + 1) * outputs,
                    ]
                    for clip in range(clips)
                ],
                axis=1,
            )
            products = dot(
                chosen, jnp.concatenate([second_rows[shift] for _, shift in taps], axis=1)
            )
            for at, (tap, _) in enumerate(taps):
                raw[1, tap] = products[:, at * wide : (at + 1) * wide]

    for layer in range(2):
        for group in range(width // 16):
            lanes = jnp.concatenate(
                [
                    raw[layer, :, pl.ds(16 * group + 8 * at, 8), :].reshape(8 * TAPS, wide)
                    for at in range(2)
                ],
                axis=1,
            )
            high, low = halves(lanes)
            mixed = (
                dot(mixers_ref[layer, 0], high)
                + dot(mixers_ref[layer, 0], low)
                + dot(mixers_ref[layer, 1], high)
            )
            rows = jnp.concatenate(
                [
                    mixed[:, at * wide : (at + 1) * wide].reshape(TAPS, 8, wide)
                    for at in range(2)
                ],
                axis=1,
            )
            out_ref[layer, :, pl.ds(16 * group, 16), :] = rows.astype(BF16)


def turned(block, axes, steps):
    sizes = [lax.axis_size(axis) for axis in axes]
    if not any(step % size for step, size in zip(steps, sizes)):
        return block
    route = []
    for place in np.ndindex(*sizes):
        target = [(at + step) % size for at, step, size in zip(place, steps, sizes)]
        route.append(
            (int(np.ravel_multi_index(place, sizes)), int(np.ravel_multi_index(target, sizes)))
        )
    return lax.ppermute(block, axes, route)


def shards(clip_input, first_kernel, second_kernel, out_grad, tap_mix, left_panels, right_panels):
    clips, frames, side, _, channels = clip_input.shape
    wide = first_kernel.shape[2]
    width = right_panels.shape[2]
    half, quarter = side // 2, side // 4
    half_frames = frames // 2
    cells = half_frames * half * half
    clip_parts = lax.axis_size("tm")
    cores, chips = lax.axis_size("core"), lax.axis_size("chip")
    equals = chips * clip_parts
    parts = equals * cores
    slices = lax.axis_size("fsdp")
    share = cells // slices
    assert clips == 1 and frames == 4
    x = clip_input.reshape(frames, half, 2, side, channels)
    grad = out_grad.reshape(quarter, quarter, channels)
    place, chip_at, core_at, half_at = (
        lax.axis_index(axis).reshape(1) for axis in ("fsdp", "chip", "core", "tm")
    )

    pick = jnp.asarray(column_picks(side), BF16)
    pad = (half // 8 + 1) * 8
    rows = quarter * quarter * channels // wide
    projected, halo = pl.pallas_call(
        project_kernel,
        out_shape=(
            jax.ShapeDtypeStruct((8 * cells + rows, wide), BF16),
            jax.ShapeDtypeStruct((half * half + rows, wide), F32),
        ),
        in_specs=[ANY] * 5,
        out_specs=(VMEM, VMEM),
        scratch_shapes=[
            pltpu.VMEM(x.shape, BF16),
            pltpu.VMEM(left_panels.shape[1:], F32),
            pltpu.VMEM(grad.shape, BF16),
            pltpu.VMEM(pick.shape, BF16),
            pltpu.VMEM((9,) + first_kernel.shape[1:], BF16),
            pltpu.VMEM((quarter * quarter, channels), F32),
            pltpu.VMEM((3, pad + half * half, wide), F32),
            pltpu.SemaphoreType.DMA((8,)),
        ],
        compiler_params=pltpu.CompilerParams(vmem_limit_bytes=58 << 20),
        cost_estimate=pl.CostEstimate(
            flops=4 * frames * side * side * channels * wide,
            bytes_accessed=PROJECT_COST,
            transcendentals=0,
        ),
    )(x, left_panels, grad, pick, first_kernel)
    if clip_parts == 2:
        prior = later = lax.ppermute(halo, "tm", [(0, 1), (1, 0)])
    else:
        prior, later = shifted(halo, "tm", 1), shifted(halo, "tm", -1)
    right = right_panels.transpose(0, 2, 1)
    right = [turned(right, ("fsdp",), (distance,)) for distance in range(slices)]
    projected, prior, later, right = lax.optimization_barrier((projected, prior, later, right))
    held = jnp.stack(
        [
            turned(projected, ("chip", "tm"), steps)
            for steps in np.ndindex(chips, clip_parts)
        ]
    )

    spread = jnp.asarray(spread_picks(half), BF16)
    acts = pl.pallas_call(
        functools.partial(hidden_kernel, clip_parts=clip_parts),
        out_shape=jax.ShapeDtypeStruct((equals, slices, 2, share, wide), BF16),
        in_specs=[SMEM] + [VMEM] * 6 + [HBM] * 2,
        out_specs=VMEM,
        scratch_shapes=[
            pltpu.VMEM((quarter * quarter, channels), F32),
            pltpu.VMEM((frames, 2, 2, half * half, channels), BF16),
            pltpu.VMEM(first_kernel.shape, BF16),
            pltpu.VMEM(second_kernel.shape, BF16),
            pltpu.VMEM((3, pad + cells, wide), F32),
            pltpu.SemaphoreType.DMA((2, 3)),
        ],
        compiler_params=pltpu.CompilerParams(vmem_limit_bytes=ROOM),
        cost_estimate=pl.CostEstimate(
            flops=3 * cells * TAPS * channels * wide,
            bytes_accessed=HIDDEN_COST,
            transcendentals=cells * wide,
        ),
    )(
        half_at, x, prior, grad, later, pick, spread, first_kernel, second_kernel,
    )
    acts, *right = lax.optimization_barrier((acts, *right))
    clip_cells = clip_parts * cells
    shift_picks, sort_picks, mixers = pl.pallas_call(
        functools.partial(tables_kernel, slices=slices, clip_parts=clip_parts, half=half),
        out_shape=(
            jax.ShapeDtypeStruct((clip_cells, 8 * clip_cells), BF16),
            jax.ShapeDtypeStruct((clip_cells, clip_cells), BF16),
            jax.ShapeDtypeStruct((2, 2, 8 * TAPS, 8 * TAPS), BF16),
        ),
        in_specs=[ANY, VMEM],
        out_specs=(VMEM,) * 3,
        compiler_params=pltpu.CompilerParams(vmem_limit_bytes=16 << 20),
        cost_estimate=pl.CostEstimate(flops=0, bytes_accessed=4 << 20, transcendentals=0),
    )(acts, tap_mix)
    every = lax.all_to_all(
        acts.reshape(equals * slices, 2, share, wide), ("chip", "tm", "fsdp"), 0, 0, tiled=True
    ).reshape(equals, slices, 2, share, wide)
    every, held = lax.optimization_barrier((every, held))
    every = [turned(every, ("core",), (cross,)) for cross in range(cores)]
    columns = pl.pallas_call(
        functools.partial(right_kernel, cores=cores),
        out_shape=jax.ShapeDtypeStruct((cores, 2 * width, equals * share), BF16),
        in_specs=[SMEM] * 2 + [VMEM] * (cores + slices),
        out_specs=VMEM,
        compiler_params=pltpu.CompilerParams(vmem_limit_bytes=16 << 20),
    )(place, core_at, *every, *right)
    columns, held = lax.optimization_barrier((columns, held))
    columns = [turned(columns, ("fsdp",), (distance,)) for distance in range(slices)]
    left_rows = [turned(held, ("core",), (cross,)) for cross in range(cores)]

    result = pl.pallas_call(
        functools.partial(
            update_kernel, slices=slices, cores=cores, clip_parts=clip_parts, half=half
        ),
        out_shape=jax.ShapeDtypeStruct((2, TAPS, width, wide), BF16),
        in_specs=[SMEM] * 4
        + [VMEM] * len(columns)
        + [ANY] * cores
        + [VMEM] * 4,
        out_specs=VMEM,
        scratch_shapes=[
            pltpu.VMEM((parts,) + projected.shape, BF16),
            pltpu.VMEM((slices, cores, 2 * width, equals * share), BF16),
            pltpu.VMEM((8, parts // clip_parts, width, clip_cells), BF16),
            pltpu.VMEM((parts * cells // 8 + (quarter + 1) * quarter + 8, wide), F32),
            pltpu.VMEM((2, TAPS, width, wide), F32),
            pltpu.SemaphoreType.DMA((parts,)),
        ],
        compiler_params=pltpu.CompilerParams(vmem_limit_bytes=40 << 20),
    )(
        place, chip_at, core_at, half_at,
        *columns, *left_rows, left_panels, mixers, shift_picks, sort_picks,
    )
    return result.transpose(0, 1, 3, 2)


def solution(mesh):
    fsdp, replica, tm = (mesh.shape[axis] for axis in ("fsdp", "replica", "tm"))
    cores = 2 if replica % 2 == 0 else 1
    assert mesh.axis_names == ("fsdp", "replica", "tm")
    mesh = Mesh(
        mesh.devices.reshape(fsdp, replica // cores, cores, tm), ("fsdp", "chip", "core", "tm")
    )
    replica = ("chip", "core")
    in_specs = (
        P(replica, "tm", None, None, None),
        P(None, None, "fsdp"),
        P(None, "fsdp", None),
        P(replica, "tm", None, None, None),
        P(),
        P(None, "fsdp", None),
        P(None, "fsdp", (*replica, "tm")),
    )
    out_specs = P(None, None, "fsdp", (*replica, "tm"))
    return jax.shard_map(shards, mesh=mesh, in_specs=in_specs, out_specs=out_specs, check_vma=False)
```

```python
import functools

import jax
import jax.numpy as jnp
import numpy as np
from jax import lax
from jax.experimental import pallas as pl
from jax.experimental.pallas import tpu as pltpu
from jax.sharding import Mesh, PartitionSpec as P

TAPS = 27
F32, BF16 = jnp.float32, jnp.bfloat16
ROOM = 50 << 20
PROJECT_COST = 16 << 20
HIDDEN_COST = 200 << 20
NT = (((1,), (1,)), ((), ()))
VMEM = pl.BlockSpec(memory_space=pltpu.VMEM)
HBM = pl.BlockSpec(memory_space=pltpu.HBM)
SMEM = pl.BlockSpec(memory_space=pltpu.SMEM)
ANY = pl.BlockSpec(memory_space=pl.ANY)


def shifted(block, axis, distance):
    devices = range(lax.axis_size(axis))
    route = [(i - distance, i) for i in devices if i - distance in devices]
    return lax.ppermute(block, axis, route)


def dot(left, right):
    return jnp.dot(left, right, preferred_element_type=F32)


def dot_nt(left, right):
    return lax.dot_general(left, right, NT, preferred_element_type=F32)


def quotient(value, size):
    return value >> (size.bit_length() - 1) if size & (size - 1) == 0 else value // size


def remainder(value, size):
    return value & (size - 1) if size & (size - 1) == 0 else value % size


def halves(value):
    high = value.astype(BF16)
    return high, (value - high.astype(F32)).astype(BF16)


def column_picks(side):
    half = side // 2
    picks = np.zeros((2, half, half, half, side), np.float32)
    for row in range(half):
        for x in range(side):
            picks[x % 2, row, x // 2, row, x] = 1
    return picks.reshape(half * side, half * side)


def spread_picks(half):
    quarter = half // 2
    picks = np.zeros((3, 3, half, half, quarter, quarter), np.float32)
    for b in range(3):
        for c in range(3):
            for out_y in range(quarter):
                for out_x in range(quarter):
                    y, x = 2 * out_y + b - 1, 2 * out_x + c - 1
                    if y >= 0 and x >= 0:
                        picks[b, c, y, x, out_y, out_x] = 1
    return picks.reshape(9 * half * half, quarter * quarter)


def parity_rows(lines, pick):
    rows = dot(pick, lines).astype(BF16)
    cells = rows.shape[0] // 2
    return rows[:cells], rows[cells:]


def folded_taps(rows, weights, shift_ref, half):
    sums = {}
    for line, column in np.ndindex(2, 2):
        taps = [(b, c) for b in ((2, 0) if line else (1,)) for c in ((2, 0) if column else (1,))]
        product = dot(rows(line, column), jnp.concatenate([weights(*tap) for tap in taps], axis=1))
        wide = product.shape[1] // len(taps)
        for at, (b, c) in enumerate(taps):
            part = product[:, at * wide : (at + 1) * wide]
            key = (int(b == 0), int(c == 0))
            sums[key] = sums[key] + part if key in sums else part
    total = sums.pop((0, 0))
    count, wide = total.shape
    pad = shift_ref.shape[1] - count
    places = lax.broadcasted_iota(jnp.int32, (count, wide), 0)
    row = remainder(quotient(places, half), half)
    column = remainder(places, half)
    for at, ((dr, dc), part) in enumerate(sums.items()):
        shift_ref[at, pl.ds(pad, count), :] = part
        moved = shift_ref[at, pl.ds(pad - (dr * half + dc), count), :]
        total += jnp.where((row >= dr) & (column >= dc), moved, 0.0)
    return total


def project_kernel(
    x_any, left_any, grad_any, pick_any, first_any,
    out_ref, halo_ref, x_ref, left_ref, grad_ref, pick_ref, first_ref, rows_ref, shift_ref, arrived,
):
    frames, half, _, side, channels = x_ref.shape
    order = [frame for time in (1, 0) for frame in range(time, frames, 2)]
    pairs_of = [
        (left_any.at[0], left_ref),
        (x_any.at[order[0]], x_ref.at[order[0]]),
        (x_any.at[order[1]], x_ref.at[order[1]]),
        (pick_any, pick_ref),
        (first_any.at[pl.ds(0, 9)], first_ref),
        (x_any.at[order[2]], x_ref.at[order[2]]),
        (x_any.at[order[3]], x_ref.at[order[3]]),
        (grad_any, grad_ref),
    ]
    copies = [
        pltpu.make_async_copy(source, target, arrived.at[at])
        for at, (source, target) in enumerate(pairs_of)
    ]
    for copy in copies:
        copy.start()
    wide = left_ref.shape[0]
    pairs = frames // 2
    size = pairs * half * side
    target = lax.broadcasted_iota(jnp.int32, (size, size), 0)
    source = lax.broadcasted_iota(jnp.int32, (size, size), 1)
    cells = size // 2
    wanted = 2 * remainder(target, cells) + quotient(target, cells)
    pick = jnp.where(source == wanted, 1.0, 0.0).astype(BF16)
    copies[0].wait()
    both = jnp.concatenate(halves(left_ref[...]), axis=0)

    def project(time):
        for row in range(2):
            block = jnp.concatenate(
                [
                    x_ref[frame, :, row].reshape(half * side, channels)
                    for frame in range(time, frames, 2)
                ],
                axis=0,
            )
            full = dot_nt(block, both)
            small = (full[:, :wide] + full[:, wide:]).astype(BF16)
            ordered = dot(pick, small).astype(BF16)
            at = (4 * time + 2 * row) * cells
            out_ref[at : at + size, :] = ordered

    copies[1].wait()
    copies[2].wait()
    project(1)
    copies[3].wait()
    classes = [
        parity_rows(x_ref[frames - 1, :, line].reshape(half * side, channels), pick_ref[...])
        for line in range(2)
    ]
    copies[4].wait()
    halo_ref[pl.ds(0, half * half), :] = folded_taps(
        lambda line, column: classes[line][column],
        lambda b, c: first_ref[3 * b + c],
        shift_ref,
        half,
    )
    copies[5].wait()
    copies[6].wait()
    project(0)
    copies[7].wait()
    grad_rows = stacked_rows(grad_ref, rows_ref)
    count = grad_rows.shape[0]
    for block in range(channels // wide):
        at = 8 * cells + block * count
        out_ref[at : at + count, :] = grad_rows[:, block * wide : (block + 1) * wide]
        at = half * half + block * count
        halo_ref[at : at + count, :] = rows_ref[:, block * wide : (block + 1) * wide]


def stacked_rows(grad_ref, rows_ref):
    quarter = grad_ref.shape[0]
    for row in range(quarter):
        rows_ref[pl.ds(row * quarter, quarter), :] = grad_ref[row].astype(F32)
    return rows_ref[...].astype(BF16)


def transposed_products(rows, kernel, taps):
    total = dot_nt(rows[0], kernel[taps[0]])
    for at in range(1, len(taps)):
        total += dot_nt(rows[at], kernel[taps[at]])
    return total


def spread_rows(picks_ref, rows, cells):
    spread = dot(picks_ref[...], rows).astype(BF16)
    return [spread[tap * cells : (tap + 1) * cells] for tap in range(9)]


def hidden_kernel(
    tm_ref, x_ref, prior_ref, grad_ref, later_ref, pick_ref, spread_ref,
    first_any, second_any, out_ref, rows_ref, classes, first, second, shift_ref, arrived, *,
    clip_parts,
):
    frames, half, _, side, channels = x_ref.shape
    cells = half * half
    has_prior = jnp.where(tm_ref[0] > 0, 1.0, 0.0)
    has_later = jnp.where(tm_ref[0] < clip_parts - 1, 1.0, 0.0)
    copies = {
        (at, a): pltpu.make_async_copy(
            source.at[pl.ds(9 * a, 9)], target.at[pl.ds(9 * a, 9)], arrived.at[at, a]
        )
        for at, (source, target) in enumerate(((second_any, second), (first_any, first)))
        for a in (1, 2, 0)
    }
    for copy in copies.values():
        copy.start()
    own_rows = stacked_rows(grad_ref, rows_ref)
    own = spread_rows(spread_ref, own_rows, cells)
    copies[0, 1].wait()
    copies[0, 2].wait()
    both = None
    for tap in range(9):
        pair = jnp.concatenate([second[9 + tap], second[18 + tap]], axis=0)
        term = dot_nt(own[tap], pair)
        both = term if both is None else both + term
    early, late = both[:, : second.shape[1]], both[:, second.shape[1] :]
    for frame in range(frames):
        for line in range(2):
            lines = x_ref[frame, :, line].reshape(half * side, channels)
            classes[frame, line, 0], classes[frame, line, 1] = parity_rows(lines, pick_ref[...])
    count = own_rows.shape[0]
    wide = first.shape[2]
    later_rows = jnp.concatenate(
        [
            later_ref[pl.ds(cells + count * block, count), :]
            for block in range(channels // wide)
        ],
        axis=1,
    )
    after = spread_rows(spread_ref, later_rows.astype(BF16), cells)
    copies[0, 0].wait()
    late += transposed_products(after, second, range(9)) * has_later
    hidden_grad = jnp.concatenate([early, late], axis=0)
    nothing = jnp.zeros((cells, channels), BF16)

    def rows_of(line, column):
        held = [classes[frame, line, column] for frame in range(frames)]
        return jnp.concatenate(
            [
                jnp.concatenate([nothing, held[0], held[1]], axis=1),
                jnp.concatenate([held[1], held[2], held[3]], axis=1),
            ],
            axis=0,
        )

    for a in (1, 2, 0):
        copies[1, a].wait()
    pre = folded_taps(
        rows_of,
        lambda b, c: jnp.concatenate([first[9 * a + 3 * b + c] for a in range(3)], axis=0),
        shift_ref,
        half,
    )
    pre += jnp.concatenate(
        [prior_ref[pl.ds(0, cells), :] * has_prior, jnp.zeros((cells, wide), F32)], axis=0
    )
    sig = jax.nn.sigmoid(pre)
    hidden = (pre * sig).astype(BF16)
    pre_grad = (hidden_grad * sig * (1.0 + pre * (1.0 - sig))).astype(BF16)
    groups, slices, _, share, _ = out_ref.shape
    for at in range(slices):
        place = slice(at * share, (at + 1) * share)
        for group in range(groups):
            out_ref[group, at, 0] = pre_grad[place]
            out_ref[group, at, 1] = hidden[place]


def right_kernel(place_ref, core_ref, *refs, cores):
    acts_refs, right_refs, out_ref = refs[:cores], refs[cores:-1], refs[-1]
    parts, slices = acts_refs[0].shape[:2]
    width = right_refs[0].shape[1]
    for layer in range(2):
        rights = [jnp.concatenate(halves(ref[layer]), axis=0) for ref in right_refs]
        for cross, acts_ref in enumerate(acts_refs):
            total = None
            for distance in range(slices):
                origin = lax.rem(place_ref[0] + (slices - distance), slices)
                rows = jnp.concatenate(
                    [acts_ref[part, origin, layer] for part in range(parts)], axis=0
                )
                term = dot_nt(rights[distance], rows)
                total = term if total is None else total + term
            core = lax.rem(core_ref[0] + cross, cores)
            out_ref[core, pl.ds(layer * width, width), :] = (total[:width] + total[width:]).astype(
                BF16
            )


def tables_kernel(after_any, mix_ref, shift_ref, sort_ref, mixers_ref, *, slices, clip_parts, half):
    del after_any
    size = shift_ref.shape[0]
    cells = size // clip_parts
    share = cells // slices
    frames = size // (half * half)
    held = lax.broadcasted_iota(jnp.int32, (size, size), 0)
    cell = lax.broadcasted_iota(jnp.int32, (size, size), 1)
    part = remainder(quotient(held, share), clip_parts)
    slot = quotient(held, share * clip_parts)
    natural = part * cells + slot * share + remainder(held, share)
    frame = quotient(cell, half * half)
    row = remainder(quotient(cell, half), half)
    column = remainder(cell, half)
    for shift in range(8):
        dt, dr, dc = shift // 4, shift // 2 % 2, shift % 2
        found = natural == cell + ((dt * half + dr) * half + dc)
        if dt:
            found &= frame < frames - 1
        if dr:
            found &= row < half - 1
        if dc:
            found &= column < half - 1
        shift_ref[:, pl.ds(shift * size, size)] = jnp.where(found, 1.0, 0.0).astype(BF16)
    quarter = half // 2
    outputs = size // 8
    kind = quotient(cell, outputs)
    frame = 2 * remainder(quotient(cell, quarter * quarter), frames // 2) + quotient(kind, 4)
    row = 2 * remainder(quotient(cell, quarter), quarter) + remainder(quotient(kind, 2), 2)
    column = 2 * remainder(cell, quarter) + remainder(kind, 2)
    found = natural == (frame * half + row) * half + column
    sort_ref[...] = jnp.where(found, 1.0, 0.0).astype(BF16)

    count = mixers_ref.shape[2]
    tap = lax.broadcasted_iota(jnp.int32, (count, TAPS), 1)
    line = lax.broadcasted_iota(jnp.int32, (count, TAPS), 0)
    spread = jnp.where(quotient(line, 8) == tap, 1.0, 0.0).astype(BF16)
    lines = lax.broadcasted_iota(jnp.int32, (count, count), 0)
    others = lax.broadcasted_iota(jnp.int32, (count, count), 1)
    same = remainder(lines, 8) == remainder(others, 8)
    for layer in range(2):
        for at, part in enumerate(halves(mix_ref[layer])):
            wider = dot_nt(dot(spread, part).astype(BF16), spread)
            mixers_ref[layer, at] = jnp.where(same, wider, 0.0).astype(BF16)


def update_kernel(
    place_ref, chip_ref, core_ref, tm_ref, *refs, slices, cores, clip_parts, half
):
    columns_refs, piece_refs = refs[:slices], refs[slices : slices + cores]
    (
        left_ref, mixers_ref, shift_ref, sort_ref,
        out_ref, left_rows_ref, columns, shifts, grads, raw, arrived,
    ) = refs[slices + cores :]
    parts = left_rows_ref.shape[0]
    chips = parts // (cores * clip_parts)
    copies = []
    for cross, piece_ref in enumerate(piece_refs):
        core = lax.rem(core_ref[0] + cross, cores)
        for at, (step, turn) in enumerate(np.ndindex(chips, clip_parts)):
            chip = lax.rem(chip_ref[0] + (chips - step), chips)
            place = lax.rem(tm_ref[0] + (clip_parts - turn), clip_parts)
            target = left_rows_ref.at[(chip * cores + core) * clip_parts + place]
            copies.append(
                pltpu.make_async_copy(piece_ref.at[at], target, arrived.at[len(copies)])
            )
    for copy in copies:
        copy.start()
    for distance in range(slices):
        origin = lax.rem(place_ref[0] + (slices - distance), slices)
        columns[origin] = columns_refs[distance][...]
    wide, channels = left_ref.shape[1:]
    width = columns.shape[2] // 2
    clips = parts // clip_parts
    share = columns.shape[3] // chips
    clip_cells = slices * share
    cells = clip_cells // clip_parts
    frames = clip_cells // (half * half)
    outputs = clip_cells // 8

    def by_clip(layer):
        return jnp.concatenate(
            [
                jnp.concatenate(
                    [
                        columns[
                            at, clip % cores, pl.ds(layer * width, width),
                            pl.ds(clip // cores * share, share),
                        ]
                        for at in range(slices)
                    ],
                    axis=1,
                )
                for clip in range(clips)
            ],
            axis=0,
        )

    first = by_clip(0)
    for shift in range(8):
        moved = dot(first, shift_ref[:, pl.ds(shift * clip_cells, clip_cells)]).astype(BF16)
        for clip in range(clips):
            shifts[shift, clip] = moved[clip * width : (clip + 1) * width]
    second = dot(by_clip(1), sort_ref[...]).astype(BF16)

    for copy in copies:
        copy.wait()
    own_outputs = outputs // clip_parts
    blocks = channels // wide
    out_grad = jnp.concatenate(
        [
            jnp.concatenate(
                [
                    left_rows_ref[part, pl.ds(8 * cells + own_outputs * at, own_outputs), :]
                    for at in range(blocks)
                ],
                axis=1,
            )
            for part in range(parts)
        ],
        axis=0,
    )
    full = dot_nt(out_grad, jnp.concatenate(halves(left_ref[1]), axis=0))
    total = parts * own_outputs
    quarter = half // 2
    grads[pl.ds(0, total), :] = full[:, :wide] + full[:, wide:]
    places = lax.broadcasted_iota(jnp.int32, (total, wide), 0)
    frame = remainder(quotient(places, quarter * quarter), frames // 2)
    row = remainder(quotient(places, quarter), quarter)
    column = remainder(places, quarter)
    second_rows = []
    for shift in range(8):
        dt, dr, dc = shift // 4, shift // 2 % 2, shift % 2
        moved = grads[pl.ds((dt * quarter + dr) * quarter + dc, total), :]
        inside = (frame + dt < frames // 2) & (row + dr < quarter) & (column + dc < quarter)
        second_rows.append(jnp.where(inside, moved, 0.0).astype(BF16))

    for time, line in np.ndindex(2, 2):
        even = [
            (9 * a + 3 * b + 1, 4 * (a == 0) + 2 * (b == 0))
            for a in ((0, 2) if time else (1,))
            for b in ((0, 2) if line else (1,))
        ]
        odd = [(tap + 1, shift) for tap, shift in even] + [
            (tap - 1, shift + 1) for tap, shift in even
        ]
        kind = 4 * time + 2 * line
        sums = None
        for clip in range(clips):
            left = jnp.concatenate([shifts[shift, clip] for _, shift in odd], axis=0)
            rows = jnp.concatenate(
                [
                    jnp.concatenate(
                        [
                            left_rows_ref[
                                clip * clip_parts + part, pl.ds((kind + at) * cells, cells), :
                            ]
                            for part in range(clip_parts)
                        ],
                        axis=0,
                    )
                    for at in range(2)
                ],
                axis=1,
            )
            term = dot(left, rows)
            sums = term if sums is None else sums + term
        for at, (tap, _) in enumerate(even):
            raw[0, tap] = sums[at * width : (at + 1) * width, :wide]
        for at, (tap, _) in enumerate(odd):
            raw[0, tap] = sums[at * width : (at + 1) * width, wide:]
        for place, taps in enumerate((even, odd)):
            chosen = jnp.concatenate(
                [
                    second[
                        clip * width : (clip + 1) * width,
                        (kind + place) * outputs : (kind + place + 1) * outputs,
                    ]
                    for clip in range(clips)
                ],
                axis=1,
            )
            products = dot(
                chosen, jnp.concatenate([second_rows[shift] for _, shift in taps], axis=1)
            )
            for at, (tap, _) in enumerate(taps):
                raw[1, tap] = products[:, at * wide : (at + 1) * wide]

    for layer in range(2):
        for group in range(width // 16):
            lanes = jnp.concatenate(
                [
                    raw[layer, :, pl.ds(16 * group + 8 * at, 8), :].reshape(8 * TAPS, wide)
                    for at in range(2)
                ],
                axis=1,
            )
            high, low = halves(lanes)
            mixed = (
                dot(mixers_ref[layer, 0], high)
                + dot(mixers_ref[layer, 0], low)
                + dot(mixers_ref[layer, 1], high)
            )
            rows = jnp.concatenate(
                [
                    mixed[:, at * wide : (at + 1) * wide].reshape(TAPS, 8, wide)
                    for at in range(2)
                ],
                axis=1,
            )
            out_ref[layer, :, pl.ds(16 * group, 16), :] = rows.astype(BF16)


def turned(block, axes, steps):
    sizes = [lax.axis_size(axis) for axis in axes]
    if not any(step % size for step, size in zip(steps, sizes)):
        return block
    route = []
    for place in np.ndindex(*sizes):
        target = [(at + step) % size for at, step, size in zip(place, steps, sizes)]
        route.append(
            (int(np.ravel_multi_index(place, sizes)), int(np.ravel_multi_index(target, sizes)))
        )
    return lax.ppermute(block, axes, route)


def shards(clip_input, first_kernel, second_kernel, out_grad, tap_mix, left_panels, right_panels):
    clips, frames, side, _, channels = clip_input.shape
    wide = first_kernel.shape[2]
    width = right_panels.shape[2]
    half, quarter = side // 2, side // 4
    half_frames = frames // 2
    cells = half_frames * half * half
    clip_parts = lax.axis_size("tm")
    cores, chips = lax.axis_size("core"), lax.axis_size("chip")
    equals = chips * clip_parts
    parts = equals * cores
    slices = lax.axis_size("fsdp")
    share = cells // slices
    assert clips == 1 and frames == 4
    x = clip_input.reshape(frames, half, 2, side, channels)
    grad = out_grad.reshape(quarter, quarter, channels)
    place, chip_at, core_at, half_at = (
        lax.axis_index(axis).reshape(1) for axis in ("fsdp", "chip", "core", "tm")
    )

    pick = jnp.asarray(column_picks(side), BF16)
    pad = (half // 8 + 1) * 8
    rows = quarter * quarter * channels // wide
    projected, halo = pl.pallas_call(
        project_kernel,
        out_shape=(
            jax.ShapeDtypeStruct((8 * cells + rows, wide), BF16),
            jax.ShapeDtypeStruct((half * half + rows, wide), F32),
        ),
        in_specs=[ANY] * 5,
        out_specs=(VMEM, VMEM),
        scratch_shapes=[
            pltpu.VMEM(x.shape, BF16),
            pltpu.VMEM(left_panels.shape[1:], F32),
            pltpu.VMEM(grad.shape, BF16),
            pltpu.VMEM(pick.shape, BF16),
            pltpu.VMEM((9,) + first_kernel.shape[1:], BF16),
            pltpu.VMEM((quarter * quarter, channels), F32),
            pltpu.VMEM((3, pad + half * half, wide), F32),
            pltpu.SemaphoreType.DMA((8,)),
        ],
        compiler_params=pltpu.CompilerParams(vmem_limit_bytes=58 << 20),
        cost_estimate=pl.CostEstimate(
            flops=4 * frames * side * side * channels * wide,
            bytes_accessed=PROJECT_COST,
            transcendentals=0,
        ),
    )(x, left_panels, grad, pick, first_kernel)
    if clip_parts == 2:
        prior = later = lax.ppermute(halo, "tm", [(0, 1), (1, 0)])
    else:
        prior, later = shifted(halo, "tm", 1), shifted(halo, "tm", -1)
    right = right_panels.transpose(0, 2, 1)
    right = [turned(right, ("fsdp",), (distance,)) for distance in range(slices)]
    projected, right = lax.optimization_barrier((projected, right))
    held = jnp.stack(
        [
            turned(projected, ("chip", "tm"), steps)
            for steps in np.ndindex(chips, clip_parts)
        ]
    )

    spread = jnp.asarray(spread_picks(half), BF16)
    acts = pl.pallas_call(
        functools.partial(hidden_kernel, clip_parts=clip_parts),
        out_shape=jax.ShapeDtypeStruct((equals, slices, 2, share, wide), BF16),
        in_specs=[SMEM] + [VMEM] * 6 + [HBM] * 2,
        out_specs=VMEM,
        scratch_shapes=[
            pltpu.VMEM((quarter * quarter, channels), F32),
            pltpu.VMEM((frames, 2, 2, half * half, channels), BF16),
            pltpu.VMEM(first_kernel.shape, BF16),
            pltpu.VMEM(second_kernel.shape, BF16),
            pltpu.VMEM((3, pad + cells, wide), F32),
            pltpu.SemaphoreType.DMA((2, 3)),
        ],
        compiler_params=pltpu.CompilerParams(vmem_limit_bytes=ROOM),
        cost_estimate=pl.CostEstimate(
            flops=3 * cells * TAPS * channels * wide,
            bytes_accessed=HIDDEN_COST,
            transcendentals=cells * wide,
        ),
    )(
        half_at, x, prior, grad, later, pick, spread, first_kernel, second_kernel,
    )
    acts, *right = lax.optimization_barrier((acts, *right))
    clip_cells = clip_parts * cells
    shift_picks, sort_picks, mixers = pl.pallas_call(
        functools.partial(tables_kernel, slices=slices, clip_parts=clip_parts, half=half),
        out_shape=(
            jax.ShapeDtypeStruct((clip_cells, 8 * clip_cells), BF16),
            jax.ShapeDtypeStruct((clip_cells, clip_cells), BF16),
            jax.ShapeDtypeStruct((2, 2, 8 * TAPS, 8 * TAPS), BF16),
        ),
        in_specs=[ANY, VMEM],
        out_specs=(VMEM,) * 3,
        compiler_params=pltpu.CompilerParams(vmem_limit_bytes=16 << 20),
        cost_estimate=pl.CostEstimate(flops=0, bytes_accessed=4 << 20, transcendentals=0),
    )(acts, tap_mix)
    every = lax.all_to_all(
        acts.reshape(equals * slices, 2, share, wide), ("chip", "tm", "fsdp"), 0, 0, tiled=True
    ).reshape(equals, slices, 2, share, wide)
    every, held = lax.optimization_barrier((every, held))
    every = [turned(every, ("core",), (cross,)) for cross in range(cores)]
    columns = pl.pallas_call(
        functools.partial(right_kernel, cores=cores),
        out_shape=jax.ShapeDtypeStruct((cores, 2 * width, equals * share), BF16),
        in_specs=[SMEM] * 2 + [VMEM] * (cores + slices),
        out_specs=VMEM,
        compiler_params=pltpu.CompilerParams(vmem_limit_bytes=16 << 20),
    )(place, core_at, *every, *right)
    columns, held = lax.optimization_barrier((columns, held))
    columns = [turned(columns, ("fsdp",), (distance,)) for distance in range(slices)]
    left_rows = [turned(held, ("core",), (cross,)) for cross in range(cores)]

    result = pl.pallas_call(
        functools.partial(
            update_kernel, slices=slices, cores=cores, clip_parts=clip_parts, half=half
        ),
        out_shape=jax.ShapeDtypeStruct((2, TAPS, width, wide), BF16),
        in_specs=[SMEM] * 4
        + [VMEM] * len(columns)
        + [ANY] * cores
        + [VMEM] * 4,
        out_specs=VMEM,
        scratch_shapes=[
            pltpu.VMEM((parts,) + projected.shape, BF16),
            pltpu.VMEM((slices, cores, 2 * width, equals * share), BF16),
            pltpu.VMEM((8, parts // clip_parts, width, clip_cells), BF16),
            pltpu.VMEM((parts * cells // 8 + (quarter + 1) * quarter + 8, wide), F32),
            pltpu.VMEM((2, TAPS, width, wide), F32),
            pltpu.SemaphoreType.DMA((parts,)),
        ],
        compiler_params=pltpu.CompilerParams(vmem_limit_bytes=40 << 20),
    )(
        place, chip_at, core_at, half_at,
        *columns, *left_rows, left_panels, mixers, shift_picks, sort_picks,
    )
    return result.transpose(0, 1, 3, 2)


def solution(mesh):
    fsdp, replica, tm = (mesh.shape[axis] for axis in ("fsdp", "replica", "tm"))
    cores = 2 if replica % 2 == 0 else 1
    assert mesh.axis_names == ("fsdp", "replica", "tm")
    mesh = Mesh(
        mesh.devices.reshape(fsdp, replica // cores, cores, tm), ("fsdp", "chip", "core", "tm")
    )
    replica = ("chip", "core")
    in_specs = (
        P(replica, "tm", None, None, None),
        P(None, None, "fsdp"),
        P(None, "fsdp", None),
        P(replica, "tm", None, None, None),
        P(),
        P(None, "fsdp", None),
        P(None, "fsdp", (*replica, "tm")),
    )
    out_specs = P(None, None, "fsdp", (*replica, "tm"))
    return jax.shard_map(shards, mesh=mesh, in_specs=in_specs, out_specs=out_specs, check_vma=False)
```

```python
import functools

import jax
import jax.numpy as jnp
import numpy as np
from jax import lax
from jax.experimental import pallas as pl
from jax.experimental.pallas import tpu as pltpu
from jax.sharding import Mesh, PartitionSpec as P

TAPS = 27
F32, BF16 = jnp.float32, jnp.bfloat16
ROOM = 50 << 20
PROJECT_COST = 16 << 20
HIDDEN_COST = 200 << 20
NT = (((1,), (1,)), ((), ()))
VMEM = pl.BlockSpec(memory_space=pltpu.VMEM)
HBM = pl.BlockSpec(memory_space=pltpu.HBM)
SMEM = pl.BlockSpec(memory_space=pltpu.SMEM)
ANY = pl.BlockSpec(memory_space=pl.ANY)


def shifted(block, axis, distance):
    devices = range(lax.axis_size(axis))
    route = [(i - distance, i) for i in devices if i - distance in devices]
    return lax.ppermute(block, axis, route)


def dot(left, right):
    return jnp.dot(left, right, preferred_element_type=F32)


def dot_nt(left, right):
    return lax.dot_general(left, right, NT, preferred_element_type=F32)


def quotient(value, size):
    return value >> (size.bit_length() - 1) if size & (size - 1) == 0 else value // size


def remainder(value, size):
    return value & (size - 1) if size & (size - 1) == 0 else value % size


def halves(value):
    high = value.astype(BF16)
    return high, (value - high.astype(F32)).astype(BF16)


def column_picks(side):
    half = side // 2
    picks = np.zeros((2, half, half, half, side), np.float32)
    for row in range(half):
        for x in range(side):
            picks[x % 2, row, x // 2, row, x] = 1
    return picks.reshape(half * side, half * side)


def spread_picks(half):
    quarter = half // 2
    picks = np.zeros((3, 3, half, half, quarter, quarter), np.float32)
    for b in range(3):
        for c in range(3):
            for out_y in range(quarter):
                for out_x in range(quarter):
                    y, x = 2 * out_y + b - 1, 2 * out_x + c - 1
                    if y >= 0 and x >= 0:
                        picks[b, c, y, x, out_y, out_x] = 1
    return picks.reshape(9 * half * half, quarter * quarter)


def parity_rows(lines, pick):
    rows = dot(pick, lines).astype(BF16)
    cells = rows.shape[0] // 2
    return rows[:cells], rows[cells:]


def folded_taps(rows, weights, shift_ref, half):
    sums = {}
    for line, column in np.ndindex(2, 2):
        taps = [(b, c) for b in ((2, 0) if line else (1,)) for c in ((2, 0) if column else (1,))]
        product = dot(rows(line, column), jnp.concatenate([weights(*tap) for tap in taps], axis=1))
        wide = product.shape[1] // len(taps)
        for at, (b, c) in enumerate(taps):
            part = product[:, at * wide : (at + 1) * wide]
            key = (int(b == 0), int(c == 0))
            sums[key] = sums[key] + part if key in sums else part
    total = sums.pop((0, 0))
    count, wide = total.shape
    pad = shift_ref.shape[1] - count
    places = lax.broadcasted_iota(jnp.int32, (count, wide), 0)
    row = remainder(quotient(places, half), half)
    column = remainder(places, half)
    for at, ((dr, dc), part) in enumerate(sums.items()):
        shift_ref[at, pl.ds(pad, count), :] = part
        moved = shift_ref[at, pl.ds(pad - (dr * half + dc), count), :]
        total += jnp.where((row >= dr) & (column >= dc), moved, 0.0)
    return total


def project_kernel(
    x_any, left_any, grad_any, pick_any, first_any,
    out_ref, halo_ref, x_ref, left_ref, grad_ref, pick_ref, first_ref, rows_ref, shift_ref, arrived,
):
    frames, half, _, side, channels = x_ref.shape
    order = [frame for time in (1, 0) for frame in range(time, frames, 2)]
    pairs_of = [
        (left_any.at[0], left_ref),
        (x_any.at[order[0]], x_ref.at[order[0]]),
        (x_any.at[order[1]], x_ref.at[order[1]]),
        (pick_any, pick_ref),
        (first_any.at[pl.ds(0, 9)], first_ref),
        (x_any.at[order[2]], x_ref.at[order[2]]),
        (x_any.at[order[3]], x_ref.at[order[3]]),
        (grad_any, grad_ref),
    ]
    copies = [
        pltpu.make_async_copy(source, target, arrived.at[at])
        for at, (source, target) in enumerate(pairs_of)
    ]
    for copy in copies:
        copy.start()
    wide = left_ref.shape[0]
    pairs = frames // 2
    size = pairs * half * side
    target = lax.broadcasted_iota(jnp.int32, (size, size), 0)
    source = lax.broadcasted_iota(jnp.int32, (size, size), 1)
    cells = size // 2
    wanted = 2 * remainder(target, cells) + quotient(target, cells)
    pick = jnp.where(source == wanted, 1.0, 0.0).astype(BF16)
    copies[0].wait()
    both = jnp.concatenate(halves(left_ref[...]), axis=0)

    def project(time):
        for row in range(2):
            block = jnp.concatenate(
                [
                    x_ref[frame, :, row].reshape(half * side, channels)
                    for frame in range(time, frames, 2)
                ],
                axis=0,
            )
            full = dot_nt(block, both)
            small = (full[:, :wide] + full[:, wide:]).astype(BF16)
            ordered = dot(pick, small).astype(BF16)
            at = (4 * time + 2 * row) * cells
            out_ref[at : at + size, :] = ordered

    copies[1].wait()
    copies[2].wait()
    project(1)
    copies[3].wait()
    classes = [
        parity_rows(x_ref[frames - 1, :, line].reshape(half * side, channels), pick_ref[...])
        for line in range(2)
    ]
    copies[4].wait()
    halo_ref[pl.ds(0, half * half), :] = folded_taps(
        lambda line, column: classes[line][column],
        lambda b, c: first_ref[3 * b + c],
        shift_ref,
        half,
    )
    copies[5].wait()
    copies[6].wait()
    project(0)
    copies[7].wait()
    grad_rows = stacked_rows(grad_ref, rows_ref)
    count = grad_rows.shape[0]
    for block in range(channels // wide):
        at = 8 * cells + block * count
        out_ref[at : at + count, :] = grad_rows[:, block * wide : (block + 1) * wide]
        at = half * half + block * count
        halo_ref[at : at + count, :] = rows_ref[:, block * wide : (block + 1) * wide]


def stacked_rows(grad_ref, rows_ref):
    quarter = grad_ref.shape[0]
    for row in range(quarter):
        rows_ref[pl.ds(row * quarter, quarter), :] = grad_ref[row].astype(F32)
    return rows_ref[...].astype(BF16)


def transposed_products(rows, kernel, taps):
    total = dot_nt(rows[0], kernel[taps[0]])
    for at in range(1, len(taps)):
        total += dot_nt(rows[at], kernel[taps[at]])
    return total


def spread_rows(picks_ref, rows, cells):
    spread = dot(picks_ref[...], rows).astype(BF16)
    return [spread[tap * cells : (tap + 1) * cells] for tap in range(9)]


def hidden_kernel(
    tm_ref, x_ref, prior_ref, grad_ref, later_ref, pick_ref, spread_ref,
    first_any, second_any, out_ref, rows_ref, classes, first, second, shift_ref, arrived, *,
    clip_parts,
):
    frames, half, _, side, channels = x_ref.shape
    cells = half * half
    has_prior = jnp.where(tm_ref[0] > 0, 1.0, 0.0)
    has_later = jnp.where(tm_ref[0] < clip_parts - 1, 1.0, 0.0)
    copies = {
        (at, a): pltpu.make_async_copy(
            source.at[pl.ds(9 * a, 9)], target.at[pl.ds(9 * a, 9)], arrived.at[at, a]
        )
        for at, (source, target) in enumerate(((second_any, second), (first_any, first)))
        for a in (1, 2, 0)
    }
    for copy in copies.values():
        copy.start()
    own_rows = stacked_rows(grad_ref, rows_ref)
    own = spread_rows(spread_ref, own_rows, cells)
    copies[0, 1].wait()
    copies[0, 2].wait()
    both = None
    for tap in range(9):
        pair = jnp.concatenate([second[9 + tap], second[18 + tap]], axis=0)
        term = dot_nt(own[tap], pair)
        both = term if both is None else both + term
    early, late = both[:, : second.shape[1]], both[:, second.shape[1] :]
    for frame in range(frames):
        for line in range(2):
            lines = x_ref[frame, :, line].reshape(half * side, channels)
            classes[frame, line, 0], classes[frame, line, 1] = parity_rows(lines, pick_ref[...])
    count = own_rows.shape[0]
    wide = first.shape[2]
    later_rows = jnp.concatenate(
        [
            later_ref[pl.ds(cells + count * block, count), :]
            for block in range(channels // wide)
        ],
        axis=1,
    )
    after = spread_rows(spread_ref, later_rows.astype(BF16), cells)
    copies[0, 0].wait()
    late += transposed_products(after, second, range(9)) * has_later
    hidden_grad = jnp.concatenate([early, late], axis=0)
    nothing = jnp.zeros((cells, channels), BF16)

    def rows_of(line, column):
        held = [classes[frame, line, column] for frame in range(frames)]
        return jnp.concatenate(
            [
                jnp.concatenate([nothing, held[0], held[1]], axis=1),
                jnp.concatenate([held[1], held[2], held[3]], axis=1),
            ],
            axis=0,
        )

    for a in (1, 2, 0):
        copies[1, a].wait()
    pre = folded_taps(
        rows_of,
        lambda b, c: jnp.concatenate([first[9 * a + 3 * b + c] for a in range(3)], axis=0),
        shift_ref,
        half,
    )
    pre += jnp.concatenate(
        [prior_ref[pl.ds(0, cells), :] * has_prior, jnp.zeros((cells, wide), F32)], axis=0
    )
    sig = jax.nn.sigmoid(pre)
    hidden = (pre * sig).astype(BF16)
    pre_grad = (hidden_grad * sig * (1.0 + pre * (1.0 - sig))).astype(BF16)
    groups, slices, _, share, _ = out_ref.shape
    for at in range(slices):
        place = slice(at * share, (at + 1) * share)
        for group in range(groups):
            out_ref[group, at, 0] = pre_grad[place]
            out_ref[group, at, 1] = hidden[place]


def right_kernel(place_ref, core_ref, *refs, cores):
    acts_refs, right_refs, out_ref = refs[:cores], refs[cores:-1], refs[-1]
    parts, slices = acts_refs[0].shape[:2]
    width = right_refs[0].shape[2]
    for layer in range(2):
        rights = [
            jnp.concatenate(halves(ref[at, layer]), axis=0)
            for ref in right_refs
            for at in range(ref.shape[0])
        ]
        for cross, acts_ref in enumerate(acts_refs):
            total = None
            for distance in range(slices):
                origin = factor_origin(place_ref[0], distance, slices)
                rows = jnp.concatenate(
                    [acts_ref[part, origin, layer] for part in range(parts)], axis=0
                )
                term = dot_nt(rights[distance], rows)
                total = term if total is None else total + term
            core = lax.rem(core_ref[0] + cross, cores)
            out_ref[core, pl.ds(layer * width, width), :] = (total[:width] + total[width:]).astype(
                BF16
            )


def tables_kernel(after_any, mix_ref, shift_ref, sort_ref, mixers_ref, *, slices, clip_parts, half):
    del after_any
    size = shift_ref.shape[0]
    cells = size // clip_parts
    share = cells // slices
    frames = size // (half * half)
    held = lax.broadcasted_iota(jnp.int32, (size, size), 0)
    cell = lax.broadcasted_iota(jnp.int32, (size, size), 1)
    part = remainder(quotient(held, share), clip_parts)
    slot = quotient(held, share * clip_parts)
    natural = part * cells + slot * share + remainder(held, share)
    frame = quotient(cell, half * half)
    row = remainder(quotient(cell, half), half)
    column = remainder(cell, half)
    for shift in range(8):
        dt, dr, dc = shift // 4, shift // 2 % 2, shift % 2
        found = natural == cell + ((dt * half + dr) * half + dc)
        if dt:
            found &= frame < frames - 1
        if dr:
            found &= row < half - 1
        if dc:
            found &= column < half - 1
        shift_ref[:, pl.ds(shift * size, size)] = jnp.where(found, 1.0, 0.0).astype(BF16)
    quarter = half // 2
    outputs = size // 8
    kind = quotient(cell, outputs)
    frame = 2 * remainder(quotient(cell, quarter * quarter), frames // 2) + quotient(kind, 4)
    row = 2 * remainder(quotient(cell, quarter), quarter) + remainder(quotient(kind, 2), 2)
    column = 2 * remainder(cell, quarter) + remainder(kind, 2)
    found = natural == (frame * half + row) * half + column
    sort_ref[...] = jnp.where(found, 1.0, 0.0).astype(BF16)

    count = mixers_ref.shape[2]
    tap = lax.broadcasted_iota(jnp.int32, (count, TAPS), 1)
    line = lax.broadcasted_iota(jnp.int32, (count, TAPS), 0)
    spread = jnp.where(quotient(line, 8) == tap, 1.0, 0.0).astype(BF16)
    lines = lax.broadcasted_iota(jnp.int32, (count, count), 0)
    others = lax.broadcasted_iota(jnp.int32, (count, count), 1)
    same = remainder(lines, 8) == remainder(others, 8)
    for layer in range(2):
        for at, part in enumerate(halves(mix_ref[layer])):
            wider = dot_nt(dot(spread, part).astype(BF16), spread)
            mixers_ref[layer, at] = jnp.where(same, wider, 0.0).astype(BF16)


def update_kernel(
    place_ref, chip_ref, core_ref, tm_ref, *refs, slices, cores, clip_parts, half
):
    columns_refs, piece_refs = refs[:slices], refs[slices : slices + cores]
    (
        left_ref, mixers_ref, shift_ref, sort_ref,
        out_ref, left_rows_ref, columns, shifts, grads, raw, arrived,
    ) = refs[slices + cores :]
    parts = left_rows_ref.shape[0]
    chips = parts // (cores * clip_parts)
    copies = []
    for cross, piece_ref in enumerate(piece_refs):
        core = lax.rem(core_ref[0] + cross, cores)
        for at, (step, turn) in enumerate(np.ndindex(chips, clip_parts)):
            chip = lax.rem(chip_ref[0] + (chips - step), chips)
            place = lax.rem(tm_ref[0] + (clip_parts - turn), clip_parts)
            target = left_rows_ref.at[(chip * cores + core) * clip_parts + place]
            copies.append(
                pltpu.make_async_copy(piece_ref.at[at], target, arrived.at[len(copies)])
            )
    for copy in copies:
        copy.start()
    for distance in range(slices):
        origin = lax.rem(place_ref[0] + (slices - distance), slices)
        columns[origin] = columns_refs[distance][...]
    wide, channels = left_ref.shape[1:]
    width = columns.shape[2] // 2
    clips = parts // clip_parts
    share = columns.shape[3] // chips
    clip_cells = slices * share
    cells = clip_cells // clip_parts
    frames = clip_cells // (half * half)
    outputs = clip_cells // 8

    def by_clip(layer):
        return jnp.concatenate(
            [
                jnp.concatenate(
                    [
                        columns[
                            at, clip % cores, pl.ds(layer * width, width),
                            pl.ds(clip // cores * share, share),
                        ]
                        for at in range(slices)
                    ],
                    axis=1,
                )
                for clip in range(clips)
            ],
            axis=0,
        )

    first = by_clip(0)
    for shift in range(8):
        moved = dot(first, shift_ref[:, pl.ds(shift * clip_cells, clip_cells)]).astype(BF16)
        for clip in range(clips):
            shifts[shift, clip] = moved[clip * width : (clip + 1) * width]
    second = dot(by_clip(1), sort_ref[...]).astype(BF16)

    for copy in copies:
        copy.wait()
    own_outputs = outputs // clip_parts
    blocks = channels // wide
    out_grad = jnp.concatenate(
        [
            jnp.concatenate(
                [
                    left_rows_ref[part, pl.ds(8 * cells + own_outputs * at, own_outputs), :]
                    for at in range(blocks)
                ],
                axis=1,
            )
            for part in range(parts)
        ],
        axis=0,
    )
    full = dot_nt(out_grad, jnp.concatenate(halves(left_ref[1]), axis=0))
    total = parts * own_outputs
    quarter = half // 2
    grads[pl.ds(0, total), :] = full[:, :wide] + full[:, wide:]
    places = lax.broadcasted_iota(jnp.int32, (total, wide), 0)
    frame = remainder(quotient(places, quarter * quarter), frames // 2)
    row = remainder(quotient(places, quarter), quarter)
    column = remainder(places, quarter)
    second_rows = []
    for shift in range(8):
        dt, dr, dc = shift // 4, shift // 2 % 2, shift % 2
        moved = grads[pl.ds((dt * quarter + dr) * quarter + dc, total), :]
        inside = (frame + dt < frames // 2) & (row + dr < quarter) & (column + dc < quarter)
        second_rows.append(jnp.where(inside, moved, 0.0).astype(BF16))

    for time, line in np.ndindex(2, 2):
        even = [
            (9 * a + 3 * b + 1, 4 * (a == 0) + 2 * (b == 0))
            for a in ((0, 2) if time else (1,))
            for b in ((0, 2) if line else (1,))
        ]
        odd = [(tap + 1, shift) for tap, shift in even] + [
            (tap - 1, shift + 1) for tap, shift in even
        ]
        kind = 4 * time + 2 * line
        sums = None
        for clip in range(clips):
            left = jnp.concatenate([shifts[shift, clip] for _, shift in odd], axis=0)
            rows = jnp.concatenate(
                [
                    jnp.concatenate(
                        [
                            left_rows_ref[
                                clip * clip_parts + part, pl.ds((kind + at) * cells, cells), :
                            ]
                            for part in range(clip_parts)
                        ],
                        axis=0,
                    )
                    for at in range(2)
                ],
                axis=1,
            )
            term = dot(left, rows)
            sums = term if sums is None else sums + term
        for at, (tap, _) in enumerate(even):
            raw[0, tap] = sums[at * width : (at + 1) * width, :wide]
        for at, (tap, _) in enumerate(odd):
            raw[0, tap] = sums[at * width : (at + 1) * width, wide:]
        for place, taps in enumerate((even, odd)):
            chosen = jnp.concatenate(
                [
                    second[
                        clip * width : (clip + 1) * width,
                        (kind + place) * outputs : (kind + place + 1) * outputs,
                    ]
                    for clip in range(clips)
                ],
                axis=1,
            )
            products = dot(
                chosen, jnp.concatenate([second_rows[shift] for _, shift in taps], axis=1)
            )
            for at, (tap, _) in enumerate(taps):
                raw[1, tap] = products[:, at * wide : (at + 1) * wide]

    for layer in range(2):
        for group in range(width // 16):
            lanes = jnp.concatenate(
                [
                    raw[layer, :, pl.ds(16 * group + 8 * at, 8), :].reshape(8 * TAPS, wide)
                    for at in range(2)
                ],
                axis=1,
            )
            high, low = halves(lanes)
            mixed = (
                dot(mixers_ref[layer, 0], high)
                + dot(mixers_ref[layer, 0], low)
                + dot(mixers_ref[layer, 1], high)
            )
            rows = jnp.concatenate(
                [
                    mixed[:, at * wide : (at + 1) * wide].reshape(TAPS, 8, wide)
                    for at in range(2)
                ],
                axis=1,
            )
            out_ref[layer, :, pl.ds(16 * group, 16), :] = rows.astype(BF16)


def turned(block, axes, steps):
    sizes = [lax.axis_size(axis) for axis in axes]
    if not any(step % size for step, size in zip(steps, sizes)):
        return block
    route = []
    for place in np.ndindex(*sizes):
        target = [(at + step) % size for at, step, size in zip(place, steps, sizes)]
        route.append(
            (int(np.ravel_multi_index(place, sizes)), int(np.ravel_multi_index(target, sizes)))
        )
    return lax.ppermute(block, axes, route)


def doubled(size):
    return size & (size - 1) == 0


def first_round(block):
    size = lax.axis_size("fsdp")
    if not doubled(size):
        return [block] + [turned(block, ("fsdp",), (distance,)) for distance in range(1, size)]
    if size == 1:
        return [block]
    return [block, lax.ppermute(block, "fsdp", [(i, i ^ 1) for i in range(size)])]


def later_rounds(blocks):
    size = lax.axis_size("fsdp")
    held = [block[None] for block in blocks]
    step = 2
    while doubled(size) and step < size:
        route = [(i, i ^ step) for i in range(size)]
        held.append(lax.ppermute(jnp.concatenate(held, axis=0), "fsdp", route))
        step *= 2
    return held


def factor_origin(place, distance, size):
    if doubled(size):
        return place ^ distance
    return lax.rem(place + (size - distance), size)


def shards(clip_input, first_kernel, second_kernel, out_grad, tap_mix, left_panels, right_panels):
    clips, frames, side, _, channels = clip_input.shape
    wide = first_kernel.shape[2]
    width = right_panels.shape[2]
    half, quarter = side // 2, side // 4
    half_frames = frames // 2
    cells = half_frames * half * half
    clip_parts = lax.axis_size("tm")
    cores, chips = lax.axis_size("core"), lax.axis_size("chip")
    equals = chips * clip_parts
    parts = equals * cores
    slices = lax.axis_size("fsdp")
    share = cells // slices
    assert clips == 1 and frames == 4
    x = clip_input.reshape(frames, half, 2, side, channels)
    grad = out_grad.reshape(quarter, quarter, channels)
    place, chip_at, core_at, half_at = (
        lax.axis_index(axis).reshape(1) for axis in ("fsdp", "chip", "core", "tm")
    )

    pick = jnp.asarray(column_picks(side), BF16)
    pad = (half // 8 + 1) * 8
    rows = quarter * quarter * channels // wide
    projected, halo = pl.pallas_call(
        project_kernel,
        out_shape=(
            jax.ShapeDtypeStruct((8 * cells + rows, wide), BF16),
            jax.ShapeDtypeStruct((half * half + rows, wide), F32),
        ),
        in_specs=[ANY] * 5,
        out_specs=(VMEM, VMEM),
        scratch_shapes=[
            pltpu.VMEM(x.shape, BF16),
            pltpu.VMEM(left_panels.shape[1:], F32),
            pltpu.VMEM(grad.shape, BF16),
            pltpu.VMEM(pick.shape, BF16),
            pltpu.VMEM((9,) + first_kernel.shape[1:], BF16),
            pltpu.VMEM((quarter * quarter, channels), F32),
            pltpu.VMEM((3, pad + half * half, wide), F32),
            pltpu.SemaphoreType.DMA((8,)),
        ],
        compiler_params=pltpu.CompilerParams(vmem_limit_bytes=58 << 20),
        cost_estimate=pl.CostEstimate(
            flops=4 * frames * side * side * channels * wide,
            bytes_accessed=PROJECT_COST,
            transcendentals=0,
        ),
    )(x, left_panels, grad, pick, first_kernel)
    if clip_parts == 2:
        prior = later = lax.ppermute(halo, "tm", [(0, 1), (1, 0)])
    else:
        prior, later = shifted(halo, "tm", 1), shifted(halo, "tm", -1)
    right = right_panels.transpose(0, 2, 1)
    right = first_round(right)
    projected, right = lax.optimization_barrier((projected, right))
    right = later_rounds(right)
    held = jnp.stack(
        [
            turned(projected, ("chip", "tm"), steps)
            for steps in np.ndindex(chips, clip_parts)
        ]
    )

    spread = jnp.asarray(spread_picks(half), BF16)
    acts = pl.pallas_call(
        functools.partial(hidden_kernel, clip_parts=clip_parts),
        out_shape=jax.ShapeDtypeStruct((equals, slices, 2, share, wide), BF16),
        in_specs=[SMEM] + [VMEM] * 6 + [HBM] * 2,
        out_specs=VMEM,
        scratch_shapes=[
            pltpu.VMEM((quarter * quarter, channels), F32),
            pltpu.VMEM((frames, 2, 2, half * half, channels), BF16),
            pltpu.VMEM(first_kernel.shape, BF16),
            pltpu.VMEM(second_kernel.shape, BF16),
            pltpu.VMEM((3, pad + cells, wide), F32),
            pltpu.SemaphoreType.DMA((2, 3)),
        ],
        compiler_params=pltpu.CompilerParams(vmem_limit_bytes=ROOM),
        cost_estimate=pl.CostEstimate(
            flops=3 * cells * TAPS * channels * wide,
            bytes_accessed=HIDDEN_COST,
            transcendentals=cells * wide,
        ),
    )(
        half_at, x, prior, grad, later, pick, spread, first_kernel, second_kernel,
    )
    acts, *right = lax.optimization_barrier((acts, *right))
    clip_cells = clip_parts * cells
    shift_picks, sort_picks, mixers = pl.pallas_call(
        functools.partial(tables_kernel, slices=slices, clip_parts=clip_parts, half=half),
        out_shape=(
            jax.ShapeDtypeStruct((clip_cells, 8 * clip_cells), BF16),
            jax.ShapeDtypeStruct((clip_cells, clip_cells), BF16),
            jax.ShapeDtypeStruct((2, 2, 8 * TAPS, 8 * TAPS), BF16),
        ),
        in_specs=[ANY, VMEM],
        out_specs=(VMEM,) * 3,
        compiler_params=pltpu.CompilerParams(vmem_limit_bytes=16 << 20),
        cost_estimate=pl.CostEstimate(flops=0, bytes_accessed=4 << 20, transcendentals=0),
    )(acts, tap_mix)
    every = lax.all_to_all(
        acts.reshape(equals * slices, 2, share, wide), ("chip", "tm", "fsdp"), 0, 0, tiled=True
    ).reshape(equals, slices, 2, share, wide)
    every, held = lax.optimization_barrier((every, held))
    every = [turned(every, ("core",), (cross,)) for cross in range(cores)]
    columns = pl.pallas_call(
        functools.partial(right_kernel, cores=cores),
        out_shape=jax.ShapeDtypeStruct((cores, 2 * width, equals * share), BF16),
        in_specs=[SMEM] * 2 + [VMEM] * (cores + len(right)),
        out_specs=VMEM,
        compiler_params=pltpu.CompilerParams(vmem_limit_bytes=16 << 20),
    )(place, core_at, *every, *right)
    columns, held = lax.optimization_barrier((columns, held))
    columns = [turned(columns, ("fsdp",), (distance,)) for distance in range(slices)]
    left_rows = [turned(held, ("core",), (cross,)) for cross in range(cores)]

    result = pl.pallas_call(
        functools.partial(
            update_kernel, slices=slices, cores=cores, clip_parts=clip_parts, half=half
        ),
        out_shape=jax.ShapeDtypeStruct((2, TAPS, width, wide), BF16),
        in_specs=[SMEM] * 4
        + [VMEM] * len(columns)
        + [ANY] * cores
        + [VMEM] * 4,
        out_specs=VMEM,
        scratch_shapes=[
            pltpu.VMEM((parts,) + projected.shape, BF16),
            pltpu.VMEM((slices, cores, 2 * width, equals * share), BF16),
            pltpu.VMEM((8, parts // clip_parts, width, clip_cells), BF16),
            pltpu.VMEM((parts * cells // 8 + (quarter + 1) * quarter + 8, wide), F32),
            pltpu.VMEM((2, TAPS, width, wide), F32),
            pltpu.SemaphoreType.DMA((parts,)),
        ],
        compiler_params=pltpu.CompilerParams(vmem_limit_bytes=40 << 20),
    )(
        place, chip_at, core_at, half_at,
        *columns, *left_rows, left_panels, mixers, shift_picks, sort_picks,
    )
    return result.transpose(0, 1, 3, 2)


def solution(mesh):
    fsdp, replica, tm = (mesh.shape[axis] for axis in ("fsdp", "replica", "tm"))
    cores = 2 if replica % 2 == 0 else 1
    assert mesh.axis_names == ("fsdp", "replica", "tm")
    mesh = Mesh(
        mesh.devices.reshape(fsdp, replica // cores, cores, tm), ("fsdp", "chip", "core", "tm")
    )
    replica = ("chip", "core")
    in_specs = (
        P(replica, "tm", None, None, None),
        P(None, None, "fsdp"),
        P(None, "fsdp", None),
        P(replica, "tm", None, None, None),
        P(),
        P(None, "fsdp", None),
        P(None, "fsdp", (*replica, "tm")),
    )
    out_specs = P(None, None, "fsdp", (*replica, "tm"))
    return jax.shard_map(shards, mesh=mesh, in_specs=in_specs, out_specs=out_specs, check_vma=False)
```

```python
import functools

import jax
import jax.numpy as jnp
import numpy as np
from jax import lax
from jax.experimental import pallas as pl
from jax.experimental.pallas import tpu as pltpu
from jax.sharding import Mesh, PartitionSpec as P

TAPS = 27
F32, BF16 = jnp.float32, jnp.bfloat16
ROOM = 50 << 20
PROJECT_COST = 16 << 20
HIDDEN_COST = 200 << 20
NT = (((1,), (1,)), ((), ()))
VMEM = pl.BlockSpec(memory_space=pltpu.VMEM)
HBM = pl.BlockSpec(memory_space=pltpu.HBM)
SMEM = pl.BlockSpec(memory_space=pltpu.SMEM)
ANY = pl.BlockSpec(memory_space=pl.ANY)


def shifted(block, axis, distance):
    devices = range(lax.axis_size(axis))
    route = [(i - distance, i) for i in devices if i - distance in devices]
    return lax.ppermute(block, axis, route)


def dot(left, right):
    return jnp.dot(left, right, preferred_element_type=F32)


def dot_nt(left, right):
    return lax.dot_general(left, right, NT, preferred_element_type=F32)


def quotient(value, size):
    return value >> (size.bit_length() - 1) if size & (size - 1) == 0 else value // size


def remainder(value, size):
    return value & (size - 1) if size & (size - 1) == 0 else value % size


def halves(value):
    high = value.astype(BF16)
    return high, (value - high.astype(F32)).astype(BF16)


def column_picks(side):
    half = side // 2
    picks = np.zeros((2, half, half, half, side), np.float32)
    for row in range(half):
        for x in range(side):
            picks[x % 2, row, x // 2, row, x] = 1
    return picks.reshape(half * side, half * side)


def spread_picks(half):
    quarter = half // 2
    picks = np.zeros((3, 3, half, half, quarter, quarter), np.float32)
    for b in range(3):
        for c in range(3):
            for out_y in range(quarter):
                for out_x in range(quarter):
                    y, x = 2 * out_y + b - 1, 2 * out_x + c - 1
                    if y >= 0 and x >= 0:
                        picks[b, c, y, x, out_y, out_x] = 1
    return picks.reshape(9 * half * half, quarter * quarter)


def parity_rows(lines, pick):
    rows = dot(pick, lines).astype(BF16)
    cells = rows.shape[0] // 2
    return rows[:cells], rows[cells:]


def folded_taps(rows, weights, shift_ref, half):
    sums = {}
    for line, column in np.ndindex(2, 2):
        taps = [(b, c) for b in ((2, 0) if line else (1,)) for c in ((2, 0) if column else (1,))]
        product = dot(rows(line, column), jnp.concatenate([weights(*tap) for tap in taps], axis=1))
        wide = product.shape[1] // len(taps)
        for at, (b, c) in enumerate(taps):
            part = product[:, at * wide : (at + 1) * wide]
            key = (int(b == 0), int(c == 0))
            sums[key] = sums[key] + part if key in sums else part
    total = sums.pop((0, 0))
    count, wide = total.shape
    pad = shift_ref.shape[1] - count
    places = lax.broadcasted_iota(jnp.int32, (count, wide), 0)
    row = remainder(quotient(places, half), half)
    column = remainder(places, half)
    for at, ((dr, dc), part) in enumerate(sums.items()):
        shift_ref[at, pl.ds(pad, count), :] = part
        moved = shift_ref[at, pl.ds(pad - (dr * half + dc), count), :]
        total += jnp.where((row >= dr) & (column >= dc), moved, 0.0)
    return total


def project_kernel(
    x_any, left_any, grad_any, pick_any, first_any,
    out_ref, halo_ref, x_ref, left_ref, grad_ref, pick_ref, first_ref, rows_ref, shift_ref, arrived,
):
    frames, half, _, side, channels = x_ref.shape
    order = [frame for time in (1, 0) for frame in range(time, frames, 2)]
    pairs_of = [
        (left_any.at[0], left_ref),
        (x_any.at[order[0]], x_ref.at[order[0]]),
        (x_any.at[order[1]], x_ref.at[order[1]]),
        (pick_any, pick_ref),
        (first_any.at[pl.ds(0, 9)], first_ref),
        (x_any.at[order[2]], x_ref.at[order[2]]),
        (x_any.at[order[3]], x_ref.at[order[3]]),
        (grad_any, grad_ref),
    ]
    copies = [
        pltpu.make_async_copy(source, target, arrived.at[at])
        for at, (source, target) in enumerate(pairs_of)
    ]
    for copy in copies:
        copy.start()
    wide = left_ref.shape[0]
    pairs = frames // 2
    size = pairs * half * side
    target = lax.broadcasted_iota(jnp.int32, (size, size), 0)
    source = lax.broadcasted_iota(jnp.int32, (size, size), 1)
    cells = size // 2
    wanted = 2 * remainder(target, cells) + quotient(target, cells)
    pick = jnp.where(source == wanted, 1.0, 0.0).astype(BF16)
    copies[0].wait()
    both = jnp.concatenate(halves(left_ref[...]), axis=0)

    def project(time):
        for row in range(2):
            block = jnp.concatenate(
                [
                    x_ref[frame, :, row].reshape(half * side, channels)
                    for frame in range(time, frames, 2)
                ],
                axis=0,
            )
            full = dot_nt(block, both)
            small = (full[:, :wide] + full[:, wide:]).astype(BF16)
            ordered = dot(pick, small).astype(BF16)
            at = (4 * time + 2 * row) * cells
            out_ref[at : at + size, :] = ordered

    copies[1].wait()
    copies[2].wait()
    project(1)
    copies[3].wait()
    classes = [
        parity_rows(x_ref[frames - 1, :, line].reshape(half * side, channels), pick_ref[...])
        for line in range(2)
    ]
    copies[4].wait()
    halo_ref[pl.ds(0, half * half), :] = folded_taps(
        lambda line, column: classes[line][column],
        lambda b, c: first_ref[3 * b + c],
        shift_ref,
        half,
    )
    copies[5].wait()
    copies[6].wait()
    project(0)
    copies[7].wait()
    grad_rows = stacked_rows(grad_ref, rows_ref)
    count = grad_rows.shape[0]
    for block in range(channels // wide):
        at = 8 * cells + block * count
        out_ref[at : at + count, :] = grad_rows[:, block * wide : (block + 1) * wide]
        at = half * half + block * count
        halo_ref[at : at + count, :] = rows_ref[:, block * wide : (block + 1) * wide]


def stacked_rows(grad_ref, rows_ref):
    quarter = grad_ref.shape[0]
    for row in range(quarter):
        rows_ref[pl.ds(row * quarter, quarter), :] = grad_ref[row].astype(F32)
    return rows_ref[...].astype(BF16)


def transposed_products(rows, kernel, taps):
    total = dot_nt(rows[0], kernel[taps[0]])
    for at in range(1, len(taps)):
        total += dot_nt(rows[at], kernel[taps[at]])
    return total


def spread_rows(picks_ref, rows, cells):
    spread = dot(picks_ref[...], rows).astype(BF16)
    return [spread[tap * cells : (tap + 1) * cells] for tap in range(9)]


def hidden_kernel(
    tm_ref, x_ref, prior_ref, grad_ref, later_ref, pick_ref, spread_ref,
    first_any, second_any, out_ref, rows_ref, classes, first, second, shift_ref, arrived, *,
    clip_parts,
):
    frames, half, _, side, channels = x_ref.shape
    cells = half * half
    has_prior = jnp.where(tm_ref[0] > 0, 1.0, 0.0)
    has_later = jnp.where(tm_ref[0] < clip_parts - 1, 1.0, 0.0)
    copies = {
        (at, a): pltpu.make_async_copy(
            source.at[pl.ds(9 * a, 9)], target.at[pl.ds(9 * a, 9)], arrived.at[at, a]
        )
        for at, (source, target) in enumerate(((second_any, second), (first_any, first)))
        for a in (1, 2, 0)
    }
    for copy in copies.values():
        copy.start()
    own_rows = stacked_rows(grad_ref, rows_ref)
    own = spread_rows(spread_ref, own_rows, cells)
    copies[0, 1].wait()
    copies[0, 2].wait()
    both = None
    for tap in range(9):
        pair = jnp.concatenate([second[9 + tap], second[18 + tap]], axis=0)
        term = dot_nt(own[tap], pair)
        both = term if both is None else both + term
    early, late = both[:, : second.shape[1]], both[:, second.shape[1] :]
    for frame in range(frames):
        for line in range(2):
            lines = x_ref[frame, :, line].reshape(half * side, channels)
            classes[frame, line, 0], classes[frame, line, 1] = parity_rows(lines, pick_ref[...])
    count = own_rows.shape[0]
    wide = first.shape[2]
    later_rows = jnp.concatenate(
        [
            later_ref[pl.ds(cells + count * block, count), :]
            for block in range(channels // wide)
        ],
        axis=1,
    )
    after = spread_rows(spread_ref, later_rows.astype(BF16), cells)
    copies[0, 0].wait()
    late += transposed_products(after, second, range(9)) * has_later
    hidden_grad = jnp.concatenate([early, late], axis=0)
    nothing = jnp.zeros((cells, channels), BF16)

    def rows_of(line, column):
        held = [classes[frame, line, column] for frame in range(frames)]
        return jnp.concatenate(
            [
                jnp.concatenate([nothing, held[0], held[1]], axis=1),
                jnp.concatenate([held[1], held[2], held[3]], axis=1),
            ],
            axis=0,
        )

    for a in (1, 2, 0):
        copies[1, a].wait()
    pre = folded_taps(
        rows_of,
        lambda b, c: jnp.concatenate([first[9 * a + 3 * b + c] for a in range(3)], axis=0),
        shift_ref,
        half,
    )
    pre += jnp.concatenate(
        [prior_ref[pl.ds(0, cells), :] * has_prior, jnp.zeros((cells, wide), F32)], axis=0
    )
    sig = jax.nn.sigmoid(pre)
    hidden = (pre * sig).astype(BF16)
    pre_grad = (hidden_grad * sig * (1.0 + pre * (1.0 - sig))).astype(BF16)
    groups, slices, _, share, _ = out_ref.shape
    for at in range(slices):
        place = slice(at * share, (at + 1) * share)
        for group in range(groups):
            out_ref[group, at, 0] = pre_grad[place]
            out_ref[group, at, 1] = hidden[place]


def right_kernel(place_ref, core_ref, *refs, cores):
    acts_refs, right_refs, out_ref = refs[:cores], refs[cores:-1], refs[-1]
    parts, slices = acts_refs[0].shape[:2]
    width = right_refs[0].shape[2]
    for layer in range(2):
        rights = [
            jnp.concatenate(halves(ref[at, layer]), axis=0)
            for ref in right_refs
            for at in range(ref.shape[0])
        ]
        for cross, acts_ref in enumerate(acts_refs):
            total = None
            for distance in range(slices):
                origin = factor_origin(place_ref[0], distance, slices)
                rows = jnp.concatenate(
                    [acts_ref[part, origin, layer] for part in range(parts)], axis=0
                )
                term = dot_nt(rights[distance], rows)
                total = term if total is None else total + term
            core = lax.rem(core_ref[0] + cross, cores)
            out_ref[core, pl.ds(layer * width, width), :] = (total[:width] + total[width:]).astype(
                BF16
            )


def tables_kernel(after_any, mix_ref, shift_ref, sort_ref, mixers_ref, *, slices, clip_parts, half):
    del after_any
    size = shift_ref.shape[0]
    cells = size // clip_parts
    share = cells // slices
    frames = size // (half * half)
    held = lax.broadcasted_iota(jnp.int32, (size, size), 0)
    cell = lax.broadcasted_iota(jnp.int32, (size, size), 1)
    part = remainder(quotient(held, share), clip_parts)
    slot = quotient(held, share * clip_parts)
    natural = part * cells + slot * share + remainder(held, share)
    frame = quotient(cell, half * half)
    row = remainder(quotient(cell, half), half)
    column = remainder(cell, half)
    for shift in range(8):
        dt, dr, dc = shift // 4, shift // 2 % 2, shift % 2
        found = natural == cell + ((dt * half + dr) * half + dc)
        if dt:
            found &= frame < frames - 1
        if dr:
            found &= row < half - 1
        if dc:
            found &= column < half - 1
        shift_ref[:, pl.ds(shift * size, size)] = jnp.where(found, 1.0, 0.0).astype(BF16)
    quarter = half // 2
    outputs = size // 8
    kind = quotient(cell, outputs)
    frame = 2 * remainder(quotient(cell, quarter * quarter), frames // 2) + quotient(kind, 4)
    row = 2 * remainder(quotient(cell, quarter), quarter) + remainder(quotient(kind, 2), 2)
    column = 2 * remainder(cell, quarter) + remainder(kind, 2)
    found = natural == (frame * half + row) * half + column
    sort_ref[...] = jnp.where(found, 1.0, 0.0).astype(BF16)

    count = mixers_ref.shape[2]
    tap = lax.broadcasted_iota(jnp.int32, (count, TAPS), 1)
    line = lax.broadcasted_iota(jnp.int32, (count, TAPS), 0)
    spread = jnp.where(quotient(line, 8) == tap, 1.0, 0.0).astype(BF16)
    lines = lax.broadcasted_iota(jnp.int32, (count, count), 0)
    others = lax.broadcasted_iota(jnp.int32, (count, count), 1)
    same = remainder(lines, 8) == remainder(others, 8)
    for layer in range(2):
        for at, part in enumerate(halves(mix_ref[layer])):
            wider = dot_nt(dot(spread, part).astype(BF16), spread)
            mixers_ref[layer, at] = jnp.where(same, wider, 0.0).astype(BF16)


def update_kernel(
    place_ref, chip_ref, core_ref, tm_ref, *refs, slices, cores, clip_parts, half
):
    columns_refs, piece_refs = refs[:slices], refs[slices : slices + cores]
    (
        left_ref, mixers_ref, shift_ref, sort_ref,
        out_ref, left_rows_ref, columns, shifts, grads, raw, arrived,
    ) = refs[slices + cores :]
    parts = left_rows_ref.shape[0]
    chips = parts // (cores * clip_parts)
    copies = []
    for cross, piece_ref in enumerate(piece_refs):
        core = lax.rem(core_ref[0] + cross, cores)
        for at, (step, turn) in enumerate(np.ndindex(chips, clip_parts)):
            chip = lax.rem(chip_ref[0] + (chips - step), chips)
            place = lax.rem(tm_ref[0] + (clip_parts - turn), clip_parts)
            target = left_rows_ref.at[(chip * cores + core) * clip_parts + place]
            copies.append(
                pltpu.make_async_copy(piece_ref.at[at], target, arrived.at[len(copies)])
            )
    for copy in copies:
        copy.start()
    for distance in range(slices):
        origin = lax.rem(place_ref[0] + (slices - distance), slices)
        columns[origin] = columns_refs[distance][...]
    wide, channels = left_ref.shape[1:]
    width = columns.shape[2] // 2
    clips = parts // clip_parts
    share = columns.shape[3] // chips
    clip_cells = slices * share
    cells = clip_cells // clip_parts
    frames = clip_cells // (half * half)
    outputs = clip_cells // 8

    def by_clip(layer):
        return jnp.concatenate(
            [
                jnp.concatenate(
                    [
                        columns[
                            at, clip % cores, pl.ds(layer * width, width),
                            pl.ds(clip // cores * share, share),
                        ]
                        for at in range(slices)
                    ],
                    axis=1,
                )
                for clip in range(clips)
            ],
            axis=0,
        )

    first = by_clip(0)
    for shift in range(8):
        moved = dot(first, shift_ref[:, pl.ds(shift * clip_cells, clip_cells)]).astype(BF16)
        for clip in range(clips):
            shifts[shift, clip] = moved[clip * width : (clip + 1) * width]
    second = dot(by_clip(1), sort_ref[...]).astype(BF16)

    for copy in copies:
        copy.wait()
    own_outputs = outputs // clip_parts
    blocks = channels // wide
    out_grad = jnp.concatenate(
        [
            jnp.concatenate(
                [
                    left_rows_ref[part, pl.ds(8 * cells + own_outputs * at, own_outputs), :]
                    for at in range(blocks)
                ],
                axis=1,
            )
            for part in range(parts)
        ],
        axis=0,
    )
    full = dot_nt(out_grad, jnp.concatenate(halves(left_ref[1]), axis=0))
    total = parts * own_outputs
    quarter = half // 2
    grads[pl.ds(0, total), :] = full[:, :wide] + full[:, wide:]
    places = lax.broadcasted_iota(jnp.int32, (total, wide), 0)
    frame = remainder(quotient(places, quarter * quarter), frames // 2)
    row = remainder(quotient(places, quarter), quarter)
    column = remainder(places, quarter)
    second_rows = []
    for shift in range(8):
        dt, dr, dc = shift // 4, shift // 2 % 2, shift % 2
        moved = grads[pl.ds((dt * quarter + dr) * quarter + dc, total), :]
        inside = (frame + dt < frames // 2) & (row + dr < quarter) & (column + dc < quarter)
        second_rows.append(jnp.where(inside, moved, 0.0).astype(BF16))

    for time, line in np.ndindex(2, 2):
        even = [
            (9 * a + 3 * b + 1, 4 * (a == 0) + 2 * (b == 0))
            for a in ((0, 2) if time else (1,))
            for b in ((0, 2) if line else (1,))
        ]
        odd = [(tap + 1, shift) for tap, shift in even] + [
            (tap - 1, shift + 1) for tap, shift in even
        ]
        kind = 4 * time + 2 * line
        sums = None
        for clip in range(clips):
            left = jnp.concatenate([shifts[shift, clip] for _, shift in odd], axis=0)
            rows = jnp.concatenate(
                [
                    jnp.concatenate(
                        [
                            left_rows_ref[
                                clip * clip_parts + part, pl.ds((kind + at) * cells, cells), :
                            ]
                            for part in range(clip_parts)
                        ],
                        axis=0,
                    )
                    for at in range(2)
                ],
                axis=1,
            )
            term = dot(left, rows)
            sums = term if sums is None else sums + term
        for at, (tap, _) in enumerate(even):
            raw[0, tap] = sums[at * width : (at + 1) * width, :wide]
        for at, (tap, _) in enumerate(odd):
            raw[0, tap] = sums[at * width : (at + 1) * width, wide:]
        for place, taps in enumerate((even, odd)):
            chosen = jnp.concatenate(
                [
                    second[
                        clip * width : (clip + 1) * width,
                        (kind + place) * outputs : (kind + place + 1) * outputs,
                    ]
                    for clip in range(clips)
                ],
                axis=1,
            )
            products = dot(
                chosen, jnp.concatenate([second_rows[shift] for _, shift in taps], axis=1)
            )
            for at, (tap, _) in enumerate(taps):
                raw[1, tap] = products[:, at * wide : (at + 1) * wide]

    for layer in range(2):
        for group in range(width // 16):
            lanes = jnp.concatenate(
                [
                    raw[layer, :, pl.ds(16 * group + 8 * at, 8), :].reshape(8 * TAPS, wide)
                    for at in range(2)
                ],
                axis=1,
            )
            high, low = halves(lanes)
            mixed = (
                dot(mixers_ref[layer, 0], high)
                + dot(mixers_ref[layer, 0], low)
                + dot(mixers_ref[layer, 1], high)
            )
            rows = jnp.concatenate(
                [
                    mixed[:, at * wide : (at + 1) * wide].reshape(TAPS, 8, wide)
                    for at in range(2)
                ],
                axis=1,
            )
            out_ref[layer, :, pl.ds(16 * group, 16), :] = rows.astype(BF16)


def turned(block, axes, steps):
    sizes = [lax.axis_size(axis) for axis in axes]
    if not any(step % size for step, size in zip(steps, sizes)):
        return block
    route = []
    for place in np.ndindex(*sizes):
        target = [(at + step) % size for at, step, size in zip(place, steps, sizes)]
        route.append(
            (int(np.ravel_multi_index(place, sizes)), int(np.ravel_multi_index(target, sizes)))
        )
    return lax.ppermute(block, axes, route)


def doubled(size):
    return size & (size - 1) == 0


def first_round(block):
    size = lax.axis_size("fsdp")
    if not doubled(size):
        return [block] + [turned(block, ("fsdp",), (distance,)) for distance in range(1, size)]
    if size == 1:
        return [block]
    return [block, lax.ppermute(block, "fsdp", [(i, i ^ 1) for i in range(size)])]


def later_rounds(blocks):
    size = lax.axis_size("fsdp")
    held = [block[None] for block in blocks]
    step = 2
    while doubled(size) and step < size:
        route = [(i, i ^ step) for i in range(size)]
        held.append(lax.ppermute(jnp.concatenate(held, axis=0), "fsdp", route))
        step *= 2
    return held


def factor_origin(place, distance, size):
    if doubled(size):
        return place ^ distance
    return lax.rem(place + (size - distance), size)


def shards(clip_input, first_kernel, second_kernel, out_grad, tap_mix, left_panels, right_panels):
    clips, frames, side, _, channels = clip_input.shape
    wide = first_kernel.shape[2]
    width = right_panels.shape[2]
    half, quarter = side // 2, side // 4
    half_frames = frames // 2
    cells = half_frames * half * half
    clip_parts = lax.axis_size("tm")
    cores, chips = lax.axis_size("core"), lax.axis_size("chip")
    equals = chips * clip_parts
    parts = equals * cores
    slices = lax.axis_size("fsdp")
    share = cells // slices
    assert clips == 1 and frames == 4
    x = clip_input.reshape(frames, half, 2, side, channels)
    grad = out_grad.reshape(quarter, quarter, channels)
    place, chip_at, core_at, half_at = (
        lax.axis_index(axis).reshape(1) for axis in ("fsdp", "chip", "core", "tm")
    )

    pick = jnp.asarray(column_picks(side), BF16)
    pad = (half // 8 + 1) * 8
    rows = quarter * quarter * channels // wide
    projected, halo = pl.pallas_call(
        project_kernel,
        out_shape=(
            jax.ShapeDtypeStruct((8 * cells + rows, wide), BF16),
            jax.ShapeDtypeStruct((half * half + rows, wide), F32),
        ),
        in_specs=[ANY] * 5,
        out_specs=(VMEM, VMEM),
        scratch_shapes=[
            pltpu.VMEM(x.shape, BF16),
            pltpu.VMEM(left_panels.shape[1:], F32),
            pltpu.VMEM(grad.shape, BF16),
            pltpu.VMEM(pick.shape, BF16),
            pltpu.VMEM((9,) + first_kernel.shape[1:], BF16),
            pltpu.VMEM((quarter * quarter, channels), F32),
            pltpu.VMEM((3, pad + half * half, wide), F32),
            pltpu.SemaphoreType.DMA((8,)),
        ],
        compiler_params=pltpu.CompilerParams(vmem_limit_bytes=58 << 20),
        cost_estimate=pl.CostEstimate(
            flops=4 * frames * side * side * channels * wide,
            bytes_accessed=PROJECT_COST,
            transcendentals=0,
        ),
    )(x, left_panels, grad, pick, first_kernel)
    if clip_parts == 2:
        prior = later = lax.ppermute(halo, "tm", [(0, 1), (1, 0)])
    else:
        prior, later = shifted(halo, "tm", 1), shifted(halo, "tm", -1)
    right = right_panels.transpose(0, 2, 1)
    right = first_round(right)
    projected, right = lax.optimization_barrier((projected, right))
    held = jnp.stack(
        [
            turned(projected, ("chip", "tm"), steps)
            for steps in np.ndindex(chips, clip_parts)
        ]
    )

    spread = jnp.asarray(spread_picks(half), BF16)
    acts = pl.pallas_call(
        functools.partial(hidden_kernel, clip_parts=clip_parts),
        out_shape=jax.ShapeDtypeStruct((equals, slices, 2, share, wide), BF16),
        in_specs=[SMEM] + [VMEM] * 6 + [HBM] * 2,
        out_specs=VMEM,
        scratch_shapes=[
            pltpu.VMEM((quarter * quarter, channels), F32),
            pltpu.VMEM((frames, 2, 2, half * half, channels), BF16),
            pltpu.VMEM(first_kernel.shape, BF16),
            pltpu.VMEM(second_kernel.shape, BF16),
            pltpu.VMEM((3, pad + cells, wide), F32),
            pltpu.SemaphoreType.DMA((2, 3)),
        ],
        compiler_params=pltpu.CompilerParams(vmem_limit_bytes=ROOM),
        cost_estimate=pl.CostEstimate(
            flops=3 * cells * TAPS * channels * wide,
            bytes_accessed=HIDDEN_COST,
            transcendentals=cells * wide,
        ),
    )(
        half_at, x, prior, grad, later, pick, spread, first_kernel, second_kernel,
    )
    _, right = lax.optimization_barrier((acts, right))
    right = later_rounds(right)
    clip_cells = clip_parts * cells
    shift_picks, sort_picks, mixers = pl.pallas_call(
        functools.partial(tables_kernel, slices=slices, clip_parts=clip_parts, half=half),
        out_shape=(
            jax.ShapeDtypeStruct((clip_cells, 8 * clip_cells), BF16),
            jax.ShapeDtypeStruct((clip_cells, clip_cells), BF16),
            jax.ShapeDtypeStruct((2, 2, 8 * TAPS, 8 * TAPS), BF16),
        ),
        in_specs=[ANY, VMEM],
        out_specs=(VMEM,) * 3,
        compiler_params=pltpu.CompilerParams(vmem_limit_bytes=16 << 20),
        cost_estimate=pl.CostEstimate(flops=0, bytes_accessed=4 << 20, transcendentals=0),
    )(acts, tap_mix)
    every = lax.all_to_all(
        acts.reshape(equals * slices, 2, share, wide), ("chip", "tm", "fsdp"), 0, 0, tiled=True
    ).reshape(equals, slices, 2, share, wide)
    every, held = lax.optimization_barrier((every, held))
    every = [turned(every, ("core",), (cross,)) for cross in range(cores)]
    columns = pl.pallas_call(
        functools.partial(right_kernel, cores=cores),
        out_shape=jax.ShapeDtypeStruct((cores, 2 * width, equals * share), BF16),
        in_specs=[SMEM] * 2 + [VMEM] * (cores + len(right)),
        out_specs=VMEM,
        compiler_params=pltpu.CompilerParams(vmem_limit_bytes=16 << 20),
    )(place, core_at, *every, *right)
    columns, held = lax.optimization_barrier((columns, held))
    columns = [turned(columns, ("fsdp",), (distance,)) for distance in range(slices)]
    left_rows = [turned(held, ("core",), (cross,)) for cross in range(cores)]

    result = pl.pallas_call(
        functools.partial(
            update_kernel, slices=slices, cores=cores, clip_parts=clip_parts, half=half
        ),
        out_shape=jax.ShapeDtypeStruct((2, TAPS, width, wide), BF16),
        in_specs=[SMEM] * 4
        + [VMEM] * len(columns)
        + [ANY] * cores
        + [VMEM] * 4,
        out_specs=VMEM,
        scratch_shapes=[
            pltpu.VMEM((parts,) + projected.shape, BF16),
            pltpu.VMEM((slices, cores, 2 * width, equals * share), BF16),
            pltpu.VMEM((8, parts // clip_parts, width, clip_cells), BF16),
            pltpu.VMEM((parts * cells // 8 + (quarter + 1) * quarter + 8, wide), F32),
            pltpu.VMEM((2, TAPS, width, wide), F32),
            pltpu.SemaphoreType.DMA((parts,)),
        ],
        compiler_params=pltpu.CompilerParams(vmem_limit_bytes=40 << 20),
    )(
        place, chip_at, core_at, half_at,
        *columns, *left_rows, left_panels, mixers, shift_picks, sort_picks,
    )
    return result.transpose(0, 1, 3, 2)


def solution(mesh):
    fsdp, replica, tm = (mesh.shape[axis] for axis in ("fsdp", "replica", "tm"))
    cores = 2 if replica % 2 == 0 else 1
    assert mesh.axis_names == ("fsdp", "replica", "tm")
    mesh = Mesh(
        mesh.devices.reshape(fsdp, replica // cores, cores, tm), ("fsdp", "chip", "core", "tm")
    )
    replica = ("chip", "core")
    in_specs = (
        P(replica, "tm", None, None, None),
        P(None, None, "fsdp"),
        P(None, "fsdp", None),
        P(replica, "tm", None, None, None),
        P(),
        P(None, "fsdp", None),
        P(None, "fsdp", (*replica, "tm")),
    )
    out_specs = P(None, None, "fsdp", (*replica, "tm"))
    return jax.shard_map(shards, mesh=mesh, in_specs=in_specs, out_specs=out_specs, check_vma=False)
```

```python
import functools

import jax
import jax.numpy as jnp
import numpy as np
from jax import lax
from jax.experimental import pallas as pl
from jax.experimental.pallas import tpu as pltpu
from jax.sharding import Mesh, PartitionSpec as P

TAPS = 27
F32, BF16 = jnp.float32, jnp.bfloat16
ROOM = 50 << 20
PROJECT_COST = 16 << 20
HIDDEN_COST = 200 << 20
NT = (((1,), (1,)), ((), ()))
VMEM = pl.BlockSpec(memory_space=pltpu.VMEM)
HBM = pl.BlockSpec(memory_space=pltpu.HBM)
SMEM = pl.BlockSpec(memory_space=pltpu.SMEM)
ANY = pl.BlockSpec(memory_space=pl.ANY)


def shifted(block, axis, distance):
    devices = range(lax.axis_size(axis))
    route = [(i - distance, i) for i in devices if i - distance in devices]
    return lax.ppermute(block, axis, route)


def dot(left, right):
    return jnp.dot(left, right, preferred_element_type=F32)


def dot_nt(left, right):
    return lax.dot_general(left, right, NT, preferred_element_type=F32)


def quotient(value, size):
    return value >> (size.bit_length() - 1) if size & (size - 1) == 0 else value // size


def remainder(value, size):
    return value & (size - 1) if size & (size - 1) == 0 else value % size


def halves(value):
    high = value.astype(BF16)
    return high, (value - high.astype(F32)).astype(BF16)


def column_picks(side):
    half = side // 2
    picks = np.zeros((2, half, half, half, side), np.float32)
    for row in range(half):
        for x in range(side):
            picks[x % 2, row, x // 2, row, x] = 1
    return picks.reshape(half * side, half * side)


def spread_picks(half):
    quarter = half // 2
    picks = np.zeros((3, 3, half, half, quarter, quarter), np.float32)
    for b in range(3):
        for c in range(3):
            for out_y in range(quarter):
                for out_x in range(quarter):
                    y, x = 2 * out_y + b - 1, 2 * out_x + c - 1
                    if y >= 0 and x >= 0:
                        picks[b, c, y, x, out_y, out_x] = 1
    return picks.reshape(9 * half * half, quarter * quarter)


def parity_rows(lines, pick):
    rows = dot(pick, lines).astype(BF16)
    cells = rows.shape[0] // 2
    return rows[:cells], rows[cells:]


def folded_taps(rows, weights, shift_ref, half):
    sums = {}
    for line, column in np.ndindex(2, 2):
        taps = [(b, c) for b in ((2, 0) if line else (1,)) for c in ((2, 0) if column else (1,))]
        product = dot(rows(line, column), jnp.concatenate([weights(*tap) for tap in taps], axis=1))
        wide = product.shape[1] // len(taps)
        for at, (b, c) in enumerate(taps):
            part = product[:, at * wide : (at + 1) * wide]
            key = (int(b == 0), int(c == 0))
            sums[key] = sums[key] + part if key in sums else part
    total = sums.pop((0, 0))
    count, wide = total.shape
    pad = shift_ref.shape[1] - count
    places = lax.broadcasted_iota(jnp.int32, (count, wide), 0)
    row = remainder(quotient(places, half), half)
    column = remainder(places, half)
    for at, ((dr, dc), part) in enumerate(sums.items()):
        shift_ref[at, pl.ds(pad, count), :] = part
        moved = shift_ref[at, pl.ds(pad - (dr * half + dc), count), :]
        total += jnp.where((row >= dr) & (column >= dc), moved, 0.0)
    return total


def project_kernel(
    x_any, left_any, grad_any, pick_any, first_any,
    out_ref, halo_ref, x_ref, left_ref, grad_ref, pick_ref, first_ref, rows_ref, shift_ref, arrived,
):
    frames, half, _, side, channels = x_ref.shape
    order = [frame for time in (1, 0) for frame in range(time, frames, 2)]
    pairs_of = [
        (left_any.at[0], left_ref),
        (x_any.at[order[0]], x_ref.at[order[0]]),
        (x_any.at[order[1]], x_ref.at[order[1]]),
        (pick_any, pick_ref),
        (first_any.at[pl.ds(0, 9)], first_ref),
        (x_any.at[order[2]], x_ref.at[order[2]]),
        (x_any.at[order[3]], x_ref.at[order[3]]),
        (grad_any, grad_ref),
    ]
    copies = [
        pltpu.make_async_copy(source, target, arrived.at[at])
        for at, (source, target) in enumerate(pairs_of)
    ]
    for copy in copies:
        copy.start()
    wide = left_ref.shape[0]
    pairs = frames // 2
    size = pairs * half * side
    target = lax.broadcasted_iota(jnp.int32, (size, size), 0)
    source = lax.broadcasted_iota(jnp.int32, (size, size), 1)
    cells = size // 2
    wanted = 2 * remainder(target, cells) + quotient(target, cells)
    pick = jnp.where(source == wanted, 1.0, 0.0).astype(BF16)
    copies[0].wait()
    both = jnp.concatenate(halves(left_ref[...]), axis=0)

    def project(time):
        for row in range(2):
            block = jnp.concatenate(
                [
                    x_ref[frame, :, row].reshape(half * side, channels)
                    for frame in range(time, frames, 2)
                ],
                axis=0,
            )
            full = dot_nt(block, both)
            small = (full[:, :wide] + full[:, wide:]).astype(BF16)
            ordered = dot(pick, small).astype(BF16)
            at = (4 * time + 2 * row) * cells
            out_ref[at : at + size, :] = ordered

    copies[1].wait()
    copies[2].wait()
    project(1)
    copies[3].wait()
    classes = [
        parity_rows(x_ref[frames - 1, :, line].reshape(half * side, channels), pick_ref[...])
        for line in range(2)
    ]
    copies[4].wait()
    halo_ref[pl.ds(0, half * half), :] = folded_taps(
        lambda line, column: classes[line][column],
        lambda b, c: first_ref[3 * b + c],
        shift_ref,
        half,
    )
    copies[5].wait()
    copies[6].wait()
    project(0)
    copies[7].wait()
    grad_rows = stacked_rows(grad_ref, rows_ref)
    count = grad_rows.shape[0]
    for block in range(channels // wide):
        at = 8 * cells + block * count
        out_ref[at : at + count, :] = grad_rows[:, block * wide : (block + 1) * wide]
        at = half * half + block * count
        halo_ref[at : at + count, :] = rows_ref[:, block * wide : (block + 1) * wide]


def stacked_rows(grad_ref, rows_ref):
    quarter = grad_ref.shape[0]
    for row in range(quarter):
        rows_ref[pl.ds(row * quarter, quarter), :] = grad_ref[row].astype(F32)
    return rows_ref[...].astype(BF16)


def transposed_products(rows, kernel, taps):
    total = dot_nt(rows[0], kernel[taps[0]])
    for at in range(1, len(taps)):
        total += dot_nt(rows[at], kernel[taps[at]])
    return total


def spread_rows(picks_ref, rows, cells):
    spread = dot(picks_ref[...], rows).astype(BF16)
    return [spread[tap * cells : (tap + 1) * cells] for tap in range(9)]


def hidden_kernel(
    tm_ref, x_ref, prior_ref, grad_ref, later_ref, pick_ref, spread_ref,
    first_any, second_any, out_ref, rows_ref, classes, first, second, shift_ref, arrived, *,
    clip_parts,
):
    frames, half, _, side, channels = x_ref.shape
    cells = half * half
    has_prior = jnp.where(tm_ref[0] > 0, 1.0, 0.0)
    has_later = jnp.where(tm_ref[0] < clip_parts - 1, 1.0, 0.0)
    copies = {
        (at, a): pltpu.make_async_copy(
            source.at[pl.ds(9 * a, 9)], target.at[pl.ds(9 * a, 9)], arrived.at[at, a]
        )
        for at, (source, target) in enumerate(((second_any, second), (first_any, first)))
        for a in (1, 2, 0)
    }
    for copy in copies.values():
        copy.start()
    own_rows = stacked_rows(grad_ref, rows_ref)
    own = spread_rows(spread_ref, own_rows, cells)
    for frame in range(frames):
        for line in range(2):
            lines = x_ref[frame, :, line].reshape(half * side, channels)
            classes[frame, line, 0], classes[frame, line, 1] = parity_rows(lines, pick_ref[...])
    copies[0, 1].wait()
    copies[0, 2].wait()
    both = None
    for tap in range(9):
        pair = jnp.concatenate([second[9 + tap], second[18 + tap]], axis=0)
        term = dot_nt(own[tap], pair)
        both = term if both is None else both + term
    early, late = both[:, : second.shape[1]], both[:, second.shape[1] :]
    count = own_rows.shape[0]
    wide = first.shape[2]
    later_rows = jnp.concatenate(
        [
            later_ref[pl.ds(cells + count * block, count), :]
            for block in range(channels // wide)
        ],
        axis=1,
    )
    after = spread_rows(spread_ref, later_rows.astype(BF16), cells)
    copies[0, 0].wait()
    late += transposed_products(after, second, range(9)) * has_later
    hidden_grad = jnp.concatenate([early, late], axis=0)
    nothing = jnp.zeros((cells, channels), BF16)

    def rows_of(line, column):
        held = [classes[frame, line, column] for frame in range(frames)]
        return jnp.concatenate(
            [
                jnp.concatenate([nothing, held[0], held[1]], axis=1),
                jnp.concatenate([held[1], held[2], held[3]], axis=1),
            ],
            axis=0,
        )

    for a in (1, 2, 0):
        copies[1, a].wait()
    pre = folded_taps(
        rows_of,
        lambda b, c: jnp.concatenate([first[9 * a + 3 * b + c] for a in range(3)], axis=0),
        shift_ref,
        half,
    )
    pre += jnp.concatenate(
        [prior_ref[pl.ds(0, cells), :] * has_prior, jnp.zeros((cells, wide), F32)], axis=0
    )
    sig = jax.nn.sigmoid(pre)
    hidden = (pre * sig).astype(BF16)
    pre_grad = (hidden_grad * sig * (1.0 + pre * (1.0 - sig))).astype(BF16)
    groups, slices, _, share, _ = out_ref.shape
    for at in range(slices):
        place = slice(at * share, (at + 1) * share)
        for group in range(groups):
            out_ref[group, at, 0] = pre_grad[place]
            out_ref[group, at, 1] = hidden[place]


def right_kernel(place_ref, core_ref, *refs, cores):
    acts_refs, right_refs, out_ref = refs[:cores], refs[cores:-1], refs[-1]
    parts, slices = acts_refs[0].shape[:2]
    width = right_refs[0].shape[2]
    for layer in range(2):
        rights = [
            jnp.concatenate(halves(ref[at, layer]), axis=0)
            for ref in right_refs
            for at in range(ref.shape[0])
        ]
        for cross, acts_ref in enumerate(acts_refs):
            total = None
            for distance in range(slices):
                origin = factor_origin(place_ref[0], distance, slices)
                rows = jnp.concatenate(
                    [acts_ref[part, origin, layer] for part in range(parts)], axis=0
                )
                term = dot_nt(rights[distance], rows)
                total = term if total is None else total + term
            core = lax.rem(core_ref[0] + cross, cores)
            out_ref[core, pl.ds(layer * width, width), :] = (total[:width] + total[width:]).astype(
                BF16
            )


def tables_kernel(after_any, mix_ref, shift_ref, sort_ref, mixers_ref, *, slices, clip_parts, half):
    del after_any
    size = shift_ref.shape[0]
    cells = size // clip_parts
    share = cells // slices
    frames = size // (half * half)
    held = lax.broadcasted_iota(jnp.int32, (size, size), 0)
    cell = lax.broadcasted_iota(jnp.int32, (size, size), 1)
    part = remainder(quotient(held, share), clip_parts)
    slot = quotient(held, share * clip_parts)
    natural = part * cells + slot * share + remainder(held, share)
    frame = quotient(cell, half * half)
    row = remainder(quotient(cell, half), half)
    column = remainder(cell, half)
    for shift in range(8):
        dt, dr, dc = shift // 4, shift // 2 % 2, shift % 2
        found = natural == cell + ((dt * half + dr) * half + dc)
        if dt:
            found &= frame < frames - 1
        if dr:
            found &= row < half - 1
        if dc:
            found &= column < half - 1
        shift_ref[:, pl.ds(shift * size, size)] = jnp.where(found, 1.0, 0.0).astype(BF16)
    quarter = half // 2
    outputs = size // 8
    kind = quotient(cell, outputs)
    frame = 2 * remainder(quotient(cell, quarter * quarter), frames // 2) + quotient(kind, 4)
    row = 2 * remainder(quotient(cell, quarter), quarter) + remainder(quotient(kind, 2), 2)
    column = 2 * remainder(cell, quarter) + remainder(kind, 2)
    found = natural == (frame * half + row) * half + column
    sort_ref[...] = jnp.where(found, 1.0, 0.0).astype(BF16)

    count = mixers_ref.shape[2]
    tap = lax.broadcasted_iota(jnp.int32, (count, TAPS), 1)
    line = lax.broadcasted_iota(jnp.int32, (count, TAPS), 0)
    spread = jnp.where(quotient(line, 8) == tap, 1.0, 0.0).astype(BF16)
    lines = lax.broadcasted_iota(jnp.int32, (count, count), 0)
    others = lax.broadcasted_iota(jnp.int32, (count, count), 1)
    same = remainder(lines, 8) == remainder(others, 8)
    for layer in range(2):
        for at, part in enumerate(halves(mix_ref[layer])):
            wider = dot_nt(dot(spread, part).astype(BF16), spread)
            mixers_ref[layer, at] = jnp.where(same, wider, 0.0).astype(BF16)


def update_kernel(
    place_ref, chip_ref, core_ref, tm_ref, *refs, slices, cores, clip_parts, half
):
    columns_refs, piece_refs = refs[:slices], refs[slices : slices + cores]
    (
        left_ref, mixers_ref, shift_ref, sort_ref,
        out_ref, left_rows_ref, columns, shifts, grads, raw, arrived,
    ) = refs[slices + cores :]
    parts = left_rows_ref.shape[0]
    chips = parts // (cores * clip_parts)
    copies = []
    for cross, piece_ref in enumerate(piece_refs):
        core = lax.rem(core_ref[0] + cross, cores)
        for at, (step, turn) in enumerate(np.ndindex(chips, clip_parts)):
            chip = lax.rem(chip_ref[0] + (chips - step), chips)
            place = lax.rem(tm_ref[0] + (clip_parts - turn), clip_parts)
            target = left_rows_ref.at[(chip * cores + core) * clip_parts + place]
            copies.append(
                pltpu.make_async_copy(piece_ref.at[at], target, arrived.at[len(copies)])
            )
    for copy in copies:
        copy.start()
    for distance in range(slices):
        origin = lax.rem(place_ref[0] + (slices - distance), slices)
        columns[origin] = columns_refs[distance][...]
    wide, channels = left_ref.shape[1:]
    width = columns.shape[2] // 2
    clips = parts // clip_parts
    share = columns.shape[3] // chips
    clip_cells = slices * share
    cells = clip_cells // clip_parts
    frames = clip_cells // (half * half)
    outputs = clip_cells // 8

    def by_clip(layer):
        return jnp.concatenate(
            [
                jnp.concatenate(
                    [
                        columns[
                            at, clip % cores, pl.ds(layer * width, width),
                            pl.ds(clip // cores * share, share),
                        ]
                        for at in range(slices)
                    ],
                    axis=1,
                )
                for clip in range(clips)
            ],
            axis=0,
        )

    first = by_clip(0)
    for shift in range(8):
        moved = dot(first, shift_ref[:, pl.ds(shift * clip_cells, clip_cells)]).astype(BF16)
        for clip in range(clips):
            shifts[shift, clip] = moved[clip * width : (clip + 1) * width]
    second = dot(by_clip(1), sort_ref[...]).astype(BF16)

    for copy in copies:
        copy.wait()
    own_outputs = outputs // clip_parts
    blocks = channels // wide
    out_grad = jnp.concatenate(
        [
            jnp.concatenate(
                [
                    left_rows_ref[part, pl.ds(8 * cells + own_outputs * at, own_outputs), :]
                    for at in range(blocks)
                ],
                axis=1,
            )
            for part in range(parts)
        ],
        axis=0,
    )
    full = dot_nt(out_grad, jnp.concatenate(halves(left_ref[1]), axis=0))
    total = parts * own_outputs
    quarter = half // 2
    grads[pl.ds(0, total), :] = full[:, :wide] + full[:, wide:]
    places = lax.broadcasted_iota(jnp.int32, (total, wide), 0)
    frame = remainder(quotient(places, quarter * quarter), frames // 2)
    row = remainder(quotient(places, quarter), quarter)
    column = remainder(places, quarter)
    second_rows = []
    for shift in range(8):
        dt, dr, dc = shift // 4, shift // 2 % 2, shift % 2
        moved = grads[pl.ds((dt * quarter + dr) * quarter + dc, total), :]
        inside = (frame + dt < frames // 2) & (row + dr < quarter) & (column + dc < quarter)
        second_rows.append(jnp.where(inside, moved, 0.0).astype(BF16))

    for time, line in np.ndindex(2, 2):
        even = [
            (9 * a + 3 * b + 1, 4 * (a == 0) + 2 * (b == 0))
            for a in ((0, 2) if time else (1,))
            for b in ((0, 2) if line else (1,))
        ]
        odd = [(tap + 1, shift) for tap, shift in even] + [
            (tap - 1, shift + 1) for tap, shift in even
        ]
        kind = 4 * time + 2 * line
        sums = None
        for clip in range(clips):
            left = jnp.concatenate([shifts[shift, clip] for _, shift in odd], axis=0)
            rows = jnp.concatenate(
                [
                    jnp.concatenate(
                        [
                            left_rows_ref[
                                clip * clip_parts + part, pl.ds((kind + at) * cells, cells), :
                            ]
                            for part in range(clip_parts)
                        ],
                        axis=0,
                    )
                    for at in range(2)
                ],
                axis=1,
            )
            term = dot(left, rows)
            sums = term if sums is None else sums + term
        for at, (tap, _) in enumerate(even):
            raw[0, tap] = sums[at * width : (at + 1) * width, :wide]
        for at, (tap, _) in enumerate(odd):
            raw[0, tap] = sums[at * width : (at + 1) * width, wide:]
        for place, taps in enumerate((even, odd)):
            chosen = jnp.concatenate(
                [
                    second[
                        clip * width : (clip + 1) * width,
                        (kind + place) * outputs : (kind + place + 1) * outputs,
                    ]
                    for clip in range(clips)
                ],
                axis=1,
            )
            products = dot(
                chosen, jnp.concatenate([second_rows[shift] for _, shift in taps], axis=1)
            )
            for at, (tap, _) in enumerate(taps):
                raw[1, tap] = products[:, at * wide : (at + 1) * wide]

    for layer in range(2):
        for group in range(width // 16):
            lanes = jnp.concatenate(
                [
                    raw[layer, :, pl.ds(16 * group + 8 * at, 8), :].reshape(8 * TAPS, wide)
                    for at in range(2)
                ],
                axis=1,
            )
            high, low = halves(lanes)
            mixed = (
                dot(mixers_ref[layer, 0], high)
                + dot(mixers_ref[layer, 0], low)
                + dot(mixers_ref[layer, 1], high)
            )
            rows = jnp.concatenate(
                [
                    mixed[:, at * wide : (at + 1) * wide].reshape(TAPS, 8, wide)
                    for at in range(2)
                ],
                axis=1,
            )
            out_ref[layer, :, pl.ds(16 * group, 16), :] = rows.astype(BF16)


def turned(block, axes, steps):
    sizes = [lax.axis_size(axis) for axis in axes]
    if not any(step % size for step, size in zip(steps, sizes)):
        return block
    route = []
    for place in np.ndindex(*sizes):
        target = [(at + step) % size for at, step, size in zip(place, steps, sizes)]
        route.append(
            (int(np.ravel_multi_index(place, sizes)), int(np.ravel_multi_index(target, sizes)))
        )
    return lax.ppermute(block, axes, route)


def doubled(size):
    return size & (size - 1) == 0


def first_round(block):
    size = lax.axis_size("fsdp")
    if not doubled(size):
        return [block] + [turned(block, ("fsdp",), (distance,)) for distance in range(1, size)]
    if size == 1:
        return [block]
    return [block, lax.ppermute(block, "fsdp", [(i, i ^ 1) for i in range(size)])]


def later_rounds(blocks):
    size = lax.axis_size("fsdp")
    held = [block[None] for block in blocks]
    step = 2
    while doubled(size) and step < size:
        route = [(i, i ^ step) for i in range(size)]
        held.append(lax.ppermute(jnp.concatenate(held, axis=0), "fsdp", route))
        step *= 2
    return held


def factor_origin(place, distance, size):
    if doubled(size):
        return place ^ distance
    return lax.rem(place + (size - distance), size)


def shards(clip_input, first_kernel, second_kernel, out_grad, tap_mix, left_panels, right_panels):
    clips, frames, side, _, channels = clip_input.shape
    wide = first_kernel.shape[2]
    width = right_panels.shape[2]
    half, quarter = side // 2, side // 4
    half_frames = frames // 2
    cells = half_frames * half * half
    clip_parts = lax.axis_size("tm")
    cores, chips = lax.axis_size("core"), lax.axis_size("chip")
    equals = chips * clip_parts
    parts = equals * cores
    slices = lax.axis_size("fsdp")
    share = cells // slices
    assert clips == 1 and frames == 4
    x = clip_input.reshape(frames, half, 2, side, channels)
    grad = out_grad.reshape(quarter, quarter, channels)
    place, chip_at, core_at, half_at = (
        lax.axis_index(axis).reshape(1) for axis in ("fsdp", "chip", "core", "tm")
    )

    pick = jnp.asarray(column_picks(side), BF16)
    pad = (half // 8 + 1) * 8
    rows = quarter * quarter * channels // wide
    projected, halo = pl.pallas_call(
        project_kernel,
        out_shape=(
            jax.ShapeDtypeStruct((8 * cells + rows, wide), BF16),
            jax.ShapeDtypeStruct((half * half + rows, wide), F32),
        ),
        in_specs=[ANY] * 5,
        out_specs=(VMEM, VMEM),
        scratch_shapes=[
            pltpu.VMEM(x.shape, BF16),
            pltpu.VMEM(left_panels.shape[1:], F32),
            pltpu.VMEM(grad.shape, BF16),
            pltpu.VMEM(pick.shape, BF16),
            pltpu.VMEM((9,) + first_kernel.shape[1:], BF16),
            pltpu.VMEM((quarter * quarter, channels), F32),
            pltpu.VMEM((3, pad + half * half, wide), F32),
            pltpu.SemaphoreType.DMA((8,)),
        ],
        compiler_params=pltpu.CompilerParams(vmem_limit_bytes=58 << 20),
        cost_estimate=pl.CostEstimate(
            flops=4 * frames * side * side * channels * wide,
            bytes_accessed=PROJECT_COST,
            transcendentals=0,
        ),
    )(x, left_panels, grad, pick, first_kernel)
    if clip_parts == 2:
        prior = later = lax.ppermute(halo, "tm", [(0, 1), (1, 0)])
    else:
        prior, later = shifted(halo, "tm", 1), shifted(halo, "tm", -1)
    right = right_panels.transpose(0, 2, 1)
    right = first_round(right)
    projected, right = lax.optimization_barrier((projected, right))
    right = later_rounds(right)
    held = jnp.stack(
        [
            turned(projected, ("chip", "tm"), steps)
            for steps in np.ndindex(chips, clip_parts)
        ]
    )

    spread = jnp.asarray(spread_picks(half), BF16)
    acts = pl.pallas_call(
        functools.partial(hidden_kernel, clip_parts=clip_parts),
        out_shape=jax.ShapeDtypeStruct((equals, slices, 2, share, wide), BF16),
        in_specs=[SMEM] + [VMEM] * 6 + [HBM] * 2,
        out_specs=VMEM,
        scratch_shapes=[
            pltpu.VMEM((quarter * quarter, channels), F32),
            pltpu.VMEM((frames, 2, 2, half * half, channels), BF16),
            pltpu.VMEM(first_kernel.shape, BF16),
            pltpu.VMEM(second_kernel.shape, BF16),
            pltpu.VMEM((3, pad + cells, wide), F32),
            pltpu.SemaphoreType.DMA((2, 3)),
        ],
        compiler_params=pltpu.CompilerParams(vmem_limit_bytes=ROOM),
        cost_estimate=pl.CostEstimate(
            flops=3 * cells * TAPS * channels * wide,
            bytes_accessed=HIDDEN_COST,
            transcendentals=cells * wide,
        ),
    )(
        half_at, x, prior, grad, later, pick, spread, first_kernel, second_kernel,
    )
    acts, *right = lax.optimization_barrier((acts, *right))
    clip_cells = clip_parts * cells
    shift_picks, sort_picks, mixers = pl.pallas_call(
        functools.partial(tables_kernel, slices=slices, clip_parts=clip_parts, half=half),
        out_shape=(
            jax.ShapeDtypeStruct((clip_cells, 8 * clip_cells), BF16),
            jax.ShapeDtypeStruct((clip_cells, clip_cells), BF16),
            jax.ShapeDtypeStruct((2, 2, 8 * TAPS, 8 * TAPS), BF16),
        ),
        in_specs=[ANY, VMEM],
        out_specs=(VMEM,) * 3,
        compiler_params=pltpu.CompilerParams(vmem_limit_bytes=16 << 20),
        cost_estimate=pl.CostEstimate(flops=0, bytes_accessed=4 << 20, transcendentals=0),
    )(acts, tap_mix)
    every = lax.all_to_all(
        acts.reshape(equals * slices, 2, share, wide), ("chip", "tm", "fsdp"), 0, 0, tiled=True
    ).reshape(equals, slices, 2, share, wide)
    every, held = lax.optimization_barrier((every, held))
    every = [turned(every, ("core",), (cross,)) for cross in range(cores)]
    columns = pl.pallas_call(
        functools.partial(right_kernel, cores=cores),
        out_shape=jax.ShapeDtypeStruct((cores, 2 * width, equals * share), BF16),
        in_specs=[SMEM] * 2 + [VMEM] * (cores + len(right)),
        out_specs=VMEM,
        compiler_params=pltpu.CompilerParams(vmem_limit_bytes=16 << 20),
    )(place, core_at, *every, *right)
    columns, held = lax.optimization_barrier((columns, held))
    columns = [turned(columns, ("fsdp",), (distance,)) for distance in range(slices)]
    left_rows = [turned(held, ("core",), (cross,)) for cross in range(cores)]

    result = pl.pallas_call(
        functools.partial(
            update_kernel, slices=slices, cores=cores, clip_parts=clip_parts, half=half
        ),
        out_shape=jax.ShapeDtypeStruct((2, TAPS, width, wide), BF16),
        in_specs=[SMEM] * 4
        + [VMEM] * len(columns)
        + [ANY] * cores
        + [VMEM] * 4,
        out_specs=VMEM,
        scratch_shapes=[
            pltpu.VMEM((parts,) + projected.shape, BF16),
            pltpu.VMEM((slices, cores, 2 * width, equals * share), BF16),
            pltpu.VMEM((8, parts // clip_parts, width, clip_cells), BF16),
            pltpu.VMEM((parts * cells // 8 + (quarter + 1) * quarter + 8, wide), F32),
            pltpu.VMEM((2, TAPS, width, wide), F32),
            pltpu.SemaphoreType.DMA((parts,)),
        ],
        compiler_params=pltpu.CompilerParams(vmem_limit_bytes=40 << 20),
    )(
        place, chip_at, core_at, half_at,
        *columns, *left_rows, left_panels, mixers, shift_picks, sort_picks,
    )
    return result.transpose(0, 1, 3, 2)


def solution(mesh):
    fsdp, replica, tm = (mesh.shape[axis] for axis in ("fsdp", "replica", "tm"))
    cores = 2 if replica % 2 == 0 else 1
    assert mesh.axis_names == ("fsdp", "replica", "tm")
    mesh = Mesh(
        mesh.devices.reshape(fsdp, replica // cores, cores, tm), ("fsdp", "chip", "core", "tm")
    )
    replica = ("chip", "core")
    in_specs = (
        P(replica, "tm", None, None, None),
        P(None, None, "fsdp"),
        P(None, "fsdp", None),
        P(replica, "tm", None, None, None),
        P(),
        P(None, "fsdp", None),
        P(None, "fsdp", (*replica, "tm")),
    )
    out_specs = P(None, None, "fsdp", (*replica, "tm"))
    return jax.shard_map(shards, mesh=mesh, in_specs=in_specs, out_specs=out_specs, check_vma=False)
```

```python
import functools

import jax
import jax.numpy as jnp
import numpy as np
from jax import lax
from jax.experimental import pallas as pl
from jax.experimental.pallas import tpu as pltpu
from jax.sharding import Mesh, PartitionSpec as P

TAPS = 27
F32, BF16 = jnp.float32, jnp.bfloat16
ROOM = 50 << 20
PROJECT_COST = 16 << 20
HIDDEN_COST = 200 << 20
NT = (((1,), (1,)), ((), ()))
VMEM = pl.BlockSpec(memory_space=pltpu.VMEM)
HBM = pl.BlockSpec(memory_space=pltpu.HBM)
SMEM = pl.BlockSpec(memory_space=pltpu.SMEM)
ANY = pl.BlockSpec(memory_space=pl.ANY)


def shifted(block, axis, distance):
    devices = range(lax.axis_size(axis))
    route = [(i - distance, i) for i in devices if i - distance in devices]
    return lax.ppermute(block, axis, route)


def dot(left, right):
    return jnp.dot(left, right, preferred_element_type=F32)


def dot_nt(left, right):
    return lax.dot_general(left, right, NT, preferred_element_type=F32)


def quotient(value, size):
    return value >> (size.bit_length() - 1) if size & (size - 1) == 0 else value // size


def remainder(value, size):
    return value & (size - 1) if size & (size - 1) == 0 else value % size


def halves(value):
    high = value.astype(BF16)
    return high, (value - high.astype(F32)).astype(BF16)


def column_picks(side):
    half = side // 2
    picks = np.zeros((2, half, half, half, side), np.float32)
    for row in range(half):
        for x in range(side):
            picks[x % 2, row, x // 2, row, x] = 1
    return picks.reshape(half * side, half * side)


def spread_picks(half):
    quarter = half // 2
    picks = np.zeros((3, 3, half, half, quarter, quarter), np.float32)
    for b in range(3):
        for c in range(3):
            for out_y in range(quarter):
                for out_x in range(quarter):
                    y, x = 2 * out_y + b - 1, 2 * out_x + c - 1
                    if y >= 0 and x >= 0:
                        picks[b, c, y, x, out_y, out_x] = 1
    return picks.reshape(9 * half * half, quarter * quarter)


def parity_rows(lines, pick):
    rows = dot(pick, lines).astype(BF16)
    cells = rows.shape[0] // 2
    return rows[:cells], rows[cells:]


def folded_taps(rows, weights, shift_ref, half):
    sums = {}
    for line, column in np.ndindex(2, 2):
        taps = [(b, c) for b in ((2, 0) if line else (1,)) for c in ((2, 0) if column else (1,))]
        product = dot(rows(line, column), jnp.concatenate([weights(*tap) for tap in taps], axis=1))
        wide = product.shape[1] // len(taps)
        for at, (b, c) in enumerate(taps):
            part = product[:, at * wide : (at + 1) * wide]
            key = (int(b == 0), int(c == 0))
            sums[key] = sums[key] + part if key in sums else part
    total = sums.pop((0, 0))
    count, wide = total.shape
    pad = shift_ref.shape[1] - count
    places = lax.broadcasted_iota(jnp.int32, (count, wide), 0)
    row = remainder(quotient(places, half), half)
    column = remainder(places, half)
    for at, ((dr, dc), part) in enumerate(sums.items()):
        shift_ref[at, pl.ds(pad, count), :] = part
        moved = shift_ref[at, pl.ds(pad - (dr * half + dc), count), :]
        total += jnp.where((row >= dr) & (column >= dc), moved, 0.0)
    return total


def project_kernel(
    x_any, left_any, grad_any, pick_any, first_any,
    out_ref, halo_ref, x_ref, left_ref, grad_ref, pick_ref, first_ref, rows_ref, shift_ref, arrived,
):
    frames, half, _, side, channels = x_ref.shape
    order = [frame for time in (1, 0) for frame in range(time, frames, 2)]
    pairs_of = [
        (left_any.at[0], left_ref),
        (x_any.at[order[0]], x_ref.at[order[0]]),
        (x_any.at[order[1]], x_ref.at[order[1]]),
        (pick_any, pick_ref),
        (first_any.at[pl.ds(0, 9)], first_ref),
        (x_any.at[order[2]], x_ref.at[order[2]]),
        (x_any.at[order[3]], x_ref.at[order[3]]),
        (grad_any, grad_ref),
    ]
    copies = [
        pltpu.make_async_copy(source, target, arrived.at[at])
        for at, (source, target) in enumerate(pairs_of)
    ]
    for copy in copies:
        copy.start()
    wide = left_ref.shape[0]
    pairs = frames // 2
    size = pairs * half * side
    target = lax.broadcasted_iota(jnp.int32, (size, size), 0)
    source = lax.broadcasted_iota(jnp.int32, (size, size), 1)
    cells = size // 2
    wanted = 2 * remainder(target, cells) + quotient(target, cells)
    pick = jnp.where(source == wanted, 1.0, 0.0).astype(BF16)
    copies[0].wait()
    both = jnp.concatenate(halves(left_ref[...]), axis=0)

    def project(time):
        for row in range(2):
            block = jnp.concatenate(
                [
                    x_ref[frame, :, row].reshape(half * side, channels)
                    for frame in range(time, frames, 2)
                ],
                axis=0,
            )
            full = dot_nt(block, both)
            small = (full[:, :wide] + full[:, wide:]).astype(BF16)
            ordered = dot(pick, small).astype(BF16)
            at = (4 * time + 2 * row) * cells
            out_ref[at : at + size, :] = ordered

    copies[1].wait()
    copies[2].wait()
    project(1)
    copies[3].wait()
    classes = [
        parity_rows(x_ref[frames - 1, :, line].reshape(half * side, channels), pick_ref[...])
        for line in range(2)
    ]
    copies[4].wait()
    halo_ref[pl.ds(0, half * half), :] = folded_taps(
        lambda line, column: classes[line][column],
        lambda b, c: first_ref[3 * b + c],
        shift_ref,
        half,
    )
    copies[5].wait()
    copies[6].wait()
    project(0)
    copies[7].wait()
    grad_rows = stacked_rows(grad_ref, rows_ref)
    count = grad_rows.shape[0]
    for block in range(channels // wide):
        at = 8 * cells + block * count
        out_ref[at : at + count, :] = grad_rows[:, block * wide : (block + 1) * wide]
        at = half * half + block * count
        halo_ref[at : at + count, :] = rows_ref[:, block * wide : (block + 1) * wide]


def stacked_rows(grad_ref, rows_ref):
    quarter = grad_ref.shape[0]
    for row in range(quarter):
        rows_ref[pl.ds(row * quarter, quarter), :] = grad_ref[row].astype(F32)
    return rows_ref[...].astype(BF16)


def transposed_products(rows, kernel, taps):
    total = dot_nt(rows[0], kernel[taps[0]])
    for at in range(1, len(taps)):
        total += dot_nt(rows[at], kernel[taps[at]])
    return total


def spread_rows(picks_ref, rows, cells):
    spread = dot(picks_ref[...], rows).astype(BF16)
    return [spread[tap * cells : (tap + 1) * cells] for tap in range(9)]


def hidden_kernel(
    tm_ref, x_ref, prior_ref, grad_ref, later_ref, pick_ref, spread_ref,
    first_any, second_any, out_ref, rows_ref, classes, first, second, shift_ref, arrived, *,
    clip_parts,
):
    frames, half, _, side, channels = x_ref.shape
    cells = half * half
    has_prior = jnp.where(tm_ref[0] > 0, 1.0, 0.0)
    has_later = jnp.where(tm_ref[0] < clip_parts - 1, 1.0, 0.0)
    copies = {
        (at, a): pltpu.make_async_copy(
            source.at[pl.ds(9 * a, 9)], target.at[pl.ds(9 * a, 9)], arrived.at[at, a]
        )
        for at, (source, target) in enumerate(((second_any, second), (first_any, first)))
        for a in (1, 2, 0)
    }
    for copy in copies.values():
        copy.start()
    own_rows = stacked_rows(grad_ref, rows_ref)
    own = spread_rows(spread_ref, own_rows, cells)
    copies[0, 1].wait()
    copies[0, 2].wait()
    both = None
    for tap in range(9):
        pair = jnp.concatenate([second[9 + tap], second[18 + tap]], axis=0)
        term = dot_nt(own[tap], pair)
        both = term if both is None else both + term
    early, late = both[:, : second.shape[1]], both[:, second.shape[1] :]
    for frame in range(frames):
        for line in range(2):
            lines = x_ref[frame, :, line].reshape(half * side, channels)
            classes[frame, line, 0], classes[frame, line, 1] = parity_rows(lines, pick_ref[...])
    count = own_rows.shape[0]
    wide = first.shape[2]
    later_rows = jnp.concatenate(
        [
            later_ref[pl.ds(cells + count * block, count), :]
            for block in range(channels // wide)
        ],
        axis=1,
    )
    after = spread_rows(spread_ref, later_rows.astype(BF16), cells)
    copies[0, 0].wait()
    late += transposed_products(after, second, range(9)) * has_later
    hidden_grad = jnp.concatenate([early, late], axis=0)
    nothing = jnp.zeros((cells, channels), BF16)

    def rows_of(line, column):
        held = [classes[frame, line, column] for frame in range(frames)]
        return jnp.concatenate(
            [
                jnp.concatenate([nothing, held[0], held[1]], axis=1),
                jnp.concatenate([held[1], held[2], held[3]], axis=1),
            ],
            axis=0,
        )

    for a in (1, 2, 0):
        copies[1, a].wait()
    pre = folded_taps(
        rows_of,
        lambda b, c: jnp.concatenate([first[9 * a + 3 * b + c] for a in range(3)], axis=0),
        shift_ref,
        half,
    )
    pre += jnp.concatenate(
        [prior_ref[pl.ds(0, cells), :] * has_prior, jnp.zeros((cells, wide), F32)], axis=0
    )
    sig = jax.nn.sigmoid(pre)
    hidden = (pre * sig).astype(BF16)
    pre_grad = (hidden_grad * sig * (1.0 + pre * (1.0 - sig))).astype(BF16)
    groups, slices, _, share, _ = out_ref.shape
    for at in range(slices):
        place = slice(at * share, (at + 1) * share)
        for group in range(groups):
            out_ref[group, at, 0] = pre_grad[place]
            out_ref[group, at, 1] = hidden[place]


def right_kernel(place_ref, core_ref, *refs, cores):
    acts_refs, right_refs, out_ref = refs[:cores], refs[cores:-1], refs[-1]
    parts, slices = acts_refs[0].shape[:2]
    width = right_refs[0].shape[2]
    for layer in range(2):
        rights = [
            jnp.concatenate(halves(ref[at, layer]), axis=0)
            for ref in right_refs
            for at in range(ref.shape[0])
        ]
        for cross, acts_ref in enumerate(acts_refs):
            total = None
            for distance in range(slices):
                origin = factor_origin(place_ref[0], distance, slices)
                rows = jnp.concatenate(
                    [acts_ref[part, origin, layer] for part in range(parts)], axis=0
                )
                term = dot_nt(rights[distance], rows)
                total = term if total is None else total + term
            core = lax.rem(core_ref[0] + cross, cores)
            out_ref[core, pl.ds(layer * width, width), :] = (total[:width] + total[width:]).astype(
                BF16
            )


def tables_kernel(after_any, mix_ref, shift_ref, sort_ref, mixers_ref, *, slices, clip_parts, half):
    del after_any
    size = shift_ref.shape[0]
    cells = size // clip_parts
    share = cells // slices
    frames = size // (half * half)
    held = lax.broadcasted_iota(jnp.int32, (size, size), 0)
    cell = lax.broadcasted_iota(jnp.int32, (size, size), 1)
    part = remainder(quotient(held, share), clip_parts)
    slot = quotient(held, share * clip_parts)
    natural = part * cells + slot * share + remainder(held, share)
    frame = quotient(cell, half * half)
    row = remainder(quotient(cell, half), half)
    column = remainder(cell, half)
    for shift in range(8):
        dt, dr, dc = shift // 4, shift // 2 % 2, shift % 2
        found = natural == cell + ((dt * half + dr) * half + dc)
        if dt:
            found &= frame < frames - 1
        if dr:
            found &= row < half - 1
        if dc:
            found &= column < half - 1
        shift_ref[:, pl.ds(shift * size, size)] = jnp.where(found, 1.0, 0.0).astype(BF16)
    quarter = half // 2
    outputs = size // 8
    kind = quotient(cell, outputs)
    frame = 2 * remainder(quotient(cell, quarter * quarter), frames // 2) + quotient(kind, 4)
    row = 2 * remainder(quotient(cell, quarter), quarter) + remainder(quotient(kind, 2), 2)
    column = 2 * remainder(cell, quarter) + remainder(kind, 2)
    found = natural == (frame * half + row) * half + column
    sort_ref[...] = jnp.where(found, 1.0, 0.0).astype(BF16)

    count = mixers_ref.shape[2]
    tap = lax.broadcasted_iota(jnp.int32, (count, TAPS), 1)
    line = lax.broadcasted_iota(jnp.int32, (count, TAPS), 0)
    spread = jnp.where(quotient(line, 8) == tap, 1.0, 0.0).astype(BF16)
    lines = lax.broadcasted_iota(jnp.int32, (count, count), 0)
    others = lax.broadcasted_iota(jnp.int32, (count, count), 1)
    same = remainder(lines, 8) == remainder(others, 8)
    for layer in range(2):
        for at, part in enumerate(halves(mix_ref[layer])):
            wider = dot_nt(dot(spread, part).astype(BF16), spread)
            mixers_ref[layer, at] = jnp.where(same, wider, 0.0).astype(BF16)


def update_kernel(
    place_ref, chip_ref, core_ref, tm_ref, *refs, slices, cores, clip_parts, half
):
    columns_refs, piece_refs = refs[:slices], refs[slices : slices + cores]
    (
        left_ref, mixers_ref, shift_ref, sort_ref,
        out_ref, left_rows_ref, columns, shifts, grads, raw, arrived,
    ) = refs[slices + cores :]
    parts = left_rows_ref.shape[0]
    chips = parts // (cores * clip_parts)
    copies = []
    for cross, piece_ref in enumerate(piece_refs):
        core = lax.rem(core_ref[0] + cross, cores)
        for at, (step, turn) in enumerate(np.ndindex(chips, clip_parts)):
            chip = lax.rem(chip_ref[0] + (chips - step), chips)
            place = lax.rem(tm_ref[0] + (clip_parts - turn), clip_parts)
            target = left_rows_ref.at[(chip * cores + core) * clip_parts + place]
            copies.append(
                pltpu.make_async_copy(piece_ref.at[at], target, arrived.at[len(copies)])
            )
    for copy in copies:
        copy.start()
    for distance in range(slices):
        origin = lax.rem(place_ref[0] + (slices - distance), slices)
        columns[origin] = columns_refs[distance][...]
    wide, channels = left_ref.shape[1:]
    width = columns.shape[2] // 2
    clips = parts // clip_parts
    share = columns.shape[3] // chips
    clip_cells = slices * share
    cells = clip_cells // clip_parts
    frames = clip_cells // (half * half)
    outputs = clip_cells // 8

    def by_clip(layer):
        return jnp.concatenate(
            [
                jnp.concatenate(
                    [
                        columns[
                            at, clip % cores, pl.ds(layer * width, width),
                            pl.ds(clip // cores * share, share),
                        ]
                        for at in range(slices)
                    ],
                    axis=1,
                )
                for clip in range(clips)
            ],
            axis=0,
        )

    first = by_clip(0)
    for shift in range(8):
        moved = dot(first, shift_ref[:, pl.ds(shift * clip_cells, clip_cells)]).astype(BF16)
        for clip in range(clips):
            shifts[shift, clip] = moved[clip * width : (clip + 1) * width]
    second = dot(by_clip(1), sort_ref[...]).astype(BF16)

    for copy in copies:
        copy.wait()
    own_outputs = outputs // clip_parts
    blocks = channels // wide
    out_grad = jnp.concatenate(
        [
            jnp.concatenate(
                [
                    left_rows_ref[part, pl.ds(8 * cells + own_outputs * at, own_outputs), :]
                    for at in range(blocks)
                ],
                axis=1,
            )
            for part in range(parts)
        ],
        axis=0,
    )
    full = dot_nt(out_grad, jnp.concatenate(halves(left_ref[1]), axis=0))
    total = parts * own_outputs
    quarter = half // 2
    grads[pl.ds(0, total), :] = full[:, :wide] + full[:, wide:]
    places = lax.broadcasted_iota(jnp.int32, (total, wide), 0)
    frame = remainder(quotient(places, quarter * quarter), frames // 2)
    row = remainder(quotient(places, quarter), quarter)
    column = remainder(places, quarter)
    second_rows = []
    for shift in range(8):
        dt, dr, dc = shift // 4, shift // 2 % 2, shift % 2
        moved = grads[pl.ds((dt * quarter + dr) * quarter + dc, total), :]
        inside = (frame + dt < frames // 2) & (row + dr < quarter) & (column + dc < quarter)
        second_rows.append(jnp.where(inside, moved, 0.0).astype(BF16))

    for time, line in np.ndindex(2, 2):
        even = [
            (9 * a + 3 * b + 1, 4 * (a == 0) + 2 * (b == 0))
            for a in ((0, 2) if time else (1,))
            for b in ((0, 2) if line else (1,))
        ]
        odd = [(tap + 1, shift) for tap, shift in even] + [
            (tap - 1, shift + 1) for tap, shift in even
        ]
        kind = 4 * time + 2 * line
        sums = None
        for clip in range(clips):
            left = jnp.concatenate([shifts[shift, clip] for _, shift in odd], axis=0)
            rows = jnp.concatenate(
                [
                    jnp.concatenate(
                        [
                            left_rows_ref[
                                clip * clip_parts + part, pl.ds((kind + at) * cells, cells), :
                            ]
                            for part in range(clip_parts)
                        ],
                        axis=0,
                    )
                    for at in range(2)
                ],
                axis=1,
            )
            term = dot(left, rows)
            sums = term if sums is None else sums + term
        for at, (tap, _) in enumerate(even):
            raw[0, tap] = sums[at * width : (at + 1) * width, :wide]
        for at, (tap, _) in enumerate(odd):
            raw[0, tap] = sums[at * width : (at + 1) * width, wide:]
        for place, taps in enumerate((even, odd)):
            chosen = jnp.concatenate(
                [
                    second[
                        clip * width : (clip + 1) * width,
                        (kind + place) * outputs : (kind + place + 1) * outputs,
                    ]
                    for clip in range(clips)
                ],
                axis=1,
            )
            products = dot(
                chosen, jnp.concatenate([second_rows[shift] for _, shift in taps], axis=1)
            )
            for at, (tap, _) in enumerate(taps):
                raw[1, tap] = products[:, at * wide : (at + 1) * wide]

    for layer in range(2):
        for group in range(width // 16):
            lanes = jnp.concatenate(
                [
                    raw[layer, :, pl.ds(16 * group + 8 * at, 8), :].reshape(8 * TAPS, wide)
                    for at in range(2)
                ],
                axis=1,
            )
            high, low = halves(lanes)
            mixed = (
                dot(mixers_ref[layer, 0], high)
                + dot(mixers_ref[layer, 0], low)
                + dot(mixers_ref[layer, 1], high)
            )
            rows = jnp.concatenate(
                [
                    mixed[:, at * wide : (at + 1) * wide].reshape(TAPS, 8, wide)
                    for at in range(2)
                ],
                axis=1,
            )
            out_ref[layer, :, pl.ds(16 * group, 16), :] = rows.astype(BF16)


def turned(block, axes, steps):
    sizes = [lax.axis_size(axis) for axis in axes]
    if not any(step % size for step, size in zip(steps, sizes)):
        return block
    route = []
    for place in np.ndindex(*sizes):
        target = [(at + step) % size for at, step, size in zip(place, steps, sizes)]
        route.append(
            (int(np.ravel_multi_index(place, sizes)), int(np.ravel_multi_index(target, sizes)))
        )
    return lax.ppermute(block, axes, route)


def doubled(size):
    return size & (size - 1) == 0


def first_round(block):
    size = lax.axis_size("fsdp")
    if not doubled(size):
        return [block] + [turned(block, ("fsdp",), (distance,)) for distance in range(1, size)]
    if size == 1:
        return [block]
    return [block, lax.ppermute(block, "fsdp", [(i, i ^ size // 2) for i in range(size)])]


def later_rounds(blocks):
    size = lax.axis_size("fsdp")
    held = [block[None] for block in blocks]
    step = size // 4
    while doubled(size) and step:
        route = [(i, i ^ step) for i in range(size)]
        held.append(lax.ppermute(jnp.concatenate(held, axis=0), "fsdp", route))
        step //= 2
    return held


def factor_origin(place, distance, size):
    if doubled(size):
        bits = range(size.bit_length() - 1)
        return place ^ sum(size >> (bit + 1) for bit in bits if distance >> bit & 1)
    return lax.rem(place + (size - distance), size)


def shards(clip_input, first_kernel, second_kernel, out_grad, tap_mix, left_panels, right_panels):
    clips, frames, side, _, channels = clip_input.shape
    wide = first_kernel.shape[2]
    width = right_panels.shape[2]
    half, quarter = side // 2, side // 4
    half_frames = frames // 2
    cells = half_frames * half * half
    clip_parts = lax.axis_size("tm")
    cores, chips = lax.axis_size("core"), lax.axis_size("chip")
    equals = chips * clip_parts
    parts = equals * cores
    slices = lax.axis_size("fsdp")
    share = cells // slices
    assert clips == 1 and frames == 4
    x = clip_input.reshape(frames, half, 2, side, channels)
    grad = out_grad.reshape(quarter, quarter, channels)
    place, chip_at, core_at, half_at = (
        lax.axis_index(axis).reshape(1) for axis in ("fsdp", "chip", "core", "tm")
    )

    pick = jnp.asarray(column_picks(side), BF16)
    pad = (half // 8 + 1) * 8
    rows = quarter * quarter * channels // wide
    projected, halo = pl.pallas_call(
        project_kernel,
        out_shape=(
            jax.ShapeDtypeStruct((8 * cells + rows, wide), BF16),
            jax.ShapeDtypeStruct((half * half + rows, wide), F32),
        ),
        in_specs=[ANY] * 5,
        out_specs=(VMEM, VMEM),
        scratch_shapes=[
            pltpu.VMEM(x.shape, BF16),
            pltpu.VMEM(left_panels.shape[1:], F32),
            pltpu.VMEM(grad.shape, BF16),
            pltpu.VMEM(pick.shape, BF16),
            pltpu.VMEM((9,) + first_kernel.shape[1:], BF16),
            pltpu.VMEM((quarter * quarter, channels), F32),
            pltpu.VMEM((3, pad + half * half, wide), F32),
            pltpu.SemaphoreType.DMA((8,)),
        ],
        compiler_params=pltpu.CompilerParams(vmem_limit_bytes=58 << 20),
        cost_estimate=pl.CostEstimate(
            flops=4 * frames * side * side * channels * wide,
            bytes_accessed=PROJECT_COST,
            transcendentals=0,
        ),
    )(x, left_panels, grad, pick, first_kernel)
    if clip_parts == 2:
        prior = later = lax.ppermute(halo, "tm", [(0, 1), (1, 0)])
    else:
        prior, later = shifted(halo, "tm", 1), shifted(halo, "tm", -1)
    right = right_panels.transpose(0, 2, 1)
    right = first_round(right)
    projected, right = lax.optimization_barrier((projected, right))
    right = later_rounds(right)
    held = jnp.stack(
        [
            turned(projected, ("chip", "tm"), steps)
            for steps in np.ndindex(chips, clip_parts)
        ]
    )

    spread = jnp.asarray(spread_picks(half), BF16)
    acts = pl.pallas_call(
        functools.partial(hidden_kernel, clip_parts=clip_parts),
        out_shape=jax.ShapeDtypeStruct((equals, slices, 2, share, wide), BF16),
        in_specs=[SMEM] + [VMEM] * 6 + [HBM] * 2,
        out_specs=VMEM,
        scratch_shapes=[
            pltpu.VMEM((quarter * quarter, channels), F32),
            pltpu.VMEM((frames, 2, 2, half * half, channels), BF16),
            pltpu.VMEM(first_kernel.shape, BF16),
            pltpu.VMEM(second_kernel.shape, BF16),
            pltpu.VMEM((3, pad + cells, wide), F32),
            pltpu.SemaphoreType.DMA((2, 3)),
        ],
        compiler_params=pltpu.CompilerParams(vmem_limit_bytes=ROOM),
        cost_estimate=pl.CostEstimate(
            flops=3 * cells * TAPS * channels * wide,
            bytes_accessed=HIDDEN_COST,
            transcendentals=cells * wide,
        ),
    )(
        half_at, x, prior, grad, later, pick, spread, first_kernel, second_kernel,
    )
    acts, *right = lax.optimization_barrier((acts, *right))
    clip_cells = clip_parts * cells
    shift_picks, sort_picks, mixers = pl.pallas_call(
        functools.partial(tables_kernel, slices=slices, clip_parts=clip_parts, half=half),
        out_shape=(
            jax.ShapeDtypeStruct((clip_cells, 8 * clip_cells), BF16),
            jax.ShapeDtypeStruct((clip_cells, clip_cells), BF16),
            jax.ShapeDtypeStruct((2, 2, 8 * TAPS, 8 * TAPS), BF16),
        ),
        in_specs=[ANY, VMEM],
        out_specs=(VMEM,) * 3,
        compiler_params=pltpu.CompilerParams(vmem_limit_bytes=16 << 20),
        cost_estimate=pl.CostEstimate(flops=0, bytes_accessed=4 << 20, transcendentals=0),
    )(acts, tap_mix)
    every = lax.all_to_all(
        acts.reshape(equals * slices, 2, share, wide), ("chip", "tm", "fsdp"), 0, 0, tiled=True
    ).reshape(equals, slices, 2, share, wide)
    every, held = lax.optimization_barrier((every, held))
    every = [turned(every, ("core",), (cross,)) for cross in range(cores)]
    columns = pl.pallas_call(
        functools.partial(right_kernel, cores=cores),
        out_shape=jax.ShapeDtypeStruct((cores, 2 * width, equals * share), BF16),
        in_specs=[SMEM] * 2 + [VMEM] * (cores + len(right)),
        out_specs=VMEM,
        compiler_params=pltpu.CompilerParams(vmem_limit_bytes=16 << 20),
    )(place, core_at, *every, *right)
    columns, held = lax.optimization_barrier((columns, held))
    columns = [turned(columns, ("fsdp",), (distance,)) for distance in range(slices)]
    left_rows = [turned(held, ("core",), (cross,)) for cross in range(cores)]

    result = pl.pallas_call(
        functools.partial(
            update_kernel, slices=slices, cores=cores, clip_parts=clip_parts, half=half
        ),
        out_shape=jax.ShapeDtypeStruct((2, TAPS, width, wide), BF16),
        in_specs=[SMEM] * 4
        + [VMEM] * len(columns)
        + [ANY] * cores
        + [VMEM] * 4,
        out_specs=VMEM,
        scratch_shapes=[
            pltpu.VMEM((parts,) + projected.shape, BF16),
            pltpu.VMEM((slices, cores, 2 * width, equals * share), BF16),
            pltpu.VMEM((8, parts // clip_parts, width, clip_cells), BF16),
            pltpu.VMEM((parts * cells // 8 + (quarter + 1) * quarter + 8, wide), F32),
            pltpu.VMEM((2, TAPS, width, wide), F32),
            pltpu.SemaphoreType.DMA((parts,)),
        ],
        compiler_params=pltpu.CompilerParams(vmem_limit_bytes=40 << 20),
    )(
        place, chip_at, core_at, half_at,
        *columns, *left_rows, left_panels, mixers, shift_picks, sort_picks,
    )
    return result.transpose(0, 1, 3, 2)


def solution(mesh):
    fsdp, replica, tm = (mesh.shape[axis] for axis in ("fsdp", "replica", "tm"))
    cores = 2 if replica % 2 == 0 else 1
    assert mesh.axis_names == ("fsdp", "replica", "tm")
    mesh = Mesh(
        mesh.devices.reshape(fsdp, replica // cores, cores, tm), ("fsdp", "chip", "core", "tm")
    )
    replica = ("chip", "core")
    in_specs = (
        P(replica, "tm", None, None, None),
        P(None, None, "fsdp"),
        P(None, "fsdp", None),
        P(replica, "tm", None, None, None),
        P(),
        P(None, "fsdp", None),
        P(None, "fsdp", (*replica, "tm")),
    )
    out_specs = P(None, None, "fsdp", (*replica, "tm"))
    return jax.shard_map(shards, mesh=mesh, in_specs=in_specs, out_specs=out_specs, check_vma=False)
```

```python
import functools

import jax
import jax.numpy as jnp
import numpy as np
from jax import lax
from jax.experimental import pallas as pl
from jax.experimental.pallas import tpu as pltpu
from jax.sharding import Mesh, PartitionSpec as P

TAPS = 27
F32, BF16 = jnp.float32, jnp.bfloat16
ROOM = 50 << 20
PROJECT_COST = 16 << 20
HIDDEN_COST = 200 << 20
NT = (((1,), (1,)), ((), ()))
VMEM = pl.BlockSpec(memory_space=pltpu.VMEM)
HBM = pl.BlockSpec(memory_space=pltpu.HBM)
SMEM = pl.BlockSpec(memory_space=pltpu.SMEM)
ANY = pl.BlockSpec(memory_space=pl.ANY)


def shifted(block, axis, distance):
    devices = range(lax.axis_size(axis))
    route = [(i - distance, i) for i in devices if i - distance in devices]
    return lax.ppermute(block, axis, route)


def dot(left, right):
    return jnp.dot(left, right, preferred_element_type=F32)


def dot_nt(left, right):
    return lax.dot_general(left, right, NT, preferred_element_type=F32)


def quotient(value, size):
    return value >> (size.bit_length() - 1) if size & (size - 1) == 0 else value // size


def remainder(value, size):
    return value & (size - 1) if size & (size - 1) == 0 else value % size


def halves(value):
    high = value.astype(BF16)
    return high, (value - high.astype(F32)).astype(BF16)


def column_picks(side):
    half = side // 2
    picks = np.zeros((2, half, half, half, side), np.float32)
    for row in range(half):
        for x in range(side):
            picks[x % 2, row, x // 2, row, x] = 1
    return picks.reshape(half * side, half * side)


def spread_picks(half):
    quarter = half // 2
    picks = np.zeros((3, 3, half, half, quarter, quarter), np.float32)
    for b in range(3):
        for c in range(3):
            for out_y in range(quarter):
                for out_x in range(quarter):
                    y, x = 2 * out_y + b - 1, 2 * out_x + c - 1
                    if y >= 0 and x >= 0:
                        picks[b, c, y, x, out_y, out_x] = 1
    return picks.reshape(9 * half * half, quarter * quarter)


def parity_rows(lines, pick):
    rows = dot(pick, lines).astype(BF16)
    cells = rows.shape[0] // 2
    return rows[:cells], rows[cells:]


def folded_taps(rows, weights, shift_ref, half):
    sums = {}
    for line, column in np.ndindex(2, 2):
        taps = [(b, c) for b in ((2, 0) if line else (1,)) for c in ((2, 0) if column else (1,))]
        product = dot(rows(line, column), jnp.concatenate([weights(*tap) for tap in taps], axis=1))
        wide = product.shape[1] // len(taps)
        for at, (b, c) in enumerate(taps):
            part = product[:, at * wide : (at + 1) * wide]
            key = (int(b == 0), int(c == 0))
            sums[key] = sums[key] + part if key in sums else part
    total = sums.pop((0, 0))
    count, wide = total.shape
    pad = shift_ref.shape[1] - count
    places = lax.broadcasted_iota(jnp.int32, (count, wide), 0)
    row = remainder(quotient(places, half), half)
    column = remainder(places, half)
    for at, ((dr, dc), part) in enumerate(sums.items()):
        shift_ref[at, pl.ds(pad, count), :] = part
        moved = shift_ref[at, pl.ds(pad - (dr * half + dc), count), :]
        total += jnp.where((row >= dr) & (column >= dc), moved, 0.0)
    return total


def project_kernel(
    x_any, left_any, grad_any, pick_any, first_any,
    out_ref, halo_ref, x_ref, left_ref, grad_ref, pick_ref, first_ref, rows_ref, shift_ref, arrived,
):
    frames, half, _, side, channels = x_ref.shape
    order = [frame for time in (1, 0) for frame in range(time, frames, 2)]
    pairs_of = [
        (left_any.at[0], left_ref),
        (x_any.at[order[0]], x_ref.at[order[0]]),
        (x_any.at[order[1]], x_ref.at[order[1]]),
        (pick_any, pick_ref),
        (first_any.at[pl.ds(0, 9)], first_ref),
        (x_any.at[order[2]], x_ref.at[order[2]]),
        (x_any.at[order[3]], x_ref.at[order[3]]),
        (grad_any, grad_ref),
    ]
    copies = [
        pltpu.make_async_copy(source, target, arrived.at[at])
        for at, (source, target) in enumerate(pairs_of)
    ]
    for copy in copies:
        copy.start()
    wide = left_ref.shape[0]
    pairs = frames // 2
    size = pairs * half * side
    target = lax.broadcasted_iota(jnp.int32, (size, size), 0)
    source = lax.broadcasted_iota(jnp.int32, (size, size), 1)
    cells = size // 2
    wanted = 2 * remainder(target, cells) + quotient(target, cells)
    pick = jnp.where(source == wanted, 1.0, 0.0).astype(BF16)
    copies[0].wait()
    both = jnp.concatenate(halves(left_ref[...]), axis=0)

    def project(time):
        for row in range(2):
            block = jnp.concatenate(
                [
                    x_ref[frame, :, row].reshape(half * side, channels)
                    for frame in range(time, frames, 2)
                ],
                axis=0,
            )
            full = dot_nt(block, both)
            small = (full[:, :wide] + full[:, wide:]).astype(BF16)
            ordered = dot(pick, small).astype(BF16)
            at = (4 * time + 2 * row) * cells
            out_ref[at : at + size, :] = ordered

    copies[1].wait()
    copies[2].wait()
    project(1)
    copies[3].wait()
    classes = [
        parity_rows(x_ref[frames - 1, :, line].reshape(half * side, channels), pick_ref[...])
        for line in range(2)
    ]
    copies[4].wait()
    halo_ref[pl.ds(0, half * half), :] = folded_taps(
        lambda line, column: classes[line][column],
        lambda b, c: first_ref[3 * b + c],
        shift_ref,
        half,
    )
    copies[5].wait()
    copies[6].wait()
    project(0)
    copies[7].wait()
    grad_rows = stacked_rows(grad_ref, rows_ref)
    count = grad_rows.shape[0]
    for block in range(channels // wide):
        at = 8 * cells + block * count
        out_ref[at : at + count, :] = grad_rows[:, block * wide : (block + 1) * wide]
        at = half * half + block * count
        halo_ref[at : at + count, :] = rows_ref[:, block * wide : (block + 1) * wide]


def stacked_rows(grad_ref, rows_ref):
    quarter = grad_ref.shape[0]
    for row in range(quarter):
        rows_ref[pl.ds(row * quarter, quarter), :] = grad_ref[row].astype(F32)
    return rows_ref[...].astype(BF16)


def transposed_products(rows, kernel, taps):
    total = dot_nt(rows[0], kernel[taps[0]])
    for at in range(1, len(taps)):
        total += dot_nt(rows[at], kernel[taps[at]])
    return total


def spread_rows(picks_ref, rows, cells):
    spread = dot(picks_ref[...], rows).astype(BF16)
    return [spread[tap * cells : (tap + 1) * cells] for tap in range(9)]


def hidden_kernel(
    tm_ref, x_ref, prior_ref, grad_ref, later_ref, pick_ref, spread_ref,
    first_any, second_any, out_ref, rows_ref, classes, first, second, shift_ref, arrived, *,
    clip_parts,
):
    frames, half, _, side, channels = x_ref.shape
    cells = half * half
    has_prior = jnp.where(tm_ref[0] > 0, 1.0, 0.0)
    has_later = jnp.where(tm_ref[0] < clip_parts - 1, 1.0, 0.0)
    copies = {
        (at, a): pltpu.make_async_copy(
            source.at[pl.ds(9 * a, 9)], target.at[pl.ds(9 * a, 9)], arrived.at[at, a]
        )
        for at, (source, target) in enumerate(((second_any, second), (first_any, first)))
        for a in (1, 2, 0)
    }
    for copy in copies.values():
        copy.start()
    own_rows = stacked_rows(grad_ref, rows_ref)
    own = spread_rows(spread_ref, own_rows, cells)
    copies[0, 1].wait()
    copies[0, 2].wait()
    both = None
    for tap in range(9):
        pair = jnp.concatenate([second[9 + tap], second[18 + tap]], axis=0)
        term = dot_nt(own[tap], pair)
        both = term if both is None else both + term
    early, late = both[:, : second.shape[1]], both[:, second.shape[1] :]
    for frame in range(frames):
        for line in range(2):
            lines = x_ref[frame, :, line].reshape(half * side, channels)
            classes[frame, line, 0], classes[frame, line, 1] = parity_rows(lines, pick_ref[...])
    count = own_rows.shape[0]
    wide = first.shape[2]
    later_rows = jnp.concatenate(
        [
            later_ref[pl.ds(cells + count * block, count), :]
            for block in range(channels // wide)
        ],
        axis=1,
    )
    after = spread_rows(spread_ref, later_rows.astype(BF16), cells)
    copies[0, 0].wait()
    late += transposed_products(after, second, range(9)) * has_later
    hidden_grad = jnp.concatenate([early, late], axis=0)
    nothing = jnp.zeros((cells, channels), BF16)

    def rows_of(line, column):
        held = [classes[frame, line, column] for frame in range(frames)]
        return jnp.concatenate(
            [
                jnp.concatenate([nothing, held[0], held[1]], axis=1),
                jnp.concatenate([held[1], held[2], held[3]], axis=1),
            ],
            axis=0,
        )

    for a in (1, 2, 0):
        copies[1, a].wait()
    pre = folded_taps(
        rows_of,
        lambda b, c: jnp.concatenate([first[9 * a + 3 * b + c] for a in range(3)], axis=0),
        shift_ref,
        half,
    )
    pre += jnp.concatenate(
        [prior_ref[pl.ds(0, cells), :] * has_prior, jnp.zeros((cells, wide), F32)], axis=0
    )
    sig = jax.nn.sigmoid(pre)
    hidden = (pre * sig).astype(BF16)
    pre_grad = (hidden_grad * sig * (1.0 + pre * (1.0 - sig))).astype(BF16)
    groups, slices, _, share, _ = out_ref.shape
    for at in range(slices):
        place = slice(at * share, (at + 1) * share)
        for group in range(groups):
            out_ref[group, at, 0] = pre_grad[place]
            out_ref[group, at, 1] = hidden[place]


def right_kernel(place_ref, core_ref, *refs, cores):
    acts_refs, right_refs, out_ref = refs[:cores], refs[cores:-1], refs[-1]
    parts, slices = acts_refs[0].shape[:2]
    width = right_refs[0].shape[2]
    for layer in range(2):
        rights = [
            jnp.concatenate(halves(ref[at, layer]), axis=0)
            for ref in right_refs
            for at in range(ref.shape[0])
        ]
        for cross, acts_ref in enumerate(acts_refs):
            total = None
            for distance in range(slices):
                origin = factor_origin(place_ref[0], distance, slices)
                rows = jnp.concatenate(
                    [acts_ref[part, origin, layer] for part in range(parts)], axis=0
                )
                term = dot_nt(rights[distance], rows)
                total = term if total is None else total + term
            core = lax.rem(core_ref[0] + cross, cores)
            out_ref[core, pl.ds(layer * width, width), :] = (total[:width] + total[width:]).astype(
                BF16
            )


def tables_kernel(after_any, mix_ref, shift_ref, sort_ref, mixers_ref, *, slices, clip_parts, half):
    del after_any
    size = shift_ref.shape[0]
    cells = size // clip_parts
    share = cells // slices
    frames = size // (half * half)
    held = lax.broadcasted_iota(jnp.int32, (size, size), 0)
    cell = lax.broadcasted_iota(jnp.int32, (size, size), 1)
    part = remainder(quotient(held, share), clip_parts)
    slot = quotient(held, share * clip_parts)
    natural = part * cells + slot * share + remainder(held, share)
    frame = quotient(cell, half * half)
    row = remainder(quotient(cell, half), half)
    column = remainder(cell, half)
    for shift in range(8):
        dt, dr, dc = shift // 4, shift // 2 % 2, shift % 2
        found = natural == cell + ((dt * half + dr) * half + dc)
        if dt:
            found &= frame < frames - 1
        if dr:
            found &= row < half - 1
        if dc:
            found &= column < half - 1
        shift_ref[:, pl.ds(shift * size, size)] = jnp.where(found, 1.0, 0.0).astype(BF16)
    quarter = half // 2
    outputs = size // 8
    kind = quotient(cell, outputs)
    frame = 2 * remainder(quotient(cell, quarter * quarter), frames // 2) + quotient(kind, 4)
    row = 2 * remainder(quotient(cell, quarter), quarter) + remainder(quotient(kind, 2), 2)
    column = 2 * remainder(cell, quarter) + remainder(kind, 2)
    found = natural == (frame * half + row) * half + column
    sort_ref[...] = jnp.where(found, 1.0, 0.0).astype(BF16)

    count = mixers_ref.shape[2]
    tap = lax.broadcasted_iota(jnp.int32, (count, TAPS), 1)
    line = lax.broadcasted_iota(jnp.int32, (count, TAPS), 0)
    spread = jnp.where(quotient(line, 8) == tap, 1.0, 0.0).astype(BF16)
    lines = lax.broadcasted_iota(jnp.int32, (count, count), 0)
    others = lax.broadcasted_iota(jnp.int32, (count, count), 1)
    same = remainder(lines, 8) == remainder(others, 8)
    for layer in range(2):
        for at, part in enumerate(halves(mix_ref[layer])):
            wider = dot_nt(dot(spread, part).astype(BF16), spread)
            mixers_ref[layer, at] = jnp.where(same, wider, 0.0).astype(BF16)


def update_kernel(
    place_ref, chip_ref, core_ref, tm_ref, *refs, slices, cores, clip_parts, half
):
    columns_refs, piece_refs = refs[:slices], refs[slices : slices + cores]
    (
        left_ref, mixers_ref, shift_ref, sort_ref,
        out_ref, left_rows_ref, columns, shifts, grads, raw, arrived,
    ) = refs[slices + cores :]
    parts = left_rows_ref.shape[0]
    chips = parts // (cores * clip_parts)
    copies = []
    for cross, piece_ref in enumerate(piece_refs):
        core = lax.rem(core_ref[0] + cross, cores)
        for at, (step, turn) in enumerate(np.ndindex(chips, clip_parts)):
            chip = lax.rem(chip_ref[0] + (chips - step), chips)
            place = lax.rem(tm_ref[0] + (clip_parts - turn), clip_parts)
            target = left_rows_ref.at[(chip * cores + core) * clip_parts + place]
            copies.append(
                pltpu.make_async_copy(piece_ref.at[at], target, arrived.at[len(copies)])
            )
    for copy in copies:
        copy.start()
    for distance in range(slices):
        origin = lax.rem(place_ref[0] + (slices - distance), slices)
        columns[origin] = columns_refs[distance][...]
    wide, channels = left_ref.shape[1:]
    width = columns.shape[2] // 2
    clips = parts // clip_parts
    share = columns.shape[3] // chips
    clip_cells = slices * share
    cells = clip_cells // clip_parts
    frames = clip_cells // (half * half)
    outputs = clip_cells // 8

    def by_clip(layer):
        return jnp.concatenate(
            [
                jnp.concatenate(
                    [
                        columns[
                            at, clip % cores, pl.ds(layer * width, width),
                            pl.ds(clip // cores * share, share),
                        ]
                        for at in range(slices)
                    ],
                    axis=1,
                )
                for clip in range(clips)
            ],
            axis=0,
        )

    first = by_clip(0)
    for shift in range(8):
        moved = dot(first, shift_ref[:, pl.ds(shift * clip_cells, clip_cells)]).astype(BF16)
        for clip in range(clips):
            shifts[shift, clip] = moved[clip * width : (clip + 1) * width]
    second = dot(by_clip(1), sort_ref[...]).astype(BF16)

    for copy in copies:
        copy.wait()
    own_outputs = outputs // clip_parts
    blocks = channels // wide
    out_grad = jnp.concatenate(
        [
            jnp.concatenate(
                [
                    left_rows_ref[part, pl.ds(8 * cells + own_outputs * at, own_outputs), :]
                    for at in range(blocks)
                ],
                axis=1,
            )
            for part in range(parts)
        ],
        axis=0,
    )
    full = dot_nt(out_grad, jnp.concatenate(halves(left_ref[1]), axis=0))
    total = parts * own_outputs
    quarter = half // 2
    grads[pl.ds(0, total), :] = full[:, :wide] + full[:, wide:]
    places = lax.broadcasted_iota(jnp.int32, (total, wide), 0)
    frame = remainder(quotient(places, quarter * quarter), frames // 2)
    row = remainder(quotient(places, quarter), quarter)
    column = remainder(places, quarter)
    second_rows = []
    for shift in range(8):
        dt, dr, dc = shift // 4, shift // 2 % 2, shift % 2
        moved = grads[pl.ds((dt * quarter + dr) * quarter + dc, total), :]
        inside = (frame + dt < frames // 2) & (row + dr < quarter) & (column + dc < quarter)
        second_rows.append(jnp.where(inside, moved, 0.0).astype(BF16))

    for time, line in np.ndindex(2, 2):
        even = [
            (9 * a + 3 * b + 1, 4 * (a == 0) + 2 * (b == 0))
            for a in ((0, 2) if time else (1,))
            for b in ((0, 2) if line else (1,))
        ]
        odd = [(tap + 1, shift) for tap, shift in even] + [
            (tap - 1, shift + 1) for tap, shift in even
        ]
        kind = 4 * time + 2 * line
        sums = None
        for clip in range(clips):
            left = jnp.concatenate([shifts[shift, clip] for _, shift in odd], axis=0)
            rows = jnp.concatenate(
                [
                    jnp.concatenate(
                        [
                            left_rows_ref[
                                clip * clip_parts + part, pl.ds((kind + at) * cells, cells), :
                            ]
                            for part in range(clip_parts)
                        ],
                        axis=0,
                    )
                    for at in range(2)
                ],
                axis=1,
            )
            term = dot(left, rows)
            sums = term if sums is None else sums + term
        for at, (tap, _) in enumerate(even):
            raw[0, tap] = sums[at * width : (at + 1) * width, :wide]
        for at, (tap, _) in enumerate(odd):
            raw[0, tap] = sums[at * width : (at + 1) * width, wide:]
        for place, taps in enumerate((even, odd)):
            chosen = jnp.concatenate(
                [
                    second[
                        clip * width : (clip + 1) * width,
                        (kind + place) * outputs : (kind + place + 1) * outputs,
                    ]
                    for clip in range(clips)
                ],
                axis=1,
            )
            products = dot(
                chosen, jnp.concatenate([second_rows[shift] for _, shift in taps], axis=1)
            )
            for at, (tap, _) in enumerate(taps):
                raw[1, tap] = products[:, at * wide : (at + 1) * wide]

    for layer in range(2):
        for group in range(width // 16):
            lanes = jnp.concatenate(
                [
                    raw[layer, :, pl.ds(16 * group + 8 * at, 8), :].reshape(8 * TAPS, wide)
                    for at in range(2)
                ],
                axis=1,
            )
            high, low = halves(lanes)
            mixed = (
                dot(mixers_ref[layer, 0], high)
                + dot(mixers_ref[layer, 0], low)
                + dot(mixers_ref[layer, 1], high)
            )
            rows = jnp.concatenate(
                [
                    mixed[:, at * wide : (at + 1) * wide].reshape(TAPS, 8, wide)
                    for at in range(2)
                ],
                axis=1,
            )
            out_ref[layer, :, pl.ds(16 * group, 16), :] = rows.astype(BF16)


def turned(block, axes, steps):
    sizes = [lax.axis_size(axis) for axis in axes]
    if not any(step % size for step, size in zip(steps, sizes)):
        return block
    route = []
    for place in np.ndindex(*sizes):
        target = [(at + step) % size for at, step, size in zip(place, steps, sizes)]
        route.append(
            (int(np.ravel_multi_index(place, sizes)), int(np.ravel_multi_index(target, sizes)))
        )
    return lax.ppermute(block, axes, route)


def doubled(size):
    return size & (size - 1) == 0


def first_round(block):
    size = lax.axis_size("fsdp")
    if not doubled(size):
        return [block] + [turned(block, ("fsdp",), (distance,)) for distance in range(1, size)]
    if size == 1:
        return [block]
    return [block, lax.ppermute(block, "fsdp", [(i, i ^ 1) for i in range(size)])]


def later_rounds(blocks):
    size = lax.axis_size("fsdp")
    held = [block[None] for block in blocks]
    step = 2
    while doubled(size) and step < size:
        route = [(i, i ^ step) for i in range(size)]
        held.append(lax.ppermute(jnp.concatenate(held, axis=0), "fsdp", route))
        step *= 2
    return held


def factor_origin(place, distance, size):
    if doubled(size):
        return place ^ distance
    return lax.rem(place + (size - distance), size)


def shards(clip_input, first_kernel, second_kernel, out_grad, tap_mix, left_panels, right_panels):
    clips, frames, side, _, channels = clip_input.shape
    wide = first_kernel.shape[2]
    width = right_panels.shape[2]
    half, quarter = side // 2, side // 4
    half_frames = frames // 2
    cells = half_frames * half * half
    clip_parts = lax.axis_size("tm")
    cores, chips = lax.axis_size("core"), lax.axis_size("chip")
    equals = chips * clip_parts
    parts = equals * cores
    slices = lax.axis_size("fsdp")
    share = cells // slices
    assert clips == 1 and frames == 4
    x = clip_input.reshape(frames, half, 2, side, channels)
    grad = out_grad.reshape(quarter, quarter, channels)
    place, chip_at, core_at, half_at = (
        lax.axis_index(axis).reshape(1) for axis in ("fsdp", "chip", "core", "tm")
    )

    pick = jnp.asarray(column_picks(side), BF16)
    pad = (half // 8 + 1) * 8
    rows = quarter * quarter * channels // wide
    projected, halo = pl.pallas_call(
        project_kernel,
        out_shape=(
            jax.ShapeDtypeStruct((8 * cells + rows, wide), BF16),
            jax.ShapeDtypeStruct((half * half + rows, wide), F32),
        ),
        in_specs=[ANY] * 5,
        out_specs=(VMEM, VMEM),
        scratch_shapes=[
            pltpu.VMEM(x.shape, BF16),
            pltpu.VMEM(left_panels.shape[1:], F32),
            pltpu.VMEM(grad.shape, BF16),
            pltpu.VMEM(pick.shape, BF16),
            pltpu.VMEM((9,) + first_kernel.shape[1:], BF16),
            pltpu.VMEM((quarter * quarter, channels), F32),
            pltpu.VMEM((3, pad + half * half, wide), F32),
            pltpu.SemaphoreType.DMA((8,)),
        ],
        compiler_params=pltpu.CompilerParams(vmem_limit_bytes=58 << 20),
        cost_estimate=pl.CostEstimate(
            flops=4 * frames * side * side * channels * wide,
            bytes_accessed=PROJECT_COST,
            transcendentals=0,
        ),
    )(x, left_panels, grad, pick, first_kernel)
    if clip_parts == 2:
        prior = later = lax.ppermute(halo, "tm", [(0, 1), (1, 0)])
    else:
        prior, later = shifted(halo, "tm", 1), shifted(halo, "tm", -1)
    right = right_panels.transpose(0, 2, 1)
    right = first_round(right)
    projected, right = lax.optimization_barrier((projected, right))
    prior, later, right = lax.optimization_barrier((prior, later, right))
    right = later_rounds(right)
    held = jnp.stack(
        [
            turned(projected, ("chip", "tm"), steps)
            for steps in np.ndindex(chips, clip_parts)
        ]
    )

    spread = jnp.asarray(spread_picks(half), BF16)
    acts = pl.pallas_call(
        functools.partial(hidden_kernel, clip_parts=clip_parts),
        out_shape=jax.ShapeDtypeStruct((equals, slices, 2, share, wide), BF16),
        in_specs=[SMEM] + [VMEM] * 6 + [HBM] * 2,
        out_specs=VMEM,
        scratch_shapes=[
            pltpu.VMEM((quarter * quarter, channels), F32),
            pltpu.VMEM((frames, 2, 2, half * half, channels), BF16),
            pltpu.VMEM(first_kernel.shape, BF16),
            pltpu.VMEM(second_kernel.shape, BF16),
            pltpu.VMEM((3, pad + cells, wide), F32),
            pltpu.SemaphoreType.DMA((2, 3)),
        ],
        compiler_params=pltpu.CompilerParams(vmem_limit_bytes=ROOM),
        cost_estimate=pl.CostEstimate(
            flops=3 * cells * TAPS * channels * wide,
            bytes_accessed=HIDDEN_COST,
            transcendentals=cells * wide,
        ),
    )(
        half_at, x, prior, grad, later, pick, spread, first_kernel, second_kernel,
    )
    acts, *right = lax.optimization_barrier((acts, *right))
    clip_cells = clip_parts * cells
    shift_picks, sort_picks, mixers = pl.pallas_call(
        functools.partial(tables_kernel, slices=slices, clip_parts=clip_parts, half=half),
        out_shape=(
            jax.ShapeDtypeStruct((clip_cells, 8 * clip_cells), BF16),
            jax.ShapeDtypeStruct((clip_cells, clip_cells), BF16),
            jax.ShapeDtypeStruct((2, 2, 8 * TAPS, 8 * TAPS), BF16),
        ),
        in_specs=[ANY, VMEM],
        out_specs=(VMEM,) * 3,
        compiler_params=pltpu.CompilerParams(vmem_limit_bytes=16 << 20),
        cost_estimate=pl.CostEstimate(flops=0, bytes_accessed=4 << 20, transcendentals=0),
    )(acts, tap_mix)
    every = lax.all_to_all(
        acts.reshape(equals * slices, 2, share, wide), ("chip", "tm", "fsdp"), 0, 0, tiled=True
    ).reshape(equals, slices, 2, share, wide)
    every, held = lax.optimization_barrier((every, held))
    every = [turned(every, ("core",), (cross,)) for cross in range(cores)]
    columns = pl.pallas_call(
        functools.partial(right_kernel, cores=cores),
        out_shape=jax.ShapeDtypeStruct((cores, 2 * width, equals * share), BF16),
        in_specs=[SMEM] * 2 + [VMEM] * (cores + len(right)),
        out_specs=VMEM,
        compiler_params=pltpu.CompilerParams(vmem_limit_bytes=16 << 20),
    )(place, core_at, *every, *right)
    columns, held = lax.optimization_barrier((columns, held))
    columns = [turned(columns, ("fsdp",), (distance,)) for distance in range(slices)]
    left_rows = [turned(held, ("core",), (cross,)) for cross in range(cores)]

    result = pl.pallas_call(
        functools.partial(
            update_kernel, slices=slices, cores=cores, clip_parts=clip_parts, half=half
        ),
        out_shape=jax.ShapeDtypeStruct((2, TAPS, width, wide), BF16),
        in_specs=[SMEM] * 4
        + [VMEM] * len(columns)
        + [ANY] * cores
        + [VMEM] * 4,
        out_specs=VMEM,
        scratch_shapes=[
            pltpu.VMEM((parts,) + projected.shape, BF16),
            pltpu.VMEM((slices, cores, 2 * width, equals * share), BF16),
            pltpu.VMEM((8, parts // clip_parts, width, clip_cells), BF16),
            pltpu.VMEM((parts * cells // 8 + (quarter + 1) * quarter + 8, wide), F32),
            pltpu.VMEM((2, TAPS, width, wide), F32),
            pltpu.SemaphoreType.DMA((parts,)),
        ],
        compiler_params=pltpu.CompilerParams(vmem_limit_bytes=40 << 20),
    )(
        place, chip_at, core_at, half_at,
        *columns, *left_rows, left_panels, mixers, shift_picks, sort_picks,
    )
    return result.transpose(0, 1, 3, 2)


def solution(mesh):
    fsdp, replica, tm = (mesh.shape[axis] for axis in ("fsdp", "replica", "tm"))
    cores = 2 if replica % 2 == 0 else 1
    assert mesh.axis_names == ("fsdp", "replica", "tm")
    mesh = Mesh(
        mesh.devices.reshape(fsdp, replica // cores, cores, tm), ("fsdp", "chip", "core", "tm")
    )
    replica = ("chip", "core")
    in_specs = (
        P(replica, "tm", None, None, None),
        P(None, None, "fsdp"),
        P(None, "fsdp", None),
        P(replica, "tm", None, None, None),
        P(),
        P(None, "fsdp", None),
        P(None, "fsdp", (*replica, "tm")),
    )
    out_specs = P(None, None, "fsdp", (*replica, "tm"))
    return jax.shard_map(shards, mesh=mesh, in_specs=in_specs, out_specs=out_specs, check_vma=False)
```
